32 devices in a mesh: row: 8 (over y, x, core), col: 4 (over z).
Axes of the slice: x: 2, y: 2, z: 4, core: 2. Of those that a mesh axis runs over, the one named last changes fastest.
Arguments:
- features: bfloat16 [64, 512, 256], P('row', 'col'), may hold values from -6 to 6
- target: bfloat16 [64, 512, 256], P('row', 'col'), may hold values from -6 to 6
- hole_mask: int32 [64, 512], P('row', 'col'), may hold values 0 or 1
- kernel_first: bfloat16 [3, 3, 256, 256], replicated, may hold values from -0.125 to 0.125
- kernel_second: bfloat16 [3, 3, 256, 256], replicated, may hold values from -0.125 to 0.125
- inputs: bfloat16 [64, 512, 512], P(('row', 'col')), may hold values from -6 to 6
- weight_in: bfloat16 [512, 192], replicated, may hold values from -0.25 to 0.25
- weight_out: bfloat16 [192, 256], replicated, may hold values from -0.4375 to 0.4375
- weight_local: bfloat16 [512, 256], replicated, may hold values from -0.25 to 0.25
- weight_mix: bfloat16 [384, 384], replicated, may hold values from -0.3125 to 0.3125
Outputs:
- grad_inputs: bfloat16 [64, 512, 512], P(('row', 'col'))
The draws below stay inside these ranges and needn't reach their ends.
Inputs may be any that keep to these rules, and one draw needn't show every extreme that they name: `hole_mask`: 1 marks a pixel to be filled.
All inputs are finite; a program needn't handle non-finite values. No bound on the sum of `hole_mask` on one device may be relied on, other than what follows from the above.
Results may differ from the reference program's by a relative error of at most 0.0095.
Values may be sent and summed in bfloat16 or wider, within the bound.
No kernel may reach another device: no remote copies, remote signals or barrier semaphores. Data moves between devices by JAX's collectives and lax.ppermute only.
A program may use at most 64 MiB of HBM per device.

```python
import math
import jax
import jax.numpy as jnp
from jax import lax

C1 = 256
CF = 512
S = 192
H = 64
W = 512


def set_ends(result, key, smallest, high):
    longest = result.shape.index(max(result.shape))
    spots = []
    for shift in (0, 1):
        where = [jax.random.randint(jax.random.fold_in(key, axis), (), 0, length) for axis, length in enumerate(result.shape)]
        where[longest] = (where[longest] + shift) % result.shape[longest]
        spots.append(tuple(where))
    return result.at[spots[0]].set(smallest).at[spots[1]].set(high)


def level_of(key, shape, cuts, low, largest):
    factor_of, own = 1.0, jax.random.fold_in(key, 6)
    for dim, shards_of in cuts:
        draws = jnp.exp(jax.random.uniform(jax.random.fold_in(own, dim), (shards_of,), jnp.float32, low / len(cuts), largest / len(cuts)))
        factor_of = factor_of * jnp.repeat(draws, shape[dim] // shards_of).reshape([-1 if axis == dim else 1 for axis in range(len(shape))])
    return factor_of


def noise(stream_key, extent, deviation, most, pieces=(), held_as=jnp.bfloat16):
    level = level_of(stream_key, extent, pieces, -0.22, 0.18) if pieces else 1.0
    values = jax.random.normal(stream_key, extent, jnp.float32) * deviation * level
    return jnp.minimum(jnp.maximum(values, -most), most).astype(held_as)


def setup_inputs(seed: int = 0) -> dict:
    splits = jax.random.split(jax.random.key(seed), 11)
    return {
        "features": noise(splits[0], (H, W, C1), 1.0, 6.0, ((0, 8), (1, 4))),
        "target": noise(splits[1], (H, W, C1), 1.0, 6.0, ((0, 8), (1, 4))),
        "hole_mask": set_ends((jax.random.randint(splits[2], (H, W), 0, 2) < 1).astype(jnp.int32), jax.random.fold_in(splits[2], 1), 0, 1),
        "kernel_first": noise(splits[3], (3, 3, C1, C1), (9 * C1) ** -0.5, 0.125),
        "kernel_second": noise(splits[4], (3, 3, C1, C1), (9 * C1) ** -0.5, 0.125),
        "inputs": noise(splits[5], (H, W, CF), 1.0, 6.0, ((0, 32),)),
        "weight_in": noise(splits[6], (CF, S), CF ** -0.5, 0.25),
        "weight_out": noise(splits[7], (S, C1), S ** -0.5, 0.4375),
        "weight_local": noise(splits[8], (CF, C1), CF ** -0.5, 0.25),
        "weight_mix": noise(splits[9], (2 * S, 2 * S), (2 * S) ** -0.5, 0.3125),
    }


def conv_valid(padded, kernel):
    output = lax.conv_general_dilated(padded[None].astype(jnp.float32), kernel.astype(jnp.float32), (1, 1), 'VALID', rhs_dilation=(2, 2), dimension_numbers=('NHWC', 'HWIO', 'NHWC'))
    return output[0]

def same_conv(signal, kernel):
    padded = jnp.pad(signal, ((2, 2), (2, 2), (0, 0)))
    return conv_valid(padded, kernel)

def adjoint_kernel(kernel):
    return jnp.transpose(jnp.flip(kernel, (0, 1)), (0, 1, 3, 2))

def silu_slope(pre_value):
    sigmoid_value = jax.nn.sigmoid(pre_value)
    return sigmoid_value * (1.0 + pre_value * (1.0 - sigmoid_value))

def dft_tables(first_ids, second_ids, length):
    phases = first_ids[:, None] * second_ids[None, :] % length
    angles = phases.astype(jnp.float32) * (2.0 * math.pi / length)
    return (jnp.cos(angles).astype(jnp.bfloat16), jnp.sin(angles).astype(jnp.bfloat16))

def column_tables(grid_width):
    freq_ids = jnp.arange(grid_width // 2, dtype=jnp.int32)
    col_ids = jnp.arange(grid_width, dtype=jnp.int32)
    cos_table, sin_table = dft_tables(freq_ids, col_ids, grid_width)
    alternate = (2 * (col_ids % 2) - 1).astype(jnp.float32).astype(jnp.bfloat16)
    sin_table = jnp.where((freq_ids == 0)[:, None], alternate[None, :], sin_table)
    return (cos_table, sin_table)

def column_transform(signal, cos_table, sin_table, norm_factor):
    cosine_part = jnp.einsum('rws,kw->rks', signal.astype(jnp.float32), cos_table.astype(jnp.float32))
    sine_part = jnp.einsum('rws,kw->rks', signal.astype(jnp.float32), sin_table.astype(jnp.float32))
    return (jnp.concatenate([cosine_part, -sine_part], axis=-1) * norm_factor).astype(jnp.bfloat16)

def row_forward(spectrum, cos_table, sin_table, norm_factor, half_width):
    cosine_part = jnp.einsum('kp,pmc->kmc', cos_table.astype(jnp.float32), spectrum.astype(jnp.float32))
    sine_part = jnp.einsum('kp,pmc->kmc', sin_table.astype(jnp.float32), spectrum.astype(jnp.float32))
    real_part = cosine_part[..., :half_width] + sine_part[..., half_width:]
    imag_part = cosine_part[..., half_width:] - sine_part[..., :half_width]
    return jnp.concatenate([real_part, imag_part], axis=-1) * norm_factor

def row_inverse(spectrum, cos_table, sin_table, norm_factor, half_width):
    cosine_part = jnp.einsum('kp,kmc->pmc', cos_table.astype(jnp.float32), spectrum.astype(jnp.float32))
    sine_part = jnp.einsum('kp,kmc->pmc', sin_table.astype(jnp.float32), spectrum.astype(jnp.float32))
    real_part = cosine_part[..., :half_width] - sine_part[..., half_width:]
    imag_part = cosine_part[..., half_width:] + sine_part[..., :half_width]
    return (jnp.concatenate([real_part, imag_part], axis=-1) * norm_factor).astype(jnp.bfloat16)

def column_inverse(spectrum, cos_table, sin_table, norm_factor, half_width):
    cosine_part = jnp.einsum('rks,kw->rws', spectrum[..., :half_width].astype(jnp.float32), cos_table.astype(jnp.float32))
    sine_part = jnp.einsum('rks,kw->rws', spectrum[..., half_width:].astype(jnp.float32), sin_table.astype(jnp.float32))
    return ((cosine_part - sine_part) * norm_factor).astype(jnp.bfloat16)

def reference(features, target, hole_mask, kernel_first, kernel_second, inputs, weight_in, weight_out, weight_local, weight_mix):
    pre_first = same_conv(features, kernel_first)
    act_first = jax.nn.silu(pre_first).astype(jnp.bfloat16)
    pre_second = same_conv(act_first, kernel_second)
    hole_weight = 1.0 + 2.0 * hole_mask.astype(jnp.float32)
    loss_grad = (hole_weight[:, :, None] * (pre_second - target.astype(jnp.float32))).astype(jnp.bfloat16)
    grad_act = same_conv(loss_grad, adjoint_kernel(kernel_second))
    grad_pre = (grad_act * silu_slope(pre_first)).astype(jnp.bfloat16)
    grad_feat = same_conv(grad_pre, adjoint_kernel(kernel_first)).astype(jnp.bfloat16)
    spatial = jnp.einsum('rwf,fs->rws', inputs.astype(jnp.float32), weight_in.astype(jnp.float32)).astype(jnp.bfloat16)
    grad_spec = jnp.einsum('rwc,sc->rws', grad_feat.astype(jnp.float32), weight_out.astype(jnp.float32)).astype(jnp.bfloat16)
    grad_local = jnp.einsum('rwc,fc->rwf', grad_feat.astype(jnp.float32), weight_local.astype(jnp.float32))
    row_ids = jnp.arange(H, dtype=jnp.int32)
    cos_cols, sin_cols = column_tables(W)
    cos_rows, sin_rows = dft_tables(row_ids, row_ids, H)
    col_factor = 1.0 / math.sqrt(W)
    row_factor = 1.0 / math.sqrt(H)
    spatial_cols = column_transform(spatial, cos_cols, sin_cols, col_factor)
    grad_cols = column_transform(grad_spec, cos_cols, sin_cols, col_factor)
    spatial_freq = row_forward(spatial_cols, cos_rows, sin_rows, row_factor, S)
    grad_freq = row_forward(grad_cols, cos_rows, sin_rows, row_factor, S)
    pre_mix = jnp.einsum('kmc,cd->kmd', spatial_freq.astype(jnp.bfloat16).astype(jnp.float32), weight_mix.astype(jnp.float32))
    grad_mix = (grad_freq * silu_slope(pre_mix)).astype(jnp.bfloat16)
    grad_back = jnp.einsum('kmd,cd->kmc', grad_mix.astype(jnp.float32), weight_mix.astype(jnp.float32)).astype(jnp.bfloat16)
    grad_rows = row_inverse(grad_back, cos_rows, sin_rows, row_factor, S)
    grad_spatial = column_inverse(grad_rows, cos_cols, sin_cols, col_factor, S)
    grad_total = jnp.einsum('rws,fs->rwf', grad_spatial.astype(jnp.float32), weight_in.astype(jnp.float32)) + grad_local
    return grad_total.astype(jnp.bfloat16)
```

```python
import functools
import math

import jax
import jax.numpy as jnp
import ml_dtypes
import numpy as np
from jax import lax
from jax.experimental import pallas as pl
from jax.experimental.pallas import tpu as pltpu
from jax.sharding import PartitionSpec as P

REACH = 8
LIMIT = 56 * 1024 * 1024


def dot(left, right):
    return jnp.dot(left, right, preferred_element_type=jnp.float32)


def dot_t(left, right):
    return lax.dot_general(left, right, (((1,), (1,)), ((), ())), preferred_element_type=jnp.float32)


def vmem_call(body, shapes, *operands, flops=0):
    spec = pl.BlockSpec(memory_space=pltpu.VMEM)
    size = sum(math.prod(a.shape) * a.dtype.itemsize for a in (*operands, *shapes))
    return pl.pallas_call(
        body,
        out_shape=shapes,
        in_specs=[spec] * len(operands),
        out_specs=[spec] * len(shapes),
        compiler_params=pltpu.CompilerParams(vmem_limit_bytes=LIMIT),
        cost_estimate=pl.CostEstimate(flops=flops, bytes_accessed=size, transcendentals=0),
    )(*operands)


def phases(first, second, length):
    angle = (first[:, None] * second[None, :] % length) * (2.0 * math.pi / length)
    return np.cos(angle).astype(ml_dtypes.bfloat16), np.sin(angle).astype(ml_dtypes.bfloat16)


def column_matrix(width, devices):
    half = width // 2
    freq, col = np.arange(half), np.arange(width)
    cos, sin = phases(freq, col, width)
    sin[0] = (2 * (col % 2) - 1).astype(ml_dtypes.bfloat16)
    both = np.stack([cos, -sin]).reshape(2, devices, half // devices, width)
    return np.ascontiguousarray(both.transpose(1, 0, 2, 3)).reshape(width, width)


def row_matrices(height, devices, owned):
    strip = height // devices
    result = []
    for row in range(strip):
        cos, sin = phases(np.arange(height), np.arange(devices) * strip + row, height)
        out = np.zeros((2, height, owned, devices, 2, owned), ml_dtypes.bfloat16)
        for freq in range(owned):
            out[0, :, freq, :, 0, freq] = cos
            out[0, :, freq, :, 1, freq] = sin
            out[1, :, freq, :, 0, freq] = -sin
            out[1, :, freq, :, 1, freq] = cos
        result.append(out.reshape(2 * height * owned, devices * 2 * owned))
    return result


def spectrum_kernel(transposed, norm, signal, weight, table, out):
    product = dot_t if transposed else dot
    rows = [product(signal[r], weight[...]).astype(jnp.bfloat16) for r in range(signal.shape[0])]
    out[...] = (dot(table[...], jnp.concatenate(rows, axis=1)) * norm).astype(jnp.bfloat16)


def row_spectrum(moved, tables, norm):
    half = moved.shape[1] // len(tables)
    total = 0.0
    for r, table in enumerate(tables):
        total = total + dot(table[...], moved[:, r * half : (r + 1) * half])
    cells = total.shape[0] // 2
    return total[:cells] * norm, total[cells:] * norm


def slope_kernel(norm, moved, mix, *rest):
    *tables, out = rest
    real, imag = row_spectrum(moved, tables, norm)
    half = real.shape[1]
    pre = dot(real.astype(jnp.bfloat16), mix[:half]) + dot(imag.astype(jnp.bfloat16), mix[half:])
    s = 1.0 / (1.0 + jnp.exp(-pre))
    out[...] = s * (1.0 + pre * (1.0 - s))


def mix_kernel(norm, strip, moved, slope, mix, *rest):
    *tables, out = rest
    real, imag = row_spectrum(moved, tables[:strip], norm)
    half = real.shape[1]
    grad = jnp.concatenate([real, imag], axis=1) * slope[...]
    back = dot_t(grad.astype(jnp.bfloat16), mix[...]).astype(jnp.bfloat16)
    stacked = jnp.concatenate([back[:, :half], back[:, half:]], axis=0)
    rows = [dot(table[...], stacked) for table in tables[strip:]]
    out[...] = (jnp.concatenate(rows, axis=1) * norm).astype(jnp.bfloat16)


def output_kernel(norm, moved, strip_grad, weight_in, weight_local, table, out):
    spatial = (dot(table[...], moved[...]) * norm).astype(jnp.bfloat16)
    half = weight_in.shape[1]
    for r in range(strip_grad.shape[0]):
        total = dot_t(spatial[:, r * half : (r + 1) * half], weight_in[...])
        total = total + dot_t(strip_grad[r], weight_local[...])
        out[r] = total.astype(jnp.bfloat16)


def conv_valid(padded, kernel):
    output = lax.conv_general_dilated(
        padded[None],
        kernel,
        (1, 1),
        "VALID",
        rhs_dilation=(2, 2),
        dimension_numbers=("NHWC", "HWIO", "NHWC"),
        preferred_element_type=jnp.float32,
    )
    return output[0]


def adjoint_kernel(kernel):
    return jnp.transpose(jnp.flip(kernel, (0, 1)), (0, 1, 3, 2))


def silu_slope(pre_value):
    sigmoid_value = jax.nn.sigmoid(pre_value)
    return sigmoid_value * (1.0 + pre_value * (1.0 - sigmoid_value))


def neighbours(axis):
    size = lax.axis_size(axis)
    up = [(i, i + 1) for i in range(size - 1)]
    return up, [(j, i) for i, j in up]


def shards(
    features,
    target,
    hole_mask,
    kernel_first,
    kernel_second,
    inputs,
    weight_in,
    weight_out,
    weight_local,
    weight_mix,
):
    tile_rows, tile_cols, channels = features.shape
    row_devices, col_devices = lax.axis_size("row"), lax.axis_size("col")
    devices = row_devices * col_devices
    height, width = tile_rows * row_devices, tile_cols * col_devices
    strip, half = inputs.shape[0], weight_in.shape[1]
    owned = width // 2 // devices
    col_norm, row_norm = 1.0 / math.sqrt(width), 1.0 / math.sqrt(height)
    table = column_matrix(width, devices)
    row_tables = row_matrices(height, devices, owned)
    table_back = jnp.asarray(np.ascontiguousarray(table.T))
    table = jnp.asarray(table)
    row_back = [jnp.asarray(np.ascontiguousarray(t.T)) for t in row_tables]
    row_tables = [jnp.asarray(t) for t in row_tables]
    axes = ("row", "col")
    bf16 = jnp.bfloat16

    def swap(spectrum):
        return lax.all_to_all(spectrum, axes, split_axis=0, concat_axis=0, tiled=True)

    up, down = neighbours("row")
    near = REACH // 2
    above = lax.ppermute(features, "row", up)
    below = lax.ppermute(features, "row", down)
    target_above = lax.ppermute(target[-near:], "row", up)
    target_below = lax.ppermute(target[:near], "row", down)
    all_mask = lax.all_gather(lax.all_gather(hole_mask, "col", axis=1, tiled=True), "row", tiled=True)

    cells = [jax.ShapeDtypeStruct((width, strip * half), bf16)]
    spatial_cols = vmem_call(
        functools.partial(spectrum_kernel, False, col_norm), cells, inputs, weight_in, table
    )[0]
    spatial_moved = swap(spatial_cols)

    tall = jnp.concatenate([above, features, below], axis=0)
    tall_target = jnp.concatenate([target_above, target, target_below], axis=0)
    left, right = neighbours("col")
    stacked = jnp.concatenate([tall, tall_target], axis=0)
    before = lax.ppermute(stacked[:, -REACH:], "col", left)
    after = lax.ppermute(stacked[:, :REACH], "col", right)
    rows_tall = tall.shape[0]
    wide = jnp.concatenate([before[:rows_tall], tall, after[:rows_tall]], axis=1)
    wide_target = jnp.concatenate(
        [before[rows_tall:, near:], tall_target, after[rows_tall:, :near]], axis=1
    )
    row0, col0 = lax.axis_index("row") * tile_rows, lax.axis_index("col") * tile_cols
    weights = jnp.pad(1.0 + 2.0 * all_mask.astype(jnp.float32), near)
    hole_weight = lax.dynamic_slice(
        weights, (row0, col0), (tile_rows + 2 * near, tile_cols + 2 * near)
    )

    def inside(margin):
        row_ids = row0 - margin + jnp.arange(tile_rows + 2 * margin, dtype=jnp.int32)
        col_ids = col0 - margin + jnp.arange(tile_cols + 2 * margin, dtype=jnp.int32)
        ok_row = (row_ids >= 0) & (row_ids < height)
        ok_col = (col_ids >= 0) & (col_ids < width)
        return (ok_row[:, None] & ok_col[None, :])[:, :, None]

    pre_first = conv_valid(wide, kernel_first)
    act = jnp.where(inside(6), jax.nn.silu(pre_first), 0.0).astype(bf16)
    pre_second = conv_valid(act, kernel_second)
    loss_grad = (hole_weight[:, :, None] * (pre_second - wide_target.astype(jnp.float32))).astype(bf16)
    grad_act = conv_valid(loss_grad, adjoint_kernel(kernel_second))
    slope_first = silu_slope(pre_first[4:-4, 4:-4])
    grad_pre = jnp.where(inside(2), grad_act * slope_first, 0.0).astype(bf16)
    grad_feat = conv_valid(grad_pre, adjoint_kernel(kernel_first)).astype(bf16)

    cell_count = height * owned
    slope = vmem_call(
        functools.partial(slope_kernel, row_norm),
        [jax.ShapeDtypeStruct((cell_count, 2 * half), jnp.float32)],
        spatial_moved,
        weight_mix,
        *row_tables,
    )[0]

    strip_grad = lax.all_to_all(grad_feat, "col", split_axis=0, concat_axis=1, tiled=True)
    grad_cols = vmem_call(
        functools.partial(spectrum_kernel, True, col_norm), cells, strip_grad, weight_out, table
    )[0]
    grad_moved = swap(grad_cols)
    grad_rows = vmem_call(
        functools.partial(mix_kernel, row_norm, strip),
        cells,
        grad_moved,
        slope,
        weight_mix,
        *row_tables,
        *row_back,
    )[0]
    returned = swap(grad_rows)
    return vmem_call(
        functools.partial(output_kernel, col_norm),
        [jax.ShapeDtypeStruct(inputs.shape, bf16)],
        returned,
        strip_grad,
        weight_in,
        weight_local,
        table_back,
    )[0]


def solution(mesh):
    in_specs = (
        P("row", "col", None),
        P("row", "col", None),
        P("row", "col"),
        P(),
        P(),
        P(("row", "col"), None, None),
        P(),
        P(),
        P(),
        P(),
    )
    out_specs = P(("row", "col"), None, None)
    return jax.shard_map(shards, mesh=mesh, in_specs=in_specs, out_specs=out_specs, check_vma=False)
```

```python
import functools
import math

import jax
import jax.numpy as jnp
import ml_dtypes
import numpy as np
from jax import lax
from jax.experimental import pallas as pl
from jax.experimental.pallas import tpu as pltpu
from jax.sharding import PartitionSpec as P

REACH = 8
NEAR = 4
MIB = 1024 * 1024
LANES = 128


def dot(left, right):
    return jnp.dot(left, right, preferred_element_type=jnp.float32)


def dot_t(left, right):
    return lax.dot_general(left, right, (((1,), (1,)), ((), ())), preferred_element_type=jnp.float32)


def vmem_call(body, shapes, *operands, flops=0, scratch=(), limit=16):
    spec = pl.BlockSpec(memory_space=pltpu.VMEM)
    size = sum(math.prod(a.shape) * a.dtype.itemsize for a in (*operands, *shapes))
    return pl.pallas_call(
        body,
        out_shape=shapes,
        in_specs=[spec] * len(operands),
        out_specs=[spec] * len(shapes),
        scratch_shapes=list(scratch),
        compiler_params=pltpu.CompilerParams(vmem_limit_bytes=limit * MIB),
        cost_estimate=pl.CostEstimate(flops=flops, bytes_accessed=size, transcendentals=0),
    )(*operands)


def phases(first, second, length):
    angle = (first[:, None] * second[None, :] % length) * (2.0 * math.pi / length)
    return np.cos(angle).astype(ml_dtypes.bfloat16), np.sin(angle).astype(ml_dtypes.bfloat16)


def column_matrix(width, devices):
    half = width // 2
    freq, col = np.arange(half), np.arange(width)
    cos, sin = phases(freq, col, width)
    sin[0] = (2 * (col % 2) - 1).astype(ml_dtypes.bfloat16)
    both = np.stack([cos, -sin]).reshape(2, devices, half // devices, width)
    return np.ascontiguousarray(both.transpose(1, 0, 2, 3)).reshape(width, width)


def row_matrix(height, devices):
    strip = height // devices
    rows = (np.arange(devices)[None, :] * strip + np.arange(strip)[:, None]).reshape(-1)
    cos, sin = phases(np.arange(height), rows, height)
    return np.block([[cos, sin], [-sin, cos]])


def spectrum_kernel(transposed, norm, signal, weight, table, out):
    product = dot_t if transposed else dot
    rows = [product(signal[r], weight[...]).astype(jnp.bfloat16) for r in range(signal.shape[0])]
    out[...] = (dot(table[...], jnp.concatenate(rows, axis=1)) * norm).astype(jnp.bfloat16)


def row_spectrum(moved, table, wide, norm, owned, devices):
    groups = moved.shape[1] // LANES
    for g in range(groups):
        wide[g] = moved[:, g * LANES : (g + 1) * LANES].astype(jnp.float32)
    strip = table.shape[1] // (2 * devices)
    half = moved.shape[1] // strip
    height = table.shape[0] // 2
    real, imag = [], []
    for freq in range(owned):
        parts = []
        for part in range(2):
            where = pl.ds(part * owned + freq, devices, stride=2 * owned)
            block = jnp.concatenate([wide[g, where, :] for g in range(groups)], axis=1)
            parts += [block[:, r * half : (r + 1) * half] for r in range(strip)]
        result = dot(table[...], jnp.concatenate(parts, axis=0).astype(jnp.bfloat16)) * norm
        real.append(result[:height])
        imag.append(result[height:])
    return jnp.concatenate(real, axis=0), jnp.concatenate(imag, axis=0)


def slope_kernel(norm, owned, devices, moved, mix, table, out, wide):
    parts = row_spectrum(moved, table, wide, norm, owned, devices)
    real, imag = [part.astype(jnp.bfloat16) for part in parts]
    for part in range(2):
        pre = dot(real, mix[0, part]) + dot(imag, mix[1, part])
        s = 1.0 / (1.0 + jnp.exp(-pre))
        out[part] = s * (1.0 + pre * (1.0 - s))


def mix_kernel(norm, owned, devices, moved, slope, mix, table, back_table, out, wide):
    real, imag = row_spectrum(moved, table, wide, norm, owned, devices)
    real = (real * slope[0]).astype(jnp.bfloat16)
    imag = (imag * slope[1]).astype(jnp.bfloat16)
    back = [(dot_t(real, mix[p, 0]) + dot_t(imag, mix[p, 1])).astype(jnp.bfloat16) for p in range(2)]
    height = table.shape[0] // 2
    strip = height // devices
    groups = out.shape[1] // LANES
    for freq in range(owned):
        cells = slice(freq * height, (freq + 1) * height)
        stacked = jnp.concatenate([back[0][cells], back[1][cells]], axis=0)
        result = dot(back_table[...], stacked) * norm
        for part in range(2):
            rows = [
                result[(part * strip + r) * devices : (part * strip + r + 1) * devices]
                for r in range(strip)
            ]
            where = pl.ds(part * owned + freq, devices, stride=2 * owned)
            values = jnp.concatenate(rows, axis=1)
            for g in range(groups):
                wide[g, where, :] = values[:, g * LANES : (g + 1) * LANES]
    for g in range(groups):
        out[:, g * LANES : (g + 1) * LANES] = wide[g].astype(jnp.bfloat16)


def output_kernel(norm, moved, strip_grad, weight_in, weight_local, table, out):
    spatial = (dot(table[...], moved[...]) * norm).astype(jnp.bfloat16)
    half = weight_in.shape[1]
    for r in range(strip_grad.shape[0]):
        total = dot_t(spatial[:, r * half : (r + 1) * half], weight_in[...])
        total = total + dot_t(strip_grad[r], weight_local[...])
        out[r] = total.astype(jnp.bfloat16)


def conv_kernel(
    above,
    features,
    below,
    target_above,
    target,
    target_below,
    before,
    after,
    guard,
    first,
    second,
    second_adjoint,
    first_adjoint,
    out,
    wide0,
    wide1,
    wide2,
    wide3,
    slopes,
):
    tile_rows, tile_cols, channels = features.shape
    stride = tile_cols + 2 * REACH
    block = NEAR
    size = block * stride
    tall = tile_rows + 2 * REACH

    def rows_of(left, middle, right):
        parts = [part.astype(jnp.float32) for part in (left, middle, right)]
        return jnp.concatenate(parts, axis=1).reshape(size, channels)

    def put(wide, row, value):
        spot = pl.ds(row * stride, size)
        wide[spot, :channels] = pltpu.roll(value, 2, 0).astype(jnp.bfloat16)
        wide[spot, channels : 2 * channels] = value.astype(jnp.bfloat16)
        wide[spot, 2 * channels :] = pltpu.roll(value, size - 2, 0).astype(jnp.bfloat16)

    def conv(wide, row, kernel):
        taps = [wide[pl.ds((row + 2 * a) * stride, size), :] for a in range(3)]
        return dot(jnp.concatenate(taps, axis=1), kernel[...])

    def lanes(start):
        columns = [guard[:, start + i : start + i + 1] for i in range(block)]
        return jnp.concatenate(columns, axis=0)

    for part, source in enumerate((above, features, below)):
        for row in range(0, tile_rows, block):
            at = part * tile_rows + row
            put(
                wide0,
                at,
                rows_of(before[at : at + block], source[row : row + block], after[at : at + block]),
            )
    for row in range(0, tall - 4, block):
        pre = conv(wide0, row, first)
        s = 1.0 / (1.0 + jnp.exp(-pre))
        ok = lanes(row + 2)
        put(wide1, row, pre * s * ok)
        if NEAR <= row < tall - 4 - NEAR:
            slopes[pl.ds((row - NEAR) * stride, size), :] = s * (1.0 + pre * (1.0 - s)) * ok
    sources = [(target_above, 0)] + [(target, r) for r in range(0, tile_rows, block)] + [(target_below, 0)]
    for index, (source, at) in enumerate(sources):
        row = index * block
        value = conv(wide1, row, second)
        edge = tall + row
        goal = rows_of(
            before[edge : edge + block], source[at : at + block], after[edge : edge + block]
        )
        put(wide2, row, lanes(tall + row) * (value - goal))
    for row in range(0, tile_rows + 4, block):
        value = conv(wide2, row, second_adjoint)
        put(wide3, row, value * slopes[pl.ds(row * stride, size), :])
    for row in range(0, tile_rows, block):
        value = conv(wide3, row, first_adjoint).reshape(block, stride, channels)
        out[row : row + block] = value[:, REACH : REACH + tile_cols].astype(jnp.bfloat16)


def conv_chain(pieces, guard, kernel_first, kernel_second):
    features = pieces[1]
    tile_rows, tile_cols, channels = features.shape
    stride = tile_cols + 2 * REACH
    bf16 = jnp.bfloat16

    def plain(kernel):
        return kernel.reshape(9 * channels, channels)

    def adjoint(kernel):
        return jnp.transpose(jnp.flip(kernel, (0, 1)), (0, 1, 3, 2)).reshape(9 * channels, channels)

    wides = [pltpu.VMEM(((tile_rows + h) * stride, 3 * channels), bf16) for h in (16, 12, 8, 4)]
    pixels = sum((tile_rows + h) * stride for h in (12, 8, 4, 0))
    return vmem_call(
        conv_kernel,
        [jax.ShapeDtypeStruct(features.shape, bf16)],
        *pieces,
        guard,
        plain(kernel_first),
        plain(kernel_second),
        adjoint(kernel_second),
        adjoint(kernel_first),
        flops=2 * 9 * channels * channels * pixels,
        scratch=[*wides, pltpu.VMEM(((tile_rows + 4) * stride, channels), jnp.float32)],
        limit=40,
    )[0]


def neighbours(axis):
    size = lax.axis_size(axis)
    up = [(i, i + 1) for i in range(size - 1)]
    return up, [(j, i) for i, j in up]


def shards(
    features,
    target,
    hole_mask,
    kernel_first,
    kernel_second,
    inputs,
    weight_in,
    weight_out,
    weight_local,
    weight_mix,
):
    tile_rows, tile_cols, channels = features.shape
    row_devices, col_devices = lax.axis_size("row"), lax.axis_size("col")
    devices = row_devices * col_devices
    height, width = tile_rows * row_devices, tile_cols * col_devices
    strip, half = inputs.shape[0], weight_in.shape[1]
    owned = width // 2 // devices
    col_norm, row_norm = 1.0 / math.sqrt(width), 1.0 / math.sqrt(height)
    table = column_matrix(width, devices)
    table_back = jnp.asarray(np.ascontiguousarray(table.T))
    table = jnp.asarray(table)
    row_table = row_matrix(height, devices)
    row_back = jnp.asarray(np.ascontiguousarray(row_table.T))
    row_table = jnp.asarray(row_table)
    bf16 = jnp.bfloat16

    def swap(spectrum):
        return lax.all_to_all(spectrum, ("row", "col"), split_axis=0, concat_axis=0, tiled=True)

    up, down = neighbours("row")
    left, right = neighbours("col")

    def mask_lanes(mask):
        return jnp.pad(mask.astype(bf16).T, ((0, 0), (0, channels - mask.shape[0])))[None]

    above = lax.ppermute(features, "row", up)
    below = lax.ppermute(features, "row", down)
    packed_above = jnp.concatenate([target[-NEAR:], mask_lanes(hole_mask[-NEAR:])], axis=0)
    packed_below = jnp.concatenate([target[:NEAR], mask_lanes(hole_mask[:NEAR])], axis=0)
    packed_above = lax.ppermute(packed_above, "row", up)
    packed_below = lax.ppermute(packed_below, "row", down)

    cells = [jax.ShapeDtypeStruct((width, strip * half), bf16)]
    spatial_cols = vmem_call(
        functools.partial(spectrum_kernel, False, col_norm), cells, inputs, weight_in, table
    )[0]
    spatial_moved = swap(spatial_cols)

    mask_tall = jnp.concatenate(
        [packed_above[NEAR, :, :NEAR], hole_mask.astype(bf16).T, packed_below[NEAR, :, :NEAR]], axis=1
    )
    mask_row = jnp.pad(mask_tall, ((0, 0), (0, channels - mask_tall.shape[1])))[None]

    def edge(cols):
        parts = [above, features, below, packed_above[:NEAR], target, packed_below[:NEAR], mask_row]
        return jnp.concatenate([part[:, cols] for part in parts], axis=0)

    before = lax.ppermute(edge(slice(tile_cols - REACH, None)), "col", left)
    after = lax.ppermute(edge(slice(0, REACH)), "col", right)

    row0, col0 = lax.axis_index("row") * tile_rows, lax.axis_index("col") * tile_cols
    tall = tile_rows + 2 * REACH
    row_ids = row0 - REACH + jnp.arange(tall, dtype=jnp.int32)
    col_ids = col0 - REACH + jnp.arange(tile_cols + 2 * REACH, dtype=jnp.int32)
    ok = ((col_ids >= 0) & (col_ids < width))[:, None] & ((row_ids >= 0) & (row_ids < height))[None]
    ok = ok.astype(jnp.float32)
    near_rows = tile_rows + 2 * NEAR
    mask_wide = jnp.concatenate(
        [before[-1, :, :near_rows], mask_tall, after[-1, :, :near_rows]], axis=0
    ).astype(jnp.float32)
    weights = (1.0 + 2.0 * mask_wide) * ok[:, NEAR : NEAR + near_rows]
    guard = jnp.concatenate([ok, weights], axis=1)

    pieces = (
        above,
        features,
        below,
        packed_above,
        target,
        packed_below,
        before,
        after,
    )
    grad_feat = conv_chain(pieces, guard, kernel_first, kernel_second)

    cell_count = height * owned
    mix = weight_mix.reshape(2, half, 2, half).transpose(0, 2, 1, 3)
    wide = [pltpu.VMEM((strip * half // LANES, width, LANES), jnp.float32)]
    slope = vmem_call(
        functools.partial(slope_kernel, row_norm, owned, devices),
        [jax.ShapeDtypeStruct((2, cell_count, half), jnp.float32)],
        spatial_moved,
        mix,
        row_table,
        scratch=wide,
    )[0]

    strip_grad = lax.all_to_all(grad_feat, "col", split_axis=0, concat_axis=1, tiled=True)
    grad_cols = vmem_call(
        functools.partial(spectrum_kernel, True, col_norm), cells, strip_grad, weight_out, table
    )[0]
    grad_moved = swap(grad_cols)
    grad_rows = vmem_call(
        functools.partial(mix_kernel, row_norm, owned, devices),
        cells,
        grad_moved,
        slope,
        mix,
        row_table,
        row_back,
        scratch=wide,
    )[0]
    returned = swap(grad_rows)
    return vmem_call(
        functools.partial(output_kernel, col_norm),
        [jax.ShapeDtypeStruct(inputs.shape, bf16)],
        returned,
        strip_grad,
        weight_in,
        weight_local,
        table_back,
    )[0]


def solution(mesh):
    in_specs = (
        P("row", "col", None),
        P("row", "col", None),
        P("row", "col"),
        P(),
        P(),
        P(("row", "col"), None, None),
        P(),
        P(),
        P(),
        P(),
    )
    out_specs = P(("row", "col"), None, None)
    return jax.shard_map(shards, mesh=mesh, in_specs=in_specs, out_specs=out_specs, check_vma=False)
```

```python
import functools
import math

import jax
import jax.numpy as jnp
import ml_dtypes
import numpy as np
from jax import lax
from jax.experimental import pallas as pl
from jax.experimental.pallas import tpu as pltpu
from jax.sharding import PartitionSpec as P

REACH = 8
NEAR = 4
MIB = 1024 * 1024
LANES = 128


def dot(left, right):
    return jnp.dot(left, right, preferred_element_type=jnp.float32)


def dot_t(left, right):
    return lax.dot_general(left, right, (((1,), (1,)), ((), ())), preferred_element_type=jnp.float32)


def vmem_call(body, shapes, *operands, flops=0, scratch=(), limit=16):
    spec = pl.BlockSpec(memory_space=pltpu.VMEM)
    size = sum(math.prod(a.shape) * a.dtype.itemsize for a in (*operands, *shapes))
    return pl.pallas_call(
        body,
        out_shape=shapes,
        in_specs=[spec] * len(operands),
        out_specs=[spec] * len(shapes),
        scratch_shapes=list(scratch),
        compiler_params=pltpu.CompilerParams(vmem_limit_bytes=limit * MIB),
        cost_estimate=pl.CostEstimate(flops=flops, bytes_accessed=size, transcendentals=0),
    )(*operands)


def phases(first, second, length):
    angle = (first[:, None] * second[None, :] % length) * (2.0 * math.pi / length)
    return np.cos(angle).astype(ml_dtypes.bfloat16), np.sin(angle).astype(ml_dtypes.bfloat16)


def column_matrix(width, devices):
    half = width // 2
    freq, col = np.arange(half), np.arange(width)
    cos, sin = phases(freq, col, width)
    sin[0] = (2 * (col % 2) - 1).astype(ml_dtypes.bfloat16)
    both = np.stack([cos, -sin]).reshape(2, devices, half // devices, width)
    return np.ascontiguousarray(both.transpose(1, 0, 2, 3)).reshape(width, width)


def row_matrix(height, devices):
    strip = height // devices
    rows = (np.arange(devices)[None, :] * strip + np.arange(strip)[:, None]).reshape(-1)
    cos, sin = phases(np.arange(height), rows, height)
    return np.block([[cos, sin], [-sin, cos]])


def strip_row(signal, r):
    if len(signal.shape) == 3:
        return signal[r]
    return jnp.concatenate([signal[block, r] for block in range(signal.shape[0])], axis=0)


def spectrum_kernel(transposed, norm, signal, weight, table, out):
    product = dot_t if transposed else dot
    count = signal.shape[0 if len(signal.shape) == 3 else 1]
    rows = [product(strip_row(signal, r), weight[...]).astype(jnp.bfloat16) for r in range(count)]
    out[...] = (dot(table[...], jnp.concatenate(rows, axis=1)) * norm).astype(jnp.bfloat16)


def row_spectrum(moved, table, wide, norm, owned, devices):
    groups = moved.shape[1] // LANES
    for g in range(groups):
        wide[g] = moved[:, g * LANES : (g + 1) * LANES].astype(jnp.float32)
    strip = table.shape[1] // (2 * devices)
    half = moved.shape[1] // strip
    height = table.shape[0] // 2
    real, imag = [], []
    for freq in range(owned):
        parts = []
        for part in range(2):
            where = pl.ds(part * owned + freq, devices, stride=2 * owned)
            block = jnp.concatenate([wide[g, where, :] for g in range(groups)], axis=1)
            parts += [block[:, r * half : (r + 1) * half] for r in range(strip)]
        result = dot(table[...], jnp.concatenate(parts, axis=0).astype(jnp.bfloat16)) * norm
        real.append(result[:height])
        imag.append(result[height:])
    return jnp.concatenate(real, axis=0), jnp.concatenate(imag, axis=0)


def slope_kernel(norm, owned, devices, moved, mix, table, out, wide):
    parts = row_spectrum(moved, table, wide, norm, owned, devices)
    real, imag = [part.astype(jnp.bfloat16) for part in parts]
    for part in range(2):
        pre = dot(real, mix[0, part]) + dot(imag, mix[1, part])
        s = 1.0 / (1.0 + jnp.exp(-pre))
        out[part] = s * (1.0 + pre * (1.0 - s))


def mix_kernel(norm, owned, devices, moved, slope, mix, table, back_table, out, wide):
    real, imag = row_spectrum(moved, table, wide, norm, owned, devices)
    real = (real * slope[0]).astype(jnp.bfloat16)
    imag = (imag * slope[1]).astype(jnp.bfloat16)
    back = [(dot_t(real, mix[p, 0]) + dot_t(imag, mix[p, 1])).astype(jnp.bfloat16) for p in range(2)]
    height = table.shape[0] // 2
    strip = height // devices
    groups = out.shape[1] // LANES
    for freq in range(owned):
        cells = slice(freq * height, (freq + 1) * height)
        stacked = jnp.concatenate([back[0][cells], back[1][cells]], axis=0)
        result = dot(back_table[...], stacked) * norm
        for part in range(2):
            rows = [
                result[(part * strip + r) * devices : (part * strip + r + 1) * devices]
                for r in range(strip)
            ]
            where = pl.ds(part * owned + freq, devices, stride=2 * owned)
            values = jnp.concatenate(rows, axis=1)
            for g in range(groups):
                wide[g, where, :] = values[:, g * LANES : (g + 1) * LANES]
    for g in range(groups):
        out[:, g * LANES : (g + 1) * LANES] = wide[g].astype(jnp.bfloat16)


def output_kernel(norm, moved, strip_grad, weight_in, weight_local, table, out):
    spatial = (dot(table[...], moved[...]) * norm).astype(jnp.bfloat16)
    half = weight_in.shape[1]
    for r in range(out.shape[0]):
        total = dot_t(spatial[:, r * half : (r + 1) * half], weight_in[...])
        total = total + dot_t(strip_row(strip_grad, r), weight_local[...])
        out[r] = total.astype(jnp.bfloat16)


def row_pack_kernel(features, target, mask, down, up):
    tile_rows, tile_cols, channels = features.shape
    lanes = jnp.concatenate(
        [
            mask[...].astype(jnp.float32),
            jnp.zeros((tile_cols - tile_rows, tile_cols), jnp.float32),
        ],
        axis=0,
    ).T
    row = jnp.concatenate([lanes] + [jnp.zeros_like(lanes)] * (channels // tile_cols - 1), axis=1)
    for pack, start in ((down, tile_rows - NEAR), (up, 0)):
        pack[:tile_rows] = features[...]
        pack[tile_rows : tile_rows + NEAR] = target[start : start + NEAR]
        pack[tile_rows + NEAR] = row.astype(jnp.bfloat16)


def row_packs(features, target, mask):
    tile_rows, tile_cols, channels = features.shape
    pack = jax.ShapeDtypeStruct((tile_rows + NEAR + 1, tile_cols, channels), features.dtype)
    return vmem_call(row_pack_kernel, [pack, pack], features, target, mask)


def edge_kernel(*refs):
    sources, outs = refs[:-2], refs[-2:]
    count = len(sources) // 2
    for out, group in zip(outs, (sources[:count], sources[count:])):
        row = 0
        for ref in group:
            out[row : row + ref.shape[0]] = ref[...]
            row += ref.shape[0]


def edges(above, features, target, mask_row, below):
    parts = [above, features, target, mask_row, below]
    channels = features.shape[2]
    last = features.shape[1] // REACH - 1

    def specs(at):
        return [pl.BlockSpec((p.shape[0], REACH, channels), lambda i, at=at: (0, at, 0)) for p in parts]

    rows = sum(p.shape[0] for p in parts)
    shape = jax.ShapeDtypeStruct((rows, REACH, channels), features.dtype)
    return pl.pallas_call(
        edge_kernel,
        grid=(1,),
        out_shape=[shape, shape],
        in_specs=specs(last) + specs(0),
        out_specs=[pl.BlockSpec(shape.shape, lambda i: (0, 0, 0))] * 2,
        cost_estimate=pl.CostEstimate(
            flops=0, bytes_accessed=8 * rows * REACH * channels, transcendentals=0
        ),
    )(*parts, *parts)


def conv_kernel(
    above,
    features,
    target,
    mask_row,
    below,
    before,
    after,
    ok,
    first,
    second,
    out,
    wide0,
    wide1,
    wide2,
    wide3,
    slopes,
):
    tile_rows, tile_cols, channels = features.shape
    stride = tile_cols + 2 * REACH
    block = NEAR
    size = block * stride
    tall = tile_rows + 2 * REACH
    pack = above.shape[0]
    below_at = pack + 2 * tile_rows + 1

    def rows_of(edge, source, row, count=block):
        parts = [before[edge : edge + count], source[row : row + count], after[edge : edge + count]]
        parts = [part.astype(jnp.float32) for part in parts]
        return jnp.concatenate(parts, axis=1).reshape(count * stride, channels)

    def put(wide, row, value):
        spot = pl.ds(row * stride, size)
        wide[spot, :channels] = pltpu.roll(value, 2, 0).astype(jnp.bfloat16)
        wide[spot, channels : 2 * channels] = value.astype(jnp.bfloat16)
        wide[spot, 2 * channels :] = pltpu.roll(value, size - 2, 0).astype(jnp.bfloat16)

    def taps(wide, row):
        return jnp.concatenate(
            [wide[pl.ds((row + 2 * a) * stride, size), :] for a in range(3)], axis=1
        )

    def conv(wide, row, kernel):
        return dot(taps(wide, row), kernel[...].reshape(9 * channels, channels))

    def conv_adjoint(wide, row, kernel):
        flipped = [kernel[2 - a, 2 - b] for a in range(3) for b in range(3)]
        return dot_t(taps(wide, row), jnp.concatenate(flipped, axis=1))

    def inside(row):
        return jnp.concatenate([ok[:, row + i : row + i + 1] for i in range(block)], axis=0)

    sources = ((above, 0), (features, pack), (below, below_at))
    for part, (source, edge) in enumerate(sources):
        for row in range(0, tile_rows, block):
            put(wide0, part * tile_rows + row, rows_of(edge + row, source, row))
    for row in range(0, tall - 4, block):
        pre = conv(wide0, row, first)
        s = 1.0 / (1.0 + jnp.exp(-pre))
        kept = inside(row + 2)
        put(wide1, row, pre * s * kept)
        if NEAR <= row < tall - 4 - NEAR:
            slopes[pl.ds((row - NEAR) * stride, size), :] = s * (1.0 + pre * (1.0 - s)) * kept
    masks = [
        rows_of(pack - 1, above, pack - 1, 1),
        rows_of(pack + 2 * tile_rows, mask_row, 0, 1),
        rows_of(below_at + pack - 1, below, pack - 1, 1),
    ]
    goals = [(tile_rows, above, tile_rows, masks[0], tile_rows - NEAR)]
    goals += [(pack + tile_rows + r, target, r, masks[1], r) for r in range(0, tile_rows, block)]
    goals += [(below_at + tile_rows, below, tile_rows, masks[2], 0)]
    for index, (edge, source, at, mask, lane) in enumerate(goals):
        row = index * block
        value = conv(wide1, row, second)
        holes = jnp.concatenate([mask[:, lane + i : lane + i + 1] for i in range(block)], axis=0)
        weight = (1.0 + 2.0 * holes) * inside(row + NEAR)
        put(wide2, row, weight * (value - rows_of(edge, source, at)))
    for row in range(0, tile_rows + 4, block):
        value = conv_adjoint(wide2, row, second)
        put(wide3, row, value * slopes[pl.ds(row * stride, size), :])
    for row in range(0, tile_rows, block):
        value = conv_adjoint(wide3, row, first).reshape(block, stride, channels)
        out[row : row + block] = value[:, REACH : REACH + tile_cols].astype(jnp.bfloat16)


def conv_chain(features, *others):
    tile_rows, tile_cols, channels = features.shape
    stride = tile_cols + 2 * REACH
    above, *rest = others
    wides = [
        pltpu.VMEM(((tile_rows + h) * stride, 3 * channels), jnp.bfloat16) for h in (16, 12, 8, 4)
    ]
    pixels = sum((tile_rows + h) * stride for h in (12, 8, 4, 0))
    return vmem_call(
        conv_kernel,
        [jax.ShapeDtypeStruct(features.shape, jnp.bfloat16)],
        above,
        features,
        *rest,
        flops=2 * 9 * channels * channels * pixels,
        scratch=[*wides, pltpu.VMEM(((tile_rows + 4) * stride, channels), jnp.float32)],
        limit=40,
    )[0]


def neighbours(axis):
    size = lax.axis_size(axis)
    up = [(i, i + 1) for i in range(size - 1)]
    return up, [(j, i) for i, j in up]


def shards(
    features,
    target,
    hole_mask,
    kernel_first,
    kernel_second,
    inputs,
    weight_in,
    weight_out,
    weight_local,
    weight_mix,
):
    tile_rows, tile_cols, channels = features.shape
    row_devices, col_devices = lax.axis_size("row"), lax.axis_size("col")
    devices = row_devices * col_devices
    height, width = tile_rows * row_devices, tile_cols * col_devices
    strip, half = inputs.shape[0], weight_in.shape[1]
    owned = width // 2 // devices
    col_norm, row_norm = 1.0 / math.sqrt(width), 1.0 / math.sqrt(height)
    table = column_matrix(width, devices)
    table_back = jnp.asarray(np.ascontiguousarray(table.T))
    table = jnp.asarray(table)
    row_table = row_matrix(height, devices)
    row_back = jnp.asarray(np.ascontiguousarray(row_table.T))
    row_table = jnp.asarray(row_table)
    bf16 = jnp.bfloat16

    def swap(spectrum):
        return lax.all_to_all(spectrum, ("row", "col"), split_axis=0, concat_axis=0, tiled=True)

    cells = [jax.ShapeDtypeStruct((width, strip * half), bf16)]
    spatial_cols = vmem_call(
        functools.partial(spectrum_kernel, False, col_norm), cells, inputs, weight_in, table
    )[0]
    spatial_moved = swap(spatial_cols)

    up, down = neighbours("row")
    left, right = neighbours("col")
    pack_down, pack_up = row_packs(features, target, hole_mask)
    mask_row = pack_up[-1:]
    above = lax.ppermute(pack_down, "row", up)
    below = lax.ppermute(pack_up, "row", down)
    above, spatial_cols = lax.optimization_barrier((above, spatial_cols))
    last, initial = edges(above, features, target, mask_row, below)
    before = lax.ppermute(last, "col", left)
    after = lax.ppermute(initial, "col", right)
    before, spatial_moved = lax.optimization_barrier((before, spatial_moved))

    row0, col0 = lax.axis_index("row") * tile_rows, lax.axis_index("col") * tile_cols
    row_ids = row0 - REACH + jnp.arange(tile_rows + 2 * REACH, dtype=jnp.int32)
    col_ids = col0 - REACH + jnp.arange(tile_cols + 2 * REACH, dtype=jnp.int32)
    ok = ((col_ids >= 0) & (col_ids < width))[:, None] & ((row_ids >= 0) & (row_ids < height))[None]
    ok = ok.astype(jnp.float32)
    grad_feat = conv_chain(
        features, above, target, mask_row, below, before, after, ok, kernel_first, kernel_second
    )

    cell_count = height * owned
    mix = weight_mix.reshape(2, half, 2, half).transpose(0, 2, 1, 3)
    wide = [pltpu.VMEM((strip * half // LANES, width, LANES), jnp.float32)]
    slope = vmem_call(
        functools.partial(slope_kernel, row_norm, owned, devices),
        [jax.ShapeDtypeStruct((2, cell_count, half), jnp.float32)],
        spatial_moved,
        mix,
        row_table,
        scratch=wide,
    )[0]

    strip_grad = lax.all_to_all(
        grad_feat.reshape(col_devices, strip, tile_cols, channels), "col", split_axis=0, concat_axis=0
    )
    grad_cols = vmem_call(
        functools.partial(spectrum_kernel, True, col_norm), cells, strip_grad, weight_out, table
    )[0]
    grad_moved = swap(grad_cols)
    grad_rows = vmem_call(
        functools.partial(mix_kernel, row_norm, owned, devices),
        cells,
        grad_moved,
        slope,
        mix,
        row_table,
        row_back,
        scratch=wide,
    )[0]
    returned = swap(grad_rows)
    return vmem_call(
        functools.partial(output_kernel, col_norm),
        [jax.ShapeDtypeStruct(inputs.shape, bf16)],
        returned,
        strip_grad,
        weight_in,
        weight_local,
        table_back,
    )[0]


def solution(mesh):
    in_specs = (
        P("row", "col", None),
        P("row", "col", None),
        P("row", "col"),
        P(),
        P(),
        P(("row", "col"), None, None),
        P(),
        P(),
        P(),
        P(),
    )
    out_specs = P(("row", "col"), None, None)
    return jax.shard_map(shards, mesh=mesh, in_specs=in_specs, out_specs=out_specs, check_vma=False)
```

```python
import functools
import math

import jax
import jax.numpy as jnp
import ml_dtypes
import numpy as np
from jax import lax
from jax.experimental import pallas as pl
from jax.experimental.pallas import tpu as pltpu
from jax.sharding import PartitionSpec as P

REACH = 8
NEAR = 4
MIB = 1024 * 1024
LANES = 128


def dot(left, right):
    return jnp.dot(left, right, preferred_element_type=jnp.float32)


def dot_t(left, right):
    return lax.dot_general(left, right, (((1,), (1,)), ((), ())), preferred_element_type=jnp.float32)


def vmem_call(body, shapes, *operands, flops=0, scratch=(), limit=16):
    spec = pl.BlockSpec(memory_space=pltpu.VMEM)
    size = sum(math.prod(a.shape) * a.dtype.itemsize for a in (*operands, *shapes))
    return pl.pallas_call(
        body,
        out_shape=shapes,
        in_specs=[spec] * len(operands),
        out_specs=[spec] * len(shapes),
        scratch_shapes=list(scratch),
        compiler_params=pltpu.CompilerParams(vmem_limit_bytes=limit * MIB),
        cost_estimate=pl.CostEstimate(flops=flops, bytes_accessed=size, transcendentals=0),
    )(*operands)


def phases(first, second, length):
    angle = (first[:, None] * second[None, :] % length) * (2.0 * math.pi / length)
    return np.cos(angle).astype(ml_dtypes.bfloat16), np.sin(angle).astype(ml_dtypes.bfloat16)


def column_matrix(width, devices):
    half = width // 2
    freq, col = np.arange(half), np.arange(width)
    cos, sin = phases(freq, col, width)
    sin[0] = (2 * (col % 2) - 1).astype(ml_dtypes.bfloat16)
    both = np.stack([cos, -sin]).reshape(2, devices, half // devices, width)
    return np.ascontiguousarray(both.transpose(1, 0, 2, 3)).reshape(width, width)


def row_matrix(height, devices):
    strip = height // devices
    rows = (np.arange(devices)[None, :] * strip + np.arange(strip)[:, None]).reshape(-1)
    cos, sin = phases(np.arange(height), rows, height)
    return np.block([[cos, sin], [-sin, cos]])


def strip_row(signal, r):
    if len(signal.shape) == 3:
        return signal[r]
    return jnp.concatenate([signal[block, r] for block in range(signal.shape[0])], axis=0)


def spectrum_kernel(transposed, norm, signal, weight, table, out):
    product = dot_t if transposed else dot
    count = signal.shape[0 if len(signal.shape) == 3 else 1]
    rows = [product(strip_row(signal, r), weight[...]).astype(jnp.bfloat16) for r in range(count)]
    out[...] = (dot(table[...], jnp.concatenate(rows, axis=1)) * norm).astype(jnp.bfloat16)


def row_spectrum(moved, table, wide, norm, owned, devices):
    groups = moved.shape[1] // LANES
    for g in range(groups):
        wide[g] = moved[:, g * LANES : (g + 1) * LANES].astype(jnp.float32)
    strip = table.shape[1] // (2 * devices)
    half = moved.shape[1] // strip
    height = table.shape[0] // 2
    real, imag = [], []
    for freq in range(owned):
        parts = []
        for part in range(2):
            where = pl.ds(part * owned + freq, devices, stride=2 * owned)
            block = jnp.concatenate([wide[g, where, :] for g in range(groups)], axis=1)
            parts += [block[:, r * half : (r + 1) * half] for r in range(strip)]
        result = dot(table[...], jnp.concatenate(parts, axis=0).astype(jnp.bfloat16)) * norm
        real.append(result[:height])
        imag.append(result[height:])
    return jnp.concatenate(real, axis=0), jnp.concatenate(imag, axis=0)


def slope_kernel(norm, owned, devices, moved, mix, table, out, wide):
    parts = row_spectrum(moved, table, wide, norm, owned, devices)
    real, imag = [part.astype(jnp.bfloat16) for part in parts]
    for part in range(2):
        pre = dot(real, mix[0, part]) + dot(imag, mix[1, part])
        s = 1.0 / (1.0 + jnp.exp(-pre))
        out[part] = s * (1.0 + pre * (1.0 - s))


def mix_kernel(norm, owned, devices, moved, slope, mix, table, back_table, out, wide):
    real, imag = row_spectrum(moved, table, wide, norm, owned, devices)
    real = (real * slope[0]).astype(jnp.bfloat16)
    imag = (imag * slope[1]).astype(jnp.bfloat16)
    back = [(dot_t(real, mix[p, 0]) + dot_t(imag, mix[p, 1])).astype(jnp.bfloat16) for p in range(2)]
    height = table.shape[0] // 2
    strip = height // devices
    groups = out.shape[1] // LANES
    for freq in range(owned):
        cells = slice(freq * height, (freq + 1) * height)
        stacked = jnp.concatenate([back[0][cells], back[1][cells]], axis=0)
        result = dot(back_table[...], stacked) * norm
        for part in range(2):
            rows = [
                result[(part * strip + r) * devices : (part * strip + r + 1) * devices]
                for r in range(strip)
            ]
            where = pl.ds(part * owned + freq, devices, stride=2 * owned)
            values = jnp.concatenate(rows, axis=1)
            for g in range(groups):
                wide[g, where, :] = values[:, g * LANES : (g + 1) * LANES]
    for g in range(groups):
        out[:, g * LANES : (g + 1) * LANES] = wide[g].astype(jnp.bfloat16)


def output_kernel(norm, moved, strip_grad, weight_in, weight_local, table, out):
    spatial = (dot(table[...], moved[...]) * norm).astype(jnp.bfloat16)
    half = weight_in.shape[1]
    for r in range(out.shape[0]):
        total = dot_t(spatial[:, r * half : (r + 1) * half], weight_in[...])
        total = total + dot_t(strip_row(strip_grad, r), weight_local[...])
        out[r] = total.astype(jnp.bfloat16)


def target_pack_kernel(first, last, mask, down, up, row):
    tile_rows, tile_cols = mask.shape
    channels = first.shape[2]
    lanes = jnp.concatenate(
        [
            mask[...].astype(jnp.float32),
            jnp.zeros((tile_cols - tile_rows, tile_cols), jnp.float32),
        ],
        axis=0,
    ).T
    lanes = jnp.concatenate([lanes] + [jnp.zeros_like(lanes)] * (channels // tile_cols - 1), axis=1)
    lanes = lanes.astype(jnp.bfloat16)
    row[0] = lanes
    for pack, part in ((down, last), (up, first)):
        pack[:NEAR] = part[...]
        pack[NEAR] = lanes


def target_packs(target, mask):
    tile_rows, tile_cols, channels = target.shape
    block = (NEAR, tile_cols, channels)
    shapes = [jax.ShapeDtypeStruct((n, tile_cols, channels), target.dtype) for n in (NEAR + 1, NEAR + 1, 1)]
    return pl.pallas_call(
        target_pack_kernel,
        grid=(1,),
        out_shape=shapes,
        in_specs=[
            pl.BlockSpec(block, lambda i: (0, 0, 0)),
            pl.BlockSpec(block, lambda i: (tile_rows // NEAR - 1, 0, 0)),
            pl.BlockSpec(mask.shape, lambda i: (0, 0)),
        ],
        out_specs=[pl.BlockSpec(shape.shape, lambda i: (0, 0, 0)) for shape in shapes],
    )(target, target, mask)


def edge_kernel(*refs):
    sources, outs = refs[:-2], refs[-2:]
    count = len(sources) // 2
    for out, group in zip(outs, (sources[:count], sources[count:])):
        row = 0
        for ref in group:
            out[row : row + ref.shape[0]] = ref[...]
            row += ref.shape[0]


def edges(*parts):
    features = parts[1]
    channels = features.shape[2]
    last = features.shape[1] // REACH - 1

    def specs(at):
        return [pl.BlockSpec((p.shape[0], REACH, channels), lambda i, at=at: (0, at, 0)) for p in parts]

    rows = sum(p.shape[0] for p in parts)
    shape = jax.ShapeDtypeStruct((rows, REACH, channels), features.dtype)
    return pl.pallas_call(
        edge_kernel,
        grid=(1,),
        out_shape=[shape, shape],
        in_specs=specs(last) + specs(0),
        out_specs=[pl.BlockSpec(shape.shape, lambda i: (0, 0, 0))] * 2,
        cost_estimate=pl.CostEstimate(
            flops=0, bytes_accessed=8 * rows * REACH * channels, transcendentals=0
        ),
    )(*parts, *parts)


FETCHED = 11


def conv_kernel(*refs):
    ok, out = refs[FETCHED : FETCHED + 2]
    held = refs[FETCHED + 2 : 2 * FETCHED + 2]
    wide0, wide1, wide2, wide3, slopes, arrived = refs[2 * FETCHED + 2 :]
    copies = [pltpu.make_async_copy(refs[i], held[i], arrived.at[i]) for i in range(FETCHED)]
    for copy in copies:
        copy.start()
    before, after, above, features, below, first = held[:6]
    target_above, target, target_below, mask_row, second = held[6:]
    tile_rows, tile_cols, channels = features.shape
    stride = tile_cols + 2 * REACH
    block = NEAR
    size = block * stride
    tall = tile_rows + 2 * REACH

    def rows_of(edge, source, row, count=block):
        parts = [before[edge : edge + count], source[row : row + count], after[edge : edge + count]]
        parts = [part.astype(jnp.float32) for part in parts]
        return jnp.concatenate(parts, axis=1).reshape(count * stride, channels)

    def put(wide, row, value):
        spot = pl.ds(row * stride, size)
        wide[spot, :channels] = pltpu.roll(value, 2, 0).astype(jnp.bfloat16)
        wide[spot, channels : 2 * channels] = value.astype(jnp.bfloat16)
        wide[spot, 2 * channels :] = pltpu.roll(value, size - 2, 0).astype(jnp.bfloat16)

    def taps(wide, row):
        return jnp.concatenate(
            [wide[pl.ds((row + 2 * a) * stride, size), :] for a in range(3)], axis=1
        )

    def conv(wide, row, kernel):
        return dot(taps(wide, row), kernel[...].reshape(9 * channels, channels))

    def conv_adjoint(wide, row, kernel):
        flipped = [kernel[2 - a, 2 - b] for a in range(3) for b in range(3)]
        return dot_t(taps(wide, row), jnp.concatenate(flipped, axis=1))

    def inside(row):
        return jnp.concatenate([ok[:, row + i : row + i + 1] for i in range(block)], axis=0)

    copies[0].wait()
    copies[1].wait()
    for part, source in enumerate((above, features, below)):
        copies[2 + part].wait()
        for row in range(0, tile_rows, block):
            at = part * tile_rows + row
            put(wide0, at, rows_of(at, source, row))
    copies[5].wait()
    for row in range(0, tall - 4, block):
        pre = conv(wide0, row, first)
        s = 1.0 / (1.0 + jnp.exp(-pre))
        kept = inside(row + 2)
        put(wide1, row, pre * s * kept)
        if NEAR <= row < tall - 4 - NEAR:
            slopes[pl.ds((row - NEAR) * stride, size), :] = s * (1.0 + pre * (1.0 - s)) * kept
    for copy in copies[6:]:
        copy.wait()
    own = tall + NEAR + 1
    masks = [
        rows_of(tall + NEAR, target_above, NEAR, 1),
        rows_of(own + tile_rows, mask_row, 0, 1),
        rows_of(own + tile_rows + 1 + NEAR, target_below, NEAR, 1),
    ]
    goals = [(tall, target_above, 0, masks[0], tile_rows - NEAR)]
    goals += [(own + r, target, r, masks[1], r) for r in range(0, tile_rows, block)]
    goals += [(own + tile_rows + 1, target_below, 0, masks[2], 0)]
    for index, (edge, source, at, mask, lane) in enumerate(goals):
        row = index * block
        value = conv(wide1, row, second)
        holes = jnp.concatenate([mask[:, lane + i : lane + i + 1] for i in range(block)], axis=0)
        weight = (1.0 + 2.0 * holes) * inside(row + NEAR)
        put(wide2, row, weight * (value - rows_of(edge, source, at)))
    for row in range(0, tile_rows + 4, block):
        value = conv_adjoint(wide2, row, second)
        put(wide3, row, value * slopes[pl.ds(row * stride, size), :])
    for row in range(0, tile_rows, block):
        value = conv_adjoint(wide3, row, first).reshape(block, stride, channels)
        out[row : row + block] = value[:, REACH : REACH + tile_cols].astype(jnp.bfloat16)


def conv_chain(fetched, ok, shape):
    tile_rows, tile_cols, channels = shape
    stride = tile_cols + 2 * REACH
    held = [pltpu.VMEM(a.shape, a.dtype) for a in fetched]
    wides = [
        pltpu.VMEM(((tile_rows + h) * stride, 3 * channels), jnp.bfloat16) for h in (16, 12, 8, 4)
    ]
    slopes = pltpu.VMEM(((tile_rows + 4) * stride, channels), jnp.float32)
    pixels = sum((tile_rows + h) * stride for h in (12, 8, 4, 0))
    in_vmem = pl.BlockSpec(memory_space=pltpu.VMEM)
    return pl.pallas_call(
        conv_kernel,
        out_shape=jax.ShapeDtypeStruct(shape, jnp.bfloat16),
        in_specs=[pl.BlockSpec(memory_space=pltpu.HBM)] * FETCHED + [in_vmem],
        out_specs=in_vmem,
        scratch_shapes=[*held, *wides, slopes, pltpu.SemaphoreType.DMA((FETCHED,))],
        compiler_params=pltpu.CompilerParams(vmem_limit_bytes=48 * MIB),
        cost_estimate=pl.CostEstimate(
            flops=2 * 9 * channels * channels * pixels, bytes_accessed=6 * MIB, transcendentals=0
        ),
    )(*fetched, ok)


def neighbours(axis):
    size = lax.axis_size(axis)
    up = [(i, i + 1) for i in range(size - 1)]
    return up, [(j, i) for i, j in up]


def shards(
    features,
    target,
    hole_mask,
    kernel_first,
    kernel_second,
    inputs,
    weight_in,
    weight_out,
    weight_local,
    weight_mix,
):
    tile_rows, tile_cols, channels = features.shape
    row_devices, col_devices = lax.axis_size("row"), lax.axis_size("col")
    devices = row_devices * col_devices
    height, width = tile_rows * row_devices, tile_cols * col_devices
    strip, half = inputs.shape[0], weight_in.shape[1]
    owned = width // 2 // devices
    col_norm, row_norm = 1.0 / math.sqrt(width), 1.0 / math.sqrt(height)
    table = column_matrix(width, devices)
    table_back = jnp.asarray(np.ascontiguousarray(table.T))
    table = jnp.asarray(table)
    row_table = row_matrix(height, devices)
    row_back = jnp.asarray(np.ascontiguousarray(row_table.T))
    row_table = jnp.asarray(row_table)
    bf16 = jnp.bfloat16

    def swap(spectrum):
        return lax.all_to_all(spectrum, ("row", "col"), split_axis=0, concat_axis=0, tiled=True)

    cells = [jax.ShapeDtypeStruct((width, strip * half), bf16)]
    spatial_cols = vmem_call(
        functools.partial(spectrum_kernel, False, col_norm), cells, inputs, weight_in, table
    )[0]
    spatial_moved = swap(spatial_cols)

    up, down = neighbours("row")
    left, right = neighbours("col")
    above = lax.ppermute(features, "row", up)
    below = lax.ppermute(features, "row", down)
    pack_down, pack_up, mask_row = target_packs(target, hole_mask)
    target_above = lax.ppermute(pack_down, "row", up)
    target_below = lax.ppermute(pack_up, "row", down)
    last, initial = edges(above, features, below, target_above, target, mask_row, target_below)
    before = lax.ppermute(last, "col", left)
    after = lax.ppermute(initial, "col", right)

    row0, col0 = lax.axis_index("row") * tile_rows, lax.axis_index("col") * tile_cols
    row_ids = row0 - REACH + jnp.arange(tile_rows + 2 * REACH, dtype=jnp.int32)
    col_ids = col0 - REACH + jnp.arange(tile_cols + 2 * REACH, dtype=jnp.int32)
    ok = ((col_ids >= 0) & (col_ids < width))[:, None] & ((row_ids >= 0) & (row_ids < height))[None]
    ok = ok.astype(jnp.float32)
    fetched = (before, after, above, features, below, kernel_first)
    fetched += (target_above, target, target_below, mask_row, kernel_second)
    grad_feat = conv_chain(fetched, ok, features.shape)
    grad_feat, spatial_moved = lax.optimization_barrier((grad_feat, spatial_moved))

    cell_count = height * owned
    mix = weight_mix.reshape(2, half, 2, half).transpose(0, 2, 1, 3)
    wide = [pltpu.VMEM((strip * half // LANES, width, LANES), jnp.float32)]
    slope = vmem_call(
        functools.partial(slope_kernel, row_norm, owned, devices),
        [jax.ShapeDtypeStruct((2, cell_count, half), jnp.float32)],
        spatial_moved,
        mix,
        row_table,
        scratch=wide,
    )[0]

    strip_grad = lax.all_to_all(
        grad_feat.reshape(col_devices, strip, tile_cols, channels), "col", split_axis=0, concat_axis=0
    )
    grad_cols = vmem_call(
        functools.partial(spectrum_kernel, True, col_norm), cells, strip_grad, weight_out, table
    )[0]
    grad_moved = swap(grad_cols)
    grad_rows = vmem_call(
        functools.partial(mix_kernel, row_norm, owned, devices),
        cells,
        grad_moved,
        slope,
        mix,
        row_table,
        row_back,
        scratch=wide,
    )[0]
    returned = swap(grad_rows)
    return vmem_call(
        functools.partial(output_kernel, col_norm),
        [jax.ShapeDtypeStruct(inputs.shape, bf16)],
        returned,
        strip_grad,
        weight_in,
        weight_local,
        table_back,
    )[0]


def solution(mesh):
    in_specs = (
        P("row", "col", None),
        P("row", "col", None),
        P("row", "col"),
        P(),
        P(),
        P(("row", "col"), None, None),
        P(),
        P(),
        P(),
        P(),
    )
    out_specs = P(("row", "col"), None, None)
    return jax.shard_map(shards, mesh=mesh, in_specs=in_specs, out_specs=out_specs, check_vma=False)
```

```python
import functools
import math

import jax
import jax.numpy as jnp
import ml_dtypes
import numpy as np
from jax import lax
from jax.experimental import pallas as pl
from jax.experimental.pallas import tpu as pltpu
from jax.sharding import PartitionSpec as P

REACH = 8
NEAR = 4
MIB = 1024 * 1024
LANES = 128


def dot(left, right):
    return jnp.dot(left, right, preferred_element_type=jnp.float32)


def dot_t(left, right):
    return lax.dot_general(left, right, (((1,), (1,)), ((), ())), preferred_element_type=jnp.float32)


def vmem_call(body, shapes, *operands, flops=0, scratch=(), limit=10):
    spec = pl.BlockSpec(memory_space=pltpu.VMEM)
    size = sum(math.prod(a.shape) * a.dtype.itemsize for a in (*operands, *shapes))
    return pl.pallas_call(
        body,
        out_shape=shapes,
        in_specs=[spec] * len(operands),
        out_specs=[spec] * len(shapes),
        scratch_shapes=list(scratch),
        compiler_params=pltpu.CompilerParams(vmem_limit_bytes=limit * MIB),
        cost_estimate=pl.CostEstimate(flops=flops, bytes_accessed=size, transcendentals=0),
    )(*operands)


def phases(first, second, length):
    angle = (first[:, None] * second[None, :] % length) * (2.0 * math.pi / length)
    return np.cos(angle).astype(ml_dtypes.bfloat16), np.sin(angle).astype(ml_dtypes.bfloat16)


def column_matrix(width, devices):
    half = width // 2
    freq, col = np.arange(half), np.arange(width)
    cos, sin = phases(freq, col, width)
    sin[0] = (2 * (col % 2) - 1).astype(ml_dtypes.bfloat16)
    both = np.stack([cos, -sin]).reshape(2, devices, half // devices, width)
    return np.ascontiguousarray(both.transpose(1, 0, 2, 3)).reshape(width, width)


def row_matrix(height, devices):
    strip = height // devices
    rows = (np.arange(devices)[None, :] * strip + np.arange(strip)[:, None]).reshape(-1)
    cos, sin = phases(np.arange(height), rows, height)
    return np.block([[cos, sin], [-sin, cos]])


def strip_row(signal, r):
    if len(signal.shape) == 3:
        return signal[r]
    return jnp.concatenate([signal[block, r] for block in range(signal.shape[0])], axis=0)


def spectrum_kernel(transposed, norm, signal, weight, table, out):
    product = dot_t if transposed else dot
    count = signal.shape[0 if len(signal.shape) == 3 else 1]
    rows = [product(strip_row(signal, r), weight[...]).astype(jnp.bfloat16) for r in range(count)]
    out[...] = (dot(table[...], jnp.concatenate(rows, axis=1)) * norm).astype(jnp.bfloat16)


def row_spectrum(moved, table, wide, norm, owned, devices):
    groups = moved.shape[1] // LANES
    for g in range(groups):
        wide[g] = moved[:, g * LANES : (g + 1) * LANES].astype(jnp.float32)
    strip = table.shape[1] // (2 * devices)
    half = moved.shape[1] // strip
    height = table.shape[0] // 2
    real, imag = [], []
    for freq in range(owned):
        parts = []
        for part in range(2):
            where = pl.ds(part * owned + freq, devices, stride=2 * owned)
            block = jnp.concatenate([wide[g, where, :] for g in range(groups)], axis=1)
            parts += [block[:, r * half : (r + 1) * half] for r in range(strip)]
        result = dot(table[...], jnp.concatenate(parts, axis=0).astype(jnp.bfloat16)) * norm
        real.append(result[:height])
        imag.append(result[height:])
    return jnp.concatenate(real, axis=0), jnp.concatenate(imag, axis=0)


def slope_kernel(norm, owned, devices, moved, mix, table, out, wide):
    parts = row_spectrum(moved, table, wide, norm, owned, devices)
    real, imag = [part.astype(jnp.bfloat16) for part in parts]
    for part in range(2):
        pre = dot(real, mix[0, part]) + dot(imag, mix[1, part])
        s = 1.0 / (1.0 + jnp.exp(-pre))
        out[part] = s * (1.0 + pre * (1.0 - s))


def mix_kernel(norm, owned, devices, moved, slope, mix, table, back_table, out, wide):
    real, imag = row_spectrum(moved, table, wide, norm, owned, devices)
    real = (real * slope[0]).astype(jnp.bfloat16)
    imag = (imag * slope[1]).astype(jnp.bfloat16)
    back = [(dot_t(real, mix[p, 0]) + dot_t(imag, mix[p, 1])).astype(jnp.bfloat16) for p in range(2)]
    height = table.shape[0] // 2
    strip = height // devices
    groups = out.shape[1] // LANES
    for freq in range(owned):
        cells = slice(freq * height, (freq + 1) * height)
        stacked = jnp.concatenate([back[0][cells], back[1][cells]], axis=0)
        result = dot(back_table[...], stacked) * norm
        for part in range(2):
            rows = [
                result[(part * strip + r) * devices : (part * strip + r + 1) * devices]
                for r in range(strip)
            ]
            where = pl.ds(part * owned + freq, devices, stride=2 * owned)
            values = jnp.concatenate(rows, axis=1)
            for g in range(groups):
                wide[g, where, :] = values[:, g * LANES : (g + 1) * LANES]
    for g in range(groups):
        out[:, g * LANES : (g + 1) * LANES] = wide[g].astype(jnp.bfloat16)


def output_kernel(norm, moved, strip_grad, weight_in, weight_local, table, out):
    spatial = (dot(table[...], moved[...]) * norm).astype(jnp.bfloat16)
    half = weight_in.shape[1]
    for r in range(out.shape[0]):
        total = dot_t(spatial[:, r * half : (r + 1) * half], weight_in[...])
        total = total + dot_t(strip_row(strip_grad, r), weight_local[...])
        out[r] = total.astype(jnp.bfloat16)


def target_pack_kernel(first, last, mask, down, up, row):
    tile_rows, tile_cols = mask.shape
    channels = first.shape[2]
    lanes = jnp.concatenate(
        [
            mask[...].astype(jnp.float32),
            jnp.zeros((tile_cols - tile_rows, tile_cols), jnp.float32),
        ],
        axis=0,
    ).T
    lanes = jnp.concatenate([lanes] + [jnp.zeros_like(lanes)] * (channels // tile_cols - 1), axis=1)
    lanes = lanes.astype(jnp.bfloat16)
    row[0] = lanes
    for pack, part in ((down, last), (up, first)):
        pack[:NEAR] = part[...]
        pack[NEAR] = lanes


def target_packs(target, mask):
    tile_rows, tile_cols, channels = target.shape
    block = (NEAR, tile_cols, channels)
    shapes = [jax.ShapeDtypeStruct((n, tile_cols, channels), target.dtype) for n in (NEAR + 1, NEAR + 1, 1)]
    return pl.pallas_call(
        target_pack_kernel,
        grid=(1,),
        out_shape=shapes,
        in_specs=[
            pl.BlockSpec(block, lambda i: (0, 0, 0)),
            pl.BlockSpec(block, lambda i: (tile_rows // NEAR - 1, 0, 0)),
            pl.BlockSpec(mask.shape, lambda i: (0, 0)),
        ],
        out_specs=[pl.BlockSpec(shape.shape, lambda i: (0, 0, 0)) for shape in shapes],
    )(target, target, mask)


def edge_kernel(*refs):
    sources, outs = refs[:-2], refs[-2:]
    count = len(sources) // 2
    for out, group in zip(outs, (sources[:count], sources[count:])):
        row = 0
        for ref in group:
            out[row : row + ref.shape[0]] = ref[...]
            row += ref.shape[0]


def edges(*parts):
    features = parts[1]
    channels = features.shape[2]
    last = features.shape[1] // REACH - 1

    def specs(at):
        return [pl.BlockSpec((p.shape[0], REACH, channels), lambda i, at=at: (0, at, 0)) for p in parts]

    rows = sum(p.shape[0] for p in parts)
    shape = jax.ShapeDtypeStruct((rows, REACH, channels), features.dtype)
    return pl.pallas_call(
        edge_kernel,
        grid=(1,),
        out_shape=[shape, shape],
        in_specs=specs(last) + specs(0),
        out_specs=[pl.BlockSpec(shape.shape, lambda i: (0, 0, 0))] * 2,
        cost_estimate=pl.CostEstimate(
            flops=0, bytes_accessed=8 * rows * REACH * channels, transcendentals=0
        ),
    )(*parts, *parts)


def conv_kernel(
    before,
    after,
    above,
    features,
    below,
    first,
    target_above,
    target,
    target_below,
    mask_row,
    second,
    ok,
    out,
    wide_even,
    wide_odd,
    slopes,
):
    tile_rows, tile_cols, channels = features.shape
    stride = tile_cols + 2 * REACH
    block = NEAR
    size = block * stride
    tall = tile_rows + 2 * REACH

    def rows_of(edge, source, row, count=block):
        parts = [before[edge : edge + count], source[row : row + count], after[edge : edge + count]]
        parts = [part.astype(jnp.float32) for part in parts]
        return jnp.concatenate(parts, axis=1).reshape(count * stride, channels)

    def put(wide, row, value):
        spot = pl.ds(row * stride, size)
        wide[spot, :channels] = pltpu.roll(value, 2, 0).astype(jnp.bfloat16)
        wide[spot, channels : 2 * channels] = value.astype(jnp.bfloat16)
        wide[spot, 2 * channels :] = pltpu.roll(value, size - 2, 0).astype(jnp.bfloat16)

    def taps(wide, row):
        return jnp.concatenate(
            [wide[pl.ds((row + 2 * a) * stride, size), :] for a in range(3)], axis=1
        )

    def conv(wide, row, kernel):
        return dot(taps(wide, row), kernel[...].reshape(9 * channels, channels))

    def conv_adjoint(wide, row, kernel):
        flipped = [kernel[2 - a, 2 - b] for a in range(3) for b in range(3)]
        return dot_t(taps(wide, row), jnp.concatenate(flipped, axis=1))

    def inside(row):
        return jnp.concatenate([ok[:, row + i : row + i + 1] for i in range(block)], axis=0)

    for part, source in enumerate((above, features, below)):
        for row in range(0, tile_rows, block):
            at = part * tile_rows + row
            put(wide_even, at, rows_of(at, source, row))
    for row in range(0, tall - 4, block):
        pre = conv(wide_even, row, first)
        s = 1.0 / (1.0 + jnp.exp(-pre))
        kept = inside(row + 2)
        put(wide_odd, row, pre * s * kept)
        if NEAR <= row < tall - 4 - NEAR:
            slopes[pl.ds((row - NEAR) * stride, size), :] = s * (1.0 + pre * (1.0 - s)) * kept
    own = tall + NEAR + 1
    masks = [
        rows_of(tall + NEAR, target_above, NEAR, 1),
        rows_of(own + tile_rows, mask_row, 0, 1),
        rows_of(own + tile_rows + 1 + NEAR, target_below, NEAR, 1),
    ]
    goals = [(tall, target_above, 0, masks[0], tile_rows - NEAR)]
    goals += [(own + r, target, r, masks[1], r) for r in range(0, tile_rows, block)]
    goals += [(own + tile_rows + 1, target_below, 0, masks[2], 0)]
    for index, (edge, source, at, mask, lane) in enumerate(goals):
        row = index * block
        value = conv(wide_odd, row, second)
        holes = jnp.concatenate([mask[:, lane + i : lane + i + 1] for i in range(block)], axis=0)
        weight = (1.0 + 2.0 * holes) * inside(row + NEAR)
        put(wide_even, row, weight * (value - rows_of(edge, source, at)))
    for row in range(0, tile_rows + 4, block):
        value = conv_adjoint(wide_even, row, second)
        put(wide_odd, row, value * slopes[pl.ds(row * stride, size), :])
    for row in range(0, tile_rows, block):
        value = conv_adjoint(wide_odd, row, first).reshape(block, stride, channels)
        out[row : row + block] = value[:, REACH : REACH + tile_cols].astype(jnp.bfloat16)


def conv_chain(shape, *operands):
    tile_rows, tile_cols, channels = shape
    stride = tile_cols + 2 * REACH
    wides = [pltpu.VMEM(((tile_rows + h) * stride, 3 * channels), jnp.bfloat16) for h in (16, 12)]
    pixels = sum((tile_rows + h) * stride for h in (12, 8, 4, 0))
    return vmem_call(
        conv_kernel,
        [jax.ShapeDtypeStruct(shape, jnp.bfloat16)],
        *operands,
        flops=2 * 9 * channels * channels * pixels,
        scratch=[*wides, pltpu.VMEM(((tile_rows + 4) * stride, channels), jnp.float32)],
        limit=20,
    )[0]


def neighbours(axis):
    size = lax.axis_size(axis)
    up = [(i, i + 1) for i in range(size - 1)]
    return up, [(j, i) for i, j in up]


def shards(
    features,
    target,
    hole_mask,
    kernel_first,
    kernel_second,
    inputs,
    weight_in,
    weight_out,
    weight_local,
    weight_mix,
):
    tile_rows, tile_cols, channels = features.shape
    row_devices, col_devices = lax.axis_size("row"), lax.axis_size("col")
    devices = row_devices * col_devices
    height, width = tile_rows * row_devices, tile_cols * col_devices
    strip, half = inputs.shape[0], weight_in.shape[1]
    owned = width // 2 // devices
    col_norm, row_norm = 1.0 / math.sqrt(width), 1.0 / math.sqrt(height)
    table = column_matrix(width, devices)
    table_back = jnp.asarray(np.ascontiguousarray(table.T))
    table = jnp.asarray(table)
    row_table = row_matrix(height, devices)
    row_back = jnp.asarray(np.ascontiguousarray(row_table.T))
    row_table = jnp.asarray(row_table)
    bf16 = jnp.bfloat16

    def swap(spectrum):
        return lax.all_to_all(spectrum, ("row", "col"), split_axis=0, concat_axis=0, tiled=True)

    cells = [jax.ShapeDtypeStruct((width, strip * half), bf16)]
    spatial_cols = vmem_call(
        functools.partial(spectrum_kernel, False, col_norm), cells, inputs, weight_in, table
    )[0]
    up, down = neighbours("row")
    left, right = neighbours("col")
    above = lax.ppermute(features, "row", up)
    below = lax.ppermute(features, "row", down)
    pack_down, pack_up, mask_row = target_packs(target, hole_mask)
    target_above = lax.ppermute(pack_down, "row", up)
    target_below = lax.ppermute(pack_up, "row", down)
    last, initial = edges(above, features, below, target_above, target, mask_row, target_below)
    before = lax.ppermute(last, "col", left)
    after = lax.ppermute(initial, "col", right)
    after, spatial_cols = lax.optimization_barrier((after, spatial_cols))
    spatial_moved = swap(spatial_cols)

    row0, col0 = lax.axis_index("row") * tile_rows, lax.axis_index("col") * tile_cols
    row_ids = row0 - REACH + jnp.arange(tile_rows + 2 * REACH, dtype=jnp.int32)
    col_ids = col0 - REACH + jnp.arange(tile_cols + 2 * REACH, dtype=jnp.int32)
    ok = ((col_ids >= 0) & (col_ids < width))[:, None] & ((row_ids >= 0) & (row_ids < height))[None]
    ok = ok.astype(jnp.float32)
    grad_feat = conv_chain(
        features.shape,
        before,
        after,
        above,
        features,
        below,
        kernel_first,
        target_above,
        target,
        target_below,
        mask_row,
        kernel_second,
        ok,
    )
    grad_feat, spatial_moved = lax.optimization_barrier((grad_feat, spatial_moved))

    cell_count = height * owned
    mix = weight_mix.reshape(2, half, 2, half).transpose(0, 2, 1, 3)
    wide = [pltpu.VMEM((strip * half // LANES, width, LANES), jnp.float32)]
    slope = vmem_call(
        functools.partial(slope_kernel, row_norm, owned, devices),
        [jax.ShapeDtypeStruct((2, cell_count, half), jnp.float32)],
        spatial_moved,
        mix,
        row_table,
        scratch=wide,
    )[0]

    strip_grad = lax.all_to_all(
        grad_feat.reshape(col_devices, strip, tile_cols, channels), "col", split_axis=0, concat_axis=0
    )
    grad_cols = vmem_call(
        functools.partial(spectrum_kernel, True, col_norm), cells, strip_grad, weight_out, table
    )[0]
    grad_moved = swap(grad_cols)
    grad_rows = vmem_call(
        functools.partial(mix_kernel, row_norm, owned, devices),
        cells,
        grad_moved,
        slope,
        mix,
        row_table,
        row_back,
        scratch=wide,
    )[0]
    returned = swap(grad_rows)
    return vmem_call(
        functools.partial(output_kernel, col_norm),
        [jax.ShapeDtypeStruct(inputs.shape, bf16)],
        returned,
        strip_grad,
        weight_in,
        weight_local,
        table_back,
    )[0]


def solution(mesh):
    in_specs = (
        P("row", "col", None),
        P("row", "col", None),
        P("row", "col"),
        P(),
        P(),
        P(("row", "col"), None, None),
        P(),
        P(),
        P(),
        P(),
    )
    out_specs = P(("row", "col"), None, None)
    return jax.shard_map(shards, mesh=mesh, in_specs=in_specs, out_specs=out_specs, check_vma=False)
```

```python
import functools
import math

import jax
import jax.numpy as jnp
import ml_dtypes
import numpy as np
from jax import lax
from jax.experimental import pallas as pl
from jax.experimental.pallas import tpu as pltpu
from jax.sharding import PartitionSpec as P

REACH = 8
NEAR = 4
MIB = 1024 * 1024
LANES = 128


def dot(left, right):
    return jnp.dot(left, right, preferred_element_type=jnp.float32)


def dot_t(left, right):
    return lax.dot_general(left, right, (((1,), (1,)), ((), ())), preferred_element_type=jnp.float32)


def vmem_call(body, shapes, *operands, flops=0, scratch=(), limit=10):
    spec = pl.BlockSpec(memory_space=pltpu.VMEM)
    size = sum(math.prod(a.shape) * a.dtype.itemsize for a in (*operands, *shapes))
    return pl.pallas_call(
        body,
        out_shape=shapes,
        in_specs=[spec] * len(operands),
        out_specs=[spec] * len(shapes),
        scratch_shapes=list(scratch),
        compiler_params=pltpu.CompilerParams(vmem_limit_bytes=limit * MIB),
        cost_estimate=pl.CostEstimate(flops=flops, bytes_accessed=size, transcendentals=0),
    )(*operands)


def phases(first, second, length):
    angle = (first[:, None] * second[None, :] % length) * (2.0 * math.pi / length)
    return np.cos(angle).astype(ml_dtypes.bfloat16), np.sin(angle).astype(ml_dtypes.bfloat16)


def column_matrix(width, devices):
    half = width // 2
    freq, col = np.arange(half), np.arange(width)
    cos, sin = phases(freq, col, width)
    sin[0] = (2 * (col % 2) - 1).astype(ml_dtypes.bfloat16)
    both = np.stack([cos, -sin]).reshape(2, devices, half // devices, width)
    return np.ascontiguousarray(both.transpose(1, 0, 2, 3)).reshape(width, width)


def row_matrix(height, devices):
    strip = height // devices
    rows = (np.arange(devices)[None, :] * strip + np.arange(strip)[:, None]).reshape(-1)
    cos, sin = phases(np.arange(height), rows, height)
    return np.block([[cos, sin], [-sin, cos]])


def strip_row(signal, r):
    if len(signal.shape) == 3:
        return signal[r]
    return jnp.concatenate([signal[block, r] for block in range(signal.shape[0])], axis=0)


def strip_spectrum(signal, product, weight, table, norm):
    count = signal.shape[0 if len(signal.shape) == 3 else 1]
    rows = [product(strip_row(signal, r), weight[...]).astype(jnp.bfloat16) for r in range(count)]
    return (dot(table[...], jnp.concatenate(rows, axis=1)) * norm).astype(jnp.bfloat16)


def spatial_kernel(norm, signal, weight, table, out):
    out[...] = strip_spectrum(signal, dot, weight, table, norm)


def grad_kernel(norm, signal, weight, table, spatial, out):
    width = spatial.shape[1]
    out[:, :width] = spatial[...]
    out[:, width:] = strip_spectrum(signal, dot_t, weight, table, norm)


def row_spectrum(moved, table, wide, norm, owned, devices):
    groups = wide.shape[0]
    for g in range(groups):
        wide[g] = moved[:, g * LANES : (g + 1) * LANES].astype(jnp.float32)
    strip = table.shape[1] // (2 * devices)
    half = moved.shape[1] // strip
    height = table.shape[0] // 2
    real, imag = [], []
    for freq in range(owned):
        parts = []
        for part in range(2):
            where = pl.ds(part * owned + freq, devices, stride=2 * owned)
            block = jnp.concatenate([wide[g, where, :] for g in range(groups)], axis=1)
            parts += [block[:, r * half : (r + 1) * half] for r in range(strip)]
        result = dot(table[...], jnp.concatenate(parts, axis=0).astype(jnp.bfloat16)) * norm
        real.append(result[:height])
        imag.append(result[height:])
    return jnp.concatenate(real, axis=0), jnp.concatenate(imag, axis=0)


def mix_kernel(norm, owned, devices, moved, mix, table, back_table, out, wide, wide_grad):
    width = out.shape[1]
    parts = row_spectrum(moved.at[:, :width], table, wide, norm, owned, devices)
    real, imag = [part.astype(jnp.bfloat16) for part in parts]
    grads = row_spectrum(moved.at[:, width:], table, wide_grad, norm, owned, devices)
    mixed = []
    for part, grad in enumerate(grads):
        pre = dot(real, mix[0, part]) + dot(imag, mix[1, part])
        s = 1.0 / (1.0 + jnp.exp(-pre))
        mixed.append((grad * (s * (1.0 + pre * (1.0 - s)))).astype(jnp.bfloat16))
    back = [dot_t(mixed[0], mix[p, 0]) + dot_t(mixed[1], mix[p, 1]) for p in range(2)]
    back = [part.astype(jnp.bfloat16) for part in back]
    height = table.shape[0] // 2
    strip = height // devices
    groups = wide.shape[0]
    for freq in range(owned):
        cells = slice(freq * height, (freq + 1) * height)
        stacked = jnp.concatenate([back[0][cells], back[1][cells]], axis=0)
        result = dot(back_table[...], stacked) * norm
        for part in range(2):
            rows = [
                result[(part * strip + r) * devices : (part * strip + r + 1) * devices]
                for r in range(strip)
            ]
            where = pl.ds(part * owned + freq, devices, stride=2 * owned)
            values = jnp.concatenate(rows, axis=1)
            for g in range(groups):
                wide[g, where, :] = values[:, g * LANES : (g + 1) * LANES]
    for g in range(groups):
        out[:, g * LANES : (g + 1) * LANES] = wide[g].astype(jnp.bfloat16)


def output_kernel(norm, moved, strip_grad, weight_in, weight_local, table, out):
    spatial = (dot(table[...], moved[...]) * norm).astype(jnp.bfloat16)
    half = weight_in.shape[1]
    for r in range(out.shape[0]):
        total = dot_t(spatial[:, r * half : (r + 1) * half], weight_in[...])
        total = total + dot_t(strip_row(strip_grad, r), weight_local[...])
        out[r] = total.astype(jnp.bfloat16)


def target_pack_kernel(first, last, mask, down, up, row):
    tile_rows, tile_cols = mask.shape
    channels = first.shape[2]
    lanes = jnp.concatenate(
        [
            mask[...].astype(jnp.float32),
            jnp.zeros((tile_cols - tile_rows, tile_cols), jnp.float32),
        ],
        axis=0,
    ).T
    lanes = jnp.concatenate([lanes] + [jnp.zeros_like(lanes)] * (channels // tile_cols - 1), axis=1)
    lanes = lanes.astype(jnp.bfloat16)
    row[0] = lanes
    for pack, part in ((down, last), (up, first)):
        pack[:NEAR] = part[...]
        pack[NEAR] = lanes


def target_packs(target, mask):
    tile_rows, tile_cols, channels = target.shape
    block = (NEAR, tile_cols, channels)
    shapes = [jax.ShapeDtypeStruct((n, tile_cols, channels), target.dtype) for n in (NEAR + 1, NEAR + 1, 1)]
    return pl.pallas_call(
        target_pack_kernel,
        grid=(1,),
        out_shape=shapes,
        in_specs=[
            pl.BlockSpec(block, lambda i: (0, 0, 0)),
            pl.BlockSpec(block, lambda i: (tile_rows // NEAR - 1, 0, 0)),
            pl.BlockSpec(mask.shape, lambda i: (0, 0)),
        ],
        out_specs=[pl.BlockSpec(shape.shape, lambda i: (0, 0, 0)) for shape in shapes],
        compiler_params=pltpu.CompilerParams(vmem_limit_bytes=6 * MIB),
    )(target, target, mask)


def edge_kernel(*refs):
    sources, outs = refs[:-2], refs[-2:]
    count = len(sources) // 2
    for out, group in zip(outs, (sources[:count], sources[count:])):
        row = 0
        for ref in group:
            out[row : row + ref.shape[0]] = ref[...]
            row += ref.shape[0]


def edges(*parts):
    features = parts[1]
    channels = features.shape[2]
    last = features.shape[1] // REACH - 1

    def specs(at):
        return [pl.BlockSpec((p.shape[0], REACH, channels), lambda i, at=at: (0, at, 0)) for p in parts]

    rows = sum(p.shape[0] for p in parts)
    shape = jax.ShapeDtypeStruct((rows, REACH, channels), features.dtype)
    return pl.pallas_call(
        edge_kernel,
        grid=(1,),
        out_shape=[shape, shape],
        in_specs=specs(last) + specs(0),
        out_specs=[pl.BlockSpec(shape.shape, lambda i: (0, 0, 0))] * 2,
        compiler_params=pltpu.CompilerParams(vmem_limit_bytes=6 * MIB),
        cost_estimate=pl.CostEstimate(
            flops=0, bytes_accessed=8 * rows * REACH * channels, transcendentals=0
        ),
    )(*parts, *parts)


def conv_kernel(
    before,
    after,
    above,
    features,
    below,
    first,
    target_above,
    target,
    target_below,
    mask_row,
    second,
    ok,
    out,
    wide_even,
    wide_odd,
    slopes,
):
    tile_rows, tile_cols, channels = features.shape
    stride = tile_cols + 2 * REACH
    block = NEAR
    size = block * stride
    tall = tile_rows + 2 * REACH

    def rows_of(edge, source, row, count=block):
        parts = [before[edge : edge + count], source[row : row + count], after[edge : edge + count]]
        parts = [part.astype(jnp.float32) for part in parts]
        return jnp.concatenate(parts, axis=1).reshape(count * stride, channels)

    def put(wide, row, value):
        spot = pl.ds(row * stride, size)
        wide[spot, :channels] = pltpu.roll(value, 2, 0).astype(jnp.bfloat16)
        wide[spot, channels : 2 * channels] = value.astype(jnp.bfloat16)
        wide[spot, 2 * channels :] = pltpu.roll(value, size - 2, 0).astype(jnp.bfloat16)

    def taps(wide, row):
        return jnp.concatenate(
            [wide[pl.ds((row + 2 * a) * stride, size), :] for a in range(3)], axis=1
        )

    def conv(wide, row, kernel):
        return dot(taps(wide, row), kernel[...].reshape(9 * channels, channels))

    def conv_adjoint(wide, row, kernel):
        flipped = [kernel[2 - a, 2 - b] for a in range(3) for b in range(3)]
        return dot_t(taps(wide, row), jnp.concatenate(flipped, axis=1))

    def inside(row):
        return jnp.concatenate([ok[:, row + i : row + i + 1] for i in range(block)], axis=0)

    for part, source in enumerate((above, features, below)):
        for row in range(0, tile_rows, block):
            at = part * tile_rows + row
            put(wide_even, at, rows_of(at, source, row))
    for row in range(0, tall - 4, block):
        pre = conv(wide_even, row, first)
        s = 1.0 / (1.0 + jnp.exp(-pre))
        kept = inside(row + 2)
        put(wide_odd, row, pre * s * kept)
        if NEAR <= row < tall - 4 - NEAR:
            slopes[pl.ds((row - NEAR) * stride, size), :] = s * (1.0 + pre * (1.0 - s)) * kept
    own = tall + NEAR + 1
    masks = [
        rows_of(tall + NEAR, target_above, NEAR, 1),
        rows_of(own + tile_rows, mask_row, 0, 1),
        rows_of(own + tile_rows + 1 + NEAR, target_below, NEAR, 1),
    ]
    goals = [(tall, target_above, 0, masks[0], tile_rows - NEAR)]
    goals += [(own + r, target, r, masks[1], r) for r in range(0, tile_rows, block)]
    goals += [(own + tile_rows + 1, target_below, 0, masks[2], 0)]
    for index, (edge, source, at, mask, lane) in enumerate(goals):
        row = index * block
        value = conv(wide_odd, row, second)
        holes = jnp.concatenate([mask[:, lane + i : lane + i + 1] for i in range(block)], axis=0)
        weight = (1.0 + 2.0 * holes) * inside(row + NEAR)
        put(wide_even, row, weight * (value - rows_of(edge, source, at)))
    for row in range(0, tile_rows + 4, block):
        value = conv_adjoint(wide_even, row, second)
        put(wide_odd, row, value * slopes[pl.ds(row * stride, size), :])
    for row in range(0, tile_rows, block):
        value = conv_adjoint(wide_odd, row, first).reshape(block, stride, channels)
        out[row : row + block] = value[:, REACH : REACH + tile_cols].astype(jnp.bfloat16)


def conv_chain(shape, *operands):
    tile_rows, tile_cols, channels = shape
    stride = tile_cols + 2 * REACH
    wides = [pltpu.VMEM(((tile_rows + h) * stride, 3 * channels), jnp.bfloat16) for h in (16, 12)]
    pixels = sum((tile_rows + h) * stride for h in (12, 8, 4, 0))
    return vmem_call(
        conv_kernel,
        [jax.ShapeDtypeStruct(shape, jnp.bfloat16)],
        *operands,
        flops=2 * 9 * channels * channels * pixels,
        scratch=[*wides, pltpu.VMEM(((tile_rows + 4) * stride, channels), jnp.float32)],
        limit=20,
    )[0]


def neighbours(axis):
    size = lax.axis_size(axis)
    up = [(i, i + 1) for i in range(size - 1)]
    return up, [(j, i) for i, j in up]


def shards(
    features,
    target,
    hole_mask,
    kernel_first,
    kernel_second,
    inputs,
    weight_in,
    weight_out,
    weight_local,
    weight_mix,
):
    tile_rows, tile_cols, channels = features.shape
    row_devices, col_devices = lax.axis_size("row"), lax.axis_size("col")
    devices = row_devices * col_devices
    height, width = tile_rows * row_devices, tile_cols * col_devices
    strip, half = inputs.shape[0], weight_in.shape[1]
    owned = width // 2 // devices
    col_norm, row_norm = 1.0 / math.sqrt(width), 1.0 / math.sqrt(height)
    table = column_matrix(width, devices)
    table_back = jnp.asarray(np.ascontiguousarray(table.T))
    table = jnp.asarray(table)
    row_table = row_matrix(height, devices)
    row_back = jnp.asarray(np.ascontiguousarray(row_table.T))
    row_table = jnp.asarray(row_table)
    bf16 = jnp.bfloat16

    def swap(spectrum):
        return lax.all_to_all(spectrum, ("row", "col"), split_axis=0, concat_axis=0, tiled=True)

    cells = [jax.ShapeDtypeStruct((width, strip * half), bf16)]
    spatial_cols = vmem_call(
        functools.partial(spatial_kernel, col_norm), cells, inputs, weight_in, table
    )[0]
    up, down = neighbours("row")
    left, right = neighbours("col")
    above = lax.ppermute(features, "row", up)
    below = lax.ppermute(features, "row", down)
    pack_down, pack_up, mask_row = target_packs(target, hole_mask)
    target_above = lax.ppermute(pack_down, "row", up)
    target_below = lax.ppermute(pack_up, "row", down)
    above, spatial_cols = lax.optimization_barrier((above, spatial_cols))
    last, initial = edges(above, features, below, target_above, target, mask_row, target_below)
    before = lax.ppermute(last, "col", left)
    after = lax.ppermute(initial, "col", right)

    row0, col0 = lax.axis_index("row") * tile_rows, lax.axis_index("col") * tile_cols
    row_ids = row0 - REACH + jnp.arange(tile_rows + 2 * REACH, dtype=jnp.int32)
    col_ids = col0 - REACH + jnp.arange(tile_cols + 2 * REACH, dtype=jnp.int32)
    ok = ((col_ids >= 0) & (col_ids < width))[:, None] & ((row_ids >= 0) & (row_ids < height))[None]
    ok = ok.astype(jnp.float32)
    grad_feat = conv_chain(
        features.shape,
        before,
        after,
        above,
        features,
        below,
        kernel_first,
        target_above,
        target,
        target_below,
        mask_row,
        kernel_second,
        ok,
    )

    strip_grad = lax.all_to_all(
        grad_feat.reshape(col_devices, strip, tile_cols, channels), "col", split_axis=0, concat_axis=0
    )
    both_cols = vmem_call(
        functools.partial(grad_kernel, col_norm),
        [jax.ShapeDtypeStruct((width, 2 * strip * half), bf16)],
        strip_grad,
        weight_out,
        table,
        spatial_cols,
    )[0]
    mix = weight_mix.reshape(2, half, 2, half).transpose(0, 2, 1, 3)
    wide = pltpu.VMEM((strip * half // LANES, width, LANES), jnp.float32)
    grad_rows = vmem_call(
        functools.partial(mix_kernel, row_norm, owned, devices),
        cells,
        swap(both_cols),
        mix,
        row_table,
        row_back,
        scratch=[wide, wide],
    )[0]
    returned = swap(grad_rows)
    return vmem_call(
        functools.partial(output_kernel, col_norm),
        [jax.ShapeDtypeStruct(inputs.shape, bf16)],
        returned,
        strip_grad,
        weight_in,
        weight_local,
        table_back,
    )[0]


def solution(mesh):
    in_specs = (
        P("row", "col", None),
        P("row", "col", None),
        P("row", "col"),
        P(),
        P(),
        P(("row", "col"), None, None),
        P(),
        P(),
        P(),
        P(),
    )
    out_specs = P(("row", "col"), None, None)
    return jax.shard_map(shards, mesh=mesh, in_specs=in_specs, out_specs=out_specs, check_vma=False)
```

```python
import functools
import math

import jax
import jax.numpy as jnp
import ml_dtypes
import numpy as np
from jax import lax
from jax.experimental import pallas as pl
from jax.experimental.pallas import tpu as pltpu
from jax.sharding import PartitionSpec as P

REACH = 8
NEAR = 4
MIB = 1024 * 1024
LANES = 128


def dot(left, right):
    return jnp.dot(left, right, preferred_element_type=jnp.float32)


def dot_t(left, right):
    return lax.dot_general(left, right, (((1,), (1,)), ((), ())), preferred_element_type=jnp.float32)


def vmem_call(body, shapes, *operands, flops=0, scratch=(), limit=10):
    spec = pl.BlockSpec(memory_space=pltpu.VMEM)
    size = sum(math.prod(a.shape) * a.dtype.itemsize for a in (*operands, *shapes))
    return pl.pallas_call(
        body,
        out_shape=shapes,
        in_specs=[spec] * len(operands),
        out_specs=[spec] * len(shapes),
        scratch_shapes=list(scratch),
        compiler_params=pltpu.CompilerParams(vmem_limit_bytes=limit * MIB),
        cost_estimate=pl.CostEstimate(flops=flops, bytes_accessed=size, transcendentals=0),
    )(*operands)


def phases(first, second, length):
    angle = (first[:, None] * second[None, :] % length) * (2.0 * math.pi / length)
    return np.cos(angle).astype(ml_dtypes.bfloat16), np.sin(angle).astype(ml_dtypes.bfloat16)


def column_matrix(width, devices):
    half = width // 2
    freq, col = np.arange(half), np.arange(width)
    cos, sin = phases(freq, col, width)
    sin[0] = (2 * (col % 2) - 1).astype(ml_dtypes.bfloat16)
    both = np.stack([cos, -sin]).reshape(2, devices, half // devices, width)
    return np.ascontiguousarray(both.transpose(1, 0, 2, 3)).reshape(width, width)


def row_matrix(height, devices):
    strip = height // devices
    rows = (np.arange(devices)[None, :] * strip + np.arange(strip)[:, None]).reshape(-1)
    cos, sin = phases(np.arange(height), rows, height)
    return np.block([[cos, sin], [-sin, cos]])


def strip_row(signal, r):
    if len(signal.shape) == 3:
        return signal[r]
    return jnp.concatenate([signal[block, r] for block in range(signal.shape[0])], axis=0)


def strip_spectrum(signal, product, weight, table, norm):
    count = signal.shape[0 if len(signal.shape) == 3 else 1]
    rows = [product(strip_row(signal, r), weight[...]).astype(jnp.bfloat16) for r in range(count)]
    return (dot(table[...], jnp.concatenate(rows, axis=1)) * norm).astype(jnp.bfloat16)


def spatial_kernel(norm, signal, weight, table, out):
    out[...] = strip_spectrum(signal, dot, weight, table, norm)


def grad_kernel(norm, signal, weight, table, spatial, out):
    width = spatial.shape[1]
    out[:, :width] = spatial[...]
    out[:, width:] = strip_spectrum(signal, dot_t, weight, table, norm)


def row_spectrum(moved, table, wide, norm, owned, devices):
    groups = wide.shape[0]
    for g in range(groups):
        wide[g] = moved[:, g * LANES : (g + 1) * LANES].astype(jnp.float32)
    strip = table.shape[1] // (2 * devices)
    half = moved.shape[1] // strip
    height = table.shape[0] // 2
    real, imag = [], []
    for freq in range(owned):
        parts = []
        for part in range(2):
            where = pl.ds(part * owned + freq, devices, stride=2 * owned)
            block = jnp.concatenate([wide[g, where, :] for g in range(groups)], axis=1)
            parts += [block[:, r * half : (r + 1) * half] for r in range(strip)]
        result = dot(table[...], jnp.concatenate(parts, axis=0).astype(jnp.bfloat16)) * norm
        real.append(result[:height])
        imag.append(result[height:])
    return jnp.concatenate(real, axis=0), jnp.concatenate(imag, axis=0)


def mix_kernel(norm, owned, devices, moved, mix, table, back_table, out, wide, wide_grad):
    width = out.shape[1]
    parts = row_spectrum(moved.at[:, :width], table, wide, norm, owned, devices)
    real, imag = [part.astype(jnp.bfloat16) for part in parts]
    grads = row_spectrum(moved.at[:, width:], table, wide_grad, norm, owned, devices)
    mixed = []
    for part, grad in enumerate(grads):
        pre = dot(real, mix[0, part]) + dot(imag, mix[1, part])
        s = 1.0 / (1.0 + jnp.exp(-pre))
        mixed.append((grad * (s * (1.0 + pre * (1.0 - s)))).astype(jnp.bfloat16))
    back = [dot_t(mixed[0], mix[p, 0]) + dot_t(mixed[1], mix[p, 1]) for p in range(2)]
    back = [part.astype(jnp.bfloat16) for part in back]
    height = table.shape[0] // 2
    strip = height // devices
    groups = wide.shape[0]
    for freq in range(owned):
        cells = slice(freq * height, (freq + 1) * height)
        stacked = jnp.concatenate([back[0][cells], back[1][cells]], axis=0)
        result = dot(back_table[...], stacked) * norm
        for part in range(2):
            rows = [
                result[(part * strip + r) * devices : (part * strip + r + 1) * devices]
                for r in range(strip)
            ]
            where = pl.ds(part * owned + freq, devices, stride=2 * owned)
            values = jnp.concatenate(rows, axis=1)
            for g in range(groups):
                wide[g, where, :] = values[:, g * LANES : (g + 1) * LANES]
    for g in range(groups):
        out[:, g * LANES : (g + 1) * LANES] = wide[g].astype(jnp.bfloat16)


def output_kernel(norm, moved, strip_grad, weight_in, weight_local, table, out):
    spatial = (dot(table[...], moved[...]) * norm).astype(jnp.bfloat16)
    half = weight_in.shape[1]
    for r in range(out.shape[0]):
        total = dot_t(spatial[:, r * half : (r + 1) * half], weight_in[...])
        total = total + dot_t(strip_row(strip_grad, r), weight_local[...])
        out[r] = total.astype(jnp.bfloat16)


def target_pack_kernel(first, last, mask, down, up, row):
    tile_rows, tile_cols = mask.shape
    channels = first.shape[2]
    lanes = jnp.concatenate(
        [
            mask[...].astype(jnp.float32),
            jnp.zeros((tile_cols - tile_rows, tile_cols), jnp.float32),
        ],
        axis=0,
    ).T
    lanes = jnp.concatenate([lanes] + [jnp.zeros_like(lanes)] * (channels // tile_cols - 1), axis=1)
    lanes = lanes.astype(jnp.bfloat16)
    row[0] = lanes
    for pack, part in ((down, last), (up, first)):
        pack[:NEAR] = part[...]
        pack[NEAR] = lanes


def target_packs(target, mask):
    tile_rows, tile_cols, channels = target.shape
    block = (NEAR, tile_cols, channels)
    shapes = [jax.ShapeDtypeStruct((n, tile_cols, channels), target.dtype) for n in (NEAR + 1, NEAR + 1, 1)]
    return pl.pallas_call(
        target_pack_kernel,
        grid=(1,),
        out_shape=shapes,
        in_specs=[
            pl.BlockSpec(block, lambda i: (0, 0, 0)),
            pl.BlockSpec(block, lambda i: (tile_rows // NEAR - 1, 0, 0)),
            pl.BlockSpec(mask.shape, lambda i: (0, 0)),
        ],
        out_specs=[pl.BlockSpec(shape.shape, lambda i: (0, 0, 0)) for shape in shapes],
        compiler_params=pltpu.CompilerParams(vmem_limit_bytes=6 * MIB),
    )(target, target, mask)


def edge_kernel(*refs):
    sources, outs = refs[:-2], refs[-2:]
    count = len(sources) // 2
    for out, group in zip(outs, (sources[:count], sources[count:])):
        row = 0
        for ref in group:
            out[row : row + ref.shape[0]] = ref[...]
            row += ref.shape[0]


def edges(*parts):
    features = parts[1]
    channels = features.shape[2]
    last = features.shape[1] // REACH - 1

    def specs(at):
        return [pl.BlockSpec((p.shape[0], REACH, channels), lambda i, at=at: (0, at, 0)) for p in parts]

    rows = sum(p.shape[0] for p in parts)
    shape = jax.ShapeDtypeStruct((rows, REACH, channels), features.dtype)
    return pl.pallas_call(
        edge_kernel,
        grid=(1,),
        out_shape=[shape, shape],
        in_specs=specs(last) + specs(0),
        out_specs=[pl.BlockSpec(shape.shape, lambda i: (0, 0, 0))] * 2,
        compiler_params=pltpu.CompilerParams(vmem_limit_bytes=6 * MIB),
        cost_estimate=pl.CostEstimate(
            flops=0, bytes_accessed=8 * rows * REACH * channels, transcendentals=0
        ),
    )(*parts, *parts)


def put(wide, row, value, stride):
    size, channels = value.shape
    spot = pl.ds(row * stride, size)
    wide[spot, :channels] = pltpu.roll(value, 2, 0).astype(jnp.bfloat16)
    wide[spot, channels : 2 * channels] = value.astype(jnp.bfloat16)
    wide[spot, 2 * channels :] = pltpu.roll(value, size - 2, 0).astype(jnp.bfloat16)


def taps(wide, row, count, stride):
    parts = [wide[pl.ds((row + 2 * a) * stride, count * stride), :] for a in range(3)]
    return jnp.concatenate(parts, axis=1)


def conv(wide, row, count, stride, kernel):
    channels = kernel.shape[-1]
    return dot(taps(wide, row, count, stride), kernel[...].reshape(9 * channels, channels))


def conv_adjoint(wide, row, count, stride, kernel):
    flipped = [kernel[2 - a, 2 - b] for a in range(3) for b in range(3)]
    return dot_t(taps(wide, row, count, stride), jnp.concatenate(flipped, axis=1))


def stacked(piece, rows):
    return jnp.concatenate([piece(row) for row in rows], axis=0)


def first_stages(stride, blocks, rows, feature, inside, first, second, wide_even, wide_odd, slopes, use):
    tall = rows + 2 * REACH
    for row in range(0, tall, NEAR):
        put(wide_even, row, stacked(feature, range(row, row + NEAR)), stride)
    count = blocks[0]
    for row in range(0, tall - 4, count):
        pre = conv(wide_even, row, count, stride, first)
        s = 1.0 / (1.0 + jnp.exp(-pre))
        kept = stacked(inside, range(row + 2, row + 2 + count))
        put(wide_odd, row, pre * s * kept, stride)
        low, high = max(row, NEAR), min(row + count, tall - 4 - NEAR)
        if low < high:
            part = slice((low - row) * stride, (high - row) * stride)
            slope = (s * (1.0 + pre * (1.0 - s)) * kept)[part]
            slopes[pl.ds((low - NEAR) * stride, (high - low) * stride), :] = slope
    count = blocks[1]
    for row in range(0, rows + 2 * NEAR, count):
        use(row, count, conv(wide_odd, row, count, stride, second))


def last_stages(stride, blocks, rows, first, second, wide_even, wide_odd, slopes, use):
    count = blocks[2]
    for row in range(0, rows + 4, count):
        value = conv_adjoint(wide_even, row, count, stride, second)
        value = value * slopes[pl.ds(row * stride, count * stride), :]
        put(wide_odd, row, value, stride)
    count = blocks[3]
    for row in range(0, rows, count):
        use(row, count, conv_adjoint(wide_odd, row, count, stride, first))


def loss_grad(row, count, value, target, hole, inside):
    near = range(row, row + count)
    weight = (1.0 + 2.0 * stacked(hole, near)) * stacked(inside, range(row + NEAR, row + count + NEAR))
    return weight * (value - stacked(target, near))


def part_of(rows, edge, above, own, below):
    def find(row):
        if row < edge:
            return above, row
        if row < edge + rows:
            return own, row - edge
        return below, row - edge - rows

    return find


TILE_BLOCKS = (4, 4, 4, 4)
SIDE_BLOCKS = (10, 8, 12, 8)


def tile_forward_kernel(above, features, below, first, second, ok, pre, slopes, wide_even, wide_odd):
    rows, stride, _ = features.shape
    find = part_of(rows, REACH, above, features, below)

    def feature(row):
        source, at = find(row)
        return source[at].astype(jnp.float32)

    def inside(row):
        return ok[REACH : REACH + stride, row : row + 1]

    def use(row, count, value):
        pre[pl.ds(row * stride, count * stride), :] = value

    first_stages(
        stride, TILE_BLOCKS, rows, feature, inside, first, second, wide_even, wide_odd, slopes, use
    )


def tile_backward_kernel(
    pre,
    slopes,
    target_above,
    target,
    target_below,
    mask_row,
    first,
    second,
    ok,
    out,
    wide_even,
    wide_odd,
):
    rows, stride, channels = target.shape
    find = part_of(rows, NEAR, target_above, target, target_below)

    def goal(row):
        source, at = find(row)
        return source[at].astype(jnp.float32)

    masks = [m[at].astype(jnp.float32) for m, at in ((target_above, NEAR), (mask_row, 0), (target_below, NEAR))]
    find_mask = part_of(rows, NEAR, (masks[0], rows - NEAR), (masks[1], 0), (masks[2], 0))

    def hole(row):
        (mask, start), at = find_mask(row)
        return mask[:, start + at : start + at + 1]

    def inside(row):
        return ok[REACH : REACH + stride, row : row + 1]

    count = NEAR
    for row in range(0, rows + 2 * NEAR, count):
        value = pre[pl.ds(row * stride, count * stride), :]
        put(wide_even, row, loss_grad(row, count, value, goal, hole, inside), stride)

    def use(row, count, value):
        out[row : row + count] = value.reshape(count, stride, channels).astype(jnp.bfloat16)

    last_stages(stride, TILE_BLOCKS, rows, first, second, wide_even, wide_odd, slopes, use)


def side_kernel(
    before,
    after,
    above,
    features,
    below,
    target_above,
    target,
    target_below,
    mask_row,
    first,
    second,
    ok,
    tile,
    out,
    wide_even,
    wide_odd,
    slopes,
):
    rows, tile_cols, channels = features.shape
    keep = 2 * REACH
    stride = 2 * (REACH + keep)
    tall = rows + 2 * REACH
    own = tall + NEAR + 1

    def joined(edge, source, at):
        parts = [before[edge], source[at, :keep], source[at, tile_cols - keep :], after[edge]]
        return jnp.concatenate([part.astype(jnp.float32) for part in parts], axis=0)

    find = part_of(rows, REACH, above, features, below)
    find_target = part_of(
        rows, NEAR, (target_above, tall), (target, own), (target_below, own + rows + 1)
    )

    def feature(row):
        return joined(row, *find(row))

    def goal(row):
        (source, edge), at = find_target(row)
        return joined(edge + at, source, at)

    masks = [
        joined(tall + NEAR, target_above, NEAR),
        joined(own + rows, mask_row, 0),
        joined(own + rows + 1 + NEAR, target_below, NEAR),
    ]
    find_mask = part_of(rows, NEAR, (masks[0], rows - NEAR), (masks[1], 0), (masks[2], 0))

    def hole(row):
        (mask, start), at = find_mask(row)
        return mask[:, start + at : start + at + 1]

    width = ok.shape[0]
    kept = jnp.concatenate([ok[: REACH + keep], ok[width - REACH - keep :]], axis=0)

    def inside(row):
        return kept[:, row : row + 1]

    def use_forward(row, count, value):
        put(wide_even, row, loss_grad(row, count, value, goal, hole, inside), stride)

    first_stages(
        stride, SIDE_BLOCKS, rows, feature, inside, first, second, wide_even, wide_odd, slopes, use_forward
    )
    out[:, REACH : tile_cols - REACH] = tile[:, REACH : tile_cols - REACH]

    def use(row, count, value):
        value = value.reshape(count, stride, channels).astype(jnp.bfloat16)
        out[row : row + count, :REACH] = value[:, REACH : 2 * REACH]
        out[row : row + count, tile_cols - REACH :] = value[:, stride - 2 * REACH : stride - REACH]

    last_stages(stride, SIDE_BLOCKS, rows, first, second, wide_even, wide_odd, slopes, use)


def wide_buffer(rows, stride, channels):
    return pltpu.VMEM((rows * stride, 3 * channels), jnp.bfloat16)


def tile_forward(above, features, below, first, second, ok):
    rows, stride, channels = features.shape
    shapes = [
        jax.ShapeDtypeStruct(((rows + h) * stride, channels), jnp.float32) for h in (2 * NEAR, 4)
    ]
    return vmem_call(
        tile_forward_kernel,
        shapes,
        above,
        features,
        below,
        first,
        second,
        ok,
        flops=2 * 9 * channels * channels * stride * (2 * rows + 20),
        scratch=[wide_buffer(rows + h, stride, channels) for h in (16, 12)],
        limit=18,
    )


def tile_backward(pre, slopes, target_above, target, target_below, mask_row, first, second, ok):
    rows, stride, channels = target.shape
    return vmem_call(
        tile_backward_kernel,
        [jax.ShapeDtypeStruct(target.shape, jnp.bfloat16)],
        pre,
        slopes,
        target_above,
        target,
        target_below,
        mask_row,
        first,
        second,
        ok,
        flops=2 * 9 * channels * channels * stride * (2 * rows + 4),
        scratch=[wide_buffer(rows + h, stride, channels) for h in (8, 4)],
        limit=16,
    )[0]


def sides(tile, *operands):
    rows, _, channels = tile.shape
    stride = 6 * REACH
    return vmem_call(
        side_kernel,
        [jax.ShapeDtypeStruct(tile.shape, jnp.bfloat16)],
        *operands,
        tile,
        flops=2 * 9 * channels * channels * stride * (4 * rows + 24),
        scratch=[wide_buffer(rows + h, stride, channels) for h in (16, 12)]
        + [pltpu.VMEM(((rows + 4) * stride, channels), jnp.float32)],
        limit=14,
    )[0]


def neighbours(axis):
    size = lax.axis_size(axis)
    up = [(i, i + 1) for i in range(size - 1)]
    return up, [(j, i) for i, j in up]


def shards(
    features,
    target,
    hole_mask,
    kernel_first,
    kernel_second,
    inputs,
    weight_in,
    weight_out,
    weight_local,
    weight_mix,
):
    tile_rows, tile_cols, channels = features.shape
    row_devices, col_devices = lax.axis_size("row"), lax.axis_size("col")
    devices = row_devices * col_devices
    height, width = tile_rows * row_devices, tile_cols * col_devices
    strip, half = inputs.shape[0], weight_in.shape[1]
    owned = width // 2 // devices
    col_norm, row_norm = 1.0 / math.sqrt(width), 1.0 / math.sqrt(height)
    table = column_matrix(width, devices)
    table_back = jnp.asarray(np.ascontiguousarray(table.T))
    table = jnp.asarray(table)
    row_table = row_matrix(height, devices)
    row_back = jnp.asarray(np.ascontiguousarray(row_table.T))
    row_table = jnp.asarray(row_table)
    bf16 = jnp.bfloat16

    def swap(spectrum):
        return lax.all_to_all(spectrum, ("row", "col"), split_axis=0, concat_axis=0, tiled=True)

    cells = [jax.ShapeDtypeStruct((width, strip * half), bf16)]
    spatial_cols = vmem_call(
        functools.partial(spatial_kernel, col_norm), cells, inputs, weight_in, table
    )[0]
    row0, col0 = lax.axis_index("row") * tile_rows, lax.axis_index("col") * tile_cols
    row_ids = row0 - REACH + jnp.arange(tile_rows + 2 * REACH, dtype=jnp.int32)
    col_ids = col0 - REACH + jnp.arange(tile_cols + 2 * REACH, dtype=jnp.int32)
    ok = ((col_ids >= 0) & (col_ids < width))[:, None] & ((row_ids >= 0) & (row_ids < height))[None]
    ok = ok.astype(jnp.float32)

    up, down = neighbours("row")
    left, right = neighbours("col")
    above = lax.ppermute(features, "row", up)
    below = lax.ppermute(features, "row", down)
    pack_down, pack_up, mask_row = target_packs(target, hole_mask)
    target_above = lax.ppermute(pack_down, "row", up)
    target_below = lax.ppermute(pack_up, "row", down)
    pre, slopes = tile_forward(above, features, below, kernel_first, kernel_second, ok)
    target_above, pre, spatial_cols = lax.optimization_barrier((target_above, pre, spatial_cols))
    last, initial = edges(above, features, below, target_above, target, mask_row, target_below)
    before = lax.ppermute(last, "col", left)
    after = lax.ppermute(initial, "col", right)
    tile = tile_backward(
        pre, slopes, target_above, target, target_below, mask_row, kernel_first, kernel_second, ok
    )
    grad_feat = sides(
        tile,
        before,
        after,
        above,
        features,
        below,
        target_above,
        target,
        target_below,
        mask_row,
        kernel_first,
        kernel_second,
        ok,
    )

    strip_grad = lax.all_to_all(
        grad_feat.reshape(col_devices, strip, tile_cols, channels), "col", split_axis=0, concat_axis=0
    )
    both_cols = vmem_call(
        functools.partial(grad_kernel, col_norm),
        [jax.ShapeDtypeStruct((width, 2 * strip * half), bf16)],
        strip_grad,
        weight_out,
        table,
        spatial_cols,
    )[0]
    mix = weight_mix.reshape(2, half, 2, half).transpose(0, 2, 1, 3)
    wide = pltpu.VMEM((strip * half // LANES, width, LANES), jnp.float32)
    grad_rows = vmem_call(
        functools.partial(mix_kernel, row_norm, owned, devices),
        cells,
        swap(both_cols),
        mix,
        row_table,
        row_back,
        scratch=[wide, wide],
    )[0]
    returned = swap(grad_rows)
    return vmem_call(
        functools.partial(output_kernel, col_norm),
        [jax.ShapeDtypeStruct(inputs.shape, bf16)],
        returned,
        strip_grad,
        weight_in,
        weight_local,
        table_back,
    )[0]


def solution(mesh):
    in_specs = (
        P("row", "col", None),
        P("row", "col", None),
        P("row", "col"),
        P(),
        P(),
        P(("row", "col"), None, None),
        P(),
        P(),
        P(),
        P(),
    )
    out_specs = P(("row", "col"), None, None)
    return jax.shard_map(shards, mesh=mesh, in_specs=in_specs, out_specs=out_specs, check_vma=False)
```

```python
import functools
import math

import jax
import jax.numpy as jnp
import ml_dtypes
import numpy as np
from jax import lax
from jax.experimental import pallas as pl
from jax.experimental.pallas import tpu as pltpu
from jax.sharding import PartitionSpec as P

REACH = 8
NEAR = 4
MIB = 1024 * 1024
LANES = 128


def dot(left, right):
    return jnp.dot(left, right, preferred_element_type=jnp.float32)


def dot_t(left, right):
    return lax.dot_general(left, right, (((1,), (1,)), ((), ())), preferred_element_type=jnp.float32)


def vmem_call(body, shapes, *operands, flops=0, scratch=(), limit=10):
    spec = pl.BlockSpec(memory_space=pltpu.VMEM)
    size = sum(math.prod(a.shape) * a.dtype.itemsize for a in (*operands, *shapes))
    return pl.pallas_call(
        body,
        out_shape=shapes,
        in_specs=[spec] * len(operands),
        out_specs=[spec] * len(shapes),
        scratch_shapes=list(scratch),
        compiler_params=pltpu.CompilerParams(vmem_limit_bytes=limit * MIB),
        cost_estimate=pl.CostEstimate(flops=flops, bytes_accessed=size, transcendentals=0),
    )(*operands)


def phases(first, second, length):
    angle = (first[:, None] * second[None, :] % length) * (2.0 * math.pi / length)
    return np.cos(angle).astype(ml_dtypes.bfloat16), np.sin(angle).astype(ml_dtypes.bfloat16)


def column_matrix(width, devices):
    half = width // 2
    freq, col = np.arange(half), np.arange(width)
    cos, sin = phases(freq, col, width)
    sin[0] = (2 * (col % 2) - 1).astype(ml_dtypes.bfloat16)
    both = np.stack([cos, -sin]).reshape(2, devices, half // devices, width)
    return np.ascontiguousarray(both.transpose(1, 0, 2, 3)).reshape(width, width)


def row_matrix(height, devices):
    strip = height // devices
    rows = (np.arange(devices)[None, :] * strip + np.arange(strip)[:, None]).reshape(-1)
    cos, sin = phases(np.arange(height), rows, height)
    return np.block([[cos, sin], [-sin, cos]])


def strip_row(signal, r):
    if len(signal.shape) == 3:
        return signal[r]
    return jnp.concatenate([signal[block, r] for block in range(signal.shape[0])], axis=0)


def strip_spectrum(signal, weight, table, norm):
    count = signal.shape[0 if len(signal.shape) == 3 else 1]
    rows = [dot_t(strip_row(signal, r), weight[...]).astype(jnp.bfloat16) for r in range(count)]
    return (dot(table[...], jnp.concatenate(rows, axis=1)) * norm).astype(jnp.bfloat16)


def spectrum_kernel(norm, signal, weight, table, out):
    out[...] = strip_spectrum(signal, weight, table, norm)


def row_spectrum(moved, table, wide, norm, owned, devices):
    groups = wide.shape[0]
    for g in range(groups):
        wide[g] = moved[:, g * LANES : (g + 1) * LANES].astype(jnp.float32)
    strip = table.shape[1] // (2 * devices)
    half = moved.shape[1] // strip
    height = table.shape[0] // 2
    real, imag = [], []
    for freq in range(owned):
        parts = []
        for part in range(2):
            where = pl.ds(part * owned + freq, devices, stride=2 * owned)
            block = jnp.concatenate([wide[g, where, :] for g in range(groups)], axis=1)
            parts += [block[:, r * half : (r + 1) * half] for r in range(strip)]
        result = dot(table[...], jnp.concatenate(parts, axis=0).astype(jnp.bfloat16)) * norm
        real.append(result[:height])
        imag.append(result[height:])
    return jnp.concatenate(real, axis=0), jnp.concatenate(imag, axis=0)


def mix_kernel(norm, owned, devices, spatial, grad, mix, table, back_table, out, wide, wide_grad):
    parts = row_spectrum(spatial, table, wide, norm, owned, devices)
    real, imag = [part.astype(jnp.bfloat16) for part in parts]
    grads = row_spectrum(grad, table, wide_grad, norm, owned, devices)
    half = real.shape[1]
    spans = (slice(0, half), slice(half, 2 * half))
    mixed = []
    for span, value in zip(spans, grads):
        pre = dot(real, mix[spans[0], span]) + dot(imag, mix[spans[1], span])
        s = 1.0 / (1.0 + jnp.exp(-pre))
        mixed.append((value * (s * (1.0 + pre * (1.0 - s)))).astype(jnp.bfloat16))
    back = [dot_t(mixed[0], mix[p, spans[0]]) + dot_t(mixed[1], mix[p, spans[1]]) for p in spans]
    back = [part.astype(jnp.bfloat16) for part in back]
    height = table.shape[0] // 2
    strip = height // devices
    groups = wide.shape[0]
    for freq in range(owned):
        cells = slice(freq * height, (freq + 1) * height)
        stacked = jnp.concatenate([back[0][cells], back[1][cells]], axis=0)
        result = dot(back_table[...], stacked) * norm
        for part in range(2):
            rows = [
                result[(part * strip + r) * devices : (part * strip + r + 1) * devices]
                for r in range(strip)
            ]
            where = pl.ds(part * owned + freq, devices, stride=2 * owned)
            values = jnp.concatenate(rows, axis=1)
            for g in range(groups):
                wide[g, where, :] = values[:, g * LANES : (g + 1) * LANES]
    for g in range(groups):
        out[:, g * LANES : (g + 1) * LANES] = wide[g].astype(jnp.bfloat16)


def output_kernel(norm, moved, strip_grad, weight_in, weight_local, table, out):
    spatial = (dot(table[...], moved[...]) * norm).astype(jnp.bfloat16)
    half = weight_in.shape[0]
    for r in range(out.shape[0]):
        total = dot(spatial[:, r * half : (r + 1) * half], weight_in[...])
        total = total + dot_t(strip_row(strip_grad, r), weight_local[...])
        out[r] = total.astype(jnp.bfloat16)


def target_pack_kernel(first, last, mask, down, up, row):
    tile_rows, tile_cols = mask.shape
    channels = first.shape[2]
    lanes = jnp.concatenate(
        [
            mask[...].astype(jnp.float32),
            jnp.zeros((tile_cols - tile_rows, tile_cols), jnp.float32),
        ],
        axis=0,
    ).T
    lanes = jnp.concatenate([lanes] + [jnp.zeros_like(lanes)] * (channels // tile_cols - 1), axis=1)
    lanes = lanes.astype(jnp.bfloat16)
    row[0] = lanes
    for pack, part in ((down, last), (up, first)):
        pack[:NEAR] = part[...]
        pack[NEAR] = lanes


def target_packs(target, mask):
    tile_rows, tile_cols, channels = target.shape
    block = (NEAR, tile_cols, channels)
    shapes = [jax.ShapeDtypeStruct((n, tile_cols, channels), target.dtype) for n in (NEAR + 1, NEAR + 1, 1)]
    return pl.pallas_call(
        target_pack_kernel,
        grid=(1,),
        out_shape=shapes,
        in_specs=[
            pl.BlockSpec(block, lambda i: (0, 0, 0)),
            pl.BlockSpec(block, lambda i: (tile_rows // NEAR - 1, 0, 0)),
            pl.BlockSpec(mask.shape, lambda i: (0, 0)),
        ],
        out_specs=[pl.BlockSpec(shape.shape, lambda i: (0, 0, 0)) for shape in shapes],
        compiler_params=pltpu.CompilerParams(vmem_limit_bytes=6 * MIB),
    )(target, target, mask)


def edge_kernel(*refs):
    sources, outs = refs[:-2], refs[-2:]
    count = len(sources) // 2
    for out, group in zip(outs, (sources[:count], sources[count:])):
        row = 0
        for ref in group:
            out[row : row + ref.shape[0]] = ref[...]
            row += ref.shape[0]


def edges(*parts):
    features = parts[1]
    channels = features.shape[2]
    last = features.shape[1] // REACH - 1

    def specs(at):
        return [pl.BlockSpec((p.shape[0], REACH, channels), lambda i, at=at: (0, at, 0)) for p in parts]

    rows = sum(p.shape[0] for p in parts)
    shape = jax.ShapeDtypeStruct((rows, REACH, channels), features.dtype)
    return pl.pallas_call(
        edge_kernel,
        grid=(1,),
        out_shape=[shape, shape],
        in_specs=specs(last) + specs(0),
        out_specs=[pl.BlockSpec(shape.shape, lambda i: (0, 0, 0))] * 2,
        compiler_params=pltpu.CompilerParams(vmem_limit_bytes=6 * MIB),
        cost_estimate=pl.CostEstimate(
            flops=0, bytes_accessed=8 * rows * REACH * channels, transcendentals=0
        ),
    )(*parts, *parts)


def put(wide, row, value, stride):
    size, channels = value.shape
    spot = pl.ds(row * stride, size)
    wide[spot, :channels] = pltpu.roll(value, 2, 0).astype(jnp.bfloat16)
    wide[spot, channels : 2 * channels] = value.astype(jnp.bfloat16)
    wide[spot, 2 * channels :] = pltpu.roll(value, size - 2, 0).astype(jnp.bfloat16)


def taps(wide, row, count, stride):
    parts = [wide[pl.ds((row + 2 * a) * stride, count * stride), :] for a in range(3)]
    return jnp.concatenate(parts, axis=1)


def conv(wide, row, count, stride, kernel):
    channels = kernel.shape[-1]
    return dot(taps(wide, row, count, stride), kernel[...].reshape(9 * channels, channels))


def conv_adjoint(wide, row, count, stride, kernel):
    flipped = [kernel[2 - a, 2 - b] for a in range(3) for b in range(3)]
    return dot_t(taps(wide, row, count, stride), jnp.concatenate(flipped, axis=1))


def stacked(piece, rows):
    return jnp.concatenate([piece(row) for row in rows], axis=0)


def first_stages(stride, blocks, rows, feature, inside, first, second, wide_even, wide_odd, slopes, use):
    tall = rows + 2 * REACH
    for row in range(0, tall, NEAR):
        put(wide_even, row, stacked(feature, range(row, row + NEAR)), stride)
    count = blocks[0]
    for row in range(0, tall - 4, count):
        pre = conv(wide_even, row, count, stride, first)
        s = 1.0 / (1.0 + jnp.exp(-pre))
        kept = stacked(inside, range(row + 2, row + 2 + count))
        put(wide_odd, row, pre * s * kept, stride)
        low, high = max(row, NEAR), min(row + count, tall - 4 - NEAR)
        if low < high:
            part = slice((low - row) * stride, (high - row) * stride)
            slope = (s * (1.0 + pre * (1.0 - s)) * kept)[part]
            slopes[pl.ds((low - NEAR) * stride, (high - low) * stride), :] = slope
    count = blocks[1]
    for row in range(0, rows + 2 * NEAR, count):
        use(row, count, conv(wide_odd, row, count, stride, second))


def last_stages(stride, blocks, rows, first, second, wide_even, wide_odd, slopes, use):
    count = blocks[2]
    for row in range(0, rows + 4, count):
        value = conv_adjoint(wide_even, row, count, stride, second)
        value = value * slopes[pl.ds(row * stride, count * stride), :]
        put(wide_odd, row, value, stride)
    count = blocks[3]
    for row in range(0, rows, count):
        use(row, count, conv_adjoint(wide_odd, row, count, stride, first))


def loss_grad(row, count, value, target, hole, inside):
    near = range(row, row + count)
    weight = (1.0 + 2.0 * stacked(hole, near)) * stacked(inside, range(row + NEAR, row + count + NEAR))
    return weight * (value - stacked(target, near))


def part_of(rows, edge, above, own, below):
    def find(row):
        if row < edge:
            return above, row
        if row < edge + rows:
            return own, row - edge
        return below, row - edge - rows

    return find


TILE_BLOCKS = (4, 4, 4, 4)
SIDE_BLOCKS = (10, 8, 12, 8)


def tile_forward_kernel(above, features, below, first, second, ok, pre, slopes, wide_even, wide_odd):
    rows, stride, _ = features.shape
    find = part_of(rows, REACH, above, features, below)

    def feature(row):
        source, at = find(row)
        return source[at].astype(jnp.float32)

    def inside(row):
        return ok[REACH : REACH + stride, row : row + 1]

    def use(row, count, value):
        pre[pl.ds(row * stride, count * stride), :] = value

    first_stages(
        stride, TILE_BLOCKS, rows, feature, inside, first, second, wide_even, wide_odd, slopes, use
    )


def tile_backward_kernel(
    pre,
    slopes,
    target_above,
    target,
    target_below,
    mask_row,
    first,
    second,
    ok,
    out,
    wide_even,
    wide_odd,
):
    rows, stride, channels = target.shape
    find = part_of(rows, NEAR, target_above, target, target_below)

    def goal(row):
        source, at = find(row)
        return source[at].astype(jnp.float32)

    masks = [m[at].astype(jnp.float32) for m, at in ((target_above, NEAR), (mask_row, 0), (target_below, NEAR))]
    find_mask = part_of(rows, NEAR, (masks[0], rows - NEAR), (masks[1], 0), (masks[2], 0))

    def hole(row):
        (mask, start), at = find_mask(row)
        return mask[:, start + at : start + at + 1]

    def inside(row):
        return ok[REACH : REACH + stride, row : row + 1]

    count = NEAR
    for row in range(0, rows + 2 * NEAR, count):
        value = pre[pl.ds(row * stride, count * stride), :]
        put(wide_even, row, loss_grad(row, count, value, goal, hole, inside), stride)

    def use(row, count, value):
        out[row : row + count] = value.reshape(count, stride, channels).astype(jnp.bfloat16)

    last_stages(stride, TILE_BLOCKS, rows, first, second, wide_even, wide_odd, slopes, use)


def side_kernel(
    before,
    after,
    above,
    features,
    below,
    target_above,
    target,
    target_below,
    mask_row,
    first,
    second,
    ok,
    tile,
    out,
    wide_even,
    wide_odd,
    slopes,
):
    rows, tile_cols, channels = features.shape
    keep = 2 * REACH
    stride = 2 * (REACH + keep)
    tall = rows + 2 * REACH
    own = tall + NEAR + 1

    def joined(edge, source, at):
        parts = [before[edge], source[at, :keep], source[at, tile_cols - keep :], after[edge]]
        return jnp.concatenate([part.astype(jnp.float32) for part in parts], axis=0)

    find = part_of(rows, REACH, above, features, below)
    find_target = part_of(
        rows, NEAR, (target_above, tall), (target, own), (target_below, own + rows + 1)
    )

    def feature(row):
        return joined(row, *find(row))

    def goal(row):
        (source, edge), at = find_target(row)
        return joined(edge + at, source, at)

    masks = [
        joined(tall + NEAR, target_above, NEAR),
        joined(own + rows, mask_row, 0),
        joined(own + rows + 1 + NEAR, target_below, NEAR),
    ]
    find_mask = part_of(rows, NEAR, (masks[0], rows - NEAR), (masks[1], 0), (masks[2], 0))

    def hole(row):
        (mask, start), at = find_mask(row)
        return mask[:, start + at : start + at + 1]

    width = ok.shape[0]
    kept = jnp.concatenate([ok[: REACH + keep], ok[width - REACH - keep :]], axis=0)

    def inside(row):
        return kept[:, row : row + 1]

    def use_forward(row, count, value):
        put(wide_even, row, loss_grad(row, count, value, goal, hole, inside), stride)

    first_stages(
        stride, SIDE_BLOCKS, rows, feature, inside, first, second, wide_even, wide_odd, slopes, use_forward
    )
    out[:, REACH : tile_cols - REACH] = tile[:, REACH : tile_cols - REACH]

    def use(row, count, value):
        value = value.reshape(count, stride, channels).astype(jnp.bfloat16)
        out[row : row + count, :REACH] = value[:, REACH : 2 * REACH]
        out[row : row + count, tile_cols - REACH :] = value[:, stride - 2 * REACH : stride - REACH]

    last_stages(stride, SIDE_BLOCKS, rows, first, second, wide_even, wide_odd, slopes, use)


def wide_buffer(rows, stride, channels):
    return pltpu.VMEM((rows * stride, 3 * channels), jnp.bfloat16)


def tile_forward(above, features, below, first, second, ok):
    rows, stride, channels = features.shape
    shapes = [
        jax.ShapeDtypeStruct(((rows + h) * stride, channels), jnp.float32) for h in (2 * NEAR, 4)
    ]
    return vmem_call(
        tile_forward_kernel,
        shapes,
        above,
        features,
        below,
        first,
        second,
        ok,
        flops=2 * 9 * channels * channels * stride * (2 * rows + 20),
        scratch=[wide_buffer(rows + h, stride, channels) for h in (16, 12)],
        limit=18,
    )


def tile_backward(pre, slopes, target_above, target, target_below, mask_row, first, second, ok):
    rows, stride, channels = target.shape
    return vmem_call(
        tile_backward_kernel,
        [jax.ShapeDtypeStruct(target.shape, jnp.bfloat16)],
        pre,
        slopes,
        target_above,
        target,
        target_below,
        mask_row,
        first,
        second,
        ok,
        flops=2 * 9 * channels * channels * stride * (2 * rows + 4),
        scratch=[wide_buffer(rows + h, stride, channels) for h in (8, 4)],
        limit=16,
    )[0]


def sides(tile, *operands):
    rows, _, channels = tile.shape
    stride = 6 * REACH
    return vmem_call(
        side_kernel,
        [jax.ShapeDtypeStruct(tile.shape, jnp.bfloat16)],
        *operands,
        tile,
        flops=2 * 9 * channels * channels * stride * (4 * rows + 24),
        scratch=[wide_buffer(rows + h, stride, channels) for h in (16, 12)]
        + [pltpu.VMEM(((rows + 4) * stride, channels), jnp.float32)],
        limit=14,
    )[0]


def neighbours(axis):
    size = lax.axis_size(axis)
    up = [(i, i + 1) for i in range(size - 1)]
    return up, [(j, i) for i, j in up]


def shards(
    features,
    target,
    hole_mask,
    kernel_first,
    kernel_second,
    inputs,
    weight_in,
    weight_out,
    weight_local,
    weight_mix,
):
    tile_rows, tile_cols, channels = features.shape
    row_devices, col_devices = lax.axis_size("row"), lax.axis_size("col")
    devices = row_devices * col_devices
    height, width = tile_rows * row_devices, tile_cols * col_devices
    strip, half = inputs.shape[0], weight_in.shape[1]
    owned = width // 2 // devices
    col_norm, row_norm = 1.0 / math.sqrt(width), 1.0 / math.sqrt(height)
    table = column_matrix(width, devices)
    table_back = jnp.asarray(np.ascontiguousarray(table.T))
    table = jnp.asarray(table)
    row_table = row_matrix(height, devices)
    row_back = jnp.asarray(np.ascontiguousarray(row_table.T))
    row_table = jnp.asarray(row_table)
    bf16 = jnp.bfloat16

    def swap(spectrum):
        return lax.all_to_all(spectrum, ("row", "col"), split_axis=0, concat_axis=0, tiled=True)

    cells = [jax.ShapeDtypeStruct((width, strip * half), bf16)]
    weight_in = weight_in.T
    spatial_cols = vmem_call(
        functools.partial(spectrum_kernel, col_norm), cells, inputs, weight_in, table
    )[0]
    spatial_moved = swap(spatial_cols)
    row0, col0 = lax.axis_index("row") * tile_rows, lax.axis_index("col") * tile_cols
    row_ids = row0 - REACH + jnp.arange(tile_rows + 2 * REACH, dtype=jnp.int32)
    col_ids = col0 - REACH + jnp.arange(tile_cols + 2 * REACH, dtype=jnp.int32)
    ok = ((col_ids >= 0) & (col_ids < width))[:, None] & ((row_ids >= 0) & (row_ids < height))[None]
    ok = ok.astype(jnp.float32)

    up, down = neighbours("row")
    left, right = neighbours("col")
    above = lax.ppermute(features, "row", up)
    below = lax.ppermute(features, "row", down)
    pack_down, pack_up, mask_row = target_packs(target, hole_mask)
    target_above = lax.ppermute(pack_down, "row", up)
    target_below = lax.ppermute(pack_up, "row", down)
    above, spatial_cols = lax.optimization_barrier((above, spatial_cols))
    pre, slopes = tile_forward(above, features, below, kernel_first, kernel_second, ok)
    target_above, pre = lax.optimization_barrier((target_above, pre))
    last, initial = edges(above, features, below, target_above, target, mask_row, target_below)
    before = lax.ppermute(last, "col", left)
    after = lax.ppermute(initial, "col", right)
    tile = tile_backward(
        pre, slopes, target_above, target, target_below, mask_row, kernel_first, kernel_second, ok
    )
    grad_feat = sides(
        tile,
        before,
        after,
        above,
        features,
        below,
        target_above,
        target,
        target_below,
        mask_row,
        kernel_first,
        kernel_second,
        ok,
    )

    grad_feat, spatial_moved = lax.optimization_barrier((grad_feat, spatial_moved))

    strip_grad = lax.all_to_all(
        grad_feat.reshape(col_devices, strip, tile_cols, channels), "col", split_axis=0, concat_axis=0
    )
    grad_cols = vmem_call(
        functools.partial(spectrum_kernel, col_norm), cells, strip_grad, weight_out, table
    )[0]
    wide = pltpu.VMEM((strip * half // LANES, width, LANES), jnp.float32)
    grad_rows = vmem_call(
        functools.partial(mix_kernel, row_norm, owned, devices),
        cells,
        spatial_moved,
        swap(grad_cols),
        weight_mix,
        row_table,
        row_back,
        scratch=[wide, wide],
    )[0]
    returned = swap(grad_rows)
    return vmem_call(
        functools.partial(output_kernel, col_norm),
        [jax.ShapeDtypeStruct(inputs.shape, bf16)],
        returned,
        strip_grad,
        weight_in,
        weight_local,
        table_back,
    )[0]


def solution(mesh):
    in_specs = (
        P("row", "col", None),
        P("row", "col", None),
        P("row", "col"),
        P(),
        P(),
        P(("row", "col"), None, None),
        P(),
        P(),
        P(),
        P(),
    )
    out_specs = P(("row", "col"), None, None)
    return jax.shard_map(shards, mesh=mesh, in_specs=in_specs, out_specs=out_specs, check_vma=False)
```

```python
import functools
import math

import jax
import jax.numpy as jnp
import ml_dtypes
import numpy as np
from jax import lax
from jax.experimental import pallas as pl
from jax.experimental.pallas import tpu as pltpu
from jax.sharding import PartitionSpec as P

REACH = 8
NEAR = 4
MIB = 1024 * 1024
LANES = 128


def dot(left, right):
    return jnp.dot(left, right, preferred_element_type=jnp.float32)


def dot_t(left, right):
    return lax.dot_general(left, right, (((1,), (1,)), ((), ())), preferred_element_type=jnp.float32)


def vmem_call(body, shapes, *operands, flops=0, scratch=(), limit=10):
    spec = pl.BlockSpec(memory_space=pltpu.VMEM)
    size = sum(math.prod(a.shape) * a.dtype.itemsize for a in (*operands, *shapes))
    return pl.pallas_call(
        body,
        out_shape=shapes,
        in_specs=[spec] * len(operands),
        out_specs=[spec] * len(shapes),
        scratch_shapes=list(scratch),
        compiler_params=pltpu.CompilerParams(vmem_limit_bytes=limit * MIB),
        cost_estimate=pl.CostEstimate(flops=flops, bytes_accessed=size, transcendentals=0),
    )(*operands)


def in_hbm(array):
    return pltpu.with_memory_space_constraint(array, pltpu.HBM)


def phases(first, second, length):
    angle = (first[:, None] * second[None, :] % length) * (2.0 * math.pi / length)
    return np.cos(angle).astype(ml_dtypes.bfloat16), np.sin(angle).astype(ml_dtypes.bfloat16)


def column_matrix(width, devices):
    half = width // 2
    freq, col = np.arange(half), np.arange(width)
    cos, sin = phases(freq, col, width)
    sin[0] = (2 * (col % 2) - 1).astype(ml_dtypes.bfloat16)
    both = np.stack([cos, -sin]).reshape(2, devices, half // devices, width)
    return np.ascontiguousarray(both.transpose(1, 0, 2, 3)).reshape(width, width)


def row_matrix(height, row_devices, col_devices):
    devices = row_devices * col_devices
    strip = height // devices
    strips = np.arange(devices).reshape(row_devices, col_devices).T.reshape(-1)
    rows = (strips[None, :] * strip + np.arange(strip)[:, None]).reshape(-1)
    cos, sin = phases(np.arange(height), rows, height)
    return np.block([[cos, sin], [-sin, cos]])


def strip_row(signal, r):
    if len(signal.shape) == 3:
        return signal[r]
    return jnp.concatenate([signal[block, r] for block in range(signal.shape[0])], axis=0)


def strip_spectrum(signal, weight, table, norm):
    count = signal.shape[0 if len(signal.shape) == 3 else 1]
    rows = [dot_t(strip_row(signal, r), weight[...]).astype(jnp.bfloat16) for r in range(count)]
    return (dot(table[...], jnp.concatenate(rows, axis=1)) * norm).astype(jnp.bfloat16)


def spectrum_kernel(norm, signal, weight, table, out):
    out[...] = strip_spectrum(signal, weight, table, norm)


def fetching_spectrum_kernel(norm, signal, weight, table, out, signal_held, weight_held, table_held, sems):
    count = signal.shape[0]
    copies = [pltpu.make_async_copy(weight, weight_held, sems.at[0])]
    copies += [
        pltpu.make_async_copy(signal.at[r], signal_held.at[r], sems.at[1 + r]) for r in range(count)
    ]
    copies.append(pltpu.make_async_copy(table, table_held, sems.at[1 + count]))
    for copy in copies:
        copy.start()
    copies[0].wait()
    rows = []
    for r in range(count):
        copies[1 + r].wait()
        rows.append(dot_t(signal_held[r], weight_held[...]).astype(jnp.bfloat16))
    copies[-1].wait()
    out[...] = (dot(table_held[...], jnp.concatenate(rows, axis=1)) * norm).astype(jnp.bfloat16)


def fetching_spectrum(norm, shape, signal, weight, table):
    operands = (signal, weight, table)
    return pl.pallas_call(
        functools.partial(fetching_spectrum_kernel, norm),
        out_shape=shape,
        in_specs=[pl.BlockSpec(memory_space=pltpu.HBM)] * 3,
        out_specs=pl.BlockSpec(memory_space=pltpu.VMEM),
        scratch_shapes=[pltpu.VMEM(a.shape, a.dtype) for a in operands]
        + [pltpu.SemaphoreType.DMA((signal.shape[0] + 2,))],
        compiler_params=pltpu.CompilerParams(vmem_limit_bytes=12 * MIB),
        cost_estimate=pl.CostEstimate(
            flops=0, bytes_accessed=2 * MIB, transcendentals=0
        ),
    )(*[in_hbm(a) for a in operands])


def row_spectrum(moved, table, wide, norm, owned, devices):
    groups = wide.shape[0]
    for g in range(groups):
        wide[g] = moved[:, g * LANES : (g + 1) * LANES].astype(jnp.float32)
    strip = table.shape[1] // (2 * devices)
    half = moved.shape[1] // strip
    height = table.shape[0] // 2
    real, imag = [], []
    for freq in range(owned):
        parts = []
        for part in range(2):
            where = pl.ds(part * owned + freq, devices, stride=2 * owned)
            block = jnp.concatenate([wide[g, where, :] for g in range(groups)], axis=1)
            parts += [block[:, r * half : (r + 1) * half] for r in range(strip)]
        result = dot(table[...], jnp.concatenate(parts, axis=0).astype(jnp.bfloat16)) * norm
        real.append(result[:height])
        imag.append(result[height:])
    return jnp.concatenate(real, axis=0), jnp.concatenate(imag, axis=0)


def mix_kernel(norm, owned, devices, spatial, grad, mix, table, back_table, out, wide, wide_grad):
    parts = row_spectrum(spatial, table, wide, norm, owned, devices)
    real, imag = [part.astype(jnp.bfloat16) for part in parts]
    grads = row_spectrum(grad, table, wide_grad, norm, owned, devices)
    half = real.shape[1]
    spans = (slice(0, half), slice(half, 2 * half))
    mixed = []
    for span, value in zip(spans, grads):
        pre = dot(real, mix[spans[0], span]) + dot(imag, mix[spans[1], span])
        s = 1.0 / (1.0 + jnp.exp(-pre))
        mixed.append((value * (s * (1.0 + pre * (1.0 - s)))).astype(jnp.bfloat16))
    back = [dot_t(mixed[0], mix[p, spans[0]]) + dot_t(mixed[1], mix[p, spans[1]]) for p in spans]
    back = [part.astype(jnp.bfloat16) for part in back]
    height = table.shape[0] // 2
    strip = height // devices
    groups = wide.shape[0]
    for freq in range(owned):
        cells = slice(freq * height, (freq + 1) * height)
        stacked = jnp.concatenate([back[0][cells], back[1][cells]], axis=0)
        result = dot(back_table[...], stacked) * norm
        for part in range(2):
            rows = [
                result[(part * strip + r) * devices : (part * strip + r + 1) * devices]
                for r in range(strip)
            ]
            where = pl.ds(part * owned + freq, devices, stride=2 * owned)
            values = jnp.concatenate(rows, axis=1)
            for g in range(groups):
                wide[g, where, :] = values[:, g * LANES : (g + 1) * LANES]
    for g in range(groups):
        out[:, g * LANES : (g + 1) * LANES] = wide[g].astype(jnp.bfloat16)


def output_kernel(norm, moved, strip_grad, weight_in, weight_local, table, out):
    spatial = (dot(table[...], moved[...]) * norm).astype(jnp.bfloat16)
    half = weight_in.shape[0]
    for r in range(out.shape[0]):
        total = dot(spatial[:, r * half : (r + 1) * half], weight_in[...])
        total = total + dot_t(strip_row(strip_grad, r), weight_local[...])
        out[r] = total.astype(jnp.bfloat16)


def target_pack_kernel(first, last, mask, down, up, row):
    tile_rows, tile_cols = mask.shape
    channels = first.shape[2]
    lanes = jnp.concatenate(
        [
            mask[...].astype(jnp.float32),
            jnp.zeros((tile_cols - tile_rows, tile_cols), jnp.float32),
        ],
        axis=0,
    ).T
    lanes = jnp.concatenate([lanes] + [jnp.zeros_like(lanes)] * (channels // tile_cols - 1), axis=1)
    lanes = lanes.astype(jnp.bfloat16)
    row[0] = lanes
    for pack, part in ((down, last), (up, first)):
        pack[:NEAR] = part[...]
        pack[NEAR] = lanes


def target_packs(target, mask):
    tile_rows, tile_cols, channels = target.shape
    block = (NEAR, tile_cols, channels)
    shapes = [jax.ShapeDtypeStruct((n, tile_cols, channels), target.dtype) for n in (NEAR + 1, NEAR + 1, 1)]
    return pl.pallas_call(
        target_pack_kernel,
        grid=(1,),
        out_shape=shapes,
        in_specs=[
            pl.BlockSpec(block, lambda i: (0, 0, 0)),
            pl.BlockSpec(block, lambda i: (tile_rows // NEAR - 1, 0, 0)),
            pl.BlockSpec(mask.shape, lambda i: (0, 0)),
        ],
        out_specs=[pl.BlockSpec(shape.shape, lambda i: (0, 0, 0)) for shape in shapes],
        compiler_params=pltpu.CompilerParams(vmem_limit_bytes=6 * MIB),
    )(target, target, mask)


def edge_kernel(*refs):
    sources, outs = refs[:-2], refs[-2:]
    count = len(sources) // 2
    for out, group in zip(outs, (sources[:count], sources[count:])):
        row = 0
        for ref in group:
            out[row : row + ref.shape[0]] = ref[...]
            row += ref.shape[0]


def edges(*parts):
    features = parts[1]
    channels = features.shape[2]
    last = features.shape[1] // REACH - 1

    def specs(at):
        return [pl.BlockSpec((p.shape[0], REACH, channels), lambda i, at=at: (0, at, 0)) for p in parts]

    rows = sum(p.shape[0] for p in parts)
    shape = jax.ShapeDtypeStruct((rows, REACH, channels), features.dtype)
    return pl.pallas_call(
        edge_kernel,
        grid=(1,),
        out_shape=[shape, shape],
        in_specs=specs(last) + specs(0),
        out_specs=[pl.BlockSpec(shape.shape, lambda i: (0, 0, 0))] * 2,
        compiler_params=pltpu.CompilerParams(vmem_limit_bytes=6 * MIB),
        cost_estimate=pl.CostEstimate(
            flops=0, bytes_accessed=8 * rows * REACH * channels, transcendentals=0
        ),
    )(*parts, *parts)


def put(wide, row, value, stride):
    size, channels = value.shape
    spot = pl.ds(row * stride, size)
    wide[spot, :channels] = pltpu.roll(value, 2, 0).astype(jnp.bfloat16)
    wide[spot, channels : 2 * channels] = value.astype(jnp.bfloat16)
    wide[spot, 2 * channels :] = pltpu.roll(value, size - 2, 0).astype(jnp.bfloat16)


def taps(wide, row, count, stride):
    parts = [wide[pl.ds((row + 2 * a) * stride, count * stride), :] for a in range(3)]
    return jnp.concatenate(parts, axis=1)


def conv(wide, row, count, stride, kernel):
    channels = kernel.shape[-1]
    return dot(taps(wide, row, count, stride), kernel[...].reshape(9 * channels, channels))


def conv_adjoint(wide, row, count, stride, kernel):
    flipped = [kernel[2 - a, 2 - b] for a in range(3) for b in range(3)]
    return dot_t(taps(wide, row, count, stride), jnp.concatenate(flipped, axis=1))


def stacked(piece, rows):
    return jnp.concatenate([piece(row) for row in rows], axis=0)


def first_stages(
    stride, blocks, rows, feature, inside, first, second, wide_even, wide_odd, slopes, use, ready=None
):
    ready = ready or (lambda which: None)
    tall = rows + 2 * REACH
    for row in range(0, tall, NEAR):
        put(wide_even, row, stacked(feature, range(row, row + NEAR)), stride)
    ready(0)
    count = blocks[0]
    for row in range(0, tall - 4, count):
        pre = conv(wide_even, row, count, stride, first)
        s = 1.0 / (1.0 + jnp.exp(-pre))
        kept = stacked(inside, range(row + 2, row + 2 + count))
        put(wide_odd, row, pre * s * kept, stride)
        low, high = max(row, NEAR), min(row + count, tall - 4 - NEAR)
        if low < high:
            part = slice((low - row) * stride, (high - row) * stride)
            slope = (s * (1.0 + pre * (1.0 - s)) * kept)[part]
            slopes[pl.ds((low - NEAR) * stride, (high - low) * stride), :] = slope
    ready(1)
    count = blocks[1]
    for row in range(0, rows + 2 * NEAR, count):
        use(row, count, conv(wide_odd, row, count, stride, second))


def last_stages(stride, blocks, rows, first, second, wide_even, wide_odd, slopes, use):
    count = blocks[2]
    for row in range(0, rows + 4, count):
        value = conv_adjoint(wide_even, row, count, stride, second)
        value = value * slopes[pl.ds(row * stride, count * stride), :]
        put(wide_odd, row, value, stride)
    count = blocks[3]
    for row in range(0, rows, count):
        use(row, count, conv_adjoint(wide_odd, row, count, stride, first))


def loss_grad(row, count, value, target, hole, inside):
    near = range(row, row + count)
    weight = (1.0 + 2.0 * stacked(hole, near)) * stacked(inside, range(row + NEAR, row + count + NEAR))
    return weight * (value - stacked(target, near))


def part_of(rows, edge, above, own, below):
    def find(row):
        if row < edge:
            return above, row
        if row < edge + rows:
            return own, row - edge
        return below, row - edge - rows

    return find


TILE_BLOCKS = (4, 4, 4, 4)
SIDE_BLOCKS = (10, 8, 12, 8)


def tile_forward_kernel(
    above, features, below, first, second, ok, pre, slopes, wide_even, wide_odd, kernels, sems
):
    rows, stride, _ = features.shape
    copies = [
        pltpu.make_async_copy(source, kernels.at[i], sems.at[i]) for i, source in enumerate((first, second))
    ]
    for copy in copies:
        copy.start()

    def ready(which):
        copies[which].wait()

    find = part_of(rows, REACH, above, features, below)

    def feature(row):
        source, at = find(row)
        return source[at].astype(jnp.float32)

    def inside(row):
        return ok[REACH : REACH + stride, row : row + 1]

    def use(row, count, value):
        pre[pl.ds(row * stride, count * stride), :] = value

    first_stages(
        stride,
        TILE_BLOCKS,
        rows,
        feature,
        inside,
        kernels.at[0],
        kernels.at[1],
        wide_even,
        wide_odd,
        slopes,
        use,
        ready,
    )


def tile_backward_kernel(
    pre,
    slopes,
    target_above,
    target,
    target_below,
    mask_row,
    first,
    second,
    ok,
    out,
    wide_even,
    wide_odd,
):
    rows, stride, channels = target.shape
    find = part_of(rows, NEAR, target_above, target, target_below)

    def goal(row):
        source, at = find(row)
        return source[at].astype(jnp.float32)

    masks = [m[at].astype(jnp.float32) for m, at in ((target_above, NEAR), (mask_row, 0), (target_below, NEAR))]
    find_mask = part_of(rows, NEAR, (masks[0], rows - NEAR), (masks[1], 0), (masks[2], 0))

    def hole(row):
        (mask, start), at = find_mask(row)
        return mask[:, start + at : start + at + 1]

    def inside(row):
        return ok[REACH : REACH + stride, row : row + 1]

    count = NEAR
    for row in range(0, rows + 2 * NEAR, count):
        value = pre[pl.ds(row * stride, count * stride), :]
        put(wide_even, row, loss_grad(row, count, value, goal, hole, inside), stride)

    def use(row, count, value):
        out[row : row + count] = value.reshape(count, stride, channels).astype(jnp.bfloat16)

    last_stages(stride, TILE_BLOCKS, rows, first, second, wide_even, wide_odd, slopes, use)


def side_kernel(
    before,
    after,
    above,
    features,
    below,
    target_above,
    target,
    target_below,
    mask_row,
    first,
    second,
    ok,
    tile,
    out,
    wide_even,
    wide_odd,
    slopes,
):
    rows, tile_cols, channels = features.shape
    keep = 2 * REACH
    stride = 2 * (REACH + keep)
    tall = rows + 2 * REACH
    own = tall + NEAR + 1

    def joined(edge, source, at):
        parts = [before[edge], source[at, :keep], source[at, tile_cols - keep :], after[edge]]
        return jnp.concatenate([part.astype(jnp.float32) for part in parts], axis=0)

    find = part_of(rows, REACH, above, features, below)
    find_target = part_of(
        rows, NEAR, (target_above, tall), (target, own), (target_below, own + rows + 1)
    )

    def feature(row):
        return joined(row, *find(row))

    def goal(row):
        (source, edge), at = find_target(row)
        return joined(edge + at, source, at)

    masks = [
        joined(tall + NEAR, target_above, NEAR),
        joined(own + rows, mask_row, 0),
        joined(own + rows + 1 + NEAR, target_below, NEAR),
    ]
    find_mask = part_of(rows, NEAR, (masks[0], rows - NEAR), (masks[1], 0), (masks[2], 0))

    def hole(row):
        (mask, start), at = find_mask(row)
        return mask[:, start + at : start + at + 1]

    width = ok.shape[0]
    kept = jnp.concatenate([ok[: REACH + keep], ok[width - REACH - keep :]], axis=0)

    def inside(row):
        return kept[:, row : row + 1]

    def use_forward(row, count, value):
        put(wide_even, row, loss_grad(row, count, value, goal, hole, inside), stride)

    first_stages(
        stride, SIDE_BLOCKS, rows, feature, inside, first, second, wide_even, wide_odd, slopes, use_forward
    )
    out[:, REACH : tile_cols - REACH] = tile[:, REACH : tile_cols - REACH]

    def use(row, count, value):
        value = value.reshape(count, stride, channels).astype(jnp.bfloat16)
        out[row : row + count, :REACH] = value[:, REACH : 2 * REACH]
        out[row : row + count, tile_cols - REACH :] = value[:, stride - 2 * REACH : stride - REACH]

    last_stages(stride, SIDE_BLOCKS, rows, first, second, wide_even, wide_odd, slopes, use)


def wide_buffer(rows, stride, channels):
    return pltpu.VMEM((rows * stride, 3 * channels), jnp.bfloat16)


def tile_forward(above, features, below, first, second, ok):
    rows, stride, channels = features.shape
    shapes = [
        jax.ShapeDtypeStruct(((rows + h) * stride, channels), jnp.float32) for h in (2 * NEAR, 4)
    ]
    in_vmem, hbm = pl.BlockSpec(memory_space=pltpu.VMEM), pl.BlockSpec(memory_space=pltpu.HBM)
    return pl.pallas_call(
        tile_forward_kernel,
        out_shape=shapes,
        in_specs=[in_vmem] * 3 + [hbm] * 2 + [in_vmem],
        out_specs=[in_vmem] * 2,
        scratch_shapes=[
            *[wide_buffer(rows + h, stride, channels) for h in (16, 12)],
            pltpu.VMEM((2, *first.shape), first.dtype),
            pltpu.SemaphoreType.DMA((2,)),
        ],
        compiler_params=pltpu.CompilerParams(vmem_limit_bytes=20 * MIB),
        cost_estimate=pl.CostEstimate(
            flops=2 * 9 * channels * channels * stride * (2 * rows + 20),
            bytes_accessed=8 * MIB,
            transcendentals=0,
        ),
    )(above, features, below, in_hbm(first), in_hbm(second), ok)


def tile_backward(pre, slopes, target_above, target, target_below, mask_row, first, second, ok):
    rows, stride, channels = target.shape
    return vmem_call(
        tile_backward_kernel,
        [jax.ShapeDtypeStruct(target.shape, jnp.bfloat16)],
        pre,
        slopes,
        target_above,
        target,
        target_below,
        mask_row,
        first,
        second,
        ok,
        flops=2 * 9 * channels * channels * stride * (2 * rows + 4),
        scratch=[wide_buffer(rows + h, stride, channels) for h in (8, 4)],
        limit=16,
    )[0]


def sides(tile, *operands):
    rows, _, channels = tile.shape
    stride = 6 * REACH
    return vmem_call(
        side_kernel,
        [jax.ShapeDtypeStruct(tile.shape, jnp.bfloat16)],
        *operands,
        tile,
        flops=2 * 9 * channels * channels * stride * (4 * rows + 24),
        scratch=[wide_buffer(rows + h, stride, channels) for h in (16, 12)]
        + [pltpu.VMEM(((rows + 4) * stride, channels), jnp.float32)],
        limit=14,
    )[0]


def neighbours(axis):
    size = lax.axis_size(axis)
    up = [(i, i + 1) for i in range(size - 1)]
    return up, [(j, i) for i, j in up]


def shards(
    features,
    target,
    hole_mask,
    kernel_first,
    kernel_second,
    inputs,
    weight_in,
    weight_out,
    weight_local,
    weight_mix,
):
    tile_rows, tile_cols, channels = features.shape
    row_devices, col_devices = lax.axis_size("row"), lax.axis_size("col")
    devices = row_devices * col_devices
    height, width = tile_rows * row_devices, tile_cols * col_devices
    strip, half = inputs.shape[0], weight_in.shape[1]
    owned = width // 2 // devices
    col_norm, row_norm = 1.0 / math.sqrt(width), 1.0 / math.sqrt(height)
    table = column_matrix(width, devices)
    table_back = jnp.asarray(np.ascontiguousarray(table.T))
    table = jnp.asarray(table)
    row_table = row_matrix(height, row_devices, col_devices)
    row_back = jnp.asarray(np.ascontiguousarray(row_table.T))
    row_table = jnp.asarray(row_table)
    bf16 = jnp.bfloat16

    def swap(spectrum):
        return lax.all_to_all(spectrum, ("col", "row"), split_axis=0, concat_axis=0, tiled=True)

    cells = [jax.ShapeDtypeStruct((width, strip * half), bf16)]
    weight_in = weight_in.T
    spatial_cols = fetching_spectrum(col_norm, cells[0], inputs, weight_in, table)
    spatial_moved = swap(spatial_cols)
    row0, col0 = lax.axis_index("row") * tile_rows, lax.axis_index("col") * tile_cols
    row_ids = row0 - REACH + jnp.arange(tile_rows + 2 * REACH, dtype=jnp.int32)
    col_ids = col0 - REACH + jnp.arange(tile_cols + 2 * REACH, dtype=jnp.int32)
    ok = ((col_ids >= 0) & (col_ids < width))[:, None] & ((row_ids >= 0) & (row_ids < height))[None]
    ok = ok.astype(jnp.float32)

    up, down = neighbours("row")
    left, right = neighbours("col")
    above = lax.ppermute(features, "row", up)
    below = lax.ppermute(features, "row", down)
    pack_down, pack_up, mask_row = target_packs(target, hole_mask)
    target_above = lax.ppermute(pack_down, "row", up)
    target_below = lax.ppermute(pack_up, "row", down)
    above, spatial_cols = lax.optimization_barrier((above, spatial_cols))
    pre, slopes = tile_forward(above, features, below, kernel_first, kernel_second, ok)
    target_above, pre = lax.optimization_barrier((target_above, pre))
    last, initial = edges(above, features, below, target_above, target, mask_row, target_below)
    before = lax.ppermute(last, "col", left)
    after = lax.ppermute(initial, "col", right)
    tile = tile_backward(
        pre, slopes, target_above, target, target_below, mask_row, kernel_first, kernel_second, ok
    )
    grad_feat = sides(
        tile,
        before,
        after,
        above,
        features,
        below,
        target_above,
        target,
        target_below,
        mask_row,
        kernel_first,
        kernel_second,
        ok,
    )

    grad_feat, spatial_moved = lax.optimization_barrier((grad_feat, spatial_moved))

    strip_grad = lax.all_to_all(
        grad_feat.reshape(col_devices, strip, tile_cols, channels), "col", split_axis=0, concat_axis=0
    )
    grad_cols = vmem_call(
        functools.partial(spectrum_kernel, col_norm), cells, strip_grad, weight_out, table
    )[0]
    wide = pltpu.VMEM((strip * half // LANES, width, LANES), jnp.float32)
    grad_rows = vmem_call(
        functools.partial(mix_kernel, row_norm, owned, devices),
        cells,
        spatial_moved,
        swap(grad_cols),
        weight_mix,
        row_table,
        row_back,
        scratch=[wide, wide],
    )[0]
    returned = swap(grad_rows)
    return vmem_call(
        functools.partial(output_kernel, col_norm),
        [jax.ShapeDtypeStruct(inputs.shape, bf16)],
        returned,
        strip_grad,
        weight_in,
        weight_local,
        table_back,
    )[0]


def solution(mesh):
    in_specs = (
        P("row", "col", None),
        P("row", "col", None),
        P("row", "col"),
        P(),
        P(),
        P(("row", "col"), None, None),
        P(),
        P(),
        P(),
        P(),
    )
    out_specs = P(("row", "col"), None, None)
    return jax.shard_map(shards, mesh=mesh, in_specs=in_specs, out_specs=out_specs, check_vma=False)
```

```python
import functools
import math

import jax
import jax.numpy as jnp
import ml_dtypes
import numpy as np
from jax import lax
from jax.experimental import pallas as pl
from jax.experimental.pallas import tpu as pltpu
from jax.sharding import PartitionSpec as P

REACH = 8
NEAR = 4
MIB = 1024 * 1024
LANES = 128


def dot(left, right):
    return jnp.dot(left, right, preferred_element_type=jnp.float32)


def dot_t(left, right):
    return lax.dot_general(left, right, (((1,), (1,)), ((), ())), preferred_element_type=jnp.float32)


def vmem_call(body, shapes, *operands, flops=0, scratch=(), limit=10):
    spec = pl.BlockSpec(memory_space=pltpu.VMEM)
    size = sum(math.prod(a.shape) * a.dtype.itemsize for a in (*operands, *shapes))
    return pl.pallas_call(
        body,
        out_shape=shapes,
        in_specs=[spec] * len(operands),
        out_specs=[spec] * len(shapes),
        scratch_shapes=list(scratch),
        compiler_params=pltpu.CompilerParams(vmem_limit_bytes=limit * MIB),
        cost_estimate=pl.CostEstimate(flops=flops, bytes_accessed=size, transcendentals=0),
    )(*operands)


def in_hbm(array):
    return pltpu.with_memory_space_constraint(array, pltpu.HBM)


def phases(first, second, length):
    angle = (first[:, None] * second[None, :] % length) * (2.0 * math.pi / length)
    return np.cos(angle).astype(ml_dtypes.bfloat16), np.sin(angle).astype(ml_dtypes.bfloat16)


def column_matrix(width, devices):
    half = width // 2
    freq, col = np.arange(half), np.arange(width)
    cos, sin = phases(freq, col, width)
    sin[0] = (2 * (col % 2) - 1).astype(ml_dtypes.bfloat16)
    both = np.stack([cos, -sin]).reshape(2, devices, half // devices, width)
    return np.ascontiguousarray(both.transpose(1, 0, 2, 3)).reshape(width, width)


def row_matrix(height, row_devices, col_devices):
    devices = row_devices * col_devices
    strip = height // devices
    strips = np.arange(devices).reshape(row_devices, col_devices).T.reshape(-1)
    rows = (strips[None, :] * strip + np.arange(strip)[:, None]).reshape(-1)
    cos, sin = phases(np.arange(height), rows, height)
    return np.block([[cos, sin], [-sin, cos]])


def strip_row(signal, r):
    if len(signal.shape) == 3:
        return signal[r]
    return jnp.concatenate([signal[block, r] for block in range(signal.shape[0])], axis=0)


def strip_spectrum(signal, weight, table, norm):
    count = signal.shape[0 if len(signal.shape) == 3 else 1]
    rows = [dot_t(strip_row(signal, r), weight[...]).astype(jnp.bfloat16) for r in range(count)]
    return (dot(table[...], jnp.concatenate(rows, axis=1)) * norm).astype(jnp.bfloat16)


def spectrum_kernel(norm, signal, weight, table, out):
    out[...] = strip_spectrum(signal, weight, table, norm)


def prepare_kernel(
    norm,
    signal,
    weight,
    table,
    target,
    first,
    second,
    mask,
    spectrum,
    down,
    up,
    mask_row,
    first_out,
    second_out,
    signal_held,
    weight_held,
    table_held,
    sems,
):
    count = signal.shape[0]
    tile_rows, tile_cols = mask.shape
    channels = target.shape[2]
    moves = [(weight, weight_held)]
    moves += [(signal.at[r], signal_held.at[r]) for r in range(count)]
    moves += [
        (table, table_held),
        (target.at[pl.ds(tile_rows - NEAR, NEAR)], down.at[pl.ds(0, NEAR)]),
        (target.at[pl.ds(0, NEAR)], up.at[pl.ds(0, NEAR)]),
        (first, first_out),
        (second, second_out),
    ]
    copies = [pltpu.make_async_copy(*move, sems.at[i]) for i, move in enumerate(moves)]
    for copy in copies:
        copy.start()
    lanes = jnp.concatenate(
        [
            mask[...].astype(jnp.float32),
            jnp.zeros((tile_cols - tile_rows, tile_cols), jnp.float32),
        ],
        axis=0,
    ).T
    lanes = jnp.concatenate([lanes] + [jnp.zeros_like(lanes)] * (channels // tile_cols - 1), axis=1)
    lanes = lanes.astype(jnp.bfloat16)
    mask_row[0] = lanes
    down[NEAR] = lanes
    up[NEAR] = lanes
    copies[0].wait()
    rows = []
    for r in range(count):
        copies[1 + r].wait()
        rows.append(dot_t(signal_held[r], weight_held[...]).astype(jnp.bfloat16))
    copies[1 + count].wait()
    product = dot(table_held[...], jnp.concatenate(rows, axis=1))
    spectrum[...] = (product * norm).astype(jnp.bfloat16)
    for copy in copies[2 + count :]:
        copy.wait()


def prepare(norm, signal, weight, table, target, first, second, mask):
    rows, tile_cols, channels = target.shape
    strip, width, _ = signal.shape
    fetched = (signal, weight, table, target, first, second)
    in_vmem, hbm = pl.BlockSpec(memory_space=pltpu.VMEM), pl.BlockSpec(memory_space=pltpu.HBM)
    shapes = [
        (width, strip * weight.shape[0]),
        (NEAR + 1, tile_cols, channels),
        (NEAR + 1, tile_cols, channels),
        (1, tile_cols, channels),
        first.shape,
        second.shape,
    ]
    return pl.pallas_call(
        functools.partial(prepare_kernel, norm),
        out_shape=[jax.ShapeDtypeStruct(shape, jnp.bfloat16) for shape in shapes],
        in_specs=[hbm] * len(fetched) + [in_vmem],
        out_specs=[in_vmem] * len(shapes),
        scratch_shapes=[pltpu.VMEM(a.shape, a.dtype) for a in (signal, weight, table)]
        + [pltpu.SemaphoreType.DMA((strip + 6,))],
        compiler_params=pltpu.CompilerParams(vmem_limit_bytes=12 * MIB),
        cost_estimate=pl.CostEstimate(flops=0, bytes_accessed=5 * MIB, transcendentals=0),
    )(*[in_hbm(a) for a in fetched], mask)


def row_spectrum(moved, table, wide, norm, owned, devices):
    groups = wide.shape[0]
    for g in range(groups):
        wide[g] = moved[:, g * LANES : (g + 1) * LANES].astype(jnp.float32)
    strip = table.shape[1] // (2 * devices)
    half = moved.shape[1] // strip
    height = table.shape[0] // 2
    real, imag = [], []
    for freq in range(owned):
        parts = []
        for part in range(2):
            where = pl.ds(part * owned + freq, devices, stride=2 * owned)
            block = jnp.concatenate([wide[g, where, :] for g in range(groups)], axis=1)
            parts += [block[:, r * half : (r + 1) * half] for r in range(strip)]
        result = dot(table[...], jnp.concatenate(parts, axis=0).astype(jnp.bfloat16)) * norm
        real.append(result[:height])
        imag.append(result[height:])
    return jnp.concatenate(real, axis=0), jnp.concatenate(imag, axis=0)


def slope_kernel(norm, owned, devices, moved, mix, table, out, wide):
    parts = row_spectrum(moved, table, wide, norm, owned, devices)
    real, imag = [part.astype(jnp.bfloat16) for part in parts]
    half = real.shape[1]
    spans = (slice(0, half), slice(half, 2 * half))
    for part, span in enumerate(spans):
        pre = dot(real, mix[spans[0], span]) + dot(imag, mix[spans[1], span])
        s = 1.0 / (1.0 + jnp.exp(-pre))
        out[part] = s * (1.0 + pre * (1.0 - s))


def mix_kernel(norm, owned, devices, moved, slope, mix, table, back_table, out, wide):
    grads = row_spectrum(moved, table, wide, norm, owned, devices)
    half = grads[0].shape[1]
    spans = (slice(0, half), slice(half, 2 * half))
    mixed = [(grad * slope[part]).astype(jnp.bfloat16) for part, grad in enumerate(grads)]
    back = [dot_t(mixed[0], mix[p, spans[0]]) + dot_t(mixed[1], mix[p, spans[1]]) for p in spans]
    back = [part.astype(jnp.bfloat16) for part in back]
    height = table.shape[0] // 2
    strip = height // devices
    groups = wide.shape[0]
    for freq in range(owned):
        cells = slice(freq * height, (freq + 1) * height)
        stacked = jnp.concatenate([back[0][cells], back[1][cells]], axis=0)
        result = dot(back_table[...], stacked) * norm
        for part in range(2):
            rows = [
                result[(part * strip + r) * devices : (part * strip + r + 1) * devices]
                for r in range(strip)
            ]
            where = pl.ds(part * owned + freq, devices, stride=2 * owned)
            values = jnp.concatenate(rows, axis=1)
            for g in range(groups):
                wide[g, where, :] = values[:, g * LANES : (g + 1) * LANES]
    for g in range(groups):
        out[:, g * LANES : (g + 1) * LANES] = wide[g].astype(jnp.bfloat16)


def output_kernel(norm, moved, strip_grad, weight_in, weight_local, table, out):
    spatial = (dot(table[...], moved[...]) * norm).astype(jnp.bfloat16)
    half = weight_in.shape[0]
    for r in range(out.shape[0]):
        total = dot(spatial[:, r * half : (r + 1) * half], weight_in[...])
        total = total + dot_t(strip_row(strip_grad, r), weight_local[...])
        out[r] = total.astype(jnp.bfloat16)


def edge_kernel(*refs):
    sources, outs = refs[:-2], refs[-2:]
    count = len(sources) // 2
    for out, group in zip(outs, (sources[:count], sources[count:])):
        row = 0
        for ref in group:
            out[row : row + ref.shape[0]] = ref[...]
            row += ref.shape[0]


def edges(*parts):
    features = parts[1]
    channels = features.shape[2]
    last = features.shape[1] // REACH - 1

    def specs(at):
        return [pl.BlockSpec((p.shape[0], REACH, channels), lambda i, at=at: (0, at, 0)) for p in parts]

    rows = sum(p.shape[0] for p in parts)
    shape = jax.ShapeDtypeStruct((rows, REACH, channels), features.dtype)
    return pl.pallas_call(
        edge_kernel,
        grid=(1,),
        out_shape=[shape, shape],
        in_specs=specs(last) + specs(0),
        out_specs=[pl.BlockSpec(shape.shape, lambda i: (0, 0, 0))] * 2,
        compiler_params=pltpu.CompilerParams(vmem_limit_bytes=6 * MIB),
        cost_estimate=pl.CostEstimate(
            flops=0, bytes_accessed=8 * rows * REACH * channels, transcendentals=0
        ),
    )(*parts, *parts)


def put(wide, row, value, stride):
    size, channels = value.shape
    spot = pl.ds(row * stride, size)
    wide[spot, :channels] = pltpu.roll(value, 2, 0).astype(jnp.bfloat16)
    wide[spot, channels : 2 * channels] = value.astype(jnp.bfloat16)
    wide[spot, 2 * channels :] = pltpu.roll(value, size - 2, 0).astype(jnp.bfloat16)


def taps(wide, row, count, stride):
    parts = [wide[pl.ds((row + 2 * a) * stride, count * stride), :] for a in range(3)]
    return jnp.concatenate(parts, axis=1)


def conv(wide, row, count, stride, kernel):
    channels = kernel.shape[-1]
    return dot(taps(wide, row, count, stride), kernel[...].reshape(9 * channels, channels))


def conv_adjoint(wide, row, count, stride, kernel):
    flipped = [kernel[2 - a, 2 - b] for a in range(3) for b in range(3)]
    return dot_t(taps(wide, row, count, stride), jnp.concatenate(flipped, axis=1))


def stacked(piece, rows):
    return jnp.concatenate([piece(row) for row in rows], axis=0)


def first_stages(
    stride, blocks, rows, feature, inside, first, second, wide_even, wide_odd, slopes, use
):
    tall = rows + 2 * REACH
    for row in range(0, tall, NEAR):
        put(wide_even, row, stacked(feature, range(row, row + NEAR)), stride)
    count = blocks[0]
    for row in range(0, tall - 4, count):
        pre = conv(wide_even, row, count, stride, first)
        s = 1.0 / (1.0 + jnp.exp(-pre))
        kept = stacked(inside, range(row + 2, row + 2 + count))
        put(wide_odd, row, pre * s * kept, stride)
        low, high = max(row, NEAR), min(row + count, tall - 4 - NEAR)
        if low < high:
            part = slice((low - row) * stride, (high - row) * stride)
            slope = (s * (1.0 + pre * (1.0 - s)) * kept)[part]
            slopes[pl.ds((low - NEAR) * stride, (high - low) * stride), :] = slope
    count = blocks[1]
    for row in range(0, rows + 2 * NEAR, count):
        use(row, count, conv(wide_odd, row, count, stride, second))


def last_stages(stride, blocks, rows, first, second, wide_even, wide_odd, slopes, use):
    count = blocks[2]
    for row in range(0, rows + 4, count):
        value = conv_adjoint(wide_even, row, count, stride, second)
        value = value * slopes[pl.ds(row * stride, count * stride), :]
        put(wide_odd, row, value, stride)
    count = blocks[3]
    for row in range(0, rows, count):
        use(row, count, conv_adjoint(wide_odd, row, count, stride, first))


def loss_grad(row, count, value, target, hole, inside):
    near = range(row, row + count)
    weight = (1.0 + 2.0 * stacked(hole, near)) * stacked(inside, range(row + NEAR, row + count + NEAR))
    return weight * (value - stacked(target, near))


def part_of(rows, edge, above, own, below):
    def find(row):
        if row < edge:
            return above, row
        if row < edge + rows:
            return own, row - edge
        return below, row - edge - rows

    return find


TILE_BLOCKS = (4, 4, 4, 4)
SIDE_BLOCKS = (10, 8, 12, 8)


def tile_forward_kernel(above, features, below, first, second, ok, pre, slopes, wide_even, wide_odd):
    rows, stride, _ = features.shape
    find = part_of(rows, REACH, above, features, below)

    def feature(row):
        source, at = find(row)
        return source[at].astype(jnp.float32)

    def inside(row):
        return ok[REACH : REACH + stride, row : row + 1]

    def use(row, count, value):
        pre[pl.ds(row * stride, count * stride), :] = value

    first_stages(
        stride, TILE_BLOCKS, rows, feature, inside, first, second, wide_even, wide_odd, slopes, use
    )


def tile_backward_kernel(
    pre,
    slopes,
    target_above,
    target,
    target_below,
    mask_row,
    first,
    second,
    ok,
    out,
    wide_even,
    wide_odd,
):
    rows, stride, channels = target.shape
    find = part_of(rows, NEAR, target_above, target, target_below)

    def goal(row):
        source, at = find(row)
        return source[at].astype(jnp.float32)

    masks = [m[at].astype(jnp.float32) for m, at in ((target_above, NEAR), (mask_row, 0), (target_below, NEAR))]
    find_mask = part_of(rows, NEAR, (masks[0], rows - NEAR), (masks[1], 0), (masks[2], 0))

    def hole(row):
        (mask, start), at = find_mask(row)
        return mask[:, start + at : start + at + 1]

    def inside(row):
        return ok[REACH : REACH + stride, row : row + 1]

    count = NEAR
    for row in range(0, rows + 2 * NEAR, count):
        value = pre[pl.ds(row * stride, count * stride), :]
        put(wide_even, row, loss_grad(row, count, value, goal, hole, inside), stride)

    def use(row, count, value):
        out[row : row + count] = value.reshape(count, stride, channels).astype(jnp.bfloat16)

    last_stages(stride, TILE_BLOCKS, rows, first, second, wide_even, wide_odd, slopes, use)


def side_kernel(
    before,
    after,
    above,
    features,
    below,
    target_above,
    target,
    target_below,
    mask_row,
    first,
    second,
    ok,
    tile,
    out,
    wide_even,
    wide_odd,
    slopes,
):
    rows, tile_cols, channels = features.shape
    keep = 2 * REACH
    stride = 2 * (REACH + keep)
    tall = rows + 2 * REACH
    own = tall + NEAR + 1

    def joined(edge, source, at):
        parts = [before[edge], source[at, :keep], source[at, tile_cols - keep :], after[edge]]
        return jnp.concatenate([part.astype(jnp.float32) for part in parts], axis=0)

    find = part_of(rows, REACH, above, features, below)
    find_target = part_of(
        rows, NEAR, (target_above, tall), (target, own), (target_below, own + rows + 1)
    )

    def feature(row):
        return joined(row, *find(row))

    def goal(row):
        (source, edge), at = find_target(row)
        return joined(edge + at, source, at)

    masks = [
        joined(tall + NEAR, target_above, NEAR),
        joined(own + rows, mask_row, 0),
        joined(own + rows + 1 + NEAR, target_below, NEAR),
    ]
    find_mask = part_of(rows, NEAR, (masks[0], rows - NEAR), (masks[1], 0), (masks[2], 0))

    def hole(row):
        (mask, start), at = find_mask(row)
        return mask[:, start + at : start + at + 1]

    width = ok.shape[0]
    kept = jnp.concatenate([ok[: REACH + keep], ok[width - REACH - keep :]], axis=0)

    def inside(row):
        return kept[:, row : row + 1]

    def use_forward(row, count, value):
        put(wide_even, row, loss_grad(row, count, value, goal, hole, inside), stride)

    first_stages(
        stride, SIDE_BLOCKS, rows, feature, inside, first, second, wide_even, wide_odd, slopes, use_forward
    )
    out[:, REACH : tile_cols - REACH] = tile[:, REACH : tile_cols - REACH]

    def use(row, count, value):
        value = value.reshape(count, stride, channels).astype(jnp.bfloat16)
        out[row : row + count, :REACH] = value[:, REACH : 2 * REACH]
        out[row : row + count, tile_cols - REACH :] = value[:, stride - 2 * REACH : stride - REACH]

    last_stages(stride, SIDE_BLOCKS, rows, first, second, wide_even, wide_odd, slopes, use)


def wide_buffer(rows, stride, channels):
    return pltpu.VMEM((rows * stride, 3 * channels), jnp.bfloat16)


def tile_forward(above, features, below, first, second, ok):
    rows, stride, channels = features.shape
    shapes = [
        jax.ShapeDtypeStruct(((rows + h) * stride, channels), jnp.float32) for h in (2 * NEAR, 4)
    ]
    return vmem_call(
        tile_forward_kernel,
        shapes,
        above,
        features,
        below,
        first,
        second,
        ok,
        flops=2 * 9 * channels * channels * stride * (2 * rows + 20),
        scratch=[wide_buffer(rows + h, stride, channels) for h in (16, 12)],
        limit=18,
    )


def tile_backward(pre, slopes, target_above, target, target_below, mask_row, first, second, ok):
    rows, stride, channels = target.shape
    return vmem_call(
        tile_backward_kernel,
        [jax.ShapeDtypeStruct(target.shape, jnp.bfloat16)],
        pre,
        slopes,
        target_above,
        target,
        target_below,
        mask_row,
        first,
        second,
        ok,
        flops=2 * 9 * channels * channels * stride * (2 * rows + 4),
        scratch=[wide_buffer(rows + h, stride, channels) for h in (8, 4)],
        limit=16,
    )[0]


def sides(tile, *operands):
    rows, _, channels = tile.shape
    stride = 6 * REACH
    return vmem_call(
        side_kernel,
        [jax.ShapeDtypeStruct(tile.shape, jnp.bfloat16)],
        *operands,
        tile,
        flops=2 * 9 * channels * channels * stride * (4 * rows + 24),
        scratch=[wide_buffer(rows + h, stride, channels) for h in (16, 12)]
        + [pltpu.VMEM(((rows + 4) * stride, channels), jnp.float32)],
        limit=14,
    )[0]


def neighbours(axis):
    size = lax.axis_size(axis)
    up = [(i, i + 1) for i in range(size - 1)]
    return up, [(j, i) for i, j in up]


def shards(
    features,
    target,
    hole_mask,
    kernel_first,
    kernel_second,
    inputs,
    weight_in,
    weight_out,
    weight_local,
    weight_mix,
):
    tile_rows, tile_cols, channels = features.shape
    row_devices, col_devices = lax.axis_size("row"), lax.axis_size("col")
    devices = row_devices * col_devices
    height, width = tile_rows * row_devices, tile_cols * col_devices
    strip, half = inputs.shape[0], weight_in.shape[1]
    owned = width // 2 // devices
    col_norm, row_norm = 1.0 / math.sqrt(width), 1.0 / math.sqrt(height)
    table = column_matrix(width, devices)
    table_back = jnp.asarray(np.ascontiguousarray(table.T))
    table = jnp.asarray(table)
    row_table = row_matrix(height, row_devices, col_devices)
    row_back = jnp.asarray(np.ascontiguousarray(row_table.T))
    row_table = jnp.asarray(row_table)
    bf16 = jnp.bfloat16

    def swap(spectrum):
        return lax.all_to_all(spectrum, ("col", "row"), split_axis=0, concat_axis=0, tiled=True)

    cells = [jax.ShapeDtypeStruct((width, strip * half), bf16)]
    weight_in = weight_in.T
    spatial_cols, pack_down, pack_up, mask_row, kernel_first, kernel_second = prepare(
        col_norm, inputs, weight_in, table, target, kernel_first, kernel_second, hole_mask
    )
    spatial_moved = swap(spatial_cols)
    row0, col0 = lax.axis_index("row") * tile_rows, lax.axis_index("col") * tile_cols
    row_ids = row0 - REACH + jnp.arange(tile_rows + 2 * REACH, dtype=jnp.int32)
    col_ids = col0 - REACH + jnp.arange(tile_cols + 2 * REACH, dtype=jnp.int32)
    ok = ((col_ids >= 0) & (col_ids < width))[:, None] & ((row_ids >= 0) & (row_ids < height))[None]
    ok = ok.astype(jnp.float32)

    up, down = neighbours("row")
    left, right = neighbours("col")
    above = lax.ppermute(features, "row", up)
    below = lax.ppermute(features, "row", down)
    target_above = lax.ppermute(pack_down, "row", up)
    target_below = lax.ppermute(pack_up, "row", down)
    above, spatial_cols = lax.optimization_barrier((above, spatial_cols))
    pre, slopes = tile_forward(above, features, below, kernel_first, kernel_second, ok)
    target_above, pre = lax.optimization_barrier((target_above, pre))
    last, initial = edges(above, features, below, target_above, target, mask_row, target_below)
    before = lax.ppermute(last, "col", left)
    after = lax.ppermute(initial, "col", right)
    tile = tile_backward(
        pre, slopes, target_above, target, target_below, mask_row, kernel_first, kernel_second, ok
    )
    grad_feat = sides(
        tile,
        before,
        after,
        above,
        features,
        below,
        target_above,
        target,
        target_below,
        mask_row,
        kernel_first,
        kernel_second,
        ok,
    )

    grad_feat, spatial_moved = lax.optimization_barrier((grad_feat, spatial_moved))

    strip_grad = lax.all_to_all(
        grad_feat.reshape(col_devices, strip, tile_cols, channels), "col", split_axis=0, concat_axis=0
    )
    grad_cols = vmem_call(
        functools.partial(spectrum_kernel, col_norm), cells, strip_grad, weight_out, table
    )[0]
    cell_count = height * owned
    wide = [pltpu.VMEM((strip * half // LANES, width, LANES), jnp.float32)]
    slope = vmem_call(
        functools.partial(slope_kernel, row_norm, owned, devices),
        [jax.ShapeDtypeStruct((2, cell_count, half), jnp.float32)],
        spatial_moved,
        weight_mix,
        row_table,
        scratch=wide,
    )[0]
    grad_rows = vmem_call(
        functools.partial(mix_kernel, row_norm, owned, devices),
        cells,
        swap(grad_cols),
        slope,
        weight_mix,
        row_table,
        row_back,
        scratch=wide,
    )[0]
    returned = swap(grad_rows)
    return vmem_call(
        functools.partial(output_kernel, col_norm),
        [jax.ShapeDtypeStruct(inputs.shape, bf16)],
        returned,
        strip_grad,
        weight_in,
        weight_local,
        table_back,
    )[0]


def solution(mesh):
    in_specs = (
        P("row", "col", None),
        P("row", "col", None),
        P("row", "col"),
        P(),
        P(),
        P(("row", "col"), None, None),
        P(),
        P(),
        P(),
        P(),
    )
    out_specs = P(("row", "col"), None, None)
    return jax.shard_map(shards, mesh=mesh, in_specs=in_specs, out_specs=out_specs, check_vma=False)
```

```python
import functools
import math

import jax
import jax.numpy as jnp
import ml_dtypes
import numpy as np
from jax import lax
from jax.experimental import pallas as pl
from jax.experimental.pallas import tpu as pltpu
from jax.sharding import PartitionSpec as P

REACH = 8
NEAR = 4
MIB = 1024 * 1024
LANES = 128


def dot(left, right):
    return jnp.dot(left, right, preferred_element_type=jnp.float32)


def dot_t(left, right):
    return lax.dot_general(left, right, (((1,), (1,)), ((), ())), preferred_element_type=jnp.float32)


def vmem_call(body, shapes, *operands, flops=0, scratch=(), limit=10):
    spec = pl.BlockSpec(memory_space=pltpu.VMEM)
    size = sum(math.prod(a.shape) * a.dtype.itemsize for a in (*operands, *shapes))
    return pl.pallas_call(
        body,
        out_shape=shapes,
        in_specs=[spec] * len(operands),
        out_specs=[spec] * len(shapes),
        scratch_shapes=list(scratch),
        compiler_params=pltpu.CompilerParams(vmem_limit_bytes=limit * MIB),
        cost_estimate=pl.CostEstimate(flops=flops, bytes_accessed=size, transcendentals=0),
    )(*operands)


def in_hbm(array):
    return pltpu.with_memory_space_constraint(array, pltpu.HBM)


def phases(first, second, length):
    angle = (first[:, None] * second[None, :] % length) * (2.0 * math.pi / length)
    return np.cos(angle).astype(ml_dtypes.bfloat16), np.sin(angle).astype(ml_dtypes.bfloat16)


def column_matrix(width, devices):
    half = width // 2
    freq, col = np.arange(half), np.arange(width)
    cos, sin = phases(freq, col, width)
    sin[0] = (2 * (col % 2) - 1).astype(ml_dtypes.bfloat16)
    both = np.stack([cos, -sin]).reshape(2, devices, half // devices, width)
    return np.ascontiguousarray(both.transpose(1, 0, 2, 3)).reshape(width, width)


def row_matrix(height, row_devices, col_devices):
    devices = row_devices * col_devices
    strip = height // devices
    strips = np.arange(devices).reshape(row_devices, col_devices).T.reshape(-1)
    rows = (strips[None, :] * strip + np.arange(strip)[:, None]).reshape(-1)
    cos, sin = phases(np.arange(height), rows, height)
    return np.block([[cos, sin], [-sin, cos]])


def strip_row(signal, r):
    if len(signal.shape) == 3:
        return signal[r]
    return jnp.concatenate([signal[block, r] for block in range(signal.shape[0])], axis=0)


def strip_spectrum(signal, weight, table, norm):
    count = signal.shape[0 if len(signal.shape) == 3 else 1]
    rows = [dot_t(strip_row(signal, r), weight[...]).astype(jnp.bfloat16) for r in range(count)]
    return (dot(table[...], jnp.concatenate(rows, axis=1)) * norm).astype(jnp.bfloat16)


def spectrum_kernel(norm, signal, weight, table, out):
    out[...] = strip_spectrum(signal, weight, table, norm)


def fetching_spectrum_kernel(norm, signal, weight, table, out, signal_held, weight_held, table_held, sems):
    count = signal.shape[0]
    copies = [pltpu.make_async_copy(weight, weight_held, sems.at[0])]
    copies += [
        pltpu.make_async_copy(signal.at[r], signal_held.at[r], sems.at[1 + r]) for r in range(count)
    ]
    copies.append(pltpu.make_async_copy(table, table_held, sems.at[1 + count]))
    for copy in copies:
        copy.start()
    copies[0].wait()
    rows = []
    for r in range(count):
        copies[1 + r].wait()
        rows.append(dot_t(signal_held[r], weight_held[...]).astype(jnp.bfloat16))
    copies[-1].wait()
    out[...] = (dot(table_held[...], jnp.concatenate(rows, axis=1)) * norm).astype(jnp.bfloat16)


def fetching_spectrum(norm, shape, signal, weight, table):
    operands = (signal, weight, table)
    return pl.pallas_call(
        functools.partial(fetching_spectrum_kernel, norm),
        out_shape=shape,
        in_specs=[pl.BlockSpec(memory_space=pltpu.HBM)] * 3,
        out_specs=pl.BlockSpec(memory_space=pltpu.VMEM),
        scratch_shapes=[pltpu.VMEM(a.shape, a.dtype) for a in operands]
        + [pltpu.SemaphoreType.DMA((signal.shape[0] + 2,))],
        compiler_params=pltpu.CompilerParams(vmem_limit_bytes=12 * MIB),
        cost_estimate=pl.CostEstimate(
            flops=0, bytes_accessed=2 * MIB, transcendentals=0
        ),
    )(*[in_hbm(a) for a in operands])


def row_spectrum(moved, table, wide, norm, owned, devices):
    groups = wide.shape[0]
    for g in range(groups):
        wide[g] = moved[:, g * LANES : (g + 1) * LANES].astype(jnp.float32)
    strip = table.shape[1] // (2 * devices)
    half = moved.shape[1] // strip
    height = table.shape[0] // 2
    real, imag = [], []
    for freq in range(owned):
        parts = []
        for part in range(2):
            where = pl.ds(part * owned + freq, devices, stride=2 * owned)
            block = jnp.concatenate([wide[g, where, :] for g in range(groups)], axis=1)
            parts += [block[:, r * half : (r + 1) * half] for r in range(strip)]
        result = dot(table[...], jnp.concatenate(parts, axis=0).astype(jnp.bfloat16)) * norm
        real.append(result[:height])
        imag.append(result[height:])
    return jnp.concatenate(real, axis=0), jnp.concatenate(imag, axis=0)


def mix_kernel(norm, owned, devices, spatial, grad, mix, table, back_table, out, wide, wide_grad):
    parts = row_spectrum(spatial, table, wide, norm, owned, devices)
    real, imag = [part.astype(jnp.bfloat16) for part in parts]
    grads = row_spectrum(grad, table, wide_grad, norm, owned, devices)
    half = real.shape[1]
    spans = (slice(0, half), slice(half, 2 * half))
    mixed = []
    for span, value in zip(spans, grads):
        pre = dot(real, mix[spans[0], span]) + dot(imag, mix[spans[1], span])
        s = 1.0 / (1.0 + jnp.exp(-pre))
        mixed.append((value * (s * (1.0 + pre * (1.0 - s)))).astype(jnp.bfloat16))
    back = [dot_t(mixed[0], mix[p, spans[0]]) + dot_t(mixed[1], mix[p, spans[1]]) for p in spans]
    back = [part.astype(jnp.bfloat16) for part in back]
    height = table.shape[0] // 2
    strip = height // devices
    groups = wide.shape[0]
    for freq in range(owned):
        cells = slice(freq * height, (freq + 1) * height)
        stacked = jnp.concatenate([back[0][cells], back[1][cells]], axis=0)
        result = dot(back_table[...], stacked) * norm
        for part in range(2):
            rows = [
                result[(part * strip + r) * devices : (part * strip + r + 1) * devices]
                for r in range(strip)
            ]
            where = pl.ds(part * owned + freq, devices, stride=2 * owned)
            values = jnp.concatenate(rows, axis=1)
            for g in range(groups):
                wide[g, where, :] = values[:, g * LANES : (g + 1) * LANES]
    for g in range(groups):
        out[:, g * LANES : (g + 1) * LANES] = wide[g].astype(jnp.bfloat16)


def output_kernel(norm, moved, strip_grad, weight_in, weight_local, table, out):
    spatial = (dot(table[...], moved[...]) * norm).astype(jnp.bfloat16)
    half = weight_in.shape[0]
    for r in range(out.shape[0]):
        total = dot(spatial[:, r * half : (r + 1) * half], weight_in[...])
        total = total + dot_t(strip_row(strip_grad, r), weight_local[...])
        out[r] = total.astype(jnp.bfloat16)


def prepare_kernel(target, mask, first, down, up, mask_row, first_out, mask_held, sems):
    tile_rows, tile_cols = mask.shape
    channels = target.shape[2]
    moves = [
        (mask, mask_held),
        (target.at[pl.ds(tile_rows - NEAR, NEAR)], down.at[pl.ds(0, NEAR)]),
        (target.at[pl.ds(0, NEAR)], up.at[pl.ds(0, NEAR)]),
        (first, first_out),
    ]
    copies = [pltpu.make_async_copy(*move, sems.at[i]) for i, move in enumerate(moves)]
    for copy in copies:
        copy.start()
    copies[0].wait()
    lanes = jnp.concatenate(
        [
            mask_held[...].astype(jnp.float32),
            jnp.zeros((tile_cols - tile_rows, tile_cols), jnp.float32),
        ],
        axis=0,
    ).T
    lanes = jnp.concatenate([lanes] + [jnp.zeros_like(lanes)] * (channels // tile_cols - 1), axis=1)
    lanes = lanes.astype(jnp.bfloat16)
    mask_row[0] = lanes
    down[NEAR] = lanes
    up[NEAR] = lanes
    for copy in copies[1:]:
        copy.wait()


def prepare(target, mask, first):
    _, tile_cols, channels = target.shape
    shapes = [(n, tile_cols, channels) for n in (NEAR + 1, NEAR + 1, 1)] + [first.shape]
    return pl.pallas_call(
        prepare_kernel,
        out_shape=[jax.ShapeDtypeStruct(shape, jnp.bfloat16) for shape in shapes],
        in_specs=[pl.BlockSpec(memory_space=pltpu.HBM)] * 3,
        out_specs=[pl.BlockSpec(memory_space=pltpu.VMEM)] * len(shapes),
        scratch_shapes=[pltpu.VMEM(mask.shape, mask.dtype), pltpu.SemaphoreType.DMA((4,))],
        compiler_params=pltpu.CompilerParams(vmem_limit_bytes=6 * MIB),
        cost_estimate=pl.CostEstimate(flops=0, bytes_accessed=2 * MIB, transcendentals=0),
    )(in_hbm(target), in_hbm(mask), in_hbm(first))


def edge_kernel(*refs):
    sources, (last, initial, own) = refs[:-3], refs[-3:]
    count = len(sources) // 2
    keep = 2 * REACH
    row = 0
    for tail, head in zip(sources[:count], sources[count:]):
        rows = slice(row, row + tail.shape[0])
        last[rows] = tail[:, REACH:]
        initial[rows] = head[:, :REACH]
        own[rows, :keep] = head[...]
        own[rows, keep:] = tail[...]
        row += tail.shape[0]


def edges(*parts):
    features = parts[1]
    channels = features.shape[2]
    keep = 2 * REACH
    tail = features.shape[1] // keep - 1

    def specs(at):
        return [pl.BlockSpec((p.shape[0], keep, channels), lambda i, at=at: (0, at, 0)) for p in parts]

    rows = sum(p.shape[0] for p in parts)
    shapes = [(rows, columns, channels) for columns in (REACH, REACH, 2 * keep)]
    return pl.pallas_call(
        edge_kernel,
        grid=(1,),
        out_shape=[jax.ShapeDtypeStruct(shape, features.dtype) for shape in shapes],
        in_specs=specs(tail) + specs(0),
        out_specs=[pl.BlockSpec(shape, lambda i: (0, 0, 0)) for shape in shapes],
        compiler_params=pltpu.CompilerParams(vmem_limit_bytes=8 * MIB),
        cost_estimate=pl.CostEstimate(
            flops=0, bytes_accessed=16 * rows * keep * channels, transcendentals=0
        ),
    )(*parts, *parts)


def put(wide, row, value, stride):
    size, channels = value.shape
    spot = pl.ds(row * stride, size)
    wide[spot, :channels] = pltpu.roll(value, 2, 0).astype(jnp.bfloat16)
    wide[spot, channels : 2 * channels] = value.astype(jnp.bfloat16)
    wide[spot, 2 * channels :] = pltpu.roll(value, size - 2, 0).astype(jnp.bfloat16)


def taps(wide, row, count, stride):
    parts = [wide[pl.ds((row + 2 * a) * stride, count * stride), :] for a in range(3)]
    return jnp.concatenate(parts, axis=1)


def conv(wide, row, count, stride, kernel):
    channels = kernel.shape[-1]
    return dot(taps(wide, row, count, stride), kernel[...].reshape(9 * channels, channels))


def conv_adjoint(wide, row, count, stride, kernel):
    flipped = [kernel[2 - a, 2 - b] for a in range(3) for b in range(3)]
    return dot_t(taps(wide, row, count, stride), jnp.concatenate(flipped, axis=1))


def stacked(piece, rows):
    return jnp.concatenate([piece(row) for row in rows], axis=0)


def first_stages(
    stride, blocks, rows, feature, inside, first, second, wide_even, wide_odd, slopes, use, between=None
):
    tall = rows + 2 * REACH
    for row in range(0, tall, NEAR):
        put(wide_even, row, stacked(feature, range(row, row + NEAR)), stride)
    count = blocks[0]
    for row in range(0, tall - 4, count):
        pre = conv(wide_even, row, count, stride, first)
        s = 1.0 / (1.0 + jnp.exp(-pre))
        kept = stacked(inside, range(row + 2, row + 2 + count))
        put(wide_odd, row, pre * s * kept, stride)
        low, high = max(row, NEAR), min(row + count, tall - 4 - NEAR)
        if low < high:
            part = slice((low - row) * stride, (high - row) * stride)
            slope = (s * (1.0 + pre * (1.0 - s)) * kept)[part]
            slopes[pl.ds((low - NEAR) * stride, (high - low) * stride), :] = slope
    if between is not None:
        between()
    count = blocks[1]
    for row in range(0, rows + 2 * NEAR, count):
        use(row, count, conv(wide_odd, row, count, stride, second))


def last_stages(stride, blocks, rows, first, second, wide_even, wide_odd, slopes, use):
    count = blocks[2]
    for row in range(0, rows + 4, count):
        value = conv_adjoint(wide_even, row, count, stride, second)
        value = value * slopes[pl.ds(row * stride, count * stride), :]
        put(wide_odd, row, value, stride)
    count = blocks[3]
    for row in range(0, rows, count):
        use(row, count, conv_adjoint(wide_odd, row, count, stride, first))


def loss_grad(row, count, value, target, hole, inside):
    near = range(row, row + count)
    weight = (1.0 + 2.0 * stacked(hole, near)) * stacked(inside, range(row + NEAR, row + count + NEAR))
    return weight * (value - stacked(target, near))


def part_of(rows, edge, above, own, below):
    def find(row):
        if row < edge:
            return above, row
        if row < edge + rows:
            return own, row - edge
        return below, row - edge - rows

    return find


TILE_BLOCKS = (4, 4, 4, 4)
SIDE_BLOCKS = (10, 8, 12, 8)


def tile_forward_kernel(
    above, features, below, first, second, ok, pre, slopes, wide_even, wide_odd, second_held, sem
):
    rows, stride, _ = features.shape
    copy = pltpu.make_async_copy(second, second_held, sem)
    copy.start()
    find = part_of(rows, REACH, above, features, below)

    def feature(row):
        source, at = find(row)
        return source[at].astype(jnp.float32)

    def inside(row):
        return ok[REACH : REACH + stride, row : row + 1]

    def use(row, count, value):
        pre[pl.ds(row * stride, count * stride), :] = value

    first_stages(
        stride,
        TILE_BLOCKS,
        rows,
        feature,
        inside,
        first,
        second_held,
        wide_even,
        wide_odd,
        slopes,
        use,
        copy.wait,
    )


def tile_backward_kernel(
    pre,
    slopes,
    target_above,
    target,
    target_below,
    mask_row,
    first,
    second,
    ok,
    out,
    wide_even,
    wide_odd,
):
    rows, stride, channels = target.shape
    find = part_of(rows, NEAR, target_above, target, target_below)

    def goal(row):
        source, at = find(row)
        return source[at].astype(jnp.float32)

    masks = [m[at].astype(jnp.float32) for m, at in ((target_above, NEAR), (mask_row, 0), (target_below, NEAR))]
    find_mask = part_of(rows, NEAR, (masks[0], rows - NEAR), (masks[1], 0), (masks[2], 0))

    def hole(row):
        (mask, start), at = find_mask(row)
        return mask[:, start + at : start + at + 1]

    def inside(row):
        return ok[REACH : REACH + stride, row : row + 1]

    count = NEAR
    for row in range(0, rows + 2 * NEAR, count):
        value = pre[pl.ds(row * stride, count * stride), :]
        put(wide_even, row, loss_grad(row, count, value, goal, hole, inside), stride)

    def use(row, count, value):
        out[row : row + count] = value.reshape(count, stride, channels).astype(jnp.bfloat16)

    last_stages(stride, TILE_BLOCKS, rows, first, second, wide_even, wide_odd, slopes, use)


def side_kernel(before, after, own, first, second, ok, tile, out, wide_even, wide_odd, slopes):
    rows, tile_cols, channels = tile.shape
    keep = 2 * REACH
    stride = 2 * (REACH + keep)
    tall = rows + 2 * REACH

    def feature(row):
        parts = [part[row].astype(jnp.float32) for part in (before, own, after)]
        return jnp.concatenate(parts, axis=0)

    find = part_of(rows, NEAR, tall, tall + NEAR + 1, tall + NEAR + 1 + rows + 1)

    def goal(row):
        start, at = find(row)
        return feature(start + at)

    masks = [feature(row) for row in (tall + NEAR, tall + NEAR + 1 + rows, before.shape[0] - 1)]
    find_mask = part_of(rows, NEAR, (masks[0], rows - NEAR), (masks[1], 0), (masks[2], 0))

    def hole(row):
        (mask, start), at = find_mask(row)
        return mask[:, start + at : start + at + 1]

    width = ok.shape[0]
    kept = jnp.concatenate([ok[: REACH + keep], ok[width - REACH - keep :]], axis=0)

    def inside(row):
        return kept[:, row : row + 1]

    def use_forward(row, count, value):
        put(wide_even, row, loss_grad(row, count, value, goal, hole, inside), stride)

    first_stages(
        stride, SIDE_BLOCKS, rows, feature, inside, first, second, wide_even, wide_odd, slopes, use_forward
    )
    out[:, REACH : tile_cols - REACH] = tile[:, REACH : tile_cols - REACH]

    def use(row, count, value):
        value = value.reshape(count, stride, channels).astype(jnp.bfloat16)
        out[row : row + count, :REACH] = value[:, REACH : 2 * REACH]
        out[row : row + count, tile_cols - REACH :] = value[:, stride - 2 * REACH : stride - REACH]

    last_stages(stride, SIDE_BLOCKS, rows, first, second, wide_even, wide_odd, slopes, use)


def wide_buffer(rows, stride, channels):
    return pltpu.VMEM((rows * stride, 3 * channels), jnp.bfloat16)


def tile_forward(above, features, below, first, second, ok):
    rows, stride, channels = features.shape
    shapes = [
        jax.ShapeDtypeStruct(((rows + h) * stride, channels), jnp.float32) for h in (2 * NEAR, 4)
    ]
    in_vmem, hbm = pl.BlockSpec(memory_space=pltpu.VMEM), pl.BlockSpec(memory_space=pltpu.HBM)
    return pl.pallas_call(
        tile_forward_kernel,
        out_shape=shapes,
        in_specs=[in_vmem] * 4 + [hbm, in_vmem],
        out_specs=[in_vmem] * 2,
        scratch_shapes=[
            *[wide_buffer(rows + h, stride, channels) for h in (16, 12)],
            pltpu.VMEM(second.shape, second.dtype),
            pltpu.SemaphoreType.DMA,
        ],
        compiler_params=pltpu.CompilerParams(vmem_limit_bytes=18 * MIB),
        cost_estimate=pl.CostEstimate(
            flops=2 * 9 * channels * channels * stride * (2 * rows + 20),
            bytes_accessed=8 * MIB,
            transcendentals=0,
        ),
    )(above, features, below, first, in_hbm(second), ok)


def tile_backward(pre, slopes, target_above, target, target_below, mask_row, first, second, ok):
    rows, stride, channels = target.shape
    return vmem_call(
        tile_backward_kernel,
        [jax.ShapeDtypeStruct(target.shape, jnp.bfloat16)],
        pre,
        slopes,
        target_above,
        target,
        target_below,
        mask_row,
        first,
        second,
        ok,
        flops=2 * 9 * channels * channels * stride * (2 * rows + 4),
        scratch=[wide_buffer(rows + h, stride, channels) for h in (8, 4)],
        limit=16,
    )[0]


def sides(tile, *operands):
    rows, _, channels = tile.shape
    stride = 6 * REACH
    return vmem_call(
        side_kernel,
        [jax.ShapeDtypeStruct(tile.shape, jnp.bfloat16)],
        *operands,
        tile,
        flops=2 * 9 * channels * channels * stride * (4 * rows + 24),
        scratch=[wide_buffer(rows + h, stride, channels) for h in (16, 12)]
        + [pltpu.VMEM(((rows + 4) * stride, channels), jnp.float32)],
        limit=14,
    )[0]


def neighbours(axis):
    size = lax.axis_size(axis)
    up = [(i, i + 1) for i in range(size - 1)]
    return up, [(j, i) for i, j in up]


def shards(
    features,
    target,
    hole_mask,
    kernel_first,
    kernel_second,
    inputs,
    weight_in,
    weight_out,
    weight_local,
    weight_mix,
):
    tile_rows, tile_cols, channels = features.shape
    row_devices, col_devices = lax.axis_size("row"), lax.axis_size("col")
    devices = row_devices * col_devices
    height, width = tile_rows * row_devices, tile_cols * col_devices
    strip, half = inputs.shape[0], weight_in.shape[1]
    owned = width // 2 // devices
    col_norm, row_norm = 1.0 / math.sqrt(width), 1.0 / math.sqrt(height)
    table = column_matrix(width, devices)
    table_back = jnp.asarray(np.ascontiguousarray(table.T))
    table = jnp.asarray(table)
    row_table = row_matrix(height, row_devices, col_devices)
    row_back = jnp.asarray(np.ascontiguousarray(row_table.T))
    row_table = jnp.asarray(row_table)
    bf16 = jnp.bfloat16

    def swap(spectrum):
        return lax.all_to_all(spectrum, ("col", "row"), split_axis=0, concat_axis=0, tiled=True)

    cells = [jax.ShapeDtypeStruct((width, strip * half), bf16)]
    weight_in = weight_in.T
    spatial_cols = fetching_spectrum(col_norm, cells[0], inputs, weight_in, table)
    spatial_moved = swap(spatial_cols)
    row0, col0 = lax.axis_index("row") * tile_rows, lax.axis_index("col") * tile_cols
    row_ids = row0 - REACH + jnp.arange(tile_rows + 2 * REACH, dtype=jnp.int32)
    col_ids = col0 - REACH + jnp.arange(tile_cols + 2 * REACH, dtype=jnp.int32)
    ok = ((col_ids >= 0) & (col_ids < width))[:, None] & ((row_ids >= 0) & (row_ids < height))[None]
    ok = ok.astype(jnp.float32)

    up, down = neighbours("row")
    left, right = neighbours("col")
    above = lax.ppermute(features, "row", up)
    below = lax.ppermute(features, "row", down)
    target_after, spatial_cols = lax.optimization_barrier((target, spatial_cols))
    pack_down, pack_up, mask_row, kernel_first = prepare(target_after, hole_mask, kernel_first)
    target_above = lax.ppermute(pack_down, "row", up)
    target_below = lax.ppermute(pack_up, "row", down)
    pre, slopes = tile_forward(above, features, below, kernel_first, kernel_second, ok)
    target_above, pre = lax.optimization_barrier((target_above, pre))
    last, initial, own = edges(above, features, below, target_above, target, mask_row, target_below)
    before = lax.ppermute(last, "col", left)
    after = lax.ppermute(initial, "col", right)
    tile = tile_backward(
        pre, slopes, target_above, target, target_below, mask_row, kernel_first, kernel_second, ok
    )
    grad_feat = sides(tile, before, after, own, kernel_first, kernel_second, ok)
    grad_feat, spatial_moved = lax.optimization_barrier((grad_feat, spatial_moved))

    strip_grad = lax.all_to_all(
        grad_feat.reshape(col_devices, strip, tile_cols, channels), "col", split_axis=0, concat_axis=0
    )
    grad_cols = vmem_call(
        functools.partial(spectrum_kernel, col_norm), cells, strip_grad, weight_out, table
    )[0]
    wide = pltpu.VMEM((strip * half // LANES, width, LANES), jnp.float32)
    grad_rows = vmem_call(
        functools.partial(mix_kernel, row_norm, owned, devices),
        cells,
        spatial_moved,
        swap(grad_cols),
        weight_mix,
        row_table,
        row_back,
        scratch=[wide, wide],
    )[0]
    returned = swap(grad_rows)
    return vmem_call(
        functools.partial(output_kernel, col_norm),
        [jax.ShapeDtypeStruct(inputs.shape, bf16)],
        returned,
        strip_grad,
        weight_in,
        weight_local,
        table_back,
    )[0]


def solution(mesh):
    in_specs = (
        P("row", "col", None),
        P("row", "col", None),
        P("row", "col"),
        P(),
        P(),
        P(("row", "col"), None, None),
        P(),
        P(),
        P(),
        P(),
    )
    out_specs = P(("row", "col"), None, None)
    return jax.shard_map(shards, mesh=mesh, in_specs=in_specs, out_specs=out_specs, check_vma=False)
```

```python
import functools
import math

import jax
import jax.numpy as jnp
import ml_dtypes
import numpy as np
from jax import lax
from jax.experimental import pallas as pl
from jax.experimental.pallas import tpu as pltpu
from jax.sharding import PartitionSpec as P

REACH = 8
NEAR = 4
MIB = 1024 * 1024
LANES = 128


def dot(left, right):
    return jnp.dot(left, right, preferred_element_type=jnp.float32)


def dot_t(left, right):
    return lax.dot_general(left, right, (((1,), (1,)), ((), ())), preferred_element_type=jnp.float32)


def vmem_call(body, shapes, *operands, flops=0, scratch=(), limit=10):
    spec = pl.BlockSpec(memory_space=pltpu.VMEM)
    size = sum(math.prod(a.shape) * a.dtype.itemsize for a in (*operands, *shapes))
    return pl.pallas_call(
        body,
        out_shape=shapes,
        in_specs=[spec] * len(operands),
        out_specs=[spec] * len(shapes),
        scratch_shapes=list(scratch),
        compiler_params=pltpu.CompilerParams(vmem_limit_bytes=limit * MIB),
        cost_estimate=pl.CostEstimate(flops=flops, bytes_accessed=size, transcendentals=0),
    )(*operands)


def in_hbm(array):
    return pltpu.with_memory_space_constraint(array, pltpu.HBM)


def phases(first, second, length):
    angle = (first[:, None] * second[None, :] % length) * (2.0 * math.pi / length)
    return np.cos(angle).astype(ml_dtypes.bfloat16), np.sin(angle).astype(ml_dtypes.bfloat16)


def column_matrix(width, devices):
    half = width // 2
    freq, col = np.arange(half), np.arange(width)
    cos, sin = phases(freq, col, width)
    sin[0] = (2 * (col % 2) - 1).astype(ml_dtypes.bfloat16)
    both = np.stack([cos, -sin]).reshape(2, devices, half // devices, width)
    return np.ascontiguousarray(both.transpose(1, 0, 2, 3)).reshape(width, width)


def row_matrix(height, row_devices, col_devices):
    devices = row_devices * col_devices
    strip = height // devices
    strips = np.arange(devices).reshape(row_devices, col_devices).T.reshape(-1)
    rows = (strips[None, :] * strip + np.arange(strip)[:, None]).reshape(-1)
    cos, sin = phases(np.arange(height), rows, height)
    return np.block([[cos, sin], [-sin, cos]])


def strip_row(signal, r):
    if len(signal.shape) == 3:
        return signal[r]
    return jnp.concatenate([signal[block, r] for block in range(signal.shape[0])], axis=0)


def strip_spectrum(signal, weight, table, norm):
    count = signal.shape[0 if len(signal.shape) == 3 else 1]
    rows = [dot_t(strip_row(signal, r), weight[...]).astype(jnp.bfloat16) for r in range(count)]
    return (dot(table[...], jnp.concatenate(rows, axis=1)) * norm).astype(jnp.bfloat16)


def spectrum_kernel(norm, signal, weight, table, out):
    out[...] = strip_spectrum(signal, weight, table, norm)


def fetching_spectrum_kernel(norm, signal, weight, table, out, signal_held, weight_held, table_held, sems):
    count = signal.shape[0]
    copies = [pltpu.make_async_copy(weight, weight_held, sems.at[0])]
    copies += [
        pltpu.make_async_copy(signal.at[r], signal_held.at[r], sems.at[1 + r]) for r in range(count)
    ]
    copies.append(pltpu.make_async_copy(table, table_held, sems.at[1 + count]))
    for copy in copies:
        copy.start()
    copies[0].wait()
    rows = []
    for r in range(count):
        copies[1 + r].wait()
        rows.append(dot_t(signal_held[r], weight_held[...]).astype(jnp.bfloat16))
    copies[-1].wait()
    out[...] = (dot(table_held[...], jnp.concatenate(rows, axis=1)) * norm).astype(jnp.bfloat16)


def fetching_spectrum(norm, shape, signal, weight, table):
    operands = (signal, weight, table)
    return pl.pallas_call(
        functools.partial(fetching_spectrum_kernel, norm),
        out_shape=shape,
        in_specs=[pl.BlockSpec(memory_space=pltpu.HBM)] * 3,
        out_specs=pl.BlockSpec(memory_space=pltpu.VMEM),
        scratch_shapes=[pltpu.VMEM(a.shape, a.dtype) for a in operands]
        + [pltpu.SemaphoreType.DMA((signal.shape[0] + 2,))],
        compiler_params=pltpu.CompilerParams(vmem_limit_bytes=12 * MIB),
        cost_estimate=pl.CostEstimate(
            flops=0, bytes_accessed=2 * MIB, transcendentals=0
        ),
    )(*[in_hbm(a) for a in operands])


def row_spectrum(moved, table, wide, norm, owned, devices):
    groups = wide.shape[0]
    for g in range(groups):
        wide[g] = moved[:, g * LANES : (g + 1) * LANES].astype(jnp.float32)
    strip = table.shape[1] // (2 * devices)
    half = moved.shape[1] // strip
    height = table.shape[0] // 2
    real, imag = [], []
    for freq in range(owned):
        parts = []
        for part in range(2):
            where = pl.ds(part * owned + freq, devices, stride=2 * owned)
            block = jnp.concatenate([wide[g, where, :] for g in range(groups)], axis=1)
            parts += [block[:, r * half : (r + 1) * half] for r in range(strip)]
        result = dot(table[...], jnp.concatenate(parts, axis=0).astype(jnp.bfloat16)) * norm
        real.append(result[:height])
        imag.append(result[height:])
    return jnp.concatenate(real, axis=0), jnp.concatenate(imag, axis=0)


def mix_kernel(norm, owned, devices, spatial, grad, mix, table, back_table, out, wide, wide_grad):
    parts = row_spectrum(spatial, table, wide, norm, owned, devices)
    real, imag = [part.astype(jnp.bfloat16) for part in parts]
    grads = row_spectrum(grad, table, wide_grad, norm, owned, devices)
    half = real.shape[1]
    spans = (slice(0, half), slice(half, 2 * half))
    mixed = []
    for span, value in zip(spans, grads):
        pre = dot(real, mix[spans[0], span]) + dot(imag, mix[spans[1], span])
        s = 1.0 / (1.0 + jnp.exp(-pre))
        mixed.append((value * (s * (1.0 + pre * (1.0 - s)))).astype(jnp.bfloat16))
    back = [dot_t(mixed[0], mix[p, spans[0]]) + dot_t(mixed[1], mix[p, spans[1]]) for p in spans]
    back = [part.astype(jnp.bfloat16) for part in back]
    height = table.shape[0] // 2
    strip = height // devices
    groups = wide.shape[0]
    for freq in range(owned):
        cells = slice(freq * height, (freq + 1) * height)
        stacked = jnp.concatenate([back[0][cells], back[1][cells]], axis=0)
        result = dot(back_table[...], stacked) * norm
        for part in range(2):
            rows = [
                result[(part * strip + r) * devices : (part * strip + r + 1) * devices]
                for r in range(strip)
            ]
            where = pl.ds(part * owned + freq, devices, stride=2 * owned)
            values = jnp.concatenate(rows, axis=1)
            for g in range(groups):
                wide[g, where, :] = values[:, g * LANES : (g + 1) * LANES]
    for g in range(groups):
        out[:, g * LANES : (g + 1) * LANES] = wide[g].astype(jnp.bfloat16)


def output_kernel(norm, moved, strip_grad, weight_in, weight_local, table, out):
    spatial = (dot(table[...], moved[...]) * norm).astype(jnp.bfloat16)
    half = weight_in.shape[0]
    for r in range(out.shape[0]):
        total = dot(spatial[:, r * half : (r + 1) * half], weight_in[...])
        total = total + dot_t(strip_row(strip_grad, r), weight_local[...])
        out[r] = total.astype(jnp.bfloat16)


def prepare_kernel(
    target, mask, first, second, down, up, mask_row, first_out, second_out, mask_held, sems
):
    tile_rows, tile_cols = mask.shape
    channels = target.shape[2]
    moves = [
        (mask, mask_held),
        (target.at[pl.ds(tile_rows - NEAR, NEAR)], down.at[pl.ds(0, NEAR)]),
        (target.at[pl.ds(0, NEAR)], up.at[pl.ds(0, NEAR)]),
        (first, first_out),
        (second, second_out),
    ]
    copies = [pltpu.make_async_copy(*move, sems.at[i]) for i, move in enumerate(moves)]
    for copy in copies:
        copy.start()
    copies[0].wait()
    lanes = jnp.concatenate(
        [
            mask_held[...].astype(jnp.float32),
            jnp.zeros((tile_cols - tile_rows, tile_cols), jnp.float32),
        ],
        axis=0,
    ).T
    lanes = jnp.concatenate([lanes] + [jnp.zeros_like(lanes)] * (channels // tile_cols - 1), axis=1)
    lanes = lanes.astype(jnp.bfloat16)
    mask_row[0] = lanes
    down[NEAR] = lanes
    up[NEAR] = lanes
    for copy in copies[1:]:
        copy.wait()


def prepare(target, mask, first, second):
    _, tile_cols, channels = target.shape
    shapes = [(n, tile_cols, channels) for n in (NEAR + 1, NEAR + 1, 1)]
    shapes += [first.shape, second.shape]
    return pl.pallas_call(
        prepare_kernel,
        out_shape=[jax.ShapeDtypeStruct(shape, jnp.bfloat16) for shape in shapes],
        in_specs=[pl.BlockSpec(memory_space=pltpu.HBM)] * 4,
        out_specs=[pl.BlockSpec(memory_space=pltpu.VMEM)] * len(shapes),
        scratch_shapes=[pltpu.VMEM(mask.shape, mask.dtype), pltpu.SemaphoreType.DMA((5,))],
        compiler_params=pltpu.CompilerParams(vmem_limit_bytes=6 * MIB),
        cost_estimate=pl.CostEstimate(flops=0, bytes_accessed=2 * MIB, transcendentals=0),
    )(*[in_hbm(a) for a in (target, mask, first, second)])


def edge_kernel(*refs):
    sources, (last, initial, own) = refs[:-3], refs[-3:]
    count = len(sources) // 2
    keep = 2 * REACH
    row = 0
    for tail, head in zip(sources[:count], sources[count:]):
        rows = slice(row, row + tail.shape[0])
        last[rows] = tail[:, REACH:]
        initial[rows] = head[:, :REACH]
        own[rows, :keep] = head[...]
        own[rows, keep:] = tail[...]
        row += tail.shape[0]


def edges(*parts):
    features = parts[1]
    channels = features.shape[2]
    keep = 2 * REACH
    tail = features.shape[1] // keep - 1

    def specs(at):
        return [pl.BlockSpec((p.shape[0], keep, channels), lambda i, at=at: (0, at, 0)) for p in parts]

    rows = sum(p.shape[0] for p in parts)
    shapes = [(rows, columns, channels) for columns in (REACH, REACH, 2 * keep)]
    return pl.pallas_call(
        edge_kernel,
        grid=(1,),
        out_shape=[jax.ShapeDtypeStruct(shape, features.dtype) for shape in shapes],
        in_specs=specs(tail) + specs(0),
        out_specs=[pl.BlockSpec(shape, lambda i: (0, 0, 0)) for shape in shapes],
        compiler_params=pltpu.CompilerParams(vmem_limit_bytes=8 * MIB),
        cost_estimate=pl.CostEstimate(
            flops=0, bytes_accessed=16 * rows * keep * channels, transcendentals=0
        ),
    )(*parts, *parts)


def put(wide, row, value, stride):
    size, channels = value.shape
    spot = pl.ds(row * stride, size)
    wide[spot, :channels] = pltpu.roll(value, 2, 0).astype(jnp.bfloat16)
    wide[spot, channels : 2 * channels] = value.astype(jnp.bfloat16)
    wide[spot, 2 * channels :] = pltpu.roll(value, size - 2, 0).astype(jnp.bfloat16)


def taps(wide, row, count, stride):
    parts = [wide[pl.ds((row + 2 * a) * stride, count * stride), :] for a in range(3)]
    return jnp.concatenate(parts, axis=1)


def conv(wide, row, count, stride, kernel):
    channels = kernel.shape[-1]
    return dot(taps(wide, row, count, stride), kernel[...].reshape(9 * channels, channels))


def conv_adjoint(wide, row, count, stride, kernel):
    flipped = [kernel[2 - a, 2 - b] for a in range(3) for b in range(3)]
    return dot_t(taps(wide, row, count, stride), jnp.concatenate(flipped, axis=1))


def stacked(piece, rows):
    return jnp.concatenate([piece(row) for row in rows], axis=0)


def first_stages(
    stride, blocks, rows, feature, inside, first, second, wide_even, wide_odd, slopes, use
):
    tall = rows + 2 * REACH
    for row in range(0, tall, NEAR):
        put(wide_even, row, stacked(feature, range(row, row + NEAR)), stride)
    count = blocks[0]
    for row in range(0, tall - 4, count):
        pre = conv(wide_even, row, count, stride, first)
        s = 1.0 / (1.0 + jnp.exp(-pre))
        kept = stacked(inside, range(row + 2, row + 2 + count))
        put(wide_odd, row, pre * s * kept, stride)
        low, high = max(row, NEAR), min(row + count, tall - 4 - NEAR)
        if low < high:
            part = slice((low - row) * stride, (high - row) * stride)
            slope = (s * (1.0 + pre * (1.0 - s)) * kept)[part]
            slopes[pl.ds((low - NEAR) * stride, (high - low) * stride), :] = slope
    count = blocks[1]
    for row in range(0, rows + 2 * NEAR, count):
        use(row, count, conv(wide_odd, row, count, stride, second))


def last_stages(stride, blocks, rows, first, second, wide_even, wide_odd, slopes, use):
    count = blocks[2]
    for row in range(0, rows + 4, count):
        value = conv_adjoint(wide_even, row, count, stride, second)
        value = value * slopes[pl.ds(row * stride, count * stride), :]
        put(wide_odd, row, value, stride)
    count = blocks[3]
    for row in range(0, rows, count):
        use(row, count, conv_adjoint(wide_odd, row, count, stride, first))


def loss_grad(row, count, value, target, hole, inside):
    near = range(row, row + count)
    weight = (1.0 + 2.0 * stacked(hole, near)) * stacked(inside, range(row + NEAR, row + count + NEAR))
    return weight * (value - stacked(target, near))


def part_of(rows, edge, above, own, below):
    def find(row):
        if row < edge:
            return above, row
        if row < edge + rows:
            return own, row - edge
        return below, row - edge - rows

    return find


TILE_BLOCKS = (4, 4, 4, 4)
SIDE_BLOCKS = (10, 8, 12, 8)


def tile_forward_kernel(above, features, below, first, second, ok, pre, slopes, wide_even, wide_odd):
    rows, stride, _ = features.shape
    find = part_of(rows, REACH, above, features, below)

    def feature(row):
        source, at = find(row)
        return source[at].astype(jnp.float32)

    def inside(row):
        return ok[REACH : REACH + stride, row : row + 1]

    def use(row, count, value):
        pre[pl.ds(row * stride, count * stride), :] = value

    first_stages(
        stride, TILE_BLOCKS, rows, feature, inside, first, second, wide_even, wide_odd, slopes, use
    )


def tile_backward_kernel(
    pre,
    slopes,
    target_above,
    target,
    target_below,
    mask_row,
    first,
    second,
    ok,
    out,
    wide_even,
    wide_odd,
):
    rows, stride, channels = target.shape
    find = part_of(rows, NEAR, target_above, target, target_below)

    def goal(row):
        source, at = find(row)
        return source[at].astype(jnp.float32)

    masks = [m[at].astype(jnp.float32) for m, at in ((target_above, NEAR), (mask_row, 0), (target_below, NEAR))]
    find_mask = part_of(rows, NEAR, (masks[0], rows - NEAR), (masks[1], 0), (masks[2], 0))

    def hole(row):
        (mask, start), at = find_mask(row)
        return mask[:, start + at : start + at + 1]

    def inside(row):
        return ok[REACH : REACH + stride, row : row + 1]

    count = NEAR
    for row in range(0, rows + 2 * NEAR, count):
        value = pre[pl.ds(row * stride, count * stride), :]
        put(wide_even, row, loss_grad(row, count, value, goal, hole, inside), stride)

    def use(row, count, value):
        out[row : row + count] = value.reshape(count, stride, channels).astype(jnp.bfloat16)

    last_stages(stride, TILE_BLOCKS, rows, first, second, wide_even, wide_odd, slopes, use)


def side_kernel(before, after, own, first, second, ok, tile, out, wide_even, wide_odd, slopes):
    rows, tile_cols, channels = tile.shape
    keep = 2 * REACH
    stride = 2 * (REACH + keep)
    tall = rows + 2 * REACH

    def feature(row):
        parts = [part[row].astype(jnp.float32) for part in (before, own, after)]
        return jnp.concatenate(parts, axis=0)

    find = part_of(rows, NEAR, tall, tall + NEAR + 1, tall + NEAR + 1 + rows + 1)

    def goal(row):
        start, at = find(row)
        return feature(start + at)

    masks = [feature(row) for row in (tall + NEAR, tall + NEAR + 1 + rows, before.shape[0] - 1)]
    find_mask = part_of(rows, NEAR, (masks[0], rows - NEAR), (masks[1], 0), (masks[2], 0))

    def hole(row):
        (mask, start), at = find_mask(row)
        return mask[:, start + at : start + at + 1]

    width = ok.shape[0]
    kept = jnp.concatenate([ok[: REACH + keep], ok[width - REACH - keep :]], axis=0)

    def inside(row):
        return kept[:, row : row + 1]

    def use_forward(row, count, value):
        put(wide_even, row, loss_grad(row, count, value, goal, hole, inside), stride)

    first_stages(
        stride, SIDE_BLOCKS, rows, feature, inside, first, second, wide_even, wide_odd, slopes, use_forward
    )
    out[:, REACH : tile_cols - REACH] = tile[:, REACH : tile_cols - REACH]

    def use(row, count, value):
        value = value.reshape(count, stride, channels).astype(jnp.bfloat16)
        out[row : row + count, :REACH] = value[:, REACH : 2 * REACH]
        out[row : row + count, tile_cols - REACH :] = value[:, stride - 2 * REACH : stride - REACH]

    last_stages(stride, SIDE_BLOCKS, rows, first, second, wide_even, wide_odd, slopes, use)


def wide_buffer(rows, stride, channels):
    return pltpu.VMEM((rows * stride, 3 * channels), jnp.bfloat16)


def tile_forward(above, features, below, first, second, ok):
    rows, stride, channels = features.shape
    shapes = [
        jax.ShapeDtypeStruct(((rows + h) * stride, channels), jnp.float32) for h in (2 * NEAR, 4)
    ]
    return vmem_call(
        tile_forward_kernel,
        shapes,
        above,
        features,
        below,
        first,
        second,
        ok,
        flops=2 * 9 * channels * channels * stride * (2 * rows + 20),
        scratch=[wide_buffer(rows + h, stride, channels) for h in (16, 12)],
        limit=18,
    )


def tile_backward(pre, slopes, target_above, target, target_below, mask_row, first, second, ok):
    rows, stride, channels = target.shape
    return vmem_call(
        tile_backward_kernel,
        [jax.ShapeDtypeStruct(target.shape, jnp.bfloat16)],
        pre,
        slopes,
        target_above,
        target,
        target_below,
        mask_row,
        first,
        second,
        ok,
        flops=2 * 9 * channels * channels * stride * (2 * rows + 4),
        scratch=[wide_buffer(rows + h, stride, channels) for h in (8, 4)],
        limit=16,
    )[0]


def sides(tile, *operands):
    rows, _, channels = tile.shape
    stride = 6 * REACH
    return vmem_call(
        side_kernel,
        [jax.ShapeDtypeStruct(tile.shape, jnp.bfloat16)],
        *operands,
        tile,
        flops=2 * 9 * channels * channels * stride * (4 * rows + 24),
        scratch=[wide_buffer(rows + h, stride, channels) for h in (16, 12)]
        + [pltpu.VMEM(((rows + 4) * stride, channels), jnp.float32)],
        limit=14,
    )[0]


def neighbours(axis):
    size = lax.axis_size(axis)
    up = [(i, i + 1) for i in range(size - 1)]
    return up, [(j, i) for i, j in up]


def shards(
    features,
    target,
    hole_mask,
    kernel_first,
    kernel_second,
    inputs,
    weight_in,
    weight_out,
    weight_local,
    weight_mix,
):
    tile_rows, tile_cols, channels = features.shape
    row_devices, col_devices = lax.axis_size("row"), lax.axis_size("col")
    devices = row_devices * col_devices
    height, width = tile_rows * row_devices, tile_cols * col_devices
    strip, half = inputs.shape[0], weight_in.shape[1]
    owned = width // 2 // devices
    col_norm, row_norm = 1.0 / math.sqrt(width), 1.0 / math.sqrt(height)
    table = column_matrix(width, devices)
    table_back = jnp.asarray(np.ascontiguousarray(table.T))
    table = jnp.asarray(table)
    row_table = row_matrix(height, row_devices, col_devices)
    row_back = jnp.asarray(np.ascontiguousarray(row_table.T))
    row_table = jnp.asarray(row_table)
    bf16 = jnp.bfloat16

    def swap(spectrum):
        return lax.all_to_all(spectrum, ("col", "row"), split_axis=0, concat_axis=0, tiled=True)

    row0, col0 = lax.axis_index("row") * tile_rows, lax.axis_index("col") * tile_cols
    row_ids = row0 - REACH + jnp.arange(tile_rows + 2 * REACH, dtype=jnp.int32)
    col_ids = col0 - REACH + jnp.arange(tile_cols + 2 * REACH, dtype=jnp.int32)
    ok = ((col_ids >= 0) & (col_ids < width))[:, None] & ((row_ids >= 0) & (row_ids < height))[None]
    ok = ok.astype(jnp.float32)
    inputs, ok = lax.optimization_barrier((inputs, ok))

    cells = [jax.ShapeDtypeStruct((width, strip * half), bf16)]
    weight_in = weight_in.T
    spatial_cols = fetching_spectrum(col_norm, cells[0], inputs, weight_in, table)
    spatial_moved = swap(spatial_cols)

    up, down = neighbours("row")
    left, right = neighbours("col")
    above = lax.ppermute(features, "row", up)
    below = lax.ppermute(features, "row", down)
    target_after, spatial_cols = lax.optimization_barrier((target, spatial_cols))
    pack_down, pack_up, mask_row, kernel_first, kernel_second = prepare(
        target_after, hole_mask, kernel_first, kernel_second
    )
    target_above = lax.ppermute(pack_down, "row", up)
    target_below = lax.ppermute(pack_up, "row", down)
    pre, slopes = tile_forward(above, features, below, kernel_first, kernel_second, ok)
    target_above, pre = lax.optimization_barrier((target_above, pre))
    last, initial, own = edges(above, features, below, target_above, target, mask_row, target_below)
    before = lax.ppermute(last, "col", left)
    after = lax.ppermute(initial, "col", right)
    tile = tile_backward(
        pre, slopes, target_above, target, target_below, mask_row, kernel_first, kernel_second, ok
    )
    grad_feat = sides(tile, before, after, own, kernel_first, kernel_second, ok)
    grad_feat, spatial_moved = lax.optimization_barrier((grad_feat, spatial_moved))

    strip_grad = lax.all_to_all(
        grad_feat.reshape(col_devices, strip, tile_cols, channels), "col", split_axis=0, concat_axis=0
    )
    grad_cols = vmem_call(
        functools.partial(spectrum_kernel, col_norm), cells, strip_grad, weight_out, table
    )[0]
    wide = pltpu.VMEM((strip * half // LANES, width, LANES), jnp.float32)
    grad_rows = vmem_call(
        functools.partial(mix_kernel, row_norm, owned, devices),
        cells,
        spatial_moved,
        swap(grad_cols),
        weight_mix,
        row_table,
        row_back,
        scratch=[wide, wide],
    )[0]
    returned = swap(grad_rows)
    return vmem_call(
        functools.partial(output_kernel, col_norm),
        [jax.ShapeDtypeStruct(inputs.shape, bf16)],
        returned,
        strip_grad,
        weight_in,
        weight_local,
        table_back,
    )[0]


def solution(mesh):
    in_specs = (
        P("row", "col", None),
        P("row", "col", None),
        P("row", "col"),
        P(),
        P(),
        P(("row", "col"), None, None),
        P(),
        P(),
        P(),
        P(),
    )
    out_specs = P(("row", "col"), None, None)
    return jax.shard_map(shards, mesh=mesh, in_specs=in_specs, out_specs=out_specs, check_vma=False)
```

```python
import functools
import math

import jax
import jax.numpy as jnp
import ml_dtypes
import numpy as np
from jax import lax
from jax.experimental import pallas as pl
from jax.experimental.pallas import tpu as pltpu
from jax.sharding import PartitionSpec as P

REACH = 8
NEAR = 4
MIB = 1024 * 1024
LANES = 128


def dot(left, right):
    return jnp.dot(left, right, preferred_element_type=jnp.float32)


def dot_t(left, right):
    return lax.dot_general(left, right, (((1,), (1,)), ((), ())), preferred_element_type=jnp.float32)


def vmem_call(body, shapes, *operands, flops=0, scratch=(), limit=10):
    spec = pl.BlockSpec(memory_space=pltpu.VMEM)
    size = sum(math.prod(a.shape) * a.dtype.itemsize for a in (*operands, *shapes))
    return pl.pallas_call(
        body,
        out_shape=shapes,
        in_specs=[spec] * len(operands),
        out_specs=[spec] * len(shapes),
        scratch_shapes=list(scratch),
        compiler_params=pltpu.CompilerParams(vmem_limit_bytes=limit * MIB),
        cost_estimate=pl.CostEstimate(flops=flops, bytes_accessed=size, transcendentals=0),
    )(*operands)


def in_hbm(array):
    return pltpu.with_memory_space_constraint(array, pltpu.HBM)


def phases(first, second, length):
    angle = (first[:, None] * second[None, :] % length) * (2.0 * math.pi / length)
    return np.cos(angle).astype(ml_dtypes.bfloat16), np.sin(angle).astype(ml_dtypes.bfloat16)


def column_matrix(width, devices):
    half = width // 2
    freq, col = np.arange(half), np.arange(width)
    cos, sin = phases(freq, col, width)
    sin[0] = (2 * (col % 2) - 1).astype(ml_dtypes.bfloat16)
    both = np.stack([cos, -sin]).reshape(2, devices, half // devices, width)
    return np.ascontiguousarray(both.transpose(1, 0, 2, 3)).reshape(width, width)


def row_matrix(height, row_devices, col_devices):
    devices = row_devices * col_devices
    strip = height // devices
    strips = np.arange(devices).reshape(row_devices, col_devices).T.reshape(-1)
    rows = (strips[None, :] * strip + np.arange(strip)[:, None]).reshape(-1)
    cos, sin = phases(np.arange(height), rows, height)
    return np.block([[cos, sin], [-sin, cos]])


def strip_row(signal, r):
    return jnp.concatenate([signal[block, r] for block in range(signal.shape[0])], axis=0)


def grad_kernel(norm, col, *refs):
    *pieces, weight, table, out, strip_out, projected = refs
    tile_cols = pieces[0].shape[1]
    for step, piece in enumerate(pieces):
        block = col[0] ^ step
        strip_out[block] = piece[...]
        rows = [dot_t(piece[r], weight[...]).astype(jnp.bfloat16) for r in range(piece.shape[0])]
        where = pl.ds(pl.multiple_of(block * tile_cols, tile_cols), tile_cols)
        projected[where, :] = jnp.concatenate(rows, axis=1)
    out[...] = (dot(table[...], projected[...]) * norm).astype(jnp.bfloat16)


def grad_spectrum(norm, col, pieces, weight, table):
    strip, tile_cols, channels = pieces[0].shape
    shape = (table.shape[0], strip * weight.shape[0])
    in_vmem = pl.BlockSpec(memory_space=pltpu.VMEM)
    return pl.pallas_call(
        functools.partial(grad_kernel, norm),
        out_shape=[
            jax.ShapeDtypeStruct(shape, jnp.bfloat16),
            jax.ShapeDtypeStruct((len(pieces), strip, tile_cols, channels), jnp.bfloat16),
        ],
        in_specs=[pl.BlockSpec(memory_space=pltpu.SMEM)] + [in_vmem] * (len(pieces) + 2),
        out_specs=[in_vmem] * 2,
        scratch_shapes=[pltpu.VMEM(shape, jnp.bfloat16)],
        compiler_params=pltpu.CompilerParams(vmem_limit_bytes=10 * MIB),
        cost_estimate=pl.CostEstimate(flops=0, bytes_accessed=2 * MIB, transcendentals=0),
    )(col, *pieces, weight, table)


def fetching_spectrum_kernel(norm, signal, weight, table, out, signal_held, weight_held, table_held, sems):
    count = signal.shape[0]
    copies = [pltpu.make_async_copy(weight, weight_held, sems.at[0])]
    copies += [
        pltpu.make_async_copy(signal.at[r], signal_held.at[r], sems.at[1 + r]) for r in range(count)
    ]
    copies.append(pltpu.make_async_copy(table, table_held, sems.at[1 + count]))
    for copy in copies:
        copy.start()
    copies[0].wait()
    rows = []
    for r in range(count):
        copies[1 + r].wait()
        rows.append(dot_t(signal_held[r], weight_held[...]).astype(jnp.bfloat16))
    copies[-1].wait()
    out[...] = (dot(table_held[...], jnp.concatenate(rows, axis=1)) * norm).astype(jnp.bfloat16)


def fetching_spectrum(norm, shape, signal, weight, table):
    operands = (signal, weight, table)
    return pl.pallas_call(
        functools.partial(fetching_spectrum_kernel, norm),
        out_shape=shape,
        in_specs=[pl.BlockSpec(memory_space=pltpu.HBM)] * 3,
        out_specs=pl.BlockSpec(memory_space=pltpu.VMEM),
        scratch_shapes=[pltpu.VMEM(a.shape, a.dtype) for a in operands]
        + [pltpu.SemaphoreType.DMA((signal.shape[0] + 2,))],
        compiler_params=pltpu.CompilerParams(vmem_limit_bytes=12 * MIB),
        cost_estimate=pl.CostEstimate(
            flops=0, bytes_accessed=2 * MIB, transcendentals=0
        ),
    )(*[in_hbm(a) for a in operands])


def row_spectrum(moved, table, wide, norm, owned, devices):
    groups = wide.shape[0]
    for g in range(groups):
        wide[g] = moved[:, g * LANES : (g + 1) * LANES].astype(jnp.float32)
    strip = table.shape[1] // (2 * devices)
    half = moved.shape[1] // strip
    height = table.shape[0] // 2
    real, imag = [], []
    for freq in range(owned):
        parts = []
        for part in range(2):
            where = pl.ds(part * owned + freq, devices, stride=2 * owned)
            block = jnp.concatenate([wide[g, where, :] for g in range(groups)], axis=1)
            parts += [block[:, r * half : (r + 1) * half] for r in range(strip)]
        result = dot(table[...], jnp.concatenate(parts, axis=0).astype(jnp.bfloat16)) * norm
        real.append(result[:height])
        imag.append(result[height:])
    return jnp.concatenate(real, axis=0), jnp.concatenate(imag, axis=0)


def mix_kernel(norm, owned, devices, spatial, grad, mix, table, back_table, out, wide, wide_grad):
    parts = row_spectrum(spatial, table, wide, norm, owned, devices)
    real, imag = [part.astype(jnp.bfloat16) for part in parts]
    grads = row_spectrum(grad, table, wide_grad, norm, owned, devices)
    half = real.shape[1]
    spans = (slice(0, half), slice(half, 2 * half))
    mixed = []
    for span, value in zip(spans, grads):
        pre = dot(real, mix[spans[0], span]) + dot(imag, mix[spans[1], span])
        s = 1.0 / (1.0 + jnp.exp(-pre))
        mixed.append((value * (s * (1.0 + pre * (1.0 - s)))).astype(jnp.bfloat16))
    back = [dot_t(mixed[0], mix[p, spans[0]]) + dot_t(mixed[1], mix[p, spans[1]]) for p in spans]
    back = [part.astype(jnp.bfloat16) for part in back]
    height = table.shape[0] // 2
    strip = height // devices
    groups = wide.shape[0]
    for freq in range(owned):
        cells = slice(freq * height, (freq + 1) * height)
        stacked = jnp.concatenate([back[0][cells], back[1][cells]], axis=0)
        result = dot(back_table[...], stacked) * norm
        for part in range(2):
            rows = [
                result[(part * strip + r) * devices : (part * strip + r + 1) * devices]
                for r in range(strip)
            ]
            where = pl.ds(part * owned + freq, devices, stride=2 * owned)
            values = jnp.concatenate(rows, axis=1)
            for g in range(groups):
                wide[g, where, :] = values[:, g * LANES : (g + 1) * LANES]
    for g in range(groups):
        out[:, g * LANES : (g + 1) * LANES] = wide[g].astype(jnp.bfloat16)


def output_kernel(norm, moved, strip_grad, weight_in, weight_local, table, out):
    spatial = (dot(table[...], moved[...]) * norm).astype(jnp.bfloat16)
    half = weight_in.shape[0]
    for r in range(out.shape[0]):
        total = dot(spatial[:, r * half : (r + 1) * half], weight_in[...])
        total = total + dot_t(strip_row(strip_grad, r), weight_local[...])
        out[r] = total.astype(jnp.bfloat16)


TAIL = 16


def turned(rows):
    count, columns = rows.shape
    rows = rows.astype(jnp.float32)
    return jnp.concatenate([rows, jnp.zeros((columns - count, columns), jnp.float32)], axis=0).T


def filled(lanes, channels):
    fill = jnp.zeros((lanes.shape[0], channels - lanes.shape[1]), jnp.float32)
    return jnp.concatenate([lanes, fill], axis=1).astype(jnp.bfloat16)


def prepare_kernel(
    target, mask, first, second, down, up, mask_row, first_out, second_out, mask_held, sems
):
    tile_rows, tile_cols = mask.shape
    channels = target.shape[2]
    moves = [(mask, mask_held)]
    for pack, start in ((down, tile_rows - NEAR), (up, 0)):
        moves += [
            (target.at[start + i], pack.at[pl.ds(i * tile_cols, tile_cols)]) for i in range(NEAR)
        ]
    moves += [(first, first_out), (second, second_out)]
    copies = [pltpu.make_async_copy(*move, sems.at[i]) for i, move in enumerate(moves)]
    for copy in copies:
        copy.start()
    copies[0].wait()
    mask_row[0] = filled(turned(mask_held[...]), channels)
    for pack, start in ((down, tile_rows - NEAR), (up, 0)):
        rows = mask_held[start : start + NEAR].astype(jnp.float32)
        rows = jnp.concatenate([rows, jnp.zeros((TAIL - NEAR, tile_cols), jnp.float32)], axis=0)
        pack[NEAR * tile_cols :] = filled(rows, channels)
    for copy in copies[1:]:
        copy.wait()


def prepare(target, mask, first, second):
    _, tile_cols, channels = target.shape
    pack = (NEAR * tile_cols + TAIL, channels)
    shapes = [pack, pack, (1, tile_cols, channels), first.shape, second.shape]
    return pl.pallas_call(
        prepare_kernel,
        out_shape=[jax.ShapeDtypeStruct(shape, jnp.bfloat16) for shape in shapes],
        in_specs=[pl.BlockSpec(memory_space=pltpu.HBM)] * 4,
        out_specs=[pl.BlockSpec(memory_space=pltpu.VMEM)] * len(shapes),
        scratch_shapes=[pltpu.VMEM(mask.shape, mask.dtype), pltpu.SemaphoreType.DMA((2 * NEAR + 3,))],
        compiler_params=pltpu.CompilerParams(vmem_limit_bytes=6 * MIB),
        cost_estimate=pl.CostEstimate(flops=0, bytes_accessed=2 * MIB, transcendentals=0),
    )(*[in_hbm(a) for a in (target, mask, first, second)])


def edge_kernel(tile_cols, *refs):
    above_pack, below_pack, *sources = refs[:-3]
    last, initial, own = refs[-3:]
    count = len(sources) // 2
    keep = 2 * REACH
    channels = own.shape[2]

    def put_rows(row, tail, head):
        rows = slice(row, row + tail.shape[0])
        last[rows] = tail[:, REACH:]
        initial[rows] = head[:, :REACH]
        own[rows, :keep] = head
        own[rows, keep:] = tail

    def put_pack(row, pack):
        for i in range(NEAR):
            pixels = pack[i * tile_cols : (i + 1) * tile_cols]
            put_rows(row + i, pixels[None, tile_cols - keep :], pixels[None, :keep])
        mask = turned(pack[NEAR * tile_cols :, :tile_cols])
        tail, head = [filled(m, channels)[None] for m in (mask[tile_cols - keep :], mask[:keep])]
        put_rows(row + NEAR, tail, head)

    row = 0
    for index, (tail, head) in enumerate(zip(sources[:count], sources[count:])):
        if index == 3:
            put_pack(row, above_pack)
            row += NEAR + 1
        put_rows(row, tail[...], head[...])
        row += tail.shape[0]
    put_pack(row, below_pack)


def edges(above, features, below, above_pack, target, mask_row, below_pack):
    parts = (above, features, below, target, mask_row)
    _, tile_cols, channels = features.shape
    keep = 2 * REACH
    tail = tile_cols // keep - 1

    def specs(at):
        return [pl.BlockSpec((p.shape[0], keep, channels), lambda i, at=at: (0, at, 0)) for p in parts]

    whole = [pl.BlockSpec(above_pack.shape, lambda i: (0, 0))] * 2
    rows = sum(p.shape[0] for p in parts) + 2 * (NEAR + 1)
    shapes = [(rows, columns, channels) for columns in (REACH, REACH, 2 * keep)]
    return pl.pallas_call(
        functools.partial(edge_kernel, tile_cols),
        grid=(1,),
        out_shape=[jax.ShapeDtypeStruct(shape, features.dtype) for shape in shapes],
        in_specs=whole + specs(tail) + specs(0),
        out_specs=[pl.BlockSpec(shape, lambda i: (0, 0, 0)) for shape in shapes],
        compiler_params=pltpu.CompilerParams(vmem_limit_bytes=8 * MIB),
        cost_estimate=pl.CostEstimate(
            flops=0, bytes_accessed=16 * rows * keep * channels, transcendentals=0
        ),
    )(above_pack, below_pack, *parts, *parts)


def put(wide, row, value, stride):
    size, channels = value.shape
    spot = pl.ds(row * stride, size)
    wide[spot, :channels] = pltpu.roll(value, 2, 0).astype(jnp.bfloat16)
    wide[spot, channels : 2 * channels] = value.astype(jnp.bfloat16)
    wide[spot, 2 * channels :] = pltpu.roll(value, size - 2, 0).astype(jnp.bfloat16)


def taps(wide, row, count, stride):
    parts = [wide[pl.ds((row + 2 * a) * stride, count * stride), :] for a in range(3)]
    return jnp.concatenate(parts, axis=1)


def conv(wide, row, count, stride, kernel):
    channels = kernel.shape[-1]
    return dot(taps(wide, row, count, stride), kernel[...].reshape(9 * channels, channels))


def conv_adjoint(wide, row, count, stride, kernel):
    flipped = [kernel[2 - a, 2 - b] for a in range(3) for b in range(3)]
    return dot_t(taps(wide, row, count, stride), jnp.concatenate(flipped, axis=1))


def stacked(piece, rows):
    return jnp.concatenate([piece(row) for row in rows], axis=0)


def first_stages(
    stride, blocks, rows, feature, inside, first, second, wide_even, wide_odd, slopes, use
):
    tall = rows + 2 * REACH
    for row in range(0, tall, NEAR):
        put(wide_even, row, stacked(feature, range(row, row + NEAR)), stride)
    count = blocks[0]
    for row in range(0, tall - 4, count):
        pre = conv(wide_even, row, count, stride, first)
        s = 1.0 / (1.0 + jnp.exp(-pre))
        kept = stacked(inside, range(row + 2, row + 2 + count))
        put(wide_odd, row, pre * s * kept, stride)
        low, high = max(row, NEAR), min(row + count, tall - 4 - NEAR)
        if low < high:
            part = slice((low - row) * stride, (high - row) * stride)
            slope = (s * (1.0 + pre * (1.0 - s)) * kept)[part]
            slopes[pl.ds((low - NEAR) * stride, (high - low) * stride), :] = slope
    count = blocks[1]
    for row in range(0, rows + 2 * NEAR, count):
        use(row, count, conv(wide_odd, row, count, stride, second))


def last_stages(stride, blocks, rows, first, second, wide_even, wide_odd, slopes, use):
    count = blocks[2]
    for row in range(0, rows + 4, count):
        value = conv_adjoint(wide_even, row, count, stride, second)
        value = value * slopes[pl.ds(row * stride, count * stride), :]
        put(wide_odd, row, value, stride)
    count = blocks[3]
    for row in range(0, rows, count):
        use(row, count, conv_adjoint(wide_odd, row, count, stride, first))


def loss_grad(row, count, value, target, hole, inside):
    near = range(row, row + count)
    weight = (1.0 + 2.0 * stacked(hole, near)) * stacked(inside, range(row + NEAR, row + count + NEAR))
    return weight * (value - stacked(target, near))


def part_of(rows, edge, above, own, below):
    def find(row):
        if row < edge:
            return above, row
        if row < edge + rows:
            return own, row - edge
        return below, row - edge - rows

    return find


TILE_BLOCKS = (4, 4, 4, 4)
SIDE_BLOCKS = (10, 8, 12, 8)


def tile_forward_kernel(above, features, below, first, second, ok, pre, slopes, wide_even, wide_odd):
    rows, stride, _ = features.shape
    find = part_of(rows, REACH, above, features, below)

    def feature(row):
        source, at = find(row)
        return source[at].astype(jnp.float32)

    def inside(row):
        return ok[REACH : REACH + stride, row : row + 1]

    def use(row, count, value):
        pre[pl.ds(row * stride, count * stride), :] = value

    first_stages(
        stride, TILE_BLOCKS, rows, feature, inside, first, second, wide_even, wide_odd, slopes, use
    )


def tile_backward_kernel(
    pre,
    slopes,
    target_above,
    target,
    target_below,
    mask_row,
    first,
    second,
    ok,
    out,
    wide_even,
    wide_odd,
):
    rows, stride, channels = target.shape
    find = part_of(rows, NEAR, target_above, target, target_below)

    def goal(row):
        source, at = find(row)
        pixels = source[at] if source is target else source[at * stride : (at + 1) * stride]
        return pixels.astype(jnp.float32)

    masks = [turned(pack[NEAR * stride :, :stride]) for pack in (target_above, target_below)]
    find_mask = part_of(rows, NEAR, (masks[0], 0), (mask_row[0].astype(jnp.float32), 0), (masks[1], 0))

    def hole(row):
        (mask, start), at = find_mask(row)
        return mask[:, start + at : start + at + 1]

    def inside(row):
        return ok[REACH : REACH + stride, row : row + 1]

    count = NEAR
    for row in range(0, rows + 2 * NEAR, count):
        value = pre[pl.ds(row * stride, count * stride), :]
        put(wide_even, row, loss_grad(row, count, value, goal, hole, inside), stride)

    def use(row, count, value):
        out[row : row + count] = value.reshape(count, stride, channels).astype(jnp.bfloat16)

    last_stages(stride, TILE_BLOCKS, rows, first, second, wide_even, wide_odd, slopes, use)


def side_kernel(col, before, after, own, first, second, ok, tile, *refs):
    *pieces, out, wide_even, wide_odd, slopes = refs
    rows, tile_cols, channels = tile.shape
    keep = 2 * REACH
    stride = 2 * (REACH + keep)
    tall = rows + 2 * REACH

    def feature(row):
        parts = [part[row].astype(jnp.float32) for part in (before, own, after)]
        return jnp.concatenate(parts, axis=0)

    find = part_of(rows, NEAR, tall, tall + NEAR + 1, tall + NEAR + 1 + rows + 1)

    def goal(row):
        start, at = find(row)
        return feature(start + at)

    masks = [feature(row) for row in (tall + NEAR, tall + NEAR + 1 + rows, before.shape[0] - 1)]
    find_mask = part_of(rows, NEAR, (masks[0], 0), (masks[1], 0), (masks[2], 0))

    def hole(row):
        (mask, start), at = find_mask(row)
        return mask[:, start + at : start + at + 1]

    width = ok.shape[0]
    kept = jnp.concatenate([ok[: REACH + keep], ok[width - REACH - keep :]], axis=0)

    def inside(row):
        return kept[:, row : row + 1]

    def use_forward(row, count, value):
        put(wide_even, row, loss_grad(row, count, value, goal, hole, inside), stride)

    first_stages(
        stride, SIDE_BLOCKS, rows, feature, inside, first, second, wide_even, wide_odd, slopes, use_forward
    )
    out[:, REACH : tile_cols - REACH] = tile[:, REACH : tile_cols - REACH]

    def use(row, count, value):
        value = value.reshape(count, stride, channels).astype(jnp.bfloat16)
        out[row : row + count, :REACH] = value[:, REACH : 2 * REACH]
        out[row : row + count, tile_cols - REACH :] = value[:, stride - 2 * REACH : stride - REACH]

    last_stages(stride, SIDE_BLOCKS, rows, first, second, wide_even, wide_odd, slopes, use)
    for step, piece in enumerate(pieces):
        piece[...] = out[pl.ds((col[0] ^ step) * piece.shape[0], piece.shape[0])]


def wide_buffer(rows, stride, channels):
    return pltpu.VMEM((rows * stride, 3 * channels), jnp.bfloat16)


def tile_forward(above, features, below, first, second, ok):
    rows, stride, channels = features.shape
    shapes = [
        jax.ShapeDtypeStruct(((rows + h) * stride, channels), jnp.float32) for h in (2 * NEAR, 4)
    ]
    return vmem_call(
        tile_forward_kernel,
        shapes,
        above,
        features,
        below,
        first,
        second,
        ok,
        flops=2 * 9 * channels * channels * stride * (2 * rows + 20),
        scratch=[wide_buffer(rows + h, stride, channels) for h in (16, 12)],
        limit=18,
    )


def tile_backward(pre, slopes, target_above, target, target_below, mask_row, first, second, ok):
    rows, stride, channels = target.shape
    return vmem_call(
        tile_backward_kernel,
        [jax.ShapeDtypeStruct(target.shape, jnp.bfloat16)],
        pre,
        slopes,
        target_above,
        target,
        target_below,
        mask_row,
        first,
        second,
        ok,
        flops=2 * 9 * channels * channels * stride * (2 * rows + 4),
        scratch=[wide_buffer(rows + h, stride, channels) for h in (8, 4)],
        limit=16,
    )[0]


def sides(col, tile, *operands):
    rows, tile_cols, channels = tile.shape
    stride = 6 * REACH
    count = lax.axis_size("col")
    piece = jax.ShapeDtypeStruct((rows // count, tile_cols, channels), jnp.bfloat16)
    in_vmem = pl.BlockSpec(memory_space=pltpu.VMEM)
    return pl.pallas_call(
        side_kernel,
        out_shape=[piece] * count,
        in_specs=[pl.BlockSpec(memory_space=pltpu.SMEM)] + [in_vmem] * (len(operands) + 1),
        out_specs=[in_vmem] * count,
        scratch_shapes=[
            pltpu.VMEM(tile.shape, tile.dtype),
            *[wide_buffer(rows + h, stride, channels) for h in (16, 12)],
            pltpu.VMEM(((rows + 4) * stride, channels), jnp.float32),
        ],
        compiler_params=pltpu.CompilerParams(vmem_limit_bytes=14 * MIB),
        cost_estimate=pl.CostEstimate(
            flops=2 * 9 * channels * channels * stride * (4 * rows + 24),
            bytes_accessed=4 * MIB,
            transcendentals=0,
        ),
    )(col, *operands, tile)


def neighbours(axis):
    size = lax.axis_size(axis)
    up = [(i, i + 1) for i in range(size - 1)]
    return up, [(j, i) for i, j in up]


def shards(
    features,
    target,
    hole_mask,
    kernel_first,
    kernel_second,
    inputs,
    weight_in,
    weight_out,
    weight_local,
    weight_mix,
):
    tile_rows, tile_cols, channels = features.shape
    row_devices, col_devices = lax.axis_size("row"), lax.axis_size("col")
    devices = row_devices * col_devices
    height, width = tile_rows * row_devices, tile_cols * col_devices
    strip, half = inputs.shape[0], weight_in.shape[1]
    owned = width // 2 // devices
    col_norm, row_norm = 1.0 / math.sqrt(width), 1.0 / math.sqrt(height)
    table = column_matrix(width, devices)
    table_back = jnp.asarray(np.ascontiguousarray(table.T))
    table = jnp.asarray(table)
    row_table = row_matrix(height, row_devices, col_devices)
    row_back = jnp.asarray(np.ascontiguousarray(row_table.T))
    row_table = jnp.asarray(row_table)
    bf16 = jnp.bfloat16

    def swap(spectrum):
        return lax.all_to_all(spectrum, ("col", "row"), split_axis=0, concat_axis=0, tiled=True)

    row0, col0 = lax.axis_index("row") * tile_rows, lax.axis_index("col") * tile_cols
    row_ids = row0 - REACH + jnp.arange(tile_rows + 2 * REACH, dtype=jnp.int32)
    col_ids = col0 - REACH + jnp.arange(tile_cols + 2 * REACH, dtype=jnp.int32)
    ok = ((col_ids >= 0) & (col_ids < width))[:, None] & ((row_ids >= 0) & (row_ids < height))[None]
    ok = ok.astype(jnp.float32)
    col = jnp.full((1,), lax.axis_index("col"), jnp.int32)
    inputs, ok, col = lax.optimization_barrier((inputs, ok, col))

    cells = [jax.ShapeDtypeStruct((width, strip * half), bf16)]
    weight_in = weight_in.T
    spatial_cols = fetching_spectrum(col_norm, cells[0], inputs, weight_in, table)
    spatial_moved = swap(spatial_cols)

    up, down = neighbours("row")
    left, right = neighbours("col")
    above = lax.ppermute(features, "row", up)
    below = lax.ppermute(features, "row", down)
    target_after, spatial_cols = lax.optimization_barrier((target, spatial_cols))
    pack_down, pack_up, mask_row, kernel_first, kernel_second = prepare(
        target_after, hole_mask, kernel_first, kernel_second
    )
    target_above = lax.ppermute(pack_down, "row", up)
    target_below = lax.ppermute(pack_up, "row", down)
    pre, slopes = tile_forward(above, features, below, kernel_first, kernel_second, ok)
    target_above, pre = lax.optimization_barrier((target_above, pre))
    last, initial, own = edges(above, features, below, target_above, target, mask_row, target_below)
    before = lax.ppermute(last, "col", left)
    after = lax.ppermute(initial, "col", right)
    tile = tile_backward(
        pre, slopes, target_above, target, target_below, mask_row, kernel_first, kernel_second, ok
    )
    pieces = sides(col, tile, before, after, own, kernel_first, kernel_second, ok)
    pieces, spatial_moved = lax.optimization_barrier((pieces, spatial_moved))
    moved = [pieces[0]]
    for step in range(1, col_devices):
        swaps = [(i, i ^ step) for i in range(col_devices)]
        moved.append(lax.ppermute(pieces[step], "col", swaps))
    grad_cols, strip_grad = grad_spectrum(col_norm, col, moved, weight_out, table)
    wide = pltpu.VMEM((strip * half // LANES, width, LANES), jnp.float32)
    grad_rows = vmem_call(
        functools.partial(mix_kernel, row_norm, owned, devices),
        cells,
        spatial_moved,
        swap(grad_cols),
        weight_mix,
        row_table,
        row_back,
        scratch=[wide, wide],
    )[0]
    returned = swap(grad_rows)
    return vmem_call(
        functools.partial(output_kernel, col_norm),
        [jax.ShapeDtypeStruct(inputs.shape, bf16)],
        returned,
        strip_grad,
        weight_in,
        weight_local,
        table_back,
    )[0]


def solution(mesh):
    in_specs = (
        P("row", "col", None),
        P("row", "col", None),
        P("row", "col"),
        P(),
        P(),
        P(("row", "col"), None, None),
        P(),
        P(),
        P(),
        P(),
    )
    out_specs = P(("row", "col"), None, None)
    return jax.shard_map(shards, mesh=mesh, in_specs=in_specs, out_specs=out_specs, check_vma=False)
```

```python
import functools
import math

import jax
import jax.numpy as jnp
import ml_dtypes
import numpy as np
from jax import lax
from jax.experimental import pallas as pl
from jax.experimental.pallas import tpu as pltpu
from jax.sharding import PartitionSpec as P

REACH = 8
NEAR = 4
MIB = 1024 * 1024
LANES = 128


def dot(left, right):
    return jnp.dot(left, right, preferred_element_type=jnp.float32)


def dot_t(left, right):
    return lax.dot_general(left, right, (((1,), (1,)), ((), ())), preferred_element_type=jnp.float32)


def vmem_call(body, shapes, *operands, flops=0, scratch=(), limit=10):
    spec = pl.BlockSpec(memory_space=pltpu.VMEM)
    size = sum(math.prod(a.shape) * a.dtype.itemsize for a in (*operands, *shapes))
    return pl.pallas_call(
        body,
        out_shape=shapes,
        in_specs=[spec] * len(operands),
        out_specs=[spec] * len(shapes),
        scratch_shapes=list(scratch),
        compiler_params=pltpu.CompilerParams(vmem_limit_bytes=limit * MIB),
        cost_estimate=pl.CostEstimate(flops=flops, bytes_accessed=size, transcendentals=0),
    )(*operands)


def in_hbm(array):
    return pltpu.with_memory_space_constraint(array, pltpu.HBM)


def phases(first, second, length):
    angle = (first[:, None] * second[None, :] % length) * (2.0 * math.pi / length)
    return np.cos(angle).astype(ml_dtypes.bfloat16), np.sin(angle).astype(ml_dtypes.bfloat16)


def column_matrix(width, devices):
    half = width // 2
    freq, col = np.arange(half), np.arange(width)
    cos, sin = phases(freq, col, width)
    sin[0] = (2 * (col % 2) - 1).astype(ml_dtypes.bfloat16)
    both = np.stack([cos, -sin]).reshape(2, devices, half // devices, width)
    return np.ascontiguousarray(both.transpose(1, 0, 2, 3)).reshape(width, width)


def row_matrix(height, row_devices, col_devices):
    devices = row_devices * col_devices
    strip = height // devices
    strips = np.arange(devices).reshape(row_devices, col_devices).T.reshape(-1)
    rows = (strips[None, :] * strip + np.arange(strip)[:, None]).reshape(-1)
    cos, sin = phases(np.arange(height), rows, height)
    return np.block([[cos, sin], [-sin, cos]])


def strip_row(signal, r):
    return jnp.concatenate([signal[block, r] for block in range(signal.shape[0])], axis=0)


def grad_kernel(norm, place, *refs):
    *pieces, weight, table, out, strip_out, projected = refs
    tile_cols = pieces[0].shape[1]
    for step, piece in enumerate(pieces):
        block = place[0] ^ step
        strip_out[block] = piece[...]
        rows = [dot_t(piece[r], weight[...]).astype(jnp.bfloat16) for r in range(piece.shape[0])]
        where = pl.ds(pl.multiple_of(block * tile_cols, tile_cols), tile_cols)
        projected[where, :] = jnp.concatenate(rows, axis=1)
    out[...] = (dot(table[...], projected[...]) * norm).astype(jnp.bfloat16)


def grad_spectrum(norm, place, pieces, weight, table):
    strip, tile_cols, channels = pieces[0].shape
    shape = (table.shape[0], strip * weight.shape[0])
    in_vmem = pl.BlockSpec(memory_space=pltpu.VMEM)
    return pl.pallas_call(
        functools.partial(grad_kernel, norm),
        out_shape=[
            jax.ShapeDtypeStruct(shape, jnp.bfloat16),
            jax.ShapeDtypeStruct((len(pieces), strip, tile_cols, channels), jnp.bfloat16),
        ],
        in_specs=[pl.BlockSpec(memory_space=pltpu.SMEM)] + [in_vmem] * (len(pieces) + 2),
        out_specs=[in_vmem] * 2,
        scratch_shapes=[pltpu.VMEM(shape, jnp.bfloat16)],
        compiler_params=pltpu.CompilerParams(vmem_limit_bytes=10 * MIB),
        cost_estimate=pl.CostEstimate(flops=0, bytes_accessed=2 * MIB, transcendentals=0),
    )(place, *pieces, weight, table)


def fetching_spectrum_kernel(norm, signal, weight, table, out, signal_held, weight_held, table_held, sems):
    count = signal.shape[0]
    copies = [pltpu.make_async_copy(weight, weight_held, sems.at[0])]
    copies += [
        pltpu.make_async_copy(signal.at[r], signal_held.at[r], sems.at[1 + r]) for r in range(count)
    ]
    copies.append(pltpu.make_async_copy(table, table_held, sems.at[1 + count]))
    for copy in copies:
        copy.start()
    copies[0].wait()
    rows = []
    for r in range(count):
        copies[1 + r].wait()
        rows.append(dot_t(signal_held[r], weight_held[...]).astype(jnp.bfloat16))
    copies[-1].wait()
    out[...] = (dot(table_held[...], jnp.concatenate(rows, axis=1)) * norm).astype(jnp.bfloat16)


def fetching_spectrum(norm, shape, signal, weight, table):
    operands = (signal, weight, table)
    return pl.pallas_call(
        functools.partial(fetching_spectrum_kernel, norm),
        out_shape=shape,
        in_specs=[pl.BlockSpec(memory_space=pltpu.HBM)] * 3,
        out_specs=pl.BlockSpec(memory_space=pltpu.VMEM),
        scratch_shapes=[pltpu.VMEM(a.shape, a.dtype) for a in operands]
        + [pltpu.SemaphoreType.DMA((signal.shape[0] + 2,))],
        compiler_params=pltpu.CompilerParams(vmem_limit_bytes=12 * MIB),
        cost_estimate=pl.CostEstimate(
            flops=0, bytes_accessed=2 * MIB, transcendentals=0
        ),
    )(*[in_hbm(a) for a in operands])


def row_spectrum(moved, table, wide, norm, owned, devices):
    groups = wide.shape[0]
    for g in range(groups):
        wide[g] = moved[:, g * LANES : (g + 1) * LANES].astype(jnp.float32)
    strip = table.shape[1] // (2 * devices)
    half = moved.shape[1] // strip
    height = table.shape[0] // 2
    real, imag = [], []
    for freq in range(owned):
        parts = []
        for part in range(2):
            where = pl.ds(part * owned + freq, devices, stride=2 * owned)
            block = jnp.concatenate([wide[g, where, :] for g in range(groups)], axis=1)
            parts += [block[:, r * half : (r + 1) * half] for r in range(strip)]
        result = dot(table[...], jnp.concatenate(parts, axis=0).astype(jnp.bfloat16)) * norm
        real.append(result[:height])
        imag.append(result[height:])
    return jnp.concatenate(real, axis=0), jnp.concatenate(imag, axis=0)


def mix_kernel(norm, owned, devices, spatial, grad, mix, table, back_table, out, wide, wide_grad):
    parts = row_spectrum(spatial, table, wide, norm, owned, devices)
    real, imag = [part.astype(jnp.bfloat16) for part in parts]
    grads = row_spectrum(grad, table, wide_grad, norm, owned, devices)
    half = real.shape[1]
    spans = (slice(0, half), slice(half, 2 * half))
    mixed = []
    for span, value in zip(spans, grads):
        pre = dot(real, mix[spans[0], span]) + dot(imag, mix[spans[1], span])
        s = 1.0 / (1.0 + jnp.exp(-pre))
        mixed.append((value * (s * (1.0 + pre * (1.0 - s)))).astype(jnp.bfloat16))
    back = [dot_t(mixed[0], mix[p, spans[0]]) + dot_t(mixed[1], mix[p, spans[1]]) for p in spans]
    back = [part.astype(jnp.bfloat16) for part in back]
    height = table.shape[0] // 2
    strip = height // devices
    groups = wide.shape[0]
    for freq in range(owned):
        cells = slice(freq * height, (freq + 1) * height)
        stacked = jnp.concatenate([back[0][cells], back[1][cells]], axis=0)
        result = dot(back_table[...], stacked) * norm
        for part in range(2):
            rows = [
                result[(part * strip + r) * devices : (part * strip + r + 1) * devices]
                for r in range(strip)
            ]
            where = pl.ds(part * owned + freq, devices, stride=2 * owned)
            values = jnp.concatenate(rows, axis=1)
            for g in range(groups):
                wide[g, where, :] = values[:, g * LANES : (g + 1) * LANES]
    for g in range(groups):
        out[:, g * LANES : (g + 1) * LANES] = wide[g].astype(jnp.bfloat16)


def output_kernel(norm, moved, strip_grad, weight_in, weight_local, table, out):
    spatial = (dot(table[...], moved[...]) * norm).astype(jnp.bfloat16)
    half = weight_in.shape[0]
    for r in range(out.shape[0]):
        total = dot(spatial[:, r * half : (r + 1) * half], weight_in[...])
        total = total + dot_t(strip_row(strip_grad, r), weight_local[...])
        out[r] = total.astype(jnp.bfloat16)


TAIL = 16


def pick(flag, left, right):
    return lax.select(flag, left.astype(jnp.float32), right.astype(jnp.float32))


def odd_row(place):
    return place[1] == 1


def odd_col(place):
    return lax.rem(place[0], 2) == 1


def turned(rows):
    count, columns = rows.shape
    rows = rows.astype(jnp.float32)
    return jnp.concatenate([rows, jnp.zeros((columns - count, columns), jnp.float32)], axis=0).T


def filled(lanes, channels):
    fill = jnp.zeros((lanes.shape[0], channels - lanes.shape[1]), jnp.float32)
    return jnp.concatenate([lanes, fill], axis=1).astype(jnp.bfloat16)


def prepare_kernel(
    place, target, mask, first, second, early, late, mask_row, first_out, second_out, mask_held, sems
):
    tile_rows, tile_cols = mask.shape
    channels = target.shape[2]
    moves = [(mask, mask_held)]
    last = tile_rows - NEAR
    for pack, start in ((early, (1 - place[1]) * last), (late, place[1] * last)):
        moves += [
            (target.at[start + i], pack.at[pl.ds(i * tile_cols, tile_cols)]) for i in range(NEAR)
        ]
    moves += [(first, first_out), (second, second_out)]
    copies = [pltpu.make_async_copy(*move, sems.at[i]) for i, move in enumerate(moves)]
    for copy in copies:
        copy.start()
    copies[0].wait()
    mask_row[0] = filled(turned(mask_held[...]), channels)
    ends = (mask_held[:NEAR], mask_held[last:])
    for pack, (one, other) in ((early, ends), (late, ends[::-1])):
        rows = pick(odd_row(place), one, other)
        rows = jnp.concatenate([rows, jnp.zeros((TAIL - NEAR, tile_cols), jnp.float32)], axis=0)
        pack[NEAR * tile_cols :] = filled(rows, channels)
    for copy in copies[1:]:
        copy.wait()


def prepare(place, target, mask, first, second):
    _, tile_cols, channels = target.shape
    pack = (NEAR * tile_cols + TAIL, channels)
    shapes = [pack, pack, (1, tile_cols, channels), first.shape, second.shape]
    return pl.pallas_call(
        prepare_kernel,
        out_shape=[jax.ShapeDtypeStruct(shape, jnp.bfloat16) for shape in shapes],
        in_specs=[pl.BlockSpec(memory_space=pltpu.SMEM)] + [pl.BlockSpec(memory_space=pltpu.HBM)] * 4,
        out_specs=[pl.BlockSpec(memory_space=pltpu.VMEM)] * len(shapes),
        scratch_shapes=[pltpu.VMEM(mask.shape, mask.dtype), pltpu.SemaphoreType.DMA((2 * NEAR + 3,))],
        compiler_params=pltpu.CompilerParams(vmem_limit_bytes=6 * MIB),
        cost_estimate=pl.CostEstimate(flops=0, bytes_accessed=2 * MIB, transcendentals=0),
    )(place, *[in_hbm(a) for a in (target, mask, first, second)])


def edge_kernel(tile_cols, place, early_pack, late_pack, *refs):
    sources, (early, late, own) = refs[:-3], refs[-3:]
    count = len(sources) // 2
    keep = 2 * REACH
    channels = own.shape[2]
    low, high = odd_row(place), odd_col(place)

    def put_rows(row, tail, head):
        rows = slice(row, row + tail.shape[0])
        last, initial = tail[:, REACH:], head[:, :REACH]
        early[rows] = pick(high, initial, last).astype(jnp.bfloat16)
        late[rows] = pick(high, last, initial).astype(jnp.bfloat16)
        own[rows, :keep] = head.astype(jnp.bfloat16)
        own[rows, keep:] = tail.astype(jnp.bfloat16)

    def put_pack(row, one, other):
        for i in range(NEAR):
            at = i * tile_cols
            tail = pick(low, one[at + tile_cols - keep : at + tile_cols], other[at + tile_cols - keep : at + tile_cols])
            head = pick(low, one[at : at + keep], other[at : at + keep])
            put_rows(row + i, tail[None], head[None])
        mask = turned(pick(low, one[NEAR * tile_cols :, :tile_cols], other[NEAR * tile_cols :, :tile_cols]))
        tail, head = [filled(m, channels)[None] for m in (mask[tile_cols - keep :], mask[:keep])]
        put_rows(row + NEAR, tail, head)

    def put_picked(row, one, other):
        put_rows(row, *[pick(low, sources[one + i * count][...], sources[other + i * count][...]) for i in (0, 1)])

    def put_own(row, index):
        put_rows(row, sources[index][...], sources[index + count][...])

    rows = sources[0].shape[0]
    put_picked(0, 0, 1)
    put_own(rows, 2)
    put_picked(2 * rows, 1, 0)
    put_pack(3 * rows, early_pack, late_pack)
    put_own(3 * rows + NEAR + 1, 3)
    put_own(4 * rows + NEAR + 1, 4)
    put_pack(4 * rows + NEAR + 2, late_pack, early_pack)


def edges(place, early, late, features, target, mask_row, early_pack, late_pack):
    parts = (early, late, features, target, mask_row)
    _, tile_cols, channels = features.shape
    keep = 2 * REACH
    tail = tile_cols // keep - 1

    def specs(at):
        return [pl.BlockSpec((p.shape[0], keep, channels), lambda i, at=at: (0, at, 0)) for p in parts]

    whole = [pl.BlockSpec(early_pack.shape, lambda i: (0, 0))] * 2
    rows = sum(p.shape[0] for p in parts) + 2 * (NEAR + 1)
    shapes = [(rows, columns, channels) for columns in (REACH, REACH, 2 * keep)]
    return pl.pallas_call(
        functools.partial(edge_kernel, tile_cols),
        grid=(1,),
        out_shape=[jax.ShapeDtypeStruct(shape, features.dtype) for shape in shapes],
        in_specs=[pl.BlockSpec(memory_space=pltpu.SMEM)] + whole + specs(tail) + specs(0),
        out_specs=[pl.BlockSpec(shape, lambda i: (0, 0, 0)) for shape in shapes],
        compiler_params=pltpu.CompilerParams(vmem_limit_bytes=8 * MIB),
        cost_estimate=pl.CostEstimate(
            flops=0, bytes_accessed=16 * rows * keep * channels, transcendentals=0
        ),
    )(place, early_pack, late_pack, *parts, *parts)


def put(wide, row, value, stride):
    size, channels = value.shape
    spot = pl.ds(row * stride, size)
    wide[spot, :channels] = pltpu.roll(value, 2, 0).astype(jnp.bfloat16)
    wide[spot, channels : 2 * channels] = value.astype(jnp.bfloat16)
    wide[spot, 2 * channels :] = pltpu.roll(value, size - 2, 0).astype(jnp.bfloat16)


def taps(wide, row, count, stride):
    parts = [wide[pl.ds((row + 2 * a) * stride, count * stride), :] for a in range(3)]
    return jnp.concatenate(parts, axis=1)


def conv(wide, row, count, stride, kernel):
    channels = kernel.shape[-1]
    return dot(taps(wide, row, count, stride), kernel[...].reshape(9 * channels, channels))


def conv_adjoint(wide, row, count, stride, kernel):
    flipped = [kernel[2 - a, 2 - b] for a in range(3) for b in range(3)]
    return dot_t(taps(wide, row, count, stride), jnp.concatenate(flipped, axis=1))


def stacked(piece, rows):
    return jnp.concatenate([piece(row) for row in rows], axis=0)


def first_stages(
    stride, blocks, rows, feature, inside, first, second, wide_even, wide_odd, slopes, use
):
    tall = rows + 2 * REACH
    for row in range(0, tall, NEAR):
        put(wide_even, row, stacked(feature, range(row, row + NEAR)), stride)
    count = blocks[0]
    for row in range(0, tall - 4, count):
        pre = conv(wide_even, row, count, stride, first)
        s = 1.0 / (1.0 + jnp.exp(-pre))
        kept = stacked(inside, range(row + 2, row + 2 + count))
        put(wide_odd, row, pre * s * kept, stride)
        low, high = max(row, NEAR), min(row + count, tall - 4 - NEAR)
        if low < high:
            part = slice((low - row) * stride, (high - row) * stride)
            slope = (s * (1.0 + pre * (1.0 - s)) * kept)[part]
            slopes[pl.ds((low - NEAR) * stride, (high - low) * stride), :] = slope
    count = blocks[1]
    for row in range(0, rows + 2 * NEAR, count):
        use(row, count, conv(wide_odd, row, count, stride, second))


def last_stages(stride, blocks, rows, first, second, wide_even, wide_odd, slopes, use):
    count = blocks[2]
    for row in range(0, rows + 4, count):
        value = conv_adjoint(wide_even, row, count, stride, second)
        value = value * slopes[pl.ds(row * stride, count * stride), :]
        put(wide_odd, row, value, stride)
    count = blocks[3]
    for row in range(0, rows, count):
        use(row, count, conv_adjoint(wide_odd, row, count, stride, first))


def loss_grad(row, count, value, target, hole, inside):
    near = range(row, row + count)
    weight = (1.0 + 2.0 * stacked(hole, near)) * stacked(inside, range(row + NEAR, row + count + NEAR))
    return weight * (value - stacked(target, near))


def part_of(rows, edge, above, own, below):
    def find(row):
        if row < edge:
            return above, row
        if row < edge + rows:
            return own, row - edge
        return below, row - edge - rows

    return find


TILE_BLOCKS = (4, 4, 4, 4)
SIDE_BLOCKS = (10, 8, 12, 8)


def tile_forward_kernel(
    place, early, features, late, first, second, ok, pre, slopes, wide_even, wide_odd
):
    rows, stride, _ = features.shape
    find = part_of(rows, REACH, (early, late), (features,), (late, early))

    def feature(row):
        sources, at = find(row)
        if len(sources) == 1:
            return features[at].astype(jnp.float32)
        return pick(odd_row(place), *[source[at] for source in sources])

    def inside(row):
        return ok[REACH : REACH + stride, row : row + 1]

    def use(row, count, value):
        pre[pl.ds(row * stride, count * stride), :] = value

    first_stages(
        stride, TILE_BLOCKS, rows, feature, inside, first, second, wide_even, wide_odd, slopes, use
    )


def tile_backward_kernel(
    place,
    pre,
    slopes,
    early_pack,
    target,
    late_pack,
    mask_row,
    first,
    second,
    ok,
    out,
    wide_even,
    wide_odd,
):
    rows, stride, channels = target.shape
    packs = (early_pack, late_pack)
    find = part_of(rows, NEAR, packs, (target,), packs[::-1])

    def picked(sources, part):
        return pick(odd_row(place), *[source[part] for source in sources])

    def goal(row):
        sources, at = find(row)
        if len(sources) == 1:
            return target[at].astype(jnp.float32)
        return picked(sources, slice(at * stride, (at + 1) * stride))

    masks = [
        turned(picked(sources, slice(NEAR * stride, None))[:, :stride]) for sources in (packs, packs[::-1])
    ]
    find_mask = part_of(rows, NEAR, (masks[0], 0), (mask_row[0].astype(jnp.float32), 0), (masks[1], 0))

    def hole(row):
        (mask, start), at = find_mask(row)
        return mask[:, start + at : start + at + 1]

    def inside(row):
        return ok[REACH : REACH + stride, row : row + 1]

    count = NEAR
    for row in range(0, rows + 2 * NEAR, count):
        value = pre[pl.ds(row * stride, count * stride), :]
        put(wide_even, row, loss_grad(row, count, value, goal, hole, inside), stride)

    def use(row, count, value):
        out[row : row + count] = value.reshape(count, stride, channels).astype(jnp.bfloat16)

    last_stages(stride, TILE_BLOCKS, rows, first, second, wide_even, wide_odd, slopes, use)


def side_kernel(place, early, late, own, first, second, ok, tile, *refs):
    *pieces, out, wide_even, wide_odd, slopes = refs
    rows, tile_cols, channels = tile.shape
    keep = 2 * REACH
    stride = 2 * (REACH + keep)
    tall = rows + 2 * REACH
    odd = odd_col(place)

    def feature(row):
        before, after = pick(odd, early[row], late[row]), pick(odd, late[row], early[row])
        return jnp.concatenate([before, own[row].astype(jnp.float32), after], axis=0)

    find = part_of(rows, NEAR, tall, tall + NEAR + 1, tall + NEAR + 1 + rows + 1)

    def goal(row):
        start, at = find(row)
        return feature(start + at)

    masks = [feature(row) for row in (tall + NEAR, tall + NEAR + 1 + rows, early.shape[0] - 1)]
    find_mask = part_of(rows, NEAR, (masks[0], 0), (masks[1], 0), (masks[2], 0))

    def hole(row):
        (mask, start), at = find_mask(row)
        return mask[:, start + at : start + at + 1]

    width = ok.shape[0]
    kept = jnp.concatenate([ok[: REACH + keep], ok[width - REACH - keep :]], axis=0)

    def inside(row):
        return kept[:, row : row + 1]

    def use_forward(row, count, value):
        put(wide_even, row, loss_grad(row, count, value, goal, hole, inside), stride)

    first_stages(
        stride, SIDE_BLOCKS, rows, feature, inside, first, second, wide_even, wide_odd, slopes, use_forward
    )
    out[:, REACH : tile_cols - REACH] = tile[:, REACH : tile_cols - REACH]

    def use(row, count, value):
        value = value.reshape(count, stride, channels).astype(jnp.bfloat16)
        out[row : row + count, :REACH] = value[:, REACH : 2 * REACH]
        out[row : row + count, tile_cols - REACH :] = value[:, stride - 2 * REACH : stride - REACH]

    last_stages(stride, SIDE_BLOCKS, rows, first, second, wide_even, wide_odd, slopes, use)
    for step, piece in enumerate(pieces):
        piece[...] = out[pl.ds((place[0] ^ step) * piece.shape[0], piece.shape[0])]


def wide_buffer(rows, stride, channels):
    return pltpu.VMEM((rows * stride, 3 * channels), jnp.bfloat16)


def tile_forward(place, early, features, late, first, second, ok):
    rows, stride, channels = features.shape
    shapes = [
        jax.ShapeDtypeStruct(((rows + h) * stride, channels), jnp.float32) for h in (2 * NEAR, 4)
    ]
    in_vmem = pl.BlockSpec(memory_space=pltpu.VMEM)
    return pl.pallas_call(
        tile_forward_kernel,
        out_shape=shapes,
        in_specs=[pl.BlockSpec(memory_space=pltpu.SMEM)] + [in_vmem] * 6,
        out_specs=[in_vmem] * 2,
        scratch_shapes=[wide_buffer(rows + h, stride, channels) for h in (16, 12)],
        compiler_params=pltpu.CompilerParams(vmem_limit_bytes=18 * MIB),
        cost_estimate=pl.CostEstimate(
            flops=2 * 9 * channels * channels * stride * (2 * rows + 20),
            bytes_accessed=8 * MIB,
            transcendentals=0,
        ),
    )(place, early, features, late, first, second, ok)


def tile_backward(place, pre, slopes, early_pack, target, *operands):
    rows, stride, channels = target.shape
    in_vmem = pl.BlockSpec(memory_space=pltpu.VMEM)
    return pl.pallas_call(
        tile_backward_kernel,
        out_shape=jax.ShapeDtypeStruct(target.shape, jnp.bfloat16),
        in_specs=[pl.BlockSpec(memory_space=pltpu.SMEM)] + [in_vmem] * (4 + len(operands)),
        out_specs=in_vmem,
        scratch_shapes=[wide_buffer(rows + h, stride, channels) for h in (8, 4)],
        compiler_params=pltpu.CompilerParams(vmem_limit_bytes=16 * MIB),
        cost_estimate=pl.CostEstimate(
            flops=2 * 9 * channels * channels * stride * (2 * rows + 4),
            bytes_accessed=8 * MIB,
            transcendentals=0,
        ),
    )(place, pre, slopes, early_pack, target, *operands)


def sides(place, tile, *operands):
    rows, tile_cols, channels = tile.shape
    stride = 6 * REACH
    count = lax.axis_size("col")
    piece = jax.ShapeDtypeStruct((rows // count, tile_cols, channels), jnp.bfloat16)
    in_vmem = pl.BlockSpec(memory_space=pltpu.VMEM)
    return pl.pallas_call(
        side_kernel,
        out_shape=[piece] * count,
        in_specs=[pl.BlockSpec(memory_space=pltpu.SMEM)] + [in_vmem] * (len(operands) + 1),
        out_specs=[in_vmem] * count,
        scratch_shapes=[
            pltpu.VMEM(tile.shape, tile.dtype),
            *[wide_buffer(rows + h, stride, channels) for h in (16, 12)],
            pltpu.VMEM(((rows + 4) * stride, channels), jnp.float32),
        ],
        compiler_params=pltpu.CompilerParams(vmem_limit_bytes=14 * MIB),
        cost_estimate=pl.CostEstimate(
            flops=2 * 9 * channels * channels * stride * (4 * rows + 24),
            bytes_accessed=4 * MIB,
            transcendentals=0,
        ),
    )(place, *operands, tile)


def pairs(axis, start):
    size = lax.axis_size(axis)
    up = [(i, i + 1) for i in range(start, size - 1, 2)]
    return up + [(j, i) for i, j in up]


def shards(
    features,
    target,
    hole_mask,
    kernel_first,
    kernel_second,
    inputs,
    weight_in,
    weight_out,
    weight_local,
    weight_mix,
):
    tile_rows, tile_cols, channels = features.shape
    row_devices, col_devices = lax.axis_size("row"), lax.axis_size("col")
    devices = row_devices * col_devices
    height, width = tile_rows * row_devices, tile_cols * col_devices
    strip, half = inputs.shape[0], weight_in.shape[1]
    owned = width // 2 // devices
    col_norm, row_norm = 1.0 / math.sqrt(width), 1.0 / math.sqrt(height)
    table = column_matrix(width, devices)
    table_back = jnp.asarray(np.ascontiguousarray(table.T))
    table = jnp.asarray(table)
    row_table = row_matrix(height, row_devices, col_devices)
    row_back = jnp.asarray(np.ascontiguousarray(row_table.T))
    row_table = jnp.asarray(row_table)
    bf16 = jnp.bfloat16

    def swap(spectrum):
        return lax.all_to_all(spectrum, ("col", "row"), split_axis=0, concat_axis=0, tiled=True)

    row0, col0 = lax.axis_index("row") * tile_rows, lax.axis_index("col") * tile_cols
    row_ids = row0 - REACH + jnp.arange(tile_rows + 2 * REACH, dtype=jnp.int32)
    col_ids = col0 - REACH + jnp.arange(tile_cols + 2 * REACH, dtype=jnp.int32)
    ok = ((col_ids >= 0) & (col_ids < width))[:, None] & ((row_ids >= 0) & (row_ids < height))[None]
    ok = ok.astype(jnp.float32)
    place = jnp.stack([lax.axis_index("col"), lax.axis_index("row") & 1]).astype(jnp.int32)
    inputs, ok, place = lax.optimization_barrier((inputs, ok, place))

    cells = [jax.ShapeDtypeStruct((width, strip * half), bf16)]
    weight_in = weight_in.T
    spatial_cols = fetching_spectrum(col_norm, cells[0], inputs, weight_in, table)
    spatial_moved = swap(spatial_cols)

    early = lax.ppermute(features, "row", pairs("row", 0))
    late = lax.ppermute(features, "row", pairs("row", 1))
    target_after, spatial_cols = lax.optimization_barrier((target, spatial_cols))
    early_pack, late_pack, mask_row, kernel_first, kernel_second = prepare(
        place, target_after, hole_mask, kernel_first, kernel_second
    )
    early_pack = lax.ppermute(early_pack, "row", pairs("row", 0))
    late_pack = lax.ppermute(late_pack, "row", pairs("row", 1))
    pre, slopes = tile_forward(place, early, features, late, kernel_first, kernel_second, ok)
    early_pack, pre = lax.optimization_barrier((early_pack, pre))
    early_edge, late_edge, own = edges(
        place, early, late, features, target, mask_row, early_pack, late_pack
    )
    early_edge = lax.ppermute(early_edge, "col", pairs("col", 0))
    late_edge = lax.ppermute(late_edge, "col", pairs("col", 1))
    tile = tile_backward(
        place, pre, slopes, early_pack, target, late_pack, mask_row, kernel_first, kernel_second, ok
    )
    pieces = sides(place, tile, early_edge, late_edge, own, kernel_first, kernel_second, ok)
    pieces, spatial_moved = lax.optimization_barrier((pieces, spatial_moved))
    moved = [pieces[0]]
    for step in range(1, col_devices):
        swaps = [(i, i ^ step) for i in range(col_devices)]
        moved.append(lax.ppermute(pieces[step], "col", swaps))
    grad_cols, strip_grad = grad_spectrum(col_norm, place, moved, weight_out, table)
    wide = pltpu.VMEM((strip * half // LANES, width, LANES), jnp.float32)
    grad_rows = vmem_call(
        functools.partial(mix_kernel, row_norm, owned, devices),
        cells,
        spatial_moved,
        swap(grad_cols),
        weight_mix,
        row_table,
        row_back,
        scratch=[wide, wide],
    )[0]
    returned = swap(grad_rows)
    return vmem_call(
        functools.partial(output_kernel, col_norm),
        [jax.ShapeDtypeStruct(inputs.shape, bf16)],
        returned,
        strip_grad,
        weight_in,
        weight_local,
        table_back,
    )[0]


def solution(mesh):
    in_specs = (
        P("row", "col", None),
        P("row", "col", None),
        P("row", "col"),
        P(),
        P(),
        P(("row", "col"), None, None),
        P(),
        P(),
        P(),
        P(),
    )
    out_specs = P(("row", "col"), None, None)
    return jax.shard_map(shards, mesh=mesh, in_specs=in_specs, out_specs=out_specs, check_vma=False)
```

```python
import functools
import math

import jax
import jax.numpy as jnp
import ml_dtypes
import numpy as np
from jax import lax
from jax.experimental import pallas as pl
from jax.experimental.pallas import tpu as pltpu
from jax.sharding import PartitionSpec as P

REACH = 8
NEAR = 4
MIB = 1024 * 1024
LANES = 128


def dot(left, right):
    return jnp.dot(left, right, preferred_element_type=jnp.float32)


def dot_t(left, right):
    return lax.dot_general(left, right, (((1,), (1,)), ((), ())), preferred_element_type=jnp.float32)


def vmem_call(body, shapes, *operands, flops=0, scratch=(), limit=10):
    spec = pl.BlockSpec(memory_space=pltpu.VMEM)
    size = sum(math.prod(a.shape) * a.dtype.itemsize for a in (*operands, *shapes))
    return pl.pallas_call(
        body,
        out_shape=shapes,
        in_specs=[spec] * len(operands),
        out_specs=[spec] * len(shapes),
        scratch_shapes=list(scratch),
        compiler_params=pltpu.CompilerParams(vmem_limit_bytes=limit * MIB),
        cost_estimate=pl.CostEstimate(flops=flops, bytes_accessed=size, transcendentals=0),
    )(*operands)


def in_hbm(array):
    return pltpu.with_memory_space_constraint(array, pltpu.HBM)


def phases(first, second, length):
    angle = (first[:, None] * second[None, :] % length) * (2.0 * math.pi / length)
    return np.cos(angle).astype(ml_dtypes.bfloat16), np.sin(angle).astype(ml_dtypes.bfloat16)


def column_matrix(width, devices):
    half = width // 2
    freq, col = np.arange(half), np.arange(width)
    cos, sin = phases(freq, col, width)
    sin[0] = (2 * (col % 2) - 1).astype(ml_dtypes.bfloat16)
    both = np.stack([cos, -sin]).reshape(2, devices, half // devices, width)
    return np.ascontiguousarray(both.transpose(1, 0, 2, 3)).reshape(width, width)


def row_matrix(height, row_devices, col_devices):
    devices = row_devices * col_devices
    strip = height // devices
    strips = np.arange(devices).reshape(row_devices, col_devices).T.reshape(-1)
    rows = (strips[None, :] * strip + np.arange(strip)[:, None]).reshape(-1)
    cos, sin = phases(np.arange(height), rows, height)
    return np.block([[cos, sin], [-sin, cos]])


def grad_kernel(norm, place, *refs):
    *pieces, weight, table, out, projected = refs
    tile_cols = pieces[0].shape[1]
    for step, piece in enumerate(pieces):
        block = place[0] ^ step
        rows = [dot_t(piece[r], weight[...]).astype(jnp.bfloat16) for r in range(piece.shape[0])]
        where = pl.ds(pl.multiple_of(block * tile_cols, tile_cols), tile_cols)
        projected[where, :] = jnp.concatenate(rows, axis=1)
    out[...] = (dot(table[...], projected[...]) * norm).astype(jnp.bfloat16)


def grad_spectrum(norm, place, pieces, weight, table):
    shape = (table.shape[0], pieces[0].shape[0] * weight.shape[0])
    in_vmem = pl.BlockSpec(memory_space=pltpu.VMEM)
    return pl.pallas_call(
        functools.partial(grad_kernel, norm),
        out_shape=jax.ShapeDtypeStruct(shape, jnp.bfloat16),
        in_specs=[pl.BlockSpec(memory_space=pltpu.SMEM)] + [in_vmem] * (len(pieces) + 2),
        out_specs=in_vmem,
        scratch_shapes=[pltpu.VMEM(shape, jnp.bfloat16)],
        compiler_params=pltpu.CompilerParams(vmem_limit_bytes=10 * MIB),
        cost_estimate=pl.CostEstimate(flops=0, bytes_accessed=2 * MIB, transcendentals=0),
    )(place, *pieces, weight, table)


def fetching_spectrum_kernel(norm, signal, weight, table, out, signal_held, weight_held, table_held, sems):
    count = signal.shape[0]
    copies = [pltpu.make_async_copy(weight, weight_held, sems.at[0])]
    copies += [
        pltpu.make_async_copy(signal.at[r], signal_held.at[r], sems.at[1 + r]) for r in range(count)
    ]
    copies.append(pltpu.make_async_copy(table, table_held, sems.at[1 + count]))
    for copy in copies:
        copy.start()
    copies[0].wait()
    rows = []
    for r in range(count):
        copies[1 + r].wait()
        rows.append(dot_t(signal_held[r], weight_held[...]).astype(jnp.bfloat16))
    copies[-1].wait()
    out[...] = (dot(table_held[...], jnp.concatenate(rows, axis=1)) * norm).astype(jnp.bfloat16)


def fetching_spectrum(norm, shape, signal, weight, table):
    operands = (signal, weight, table)
    return pl.pallas_call(
        functools.partial(fetching_spectrum_kernel, norm),
        out_shape=shape,
        in_specs=[pl.BlockSpec(memory_space=pltpu.HBM)] * 3,
        out_specs=pl.BlockSpec(memory_space=pltpu.VMEM),
        scratch_shapes=[pltpu.VMEM(a.shape, a.dtype) for a in operands]
        + [pltpu.SemaphoreType.DMA((signal.shape[0] + 2,))],
        compiler_params=pltpu.CompilerParams(vmem_limit_bytes=12 * MIB),
        cost_estimate=pl.CostEstimate(
            flops=0, bytes_accessed=2 * MIB, transcendentals=0
        ),
    )(*[in_hbm(a) for a in operands])


def row_spectrum(moved, table, wide, norm, owned, devices):
    groups = wide.shape[0]
    for g in range(groups):
        wide[g] = moved[:, g * LANES : (g + 1) * LANES].astype(jnp.float32)
    strip = table.shape[1] // (2 * devices)
    half = moved.shape[1] // strip
    height = table.shape[0] // 2
    real, imag = [], []
    for freq in range(owned):
        parts = []
        for part in range(2):
            where = pl.ds(part * owned + freq, devices, stride=2 * owned)
            block = jnp.concatenate([wide[g, where, :] for g in range(groups)], axis=1)
            parts += [block[:, r * half : (r + 1) * half] for r in range(strip)]
        result = dot(table[...], jnp.concatenate(parts, axis=0).astype(jnp.bfloat16)) * norm
        real.append(result[:height])
        imag.append(result[height:])
    return jnp.concatenate(real, axis=0), jnp.concatenate(imag, axis=0)


def mix_kernel(norm, owned, devices, spatial, grad, mix, table, back_table, out, wide, wide_grad):
    parts = row_spectrum(spatial, table, wide, norm, owned, devices)
    real, imag = [part.astype(jnp.bfloat16) for part in parts]
    grads = row_spectrum(grad, table, wide_grad, norm, owned, devices)
    half = real.shape[1]
    spans = (slice(0, half), slice(half, 2 * half))
    mixed = []
    for span, value in zip(spans, grads):
        pre = dot(real, mix[spans[0], span]) + dot(imag, mix[spans[1], span])
        s = 1.0 / (1.0 + jnp.exp(-pre))
        mixed.append((value * (s * (1.0 + pre * (1.0 - s)))).astype(jnp.bfloat16))
    back = [dot_t(mixed[0], mix[p, spans[0]]) + dot_t(mixed[1], mix[p, spans[1]]) for p in spans]
    back = [part.astype(jnp.bfloat16) for part in back]
    height = table.shape[0] // 2
    strip = height // devices
    groups = wide.shape[0]
    for freq in range(owned):
        cells = slice(freq * height, (freq + 1) * height)
        stacked = jnp.concatenate([back[0][cells], back[1][cells]], axis=0)
        result = dot(back_table[...], stacked) * norm
        for part in range(2):
            rows = [
                result[(part * strip + r) * devices : (part * strip + r + 1) * devices]
                for r in range(strip)
            ]
            where = pl.ds(part * owned + freq, devices, stride=2 * owned)
            values = jnp.concatenate(rows, axis=1)
            for g in range(groups):
                wide[g, where, :] = values[:, g * LANES : (g + 1) * LANES]
    for g in range(groups):
        out[:, g * LANES : (g + 1) * LANES] = wide[g].astype(jnp.bfloat16)


def output_kernel(norm, place, moved, weight_in, weight_local, table, *refs):
    *pieces, out, spatial = refs
    spatial[...] = (dot(table[...], moved[...]) * norm).astype(jnp.bfloat16)
    half, tile_cols = weight_in.shape[0], pieces[0].shape[1]
    for step, piece in enumerate(pieces):
        start = pl.multiple_of((place[0] ^ step) * tile_cols, tile_cols)
        part = spatial[pl.ds(start, tile_cols), :]
        for r in range(out.shape[0]):
            total = dot(part[:, r * half : (r + 1) * half], weight_in[...])
            total = total + dot_t(piece[r], weight_local[...])
            out[r, pl.ds(start, tile_cols), :] = total.astype(jnp.bfloat16)


def output(norm, place, moved, weight_in, weight_local, table, pieces, shape):
    in_vmem = pl.BlockSpec(memory_space=pltpu.VMEM)
    return pl.pallas_call(
        functools.partial(output_kernel, norm),
        out_shape=jax.ShapeDtypeStruct(shape, jnp.bfloat16),
        in_specs=[pl.BlockSpec(memory_space=pltpu.SMEM)] + [in_vmem] * (len(pieces) + 4),
        out_specs=in_vmem,
        scratch_shapes=[pltpu.VMEM(moved.shape, jnp.bfloat16)],
        compiler_params=pltpu.CompilerParams(vmem_limit_bytes=10 * MIB),
        cost_estimate=pl.CostEstimate(flops=0, bytes_accessed=3 * MIB, transcendentals=0),
    )(place, moved, weight_in, weight_local, table, *pieces)


TAIL = 16


def pick(flag, left, right):
    return lax.select(flag, left, right)


def odd_row(place):
    return place[1] == 1


def odd_col(place):
    return lax.rem(place[0], 2) == 1


def turned(rows):
    count, columns = rows.shape
    rows = rows.astype(jnp.float32)
    return jnp.concatenate([rows, jnp.zeros((columns - count, columns), jnp.float32)], axis=0).T


def filled(lanes, channels):
    fill = jnp.zeros((lanes.shape[0], channels - lanes.shape[1]), jnp.float32)
    return jnp.concatenate([lanes, fill], axis=1).astype(jnp.bfloat16)


def pack_kernel(place, target, mask, early, late, mask_row, mask_held, sems):
    tile_rows, tile_cols = mask.shape
    channels = target.shape[1]
    last = tile_rows - NEAR
    pixels = NEAR * tile_cols
    moves = [(mask, mask_held)]
    for pack, row in ((early, (1 - place[1]) * last), (late, place[1] * last)):
        moves.append((target.at[pl.ds(row * tile_cols, pixels)], pack.at[pl.ds(0, pixels)]))
    copies = [pltpu.make_async_copy(*move, sems.at[i]) for i, move in enumerate(moves)]
    for copy in copies:
        copy.start()
    copies[0].wait()
    mask_row[0] = filled(turned(mask_held[...]), channels)
    ends = (mask_held[:NEAR], mask_held[last:])
    for pack, (one, other) in ((early, ends), (late, ends[::-1])):
        rows = pick(odd_row(place), one.astype(jnp.float32), other.astype(jnp.float32))
        rows = jnp.concatenate([rows, jnp.zeros((TAIL - NEAR, tile_cols), jnp.float32)], axis=0)
        pack[pixels:] = filled(rows, channels)
    for copy in copies[1:]:
        copy.wait()


def target_packs(place, target, mask):
    tile_rows, tile_cols, channels = target.shape
    pack = (NEAR * tile_cols + TAIL, channels)
    hbm = pl.BlockSpec(memory_space=pltpu.HBM)
    shapes = [pack, pack, (1, tile_cols, channels)]
    return pl.pallas_call(
        pack_kernel,
        out_shape=[jax.ShapeDtypeStruct(shape, jnp.bfloat16) for shape in shapes],
        in_specs=[pl.BlockSpec(memory_space=pltpu.SMEM), hbm, hbm],
        out_specs=[pl.BlockSpec(memory_space=pltpu.VMEM)] * len(shapes),
        scratch_shapes=[pltpu.VMEM(mask.shape, mask.dtype), pltpu.SemaphoreType.DMA((3,))],
        compiler_params=pltpu.CompilerParams(vmem_limit_bytes=4 * MIB),
        cost_estimate=pl.CostEstimate(flops=0, bytes_accessed=MIB, transcendentals=0),
    )(place, in_hbm(target.reshape(tile_rows * tile_cols, channels)), in_hbm(mask))


def fetch_kernel(*refs):
    count = len(refs) // 2
    sems = refs[-1]
    copies = [pltpu.make_async_copy(refs[i], refs[count + i], sems.at[i]) for i in range(count)]
    for copy in copies:
        copy.start()
    for copy in copies:
        copy.wait()


def fetch(*arrays):
    return pl.pallas_call(
        fetch_kernel,
        out_shape=[jax.ShapeDtypeStruct(a.shape, a.dtype) for a in arrays],
        in_specs=[pl.BlockSpec(memory_space=pltpu.HBM)] * len(arrays),
        out_specs=[pl.BlockSpec(memory_space=pltpu.VMEM)] * len(arrays),
        scratch_shapes=[pltpu.SemaphoreType.DMA((len(arrays),))],
        compiler_params=pltpu.CompilerParams(vmem_limit_bytes=4 * MIB),
        cost_estimate=pl.CostEstimate(flops=0, bytes_accessed=5 * MIB, transcendentals=0),
    )(*[in_hbm(a) for a in arrays])


def edge_kernel(tile_cols, place, early_pack, late_pack, *refs):
    sources, (early, late, own) = refs[:-3], refs[-3:]
    count = len(sources) // 2
    keep = 2 * REACH
    channels = own.shape[2]
    low, high = odd_row(place), odd_col(place)

    def put_rows(row, tail, head):
        rows = slice(row, row + tail.shape[0])
        last, initial = tail[:, REACH:], head[:, :REACH]
        early[rows] = pick(high, initial, last)
        late[rows] = pick(high, last, initial)
        own[rows, :keep] = head
        own[rows, keep:] = tail

    def put_pack(row, one, other):
        for i in range(NEAR):
            at = i * tile_cols
            tail = pick(low, one[at + tile_cols - keep : at + tile_cols], other[at + tile_cols - keep : at + tile_cols])
            head = pick(low, one[at : at + keep], other[at : at + keep])
            put_rows(row + i, tail[None], head[None])
        mask = turned(pick(low, one[NEAR * tile_cols :, :tile_cols], other[NEAR * tile_cols :, :tile_cols]))
        tail, head = [filled(m, channels)[None] for m in (mask[tile_cols - keep :], mask[:keep])]
        put_rows(row + NEAR, tail, head)

    def put_picked(row, one, other):
        put_rows(row, *[pick(low, sources[one + i * count][...], sources[other + i * count][...]) for i in (0, 1)])

    def put_own(row, index):
        put_rows(row, sources[index][...], sources[index + count][...])

    rows = sources[0].shape[0]
    put_picked(0, 0, 1)
    put_own(rows, 2)
    put_picked(2 * rows, 1, 0)
    put_pack(3 * rows, early_pack, late_pack)
    put_own(3 * rows + NEAR + 1, 3)
    put_own(4 * rows + NEAR + 1, 4)
    put_pack(4 * rows + NEAR + 2, late_pack, early_pack)


def edges(place, early, late, features, target, mask_row, early_pack, late_pack):
    parts = (early, late, features, target, mask_row)
    _, tile_cols, channels = features.shape
    keep = 2 * REACH
    tail = tile_cols // keep - 1

    def specs(at):
        return [pl.BlockSpec((p.shape[0], keep, channels), lambda i, at=at: (0, at, 0)) for p in parts]

    whole = [pl.BlockSpec(early_pack.shape, lambda i: (0, 0))] * 2
    rows = sum(p.shape[0] for p in parts) + 2 * (NEAR + 1)
    shapes = [(rows, columns, channels) for columns in (REACH, REACH, 2 * keep)]
    return pl.pallas_call(
        functools.partial(edge_kernel, tile_cols),
        grid=(1,),
        out_shape=[jax.ShapeDtypeStruct(shape, features.dtype) for shape in shapes],
        in_specs=[pl.BlockSpec(memory_space=pltpu.SMEM)] + whole + specs(tail) + specs(0),
        out_specs=[pl.BlockSpec(shape, lambda i: (0, 0, 0)) for shape in shapes],
        compiler_params=pltpu.CompilerParams(vmem_limit_bytes=8 * MIB),
        cost_estimate=pl.CostEstimate(
            flops=0, bytes_accessed=16 * rows * keep * channels, transcendentals=0
        ),
    )(place, early_pack, late_pack, *parts, *parts)


def put(wide, row, value, stride):
    size, channels = value.shape
    spot = pl.ds(row * stride, size)
    wide[spot, :channels] = pltpu.roll(value, 2, 0).astype(jnp.bfloat16)
    wide[spot, channels : 2 * channels] = value.astype(jnp.bfloat16)
    wide[spot, 2 * channels :] = pltpu.roll(value, size - 2, 0).astype(jnp.bfloat16)


def taps(wide, row, count, stride):
    parts = [wide[pl.ds((row + 2 * a) * stride, count * stride), :] for a in range(3)]
    return jnp.concatenate(parts, axis=1)


def conv(wide, row, count, stride, kernel):
    channels = kernel.shape[-1]
    return dot(taps(wide, row, count, stride), kernel[...].reshape(9 * channels, channels))


def conv_adjoint(wide, row, count, stride, kernel):
    flipped = [kernel[2 - a, 2 - b] for a in range(3) for b in range(3)]
    return dot_t(taps(wide, row, count, stride), jnp.concatenate(flipped, axis=1))


def stacked(piece, rows):
    return jnp.concatenate([piece(row) for row in rows], axis=0)


def first_stages(
    stride, blocks, rows, feature, inside, first, second, wide_even, wide_odd, slopes, use
):
    tall = rows + 2 * REACH
    for row in range(0, tall, NEAR):
        put(wide_even, row, stacked(feature, range(row, row + NEAR)), stride)
    count = blocks[0]
    for row in range(0, tall - 4, count):
        pre = conv(wide_even, row, count, stride, first)
        s = 1.0 / (1.0 + jnp.exp(-pre))
        kept = stacked(inside, range(row + 2, row + 2 + count))
        put(wide_odd, row, pre * s * kept, stride)
        low, high = max(row, NEAR), min(row + count, tall - 4 - NEAR)
        if low < high:
            part = slice((low - row) * stride, (high - row) * stride)
            slope = (s * (1.0 + pre * (1.0 - s)) * kept)[part]
            slopes[pl.ds((low - NEAR) * stride, (high - low) * stride), :] = slope
    count = blocks[1]
    for row in range(0, rows + 2 * NEAR, count):
        use(row, count, conv(wide_odd, row, count, stride, second))


def last_stages(stride, blocks, rows, first, second, wide_even, wide_odd, slopes, use):
    count = blocks[2]
    for row in range(0, rows + 4, count):
        value = conv_adjoint(wide_even, row, count, stride, second)
        value = value * slopes[pl.ds(row * stride, count * stride), :]
        put(wide_odd, row, value, stride)
    count = blocks[3]
    for row in range(0, rows, count):
        use(row, count, conv_adjoint(wide_odd, row, count, stride, first))


def loss_grad(row, count, value, target, hole, inside):
    near = range(row, row + count)
    weight = (1.0 + 2.0 * stacked(hole, near)) * stacked(inside, range(row + NEAR, row + count + NEAR))
    return weight * (value - stacked(target, near))


def part_of(rows, edge, above, own, below):
    def find(row):
        if row < edge:
            return above, row
        if row < edge + rows:
            return own, row - edge
        return below, row - edge - rows

    return find


TILE_BLOCKS = (4, 4, 4, 4)
SIDE_BLOCKS = (10, 8, 12, 8)


def tile_forward_kernel(
    place, early, features, late, first, second, ok, pre, slopes, wide_even, wide_odd
):
    rows, stride, _ = features.shape
    find = part_of(rows, REACH, (early, late), (features,), (late, early))

    def feature(row):
        sources, at = find(row)
        if len(sources) == 1:
            return features[at].astype(jnp.float32)
        return pick(odd_row(place), *[source[at] for source in sources]).astype(jnp.float32)

    def inside(row):
        return ok[REACH : REACH + stride, row : row + 1]

    def use(row, count, value):
        pre[pl.ds(row * stride, count * stride), :] = value

    first_stages(
        stride, TILE_BLOCKS, rows, feature, inside, first, second, wide_even, wide_odd, slopes, use
    )


def tile_backward_kernel(
    place,
    pre,
    slopes,
    early_pack,
    target,
    late_pack,
    mask_row,
    first,
    second,
    ok,
    out,
    wide_even,
    wide_odd,
):
    rows, stride, channels = target.shape
    packs = (early_pack, late_pack)
    find = part_of(rows, NEAR, packs, (target,), packs[::-1])

    def picked(sources, part):
        return pick(odd_row(place), *[source[part] for source in sources]).astype(jnp.float32)

    def goal(row):
        sources, at = find(row)
        if len(sources) == 1:
            return target[at].astype(jnp.float32)
        return picked(sources, slice(at * stride, (at + 1) * stride))

    masks = [
        turned(picked(sources, slice(NEAR * stride, None))[:, :stride]) for sources in (packs, packs[::-1])
    ]
    find_mask = part_of(rows, NEAR, (masks[0], 0), (mask_row[0].astype(jnp.float32), 0), (masks[1], 0))

    def hole(row):
        (mask, start), at = find_mask(row)
        return mask[:, start + at : start + at + 1]

    def inside(row):
        return ok[REACH : REACH + stride, row : row + 1]

    count = NEAR
    for row in range(0, rows + 2 * NEAR, count):
        value = pre[pl.ds(row * stride, count * stride), :]
        put(wide_even, row, loss_grad(row, count, value, goal, hole, inside), stride)

    def use(row, count, value):
        out[row : row + count] = value.reshape(count, stride, channels).astype(jnp.bfloat16)

    last_stages(stride, TILE_BLOCKS, rows, first, second, wide_even, wide_odd, slopes, use)


def side_kernel(place, early, late, own, first, second, ok, tile, *refs):
    *pieces, out, wide_even, wide_odd, slopes = refs
    rows, tile_cols, channels = tile.shape
    keep = 2 * REACH
    stride = 2 * (REACH + keep)
    tall = rows + 2 * REACH
    odd = odd_col(place)

    def feature(row):
        before, after = pick(odd, early[row], late[row]), pick(odd, late[row], early[row])
        parts = [part.astype(jnp.float32) for part in (before, own[row], after)]
        return jnp.concatenate(parts, axis=0)

    find = part_of(rows, NEAR, tall, tall + NEAR + 1, tall + NEAR + 1 + rows + 1)

    def goal(row):
        start, at = find(row)
        return feature(start + at)

    masks = [feature(row) for row in (tall + NEAR, tall + NEAR + 1 + rows, early.shape[0] - 1)]
    find_mask = part_of(rows, NEAR, (masks[0], 0), (masks[1], 0), (masks[2], 0))

    def hole(row):
        (mask, start), at = find_mask(row)
        return mask[:, start + at : start + at + 1]

    width = ok.shape[0]
    kept = jnp.concatenate([ok[: REACH + keep], ok[width - REACH - keep :]], axis=0)

    def inside(row):
        return kept[:, row : row + 1]

    def use_forward(row, count, value):
        put(wide_even, row, loss_grad(row, count, value, goal, hole, inside), stride)

    first_stages(
        stride, SIDE_BLOCKS, rows, feature, inside, first, second, wide_even, wide_odd, slopes, use_forward
    )
    out[:, REACH : tile_cols - REACH] = tile[:, REACH : tile_cols - REACH]

    def use(row, count, value):
        value = value.reshape(count, stride, channels).astype(jnp.bfloat16)
        out[row : row + count, :REACH] = value[:, REACH : 2 * REACH]
        out[row : row + count, tile_cols - REACH :] = value[:, stride - 2 * REACH : stride - REACH]

    last_stages(stride, SIDE_BLOCKS, rows, first, second, wide_even, wide_odd, slopes, use)
    for step, piece in enumerate(pieces):
        piece[...] = out[pl.ds((place[0] ^ step) * piece.shape[0], piece.shape[0])]


def wide_buffer(rows, stride, channels):
    return pltpu.VMEM((rows * stride, 3 * channels), jnp.bfloat16)


def tile_forward(place, early, features, late, first, second, ok):
    rows, stride, channels = features.shape
    shapes = [
        jax.ShapeDtypeStruct(((rows + h) * stride, channels), jnp.float32) for h in (2 * NEAR, 4)
    ]
    in_vmem = pl.BlockSpec(memory_space=pltpu.VMEM)
    return pl.pallas_call(
        tile_forward_kernel,
        out_shape=shapes,
        in_specs=[pl.BlockSpec(memory_space=pltpu.SMEM)] + [in_vmem] * 6,
        out_specs=[in_vmem] * 2,
        scratch_shapes=[wide_buffer(rows + h, stride, channels) for h in (16, 12)],
        compiler_params=pltpu.CompilerParams(vmem_limit_bytes=18 * MIB),
        cost_estimate=pl.CostEstimate(
            flops=2 * 9 * channels * channels * stride * (2 * rows + 20),
            bytes_accessed=8 * MIB,
            transcendentals=0,
        ),
    )(place, early, features, late, first, second, ok)


def tile_backward(place, pre, slopes, early_pack, target, *operands):
    rows, stride, channels = target.shape
    in_vmem = pl.BlockSpec(memory_space=pltpu.VMEM)
    return pl.pallas_call(
        tile_backward_kernel,
        out_shape=jax.ShapeDtypeStruct(target.shape, jnp.bfloat16),
        in_specs=[pl.BlockSpec(memory_space=pltpu.SMEM)] + [in_vmem] * (4 + len(operands)),
        out_specs=in_vmem,
        scratch_shapes=[wide_buffer(rows + h, stride, channels) for h in (8, 4)],
        compiler_params=pltpu.CompilerParams(vmem_limit_bytes=16 * MIB),
        cost_estimate=pl.CostEstimate(
            flops=2 * 9 * channels * channels * stride * (2 * rows + 4),
            bytes_accessed=8 * MIB,
            transcendentals=0,
        ),
    )(place, pre, slopes, early_pack, target, *operands)


def sides(place, tile, *operands):
    rows, tile_cols, channels = tile.shape
    stride = 6 * REACH
    count = lax.axis_size("col")
    piece = jax.ShapeDtypeStruct((rows // count, tile_cols, channels), jnp.bfloat16)
    in_vmem = pl.BlockSpec(memory_space=pltpu.VMEM)
    return pl.pallas_call(
        side_kernel,
        out_shape=[piece] * count,
        in_specs=[pl.BlockSpec(memory_space=pltpu.SMEM)] + [in_vmem] * (len(operands) + 1),
        out_specs=[in_vmem] * count,
        scratch_shapes=[
            pltpu.VMEM(tile.shape, tile.dtype),
            *[wide_buffer(rows + h, stride, channels) for h in (16, 12)],
            pltpu.VMEM(((rows + 4) * stride, channels), jnp.float32),
        ],
        compiler_params=pltpu.CompilerParams(vmem_limit_bytes=14 * MIB),
        cost_estimate=pl.CostEstimate(
            flops=2 * 9 * channels * channels * stride * (4 * rows + 24),
            bytes_accessed=4 * MIB,
            transcendentals=0,
        ),
    )(place, *operands, tile)


def pairs(axis, start):
    size = lax.axis_size(axis)
    up = [(i, i + 1) for i in range(start, size - 1, 2)]
    return up + [(j, i) for i, j in up]


def shards(
    features,
    target,
    hole_mask,
    kernel_first,
    kernel_second,
    inputs,
    weight_in,
    weight_out,
    weight_local,
    weight_mix,
):
    tile_rows, tile_cols, channels = features.shape
    row_devices, col_devices = lax.axis_size("row"), lax.axis_size("col")
    devices = row_devices * col_devices
    height, width = tile_rows * row_devices, tile_cols * col_devices
    strip, half = inputs.shape[0], weight_in.shape[1]
    owned = width // 2 // devices
    col_norm, row_norm = 1.0 / math.sqrt(width), 1.0 / math.sqrt(height)
    table = column_matrix(width, devices)
    table_back = jnp.asarray(np.ascontiguousarray(table.T))
    table = jnp.asarray(table)
    row_table = row_matrix(height, row_devices, col_devices)
    row_back = jnp.asarray(np.ascontiguousarray(row_table.T))
    row_table = jnp.asarray(row_table)
    bf16 = jnp.bfloat16

    def swap(spectrum):
        return lax.all_to_all(spectrum, ("col", "row"), split_axis=0, concat_axis=0, tiled=True)

    row0, col0 = lax.axis_index("row") * tile_rows, lax.axis_index("col") * tile_cols
    row_ids = row0 - REACH + jnp.arange(tile_rows + 2 * REACH, dtype=jnp.int32)
    col_ids = col0 - REACH + jnp.arange(tile_cols + 2 * REACH, dtype=jnp.int32)
    ok = ((col_ids >= 0) & (col_ids < width))[:, None] & ((row_ids >= 0) & (row_ids < height))[None]
    ok = ok.astype(jnp.float32)
    place = jnp.stack([lax.axis_index("col"), lax.axis_index("row") & 1]).astype(jnp.int32)
    early_pack, late_pack, mask_row = target_packs(place, target, hole_mask)
    inputs, ok, early_pack = lax.optimization_barrier((inputs, ok, early_pack))

    cells = [jax.ShapeDtypeStruct((width, strip * half), bf16)]
    weight_in = weight_in.T
    spatial_cols = fetching_spectrum(col_norm, cells[0], inputs, weight_in, table)
    spatial_moved = swap(spatial_cols)

    early = lax.ppermute(features, "row", pairs("row", 0))
    late = lax.ppermute(features, "row", pairs("row", 1))
    kernel_first, spatial_cols = lax.optimization_barrier((kernel_first, spatial_cols))
    kernel_first, kernel_second = fetch(kernel_first, kernel_second)
    early_pack = lax.ppermute(early_pack, "row", pairs("row", 0))
    late_pack = lax.ppermute(late_pack, "row", pairs("row", 1))
    pre, slopes = tile_forward(place, early, features, late, kernel_first, kernel_second, ok)
    early_pack, pre = lax.optimization_barrier((early_pack, pre))
    early_edge, late_edge, own = edges(
        place, early, late, features, target, mask_row, early_pack, late_pack
    )
    early_edge = lax.ppermute(early_edge, "col", pairs("col", 0))
    late_edge = lax.ppermute(late_edge, "col", pairs("col", 1))
    tile = tile_backward(
        place, pre, slopes, early_pack, target, late_pack, mask_row, kernel_first, kernel_second, ok
    )
    pieces = sides(place, tile, early_edge, late_edge, own, kernel_first, kernel_second, ok)
    (*pieces, spatial_moved) = lax.optimization_barrier((*pieces, spatial_moved))
    for step in reversed(range(1, col_devices)):
        swaps = [(i, i ^ step) for i in range(col_devices)]
        pieces[step] = lax.ppermute(pieces[step], "col", swaps)
    grad_cols = grad_spectrum(col_norm, place, pieces, weight_out, table)
    wide = pltpu.VMEM((strip * half // LANES, width, LANES), jnp.float32)
    grad_rows = vmem_call(
        functools.partial(mix_kernel, row_norm, owned, devices),
        cells,
        spatial_moved,
        swap(grad_cols),
        weight_mix,
        row_table,
        row_back,
        scratch=[wide, wide],
    )[0]
    returned = swap(grad_rows)
    return output(
        col_norm, place, returned, weight_in, weight_local, table_back, pieces, inputs.shape
    )


def solution(mesh):
    in_specs = (
        P("row", "col", None),
        P("row", "col", None),
        P("row", "col"),
        P(),
        P(),
        P(("row", "col"), None, None),
        P(),
        P(),
        P(),
        P(),
    )
    out_specs = P(("row", "col"), None, None)
    return jax.shard_map(shards, mesh=mesh, in_specs=in_specs, out_specs=out_specs, check_vma=False)
```

```python
import functools
import math

import jax
import jax.numpy as jnp
import ml_dtypes
import numpy as np
from jax import lax
from jax.experimental import pallas as pl
from jax.experimental.pallas import tpu as pltpu
from jax.sharding import PartitionSpec as P

REACH = 8
NEAR = 4
MIB = 1024 * 1024
LANES = 128


def dot(left, right):
    return jnp.dot(left, right, preferred_element_type=jnp.float32)


def dot_t(left, right):
    return lax.dot_general(left, right, (((1,), (1,)), ((), ())), preferred_element_type=jnp.float32)


def vmem_call(body, shapes, *operands, flops=0, scratch=(), limit=10):
    spec = pl.BlockSpec(memory_space=pltpu.VMEM)
    size = sum(math.prod(a.shape) * a.dtype.itemsize for a in (*operands, *shapes))
    return pl.pallas_call(
        body,
        out_shape=shapes,
        in_specs=[spec] * len(operands),
        out_specs=[spec] * len(shapes),
        scratch_shapes=list(scratch),
        compiler_params=pltpu.CompilerParams(vmem_limit_bytes=limit * MIB),
        cost_estimate=pl.CostEstimate(flops=flops, bytes_accessed=size, transcendentals=0),
    )(*operands)


def in_hbm(array):
    return pltpu.with_memory_space_constraint(array, pltpu.HBM)


def phases(first, second, length):
    angle = (first[:, None] * second[None, :] % length) * (2.0 * math.pi / length)
    return np.cos(angle).astype(ml_dtypes.bfloat16), np.sin(angle).astype(ml_dtypes.bfloat16)


def column_matrix(width, devices):
    half = width // 2
    freq, col = np.arange(half), np.arange(width)
    cos, sin = phases(freq, col, width)
    sin[0] = (2 * (col % 2) - 1).astype(ml_dtypes.bfloat16)
    both = np.stack([cos, -sin]).reshape(2, devices, half // devices, width)
    return np.ascontiguousarray(both.transpose(1, 0, 2, 3)).reshape(width, width)


def row_matrix(height, row_devices, col_devices):
    devices = row_devices * col_devices
    strip = height // devices
    strips = np.arange(devices).reshape(row_devices, col_devices).T.reshape(-1)
    rows = (strips[None, :] * strip + np.arange(strip)[:, None]).reshape(-1)
    cos, sin = phases(np.arange(height), rows, height)
    return np.block([[cos, sin], [-sin, cos]])


def strip_row(signal, r):
    return jnp.concatenate([signal[block, r] for block in range(signal.shape[0])], axis=0)


def grad_kernel(norm, col, low, *refs):
    *pieces, weight, table, out, strip_out, projected = refs
    place = col[0], low[0]
    tile_cols = pieces[0].shape[1]
    for step, piece in enumerate(pieces):
        block = place[0] ^ step
        strip_out[block] = piece[...]
        rows = [dot_t(piece[r], weight[...]).astype(jnp.bfloat16) for r in range(piece.shape[0])]
        where = pl.ds(pl.multiple_of(block * tile_cols, tile_cols), tile_cols)
        projected[where, :] = jnp.concatenate(rows, axis=1)
    out[...] = (dot(table[...], projected[...]) * norm).astype(jnp.bfloat16)


def grad_spectrum(norm, place, pieces, weight, table):
    strip, tile_cols, channels = pieces[0].shape
    shape = (table.shape[0], strip * weight.shape[0])
    in_vmem = pl.BlockSpec(memory_space=pltpu.VMEM)
    return pl.pallas_call(
        functools.partial(grad_kernel, norm),
        out_shape=[
            jax.ShapeDtypeStruct(shape, jnp.bfloat16),
            jax.ShapeDtypeStruct((len(pieces), strip, tile_cols, channels), jnp.bfloat16),
        ],
        in_specs=[pl.BlockSpec(memory_space=pltpu.SMEM)] * 2 + [in_vmem] * (len(pieces) + 2),
        out_specs=[in_vmem] * 2,
        scratch_shapes=[pltpu.VMEM(shape, jnp.bfloat16)],
        compiler_params=pltpu.CompilerParams(vmem_limit_bytes=10 * MIB),
        cost_estimate=pl.CostEstimate(flops=0, bytes_accessed=2 * MIB, transcendentals=0),
    )(*place, *pieces, weight, table)


def fetching_spectrum_kernel(norm, signal, weight, table, out, signal_held, weight_held, table_held, sems):
    count = signal.shape[0]
    copies = [pltpu.make_async_copy(weight, weight_held, sems.at[0])]
    copies += [
        pltpu.make_async_copy(signal.at[r], signal_held.at[r], sems.at[1 + r]) for r in range(count)
    ]
    copies.append(pltpu.make_async_copy(table, table_held, sems.at[1 + count]))
    for copy in copies:
        copy.start()
    copies[0].wait()
    rows = []
    for r in range(count):
        copies[1 + r].wait()
        rows.append(dot_t(signal_held[r], weight_held[...]).astype(jnp.bfloat16))
    copies[-1].wait()
    out[...] = (dot(table_held[...], jnp.concatenate(rows, axis=1)) * norm).astype(jnp.bfloat16)


def fetching_spectrum(norm, shape, signal, weight, table):
    operands = (signal, weight, table)
    return pl.pallas_call(
        functools.partial(fetching_spectrum_kernel, norm),
        out_shape=shape,
        in_specs=[pl.BlockSpec(memory_space=pltpu.HBM)] * 3,
        out_specs=pl.BlockSpec(memory_space=pltpu.VMEM),
        scratch_shapes=[pltpu.VMEM(a.shape, a.dtype) for a in operands]
        + [pltpu.SemaphoreType.DMA((signal.shape[0] + 2,))],
        compiler_params=pltpu.CompilerParams(vmem_limit_bytes=12 * MIB),
        cost_estimate=pl.CostEstimate(
            flops=0, bytes_accessed=2 * MIB, transcendentals=0
        ),
    )(*[in_hbm(a) for a in operands])


def row_spectrum(moved, table, wide, norm, owned, devices):
    groups = wide.shape[0]
    for g in range(groups):
        wide[g] = moved[:, g * LANES : (g + 1) * LANES].astype(jnp.float32)
    strip = table.shape[1] // (2 * devices)
    half = moved.shape[1] // strip
    height = table.shape[0] // 2
    real, imag = [], []
    for freq in range(owned):
        parts = []
        for part in range(2):
            where = pl.ds(part * owned + freq, devices, stride=2 * owned)
            block = jnp.concatenate([wide[g, where, :] for g in range(groups)], axis=1)
            parts += [block[:, r * half : (r + 1) * half] for r in range(strip)]
        result = dot(table[...], jnp.concatenate(parts, axis=0).astype(jnp.bfloat16)) * norm
        real.append(result[:height])
        imag.append(result[height:])
    return jnp.concatenate(real, axis=0), jnp.concatenate(imag, axis=0)


def mix_kernel(norm, owned, devices, spatial, grad, mix, table, back_table, out, wide, wide_grad):
    parts = row_spectrum(spatial, table, wide, norm, owned, devices)
    real, imag = [part.astype(jnp.bfloat16) for part in parts]
    grads = row_spectrum(grad, table, wide_grad, norm, owned, devices)
    half = real.shape[1]
    spans = (slice(0, half), slice(half, 2 * half))
    mixed = []
    for span, value in zip(spans, grads):
        pre = dot(real, mix[spans[0], span]) + dot(imag, mix[spans[1], span])
        s = 1.0 / (1.0 + jnp.exp(-pre))
        mixed.append((value * (s * (1.0 + pre * (1.0 - s)))).astype(jnp.bfloat16))
    back = [dot_t(mixed[0], mix[p, spans[0]]) + dot_t(mixed[1], mix[p, spans[1]]) for p in spans]
    back = [part.astype(jnp.bfloat16) for part in back]
    height = table.shape[0] // 2
    strip = height // devices
    groups = wide.shape[0]
    for freq in range(owned):
        cells = slice(freq * height, (freq + 1) * height)
        stacked = jnp.concatenate([back[0][cells], back[1][cells]], axis=0)
        result = dot(back_table[...], stacked) * norm
        for part in range(2):
            rows = [
                result[(part * strip + r) * devices : (part * strip + r + 1) * devices]
                for r in range(strip)
            ]
            where = pl.ds(part * owned + freq, devices, stride=2 * owned)
            values = jnp.concatenate(rows, axis=1)
            for g in range(groups):
                wide[g, where, :] = values[:, g * LANES : (g + 1) * LANES]
    for g in range(groups):
        out[:, g * LANES : (g + 1) * LANES] = wide[g].astype(jnp.bfloat16)


def output_kernel(norm, moved, strip_grad, weight_in, weight_local, table, out):
    spatial = (dot(table[...], moved[...]) * norm).astype(jnp.bfloat16)
    half = weight_in.shape[0]
    for r in range(out.shape[0]):
        total = dot(spatial[:, r * half : (r + 1) * half], weight_in[...])
        total = total + dot_t(strip_row(strip_grad, r), weight_local[...])
        out[r] = total.astype(jnp.bfloat16)


TAIL = 16


def pick(flag, left, right):
    return lax.select(flag, left, right)


def odd_row(place):
    return place[1] == 1


def odd_col(place):
    return lax.rem(place[0], 2) == 1


def turned(rows):
    count, columns = rows.shape
    rows = rows.astype(jnp.float32)
    return jnp.concatenate([rows, jnp.zeros((columns - count, columns), jnp.float32)], axis=0).T


def filled(lanes, channels):
    fill = jnp.zeros((lanes.shape[0], channels - lanes.shape[1]), jnp.float32)
    return jnp.concatenate([lanes, fill], axis=1).astype(jnp.bfloat16)


def pack_kernel(col, low, target, mask, early, late, mask_row, mask_held, sems):
    place = col[0], low[0]
    tile_rows, tile_cols = mask.shape
    channels = target.shape[1]
    last = tile_rows - NEAR
    pixels = NEAR * tile_cols
    moves = [(mask, mask_held)]
    for pack, row in ((early, (1 - place[1]) * last), (late, place[1] * last)):
        moves.append((target.at[pl.ds(row * tile_cols, pixels)], pack.at[pl.ds(0, pixels)]))
    copies = [pltpu.make_async_copy(*move, sems.at[i]) for i, move in enumerate(moves)]
    for copy in copies:
        copy.start()
    copies[0].wait()
    mask_row[0] = filled(turned(mask_held[...]), channels)
    ends = (mask_held[:NEAR], mask_held[last:])
    for pack, (one, other) in ((early, ends), (late, ends[::-1])):
        rows = pick(odd_row(place), one.astype(jnp.float32), other.astype(jnp.float32))
        rows = jnp.concatenate([rows, jnp.zeros((TAIL - NEAR, tile_cols), jnp.float32)], axis=0)
        pack[pixels:] = filled(rows, channels)
    for copy in copies[1:]:
        copy.wait()


def target_packs(place, target, mask):
    tile_rows, tile_cols, channels = target.shape
    pack = (NEAR * tile_cols + TAIL, channels)
    hbm = pl.BlockSpec(memory_space=pltpu.HBM)
    shapes = [pack, pack, (1, tile_cols, channels)]
    return pl.pallas_call(
        pack_kernel,
        out_shape=[jax.ShapeDtypeStruct(shape, jnp.bfloat16) for shape in shapes],
        in_specs=[pl.BlockSpec(memory_space=pltpu.SMEM)] * 2 + [hbm, hbm],
        out_specs=[pl.BlockSpec(memory_space=pltpu.VMEM)] * len(shapes),
        scratch_shapes=[pltpu.VMEM(mask.shape, mask.dtype), pltpu.SemaphoreType.DMA((3,))],
        compiler_params=pltpu.CompilerParams(vmem_limit_bytes=4 * MIB),
        cost_estimate=pl.CostEstimate(flops=0, bytes_accessed=MIB, transcendentals=0),
    )(*place, in_hbm(target.reshape(tile_rows * tile_cols, channels)), in_hbm(mask))


def fetch_kernel(*refs):
    count = len(refs) // 2
    sems = refs[-1]
    copies = [pltpu.make_async_copy(refs[i], refs[count + i], sems.at[i]) for i in range(count)]
    for copy in copies:
        copy.start()
    for copy in copies:
        copy.wait()


def fetch(*arrays):
    return pl.pallas_call(
        fetch_kernel,
        out_shape=[jax.ShapeDtypeStruct(a.shape, a.dtype) for a in arrays],
        in_specs=[pl.BlockSpec(memory_space=pltpu.HBM)] * len(arrays),
        out_specs=[pl.BlockSpec(memory_space=pltpu.VMEM)] * len(arrays),
        scratch_shapes=[pltpu.SemaphoreType.DMA((len(arrays),))],
        compiler_params=pltpu.CompilerParams(vmem_limit_bytes=4 * MIB),
        cost_estimate=pl.CostEstimate(flops=0, bytes_accessed=5 * MIB, transcendentals=0),
    )(*[in_hbm(a) for a in arrays])


def edge_kernel(tile_cols, col, low, early_pack, late_pack, *refs):
    place = col[0], low[0]
    sources, (early, late, own) = refs[:-3], refs[-3:]
    count = len(sources) // 2
    keep = 2 * REACH
    channels = own.shape[2]
    lower, high = odd_row(place), odd_col(place)

    def put_rows(row, tail, head):
        rows = slice(row, row + tail.shape[0])
        last, initial = tail[:, REACH:], head[:, :REACH]
        early[rows] = pick(high, initial, last)
        late[rows] = pick(high, last, initial)
        own[rows, :keep] = head
        own[rows, keep:] = tail

    def put_pack(row, one, other):
        for i in range(NEAR):
            at = i * tile_cols
            tail = pick(lower, one[at + tile_cols - keep : at + tile_cols], other[at + tile_cols - keep : at + tile_cols])
            head = pick(lower, one[at : at + keep], other[at : at + keep])
            put_rows(row + i, tail[None], head[None])
        mask = turned(pick(lower, one[NEAR * tile_cols :, :tile_cols], other[NEAR * tile_cols :, :tile_cols]))
        tail, head = [filled(m, channels)[None] for m in (mask[tile_cols - keep :], mask[:keep])]
        put_rows(row + NEAR, tail, head)

    def put_picked(row, one, other):
        put_rows(row, *[pick(lower, sources[one + i * count][...], sources[other + i * count][...]) for i in (0, 1)])

    def put_own(row, index):
        put_rows(row, sources[index][...], sources[index + count][...])

    rows = sources[0].shape[0]
    put_picked(0, 0, 1)
    put_own(rows, 2)
    put_picked(2 * rows, 1, 0)
    put_pack(3 * rows, early_pack, late_pack)
    put_own(3 * rows + NEAR + 1, 3)
    put_own(4 * rows + NEAR + 1, 4)
    put_pack(4 * rows + NEAR + 2, late_pack, early_pack)


def edges(place, early, late, features, target, mask_row, early_pack, late_pack):
    parts = (early, late, features, target, mask_row)
    _, tile_cols, channels = features.shape
    keep = 2 * REACH
    tail = tile_cols // keep - 1

    def specs(at):
        return [pl.BlockSpec((p.shape[0], keep, channels), lambda i, at=at: (0, at, 0)) for p in parts]

    whole = [pl.BlockSpec(early_pack.shape, lambda i: (0, 0))] * 2
    rows = sum(p.shape[0] for p in parts) + 2 * (NEAR + 1)
    shapes = [(rows, columns, channels) for columns in (REACH, REACH, 2 * keep)]
    return pl.pallas_call(
        functools.partial(edge_kernel, tile_cols),
        grid=(1,),
        out_shape=[jax.ShapeDtypeStruct(shape, features.dtype) for shape in shapes],
        in_specs=[pl.BlockSpec(memory_space=pltpu.SMEM)] * 2 + whole + specs(tail) + specs(0),
        out_specs=[pl.BlockSpec(shape, lambda i: (0, 0, 0)) for shape in shapes],
        compiler_params=pltpu.CompilerParams(vmem_limit_bytes=8 * MIB),
        cost_estimate=pl.CostEstimate(
            flops=0, bytes_accessed=16 * rows * keep * channels, transcendentals=0
        ),
    )(*place, early_pack, late_pack, *parts, *parts)


def put(wide, row, value, stride):
    size, channels = value.shape
    spot = pl.ds(row * stride, size)
    wide[spot, :channels] = pltpu.roll(value, 2, 0).astype(jnp.bfloat16)
    wide[spot, channels : 2 * channels] = value.astype(jnp.bfloat16)
    wide[spot, 2 * channels :] = pltpu.roll(value, size - 2, 0).astype(jnp.bfloat16)


def taps(wide, row, count, stride):
    parts = [wide[pl.ds((row + 2 * a) * stride, count * stride), :] for a in range(3)]
    return jnp.concatenate(parts, axis=1)


def conv(wide, row, count, stride, kernel):
    channels = kernel.shape[-1]
    return dot(taps(wide, row, count, stride), kernel[...].reshape(9 * channels, channels))


def conv_adjoint(wide, row, count, stride, kernel):
    flipped = [kernel[2 - a, 2 - b] for a in range(3) for b in range(3)]
    return dot_t(taps(wide, row, count, stride), jnp.concatenate(flipped, axis=1))


def stacked(piece, rows):
    return jnp.concatenate([piece(row) for row in rows], axis=0)


def first_stages(
    stride, blocks, rows, feature, inside, first, second, wide_even, wide_odd, slopes, use
):
    tall = rows + 2 * REACH
    for row in range(0, tall, NEAR):
        put(wide_even, row, stacked(feature, range(row, row + NEAR)), stride)
    count = blocks[0]
    for row in range(0, tall - 4, count):
        pre = conv(wide_even, row, count, stride, first)
        s = 1.0 / (1.0 + jnp.exp(-pre))
        kept = stacked(inside, range(row + 2, row + 2 + count))
        put(wide_odd, row, pre * s * kept, stride)
        low, high = max(row, NEAR), min(row + count, tall - 4 - NEAR)
        if low < high:
            part = slice((low - row) * stride, (high - row) * stride)
            slope = (s * (1.0 + pre * (1.0 - s)) * kept)[part]
            slopes[pl.ds((low - NEAR) * stride, (high - low) * stride), :] = slope
    count = blocks[1]
    for row in range(0, rows + 2 * NEAR, count):
        use(row, count, conv(wide_odd, row, count, stride, second))


def last_stages(stride, blocks, rows, first, second, wide_even, wide_odd, slopes, use):
    count = blocks[2]
    for row in range(0, rows + 4, count):
        value = conv_adjoint(wide_even, row, count, stride, second)
        value = value * slopes[pl.ds(row * stride, count * stride), :]
        put(wide_odd, row, value, stride)
    count = blocks[3]
    for row in range(0, rows, count):
        use(row, count, conv_adjoint(wide_odd, row, count, stride, first))


def loss_grad(row, count, value, target, hole, inside):
    near = range(row, row + count)
    weight = (1.0 + 2.0 * stacked(hole, near)) * stacked(inside, range(row + NEAR, row + count + NEAR))
    return weight * (value - stacked(target, near))


def part_of(rows, edge, above, own, below):
    def find(row):
        if row < edge:
            return above, row
        if row < edge + rows:
            return own, row - edge
        return below, row - edge - rows

    return find


TILE_BLOCKS = (4, 4, 4, 4)
SIDE_BLOCKS = (10, 8, 12, 8)


def tile_forward_kernel(
    col, low, early, features, late, first, second, ok, pre, slopes, wide_even, wide_odd
):
    place = col[0], low[0]
    rows, stride, _ = features.shape
    find = part_of(rows, REACH, (early, late), (features,), (late, early))

    def feature(row):
        sources, at = find(row)
        if len(sources) == 1:
            return features[at].astype(jnp.float32)
        return pick(odd_row(place), *[source[at] for source in sources]).astype(jnp.float32)

    def inside(row):
        return ok[REACH : REACH + stride, row : row + 1]

    def use(row, count, value):
        pre[pl.ds(row * stride, count * stride), :] = value

    first_stages(
        stride, TILE_BLOCKS, rows, feature, inside, first, second, wide_even, wide_odd, slopes, use
    )


def tile_backward_kernel(
    col,
    low,
    pre,
    slopes,
    early_pack,
    target,
    late_pack,
    mask_row,
    first,
    second,
    ok,
    out,
    wide_even,
    wide_odd,
):
    place = col[0], low[0]
    rows, stride, channels = target.shape
    packs = (early_pack, late_pack)
    find = part_of(rows, NEAR, packs, (target,), packs[::-1])

    def picked(sources, part):
        return pick(odd_row(place), *[source[part] for source in sources]).astype(jnp.float32)

    def goal(row):
        sources, at = find(row)
        if len(sources) == 1:
            return target[at].astype(jnp.float32)
        return picked(sources, slice(at * stride, (at + 1) * stride))

    masks = [
        turned(picked(sources, slice(NEAR * stride, None))[:, :stride]) for sources in (packs, packs[::-1])
    ]
    find_mask = part_of(rows, NEAR, (masks[0], 0), (mask_row[0].astype(jnp.float32), 0), (masks[1], 0))

    def hole(row):
        (mask, start), at = find_mask(row)
        return mask[:, start + at : start + at + 1]

    def inside(row):
        return ok[REACH : REACH + stride, row : row + 1]

    count = NEAR
    for row in range(0, rows + 2 * NEAR, count):
        value = pre[pl.ds(row * stride, count * stride), :]
        put(wide_even, row, loss_grad(row, count, value, goal, hole, inside), stride)

    def use(row, count, value):
        out[row : row + count] = value.reshape(count, stride, channels).astype(jnp.bfloat16)

    last_stages(stride, TILE_BLOCKS, rows, first, second, wide_even, wide_odd, slopes, use)


def side_kernel(col, low, early, late, own, first, second, ok, tile, *refs):
    *pieces, out, wide_even, wide_odd, slopes = refs
    place = col[0], low[0]
    rows, tile_cols, channels = tile.shape
    keep = 2 * REACH
    stride = 2 * (REACH + keep)
    tall = rows + 2 * REACH
    odd = odd_col(place)

    def feature(row):
        before, after = pick(odd, early[row], late[row]), pick(odd, late[row], early[row])
        parts = [part.astype(jnp.float32) for part in (before, own[row], after)]
        return jnp.concatenate(parts, axis=0)

    find = part_of(rows, NEAR, tall, tall + NEAR + 1, tall + NEAR + 1 + rows + 1)

    def goal(row):
        start, at = find(row)
        return feature(start + at)

    masks = [feature(row) for row in (tall + NEAR, tall + NEAR + 1 + rows, early.shape[0] - 1)]
    find_mask = part_of(rows, NEAR, (masks[0], 0), (masks[1], 0), (masks[2], 0))

    def hole(row):
        (mask, start), at = find_mask(row)
        return mask[:, start + at : start + at + 1]

    width = ok.shape[0]
    kept = jnp.concatenate([ok[: REACH + keep], ok[width - REACH - keep :]], axis=0)

    def inside(row):
        return kept[:, row : row + 1]

    def use_forward(row, count, value):
        put(wide_even, row, loss_grad(row, count, value, goal, hole, inside), stride)

    first_stages(
        stride, SIDE_BLOCKS, rows, feature, inside, first, second, wide_even, wide_odd, slopes, use_forward
    )
    out[:, REACH : tile_cols - REACH] = tile[:, REACH : tile_cols - REACH]

    def use(row, count, value):
        value = value.reshape(count, stride, channels).astype(jnp.bfloat16)
        out[row : row + count, :REACH] = value[:, REACH : 2 * REACH]
        out[row : row + count, tile_cols - REACH :] = value[:, stride - 2 * REACH : stride - REACH]

    last_stages(stride, SIDE_BLOCKS, rows, first, second, wide_even, wide_odd, slopes, use)
    for step, piece in enumerate(pieces):
        piece[...] = out[pl.ds((place[0] ^ step) * piece.shape[0], piece.shape[0])]


def wide_buffer(rows, stride, channels):
    return pltpu.VMEM((rows * stride, 3 * channels), jnp.bfloat16)


def tile_forward(place, early, features, late, first, second, ok):
    rows, stride, channels = features.shape
    shapes = [
        jax.ShapeDtypeStruct(((rows + h) * stride, channels), jnp.float32) for h in (2 * NEAR, 4)
    ]
    in_vmem = pl.BlockSpec(memory_space=pltpu.VMEM)
    return pl.pallas_call(
        tile_forward_kernel,
        out_shape=shapes,
        in_specs=[pl.BlockSpec(memory_space=pltpu.SMEM)] * 2 + [in_vmem] * 6,
        out_specs=[in_vmem] * 2,
        scratch_shapes=[wide_buffer(rows + h, stride, channels) for h in (16, 12)],
        compiler_params=pltpu.CompilerParams(vmem_limit_bytes=18 * MIB),
        cost_estimate=pl.CostEstimate(
            flops=2 * 9 * channels * channels * stride * (2 * rows + 20),
            bytes_accessed=8 * MIB,
            transcendentals=0,
        ),
    )(*place, early, features, late, first, second, ok)


def tile_backward(place, pre, slopes, early_pack, target, *operands):
    rows, stride, channels = target.shape
    in_vmem = pl.BlockSpec(memory_space=pltpu.VMEM)
    return pl.pallas_call(
        tile_backward_kernel,
        out_shape=jax.ShapeDtypeStruct(target.shape, jnp.bfloat16),
        in_specs=[pl.BlockSpec(memory_space=pltpu.SMEM)] * 2 + [in_vmem] * (4 + len(operands)),
        out_specs=in_vmem,
        scratch_shapes=[wide_buffer(rows + h, stride, channels) for h in (8, 4)],
        compiler_params=pltpu.CompilerParams(vmem_limit_bytes=16 * MIB),
        cost_estimate=pl.CostEstimate(
            flops=2 * 9 * channels * channels * stride * (2 * rows + 4),
            bytes_accessed=8 * MIB,
            transcendentals=0,
        ),
    )(*place, pre, slopes, early_pack, target, *operands)


def sides(place, tile, *operands):
    rows, tile_cols, channels = tile.shape
    stride = 6 * REACH
    count = lax.axis_size("col")
    piece = jax.ShapeDtypeStruct((rows // count, tile_cols, channels), jnp.bfloat16)
    in_vmem = pl.BlockSpec(memory_space=pltpu.VMEM)
    return pl.pallas_call(
        side_kernel,
        out_shape=[piece] * count,
        in_specs=[pl.BlockSpec(memory_space=pltpu.SMEM)] * 2 + [in_vmem] * (len(operands) + 1),
        out_specs=[in_vmem] * count,
        scratch_shapes=[
            pltpu.VMEM(tile.shape, tile.dtype),
            *[wide_buffer(rows + h, stride, channels) for h in (16, 12)],
            pltpu.VMEM(((rows + 4) * stride, channels), jnp.float32),
        ],
        compiler_params=pltpu.CompilerParams(vmem_limit_bytes=14 * MIB),
        cost_estimate=pl.CostEstimate(
            flops=2 * 9 * channels * channels * stride * (4 * rows + 24),
            bytes_accessed=4 * MIB,
            transcendentals=0,
        ),
    )(*place, *operands, tile)


def pairs(axis, start):
    size = lax.axis_size(axis)
    up = [(i, i + 1) for i in range(start, size - 1, 2)]
    return up + [(j, i) for i, j in up]


def shards(
    features,
    target,
    hole_mask,
    kernel_first,
    kernel_second,
    inputs,
    weight_in,
    weight_out,
    weight_local,
    weight_mix,
):
    tile_rows, tile_cols, channels = features.shape
    row_devices, col_devices = lax.axis_size("row"), lax.axis_size("col")
    devices = row_devices * col_devices
    height, width = tile_rows * row_devices, tile_cols * col_devices
    strip, half = inputs.shape[0], weight_in.shape[1]
    owned = width // 2 // devices
    col_norm, row_norm = 1.0 / math.sqrt(width), 1.0 / math.sqrt(height)
    table = column_matrix(width, devices)
    table_back = jnp.asarray(np.ascontiguousarray(table.T))
    table = jnp.asarray(table)
    row_table = row_matrix(height, row_devices, col_devices)
    row_back = jnp.asarray(np.ascontiguousarray(row_table.T))
    row_table = jnp.asarray(row_table)
    bf16 = jnp.bfloat16

    def swap(spectrum):
        return lax.all_to_all(spectrum, ("col", "row"), split_axis=0, concat_axis=0, tiled=True)

    row0, col0 = lax.axis_index("row") * tile_rows, lax.axis_index("col") * tile_cols
    row_ids = row0 - REACH + jnp.arange(tile_rows + 2 * REACH, dtype=jnp.int32)
    col_ids = col0 - REACH + jnp.arange(tile_cols + 2 * REACH, dtype=jnp.int32)
    ok = ((col_ids >= 0) & (col_ids < width))[:, None] & ((row_ids >= 0) & (row_ids < height))[None]
    ok = ok.astype(jnp.float32)
    place = tuple(jnp.full((1,), i, jnp.int32) for i in (lax.axis_index("col"), lax.axis_index("row") & 1))
    early_pack, late_pack, mask_row = target_packs(place, target, hole_mask)
    inputs, ok, early_pack = lax.optimization_barrier((inputs, ok, early_pack))

    cells = [jax.ShapeDtypeStruct((width, strip * half), bf16)]
    weight_in = weight_in.T
    spatial_cols = fetching_spectrum(col_norm, cells[0], inputs, weight_in, table)
    spatial_moved = swap(spatial_cols)

    early = lax.ppermute(features, "row", pairs("row", 0))
    late = lax.ppermute(features, "row", pairs("row", 1))
    kernel_first, spatial_cols = lax.optimization_barrier((kernel_first, spatial_cols))
    kernel_first, kernel_second = fetch(kernel_first, kernel_second)
    early_pack = lax.ppermute(early_pack, "row", pairs("row", 0))
    late_pack = lax.ppermute(late_pack, "row", pairs("row", 1))
    pre, slopes = tile_forward(place, early, features, late, kernel_first, kernel_second, ok)
    early_pack, pre = lax.optimization_barrier((early_pack, pre))
    early_edge, late_edge, own = edges(
        place, early, late, features, target, mask_row, early_pack, late_pack
    )
    early_edge = lax.ppermute(early_edge, "col", pairs("col", 0))
    late_edge = lax.ppermute(late_edge, "col", pairs("col", 1))
    tile = tile_backward(
        place, pre, slopes, early_pack, target, late_pack, mask_row, kernel_first, kernel_second, ok
    )
    pieces = sides(place, tile, early_edge, late_edge, own, kernel_first, kernel_second, ok)
    (*pieces, spatial_moved) = lax.optimization_barrier((*pieces, spatial_moved))
    for step in reversed(range(1, col_devices)):
        swaps = [(i, i ^ step) for i in range(col_devices)]
        pieces[step] = lax.ppermute(pieces[step], "col", swaps)
    grad_cols, strip_grad = grad_spectrum(col_norm, place, pieces, weight_out, table)
    wide = pltpu.VMEM((strip * half // LANES, width, LANES), jnp.float32)
    grad_rows = vmem_call(
        functools.partial(mix_kernel, row_norm, owned, devices),
        cells,
        spatial_moved,
        swap(grad_cols),
        weight_mix,
        row_table,
        row_back,
        scratch=[wide, wide],
    )[0]
    returned = swap(grad_rows)
    return vmem_call(
        functools.partial(output_kernel, col_norm),
        [jax.ShapeDtypeStruct(inputs.shape, bf16)],
        returned,
        strip_grad,
        weight_in,
        weight_local,
        table_back,
    )[0]


def solution(mesh):
    in_specs = (
        P("row", "col", None),
        P("row", "col", None),
        P("row", "col"),
        P(),
        P(),
        P(("row", "col"), None, None),
        P(),
        P(),
        P(),
        P(),
    )
    out_specs = P(("row", "col"), None, None)
    return jax.shard_map(shards, mesh=mesh, in_specs=in_specs, out_specs=out_specs, check_vma=False)
```

```python
import functools
import math

import jax
import jax.numpy as jnp
import ml_dtypes
import numpy as np
from jax import lax
from jax.experimental import pallas as pl
from jax.experimental.pallas import tpu as pltpu
from jax.sharding import PartitionSpec as P

REACH = 8
NEAR = 4
MIB = 1024 * 1024
LANES = 128


def dot(left, right):
    return jnp.dot(left, right, preferred_element_type=jnp.float32)


def dot_t(left, right):
    return lax.dot_general(left, right, (((1,), (1,)), ((), ())), preferred_element_type=jnp.float32)


def vmem_call(body, shapes, *operands, flops=0, scratch=(), limit=10):
    spec = pl.BlockSpec(memory_space=pltpu.VMEM)
    size = sum(math.prod(a.shape) * a.dtype.itemsize for a in (*operands, *shapes))
    return pl.pallas_call(
        body,
        out_shape=shapes,
        in_specs=[spec] * len(operands),
        out_specs=[spec] * len(shapes),
        scratch_shapes=list(scratch),
        compiler_params=pltpu.CompilerParams(vmem_limit_bytes=limit * MIB),
        cost_estimate=pl.CostEstimate(flops=flops, bytes_accessed=size, transcendentals=0),
    )(*operands)


def in_hbm(array):
    return pltpu.with_memory_space_constraint(array, pltpu.HBM)


def phases(first, second, length):
    angle = (first[:, None] * second[None, :] % length) * (2.0 * math.pi / length)
    return np.cos(angle).astype(ml_dtypes.bfloat16), np.sin(angle).astype(ml_dtypes.bfloat16)


def column_matrix(width, devices):
    half = width // 2
    freq, col = np.arange(half), np.arange(width)
    cos, sin = phases(freq, col, width)
    sin[0] = (2 * (col % 2) - 1).astype(ml_dtypes.bfloat16)
    both = np.stack([cos, -sin]).reshape(2, devices, half // devices, width)
    return np.ascontiguousarray(both.transpose(1, 0, 2, 3)).reshape(width, width)


def row_matrix(height, row_devices, col_devices):
    devices = row_devices * col_devices
    strip = height // devices
    strips = np.arange(devices).reshape(row_devices, col_devices).T.reshape(-1)
    rows = (strips[None, :] * strip + np.arange(strip)[:, None]).reshape(-1)
    cos, sin = phases(np.arange(height), rows, height)
    return np.block([[cos, sin], [-sin, cos]])


def strip_row(signal, r):
    return jnp.concatenate([signal[block, r] for block in range(signal.shape[0])], axis=0)


def grad_kernel(norm, col, low, *refs):
    *pieces, weight, table, out, strip_out, projected = refs
    count = len(pieces) // 2
    _, strip, tile_cols, _ = strip_out.shape
    for step, (inner, outer) in enumerate(zip(pieces[:count], pieces[count:])):
        block = col[0] ^ step
        strip_out[block, :, REACH : tile_cols - REACH] = inner[...]
        strip_out[block, :, :REACH] = outer[:, :REACH]
        strip_out[block, :, tile_cols - REACH :] = outer[:, REACH:]
        rows = [dot_t(strip_out[block, r], weight[...]).astype(jnp.bfloat16) for r in range(strip)]
        where = pl.ds(pl.multiple_of(block * tile_cols, tile_cols), tile_cols)
        projected[where, :] = jnp.concatenate(rows, axis=1)
    out[...] = (dot(table[...], projected[...]) * norm).astype(jnp.bfloat16)


def grad_spectrum(norm, place, inner, outer, weight, table):
    strip, columns, channels = inner[0].shape
    shape = (table.shape[0], strip * weight.shape[0])
    in_vmem = pl.BlockSpec(memory_space=pltpu.VMEM)
    return pl.pallas_call(
        functools.partial(grad_kernel, norm),
        out_shape=[
            jax.ShapeDtypeStruct(shape, jnp.bfloat16),
            jax.ShapeDtypeStruct((len(inner), strip, columns + 2 * REACH, channels), jnp.bfloat16),
        ],
        in_specs=[pl.BlockSpec(memory_space=pltpu.SMEM)] * 2 + [in_vmem] * (2 * len(inner) + 2),
        out_specs=[in_vmem] * 2,
        scratch_shapes=[pltpu.VMEM(shape, jnp.bfloat16)],
        compiler_params=pltpu.CompilerParams(vmem_limit_bytes=10 * MIB),
        cost_estimate=pl.CostEstimate(flops=0, bytes_accessed=2 * MIB, transcendentals=0),
    )(*place, *inner, *outer, weight, table)


def fetching_spectrum_kernel(norm, signal, weight, table, out, signal_held, weight_held, table_held, sems):
    count = signal.shape[0]
    copies = [pltpu.make_async_copy(weight, weight_held, sems.at[0])]
    copies += [
        pltpu.make_async_copy(signal.at[r], signal_held.at[r], sems.at[1 + r]) for r in range(count)
    ]
    copies.append(pltpu.make_async_copy(table, table_held, sems.at[1 + count]))
    for copy in copies:
        copy.start()
    copies[0].wait()
    rows = []
    for r in range(count):
        copies[1 + r].wait()
        rows.append(dot_t(signal_held[r], weight_held[...]).astype(jnp.bfloat16))
    copies[-1].wait()
    out[...] = (dot(table_held[...], jnp.concatenate(rows, axis=1)) * norm).astype(jnp.bfloat16)


def fetching_spectrum(norm, shape, signal, weight, table):
    operands = (signal, weight, table)
    return pl.pallas_call(
        functools.partial(fetching_spectrum_kernel, norm),
        out_shape=shape,
        in_specs=[pl.BlockSpec(memory_space=pltpu.HBM)] * 3,
        out_specs=pl.BlockSpec(memory_space=pltpu.VMEM),
        scratch_shapes=[pltpu.VMEM(a.shape, a.dtype) for a in operands]
        + [pltpu.SemaphoreType.DMA((signal.shape[0] + 2,))],
        compiler_params=pltpu.CompilerParams(vmem_limit_bytes=12 * MIB),
        cost_estimate=pl.CostEstimate(
            flops=0, bytes_accessed=2 * MIB, transcendentals=0
        ),
    )(*[in_hbm(a) for a in operands])


def row_spectrum(moved, table, wide, norm, owned, devices):
    groups = wide.shape[0]
    for g in range(groups):
        wide[g] = moved[:, g * LANES : (g + 1) * LANES].astype(jnp.float32)
    strip = table.shape[1] // (2 * devices)
    half = moved.shape[1] // strip
    height = table.shape[0] // 2
    real, imag = [], []
    for freq in range(owned):
        parts = []
        for part in range(2):
            where = pl.ds(part * owned + freq, devices, stride=2 * owned)
            block = jnp.concatenate([wide[g, where, :] for g in range(groups)], axis=1)
            parts += [block[:, r * half : (r + 1) * half] for r in range(strip)]
        result = dot(table[...], jnp.concatenate(parts, axis=0).astype(jnp.bfloat16)) * norm
        real.append(result[:height])
        imag.append(result[height:])
    return jnp.concatenate(real, axis=0), jnp.concatenate(imag, axis=0)


def slope_kernel(norm, owned, devices, moved, mix, table, out, wide):
    parts = row_spectrum(moved, table, wide, norm, owned, devices)
    real, imag = [part.astype(jnp.bfloat16) for part in parts]
    half = real.shape[1]
    spans = (slice(0, half), slice(half, 2 * half))
    for part, span in enumerate(spans):
        pre = dot(real, mix[spans[0], span]) + dot(imag, mix[spans[1], span])
        s = 1.0 / (1.0 + jnp.exp(-pre))
        out[part] = s * (1.0 + pre * (1.0 - s))


def mix_kernel(norm, owned, devices, moved, slope, mix, table, back_table, out, wide):
    grads = row_spectrum(moved, table, wide, norm, owned, devices)
    half = grads[0].shape[1]
    spans = (slice(0, half), slice(half, 2 * half))
    mixed = [(grad * slope[part]).astype(jnp.bfloat16) for part, grad in enumerate(grads)]
    back = [dot_t(mixed[0], mix[p, spans[0]]) + dot_t(mixed[1], mix[p, spans[1]]) for p in spans]
    back = [part.astype(jnp.bfloat16) for part in back]
    height = table.shape[0] // 2
    strip = height // devices
    groups = wide.shape[0]
    for freq in range(owned):
        cells = slice(freq * height, (freq + 1) * height)
        stacked = jnp.concatenate([back[0][cells], back[1][cells]], axis=0)
        result = dot(back_table[...], stacked) * norm
        for part in range(2):
            rows = [
                result[(part * strip + r) * devices : (part * strip + r + 1) * devices]
                for r in range(strip)
            ]
            where = pl.ds(part * owned + freq, devices, stride=2 * owned)
            values = jnp.concatenate(rows, axis=1)
            for g in range(groups):
                wide[g, where, :] = values[:, g * LANES : (g + 1) * LANES]
    for g in range(groups):
        out[:, g * LANES : (g + 1) * LANES] = wide[g].astype(jnp.bfloat16)


def output_kernel(norm, moved, strip_grad, weight_in, weight_local, table, out):
    spatial = (dot(table[...], moved[...]) * norm).astype(jnp.bfloat16)
    half = weight_in.shape[0]
    for r in range(out.shape[0]):
        total = dot(spatial[:, r * half : (r + 1) * half], weight_in[...])
        total = total + dot_t(strip_row(strip_grad, r), weight_local[...])
        out[r] = total.astype(jnp.bfloat16)


TAIL = 16


def pick(flag, left, right):
    return lax.select(flag, left, right)


def odd_row(place):
    return place[1] == 1


def odd_col(place):
    return lax.rem(place[0], 2) == 1


def turned(rows):
    count, columns = rows.shape
    rows = rows.astype(jnp.float32)
    return jnp.concatenate([rows, jnp.zeros((columns - count, columns), jnp.float32)], axis=0).T


def filled(lanes, channels):
    fill = jnp.zeros((lanes.shape[0], channels - lanes.shape[1]), jnp.float32)
    return jnp.concatenate([lanes, fill], axis=1).astype(jnp.bfloat16)


def pack_kernel(col, low, target, mask, early, late, mask_row, mask_held, sems):
    place = col[0], low[0]
    tile_rows, tile_cols = mask.shape
    channels = target.shape[1]
    last = tile_rows - NEAR
    pixels = NEAR * tile_cols
    moves = [(mask, mask_held)]
    for pack, row in ((early, (1 - place[1]) * last), (late, place[1] * last)):
        moves.append((target.at[pl.ds(row * tile_cols, pixels)], pack.at[pl.ds(0, pixels)]))
    copies = [pltpu.make_async_copy(*move, sems.at[i]) for i, move in enumerate(moves)]
    for copy in copies:
        copy.start()
    copies[0].wait()
    mask_row[0] = filled(turned(mask_held[...]), channels)
    ends = (mask_held[:NEAR], mask_held[last:])
    for pack, (one, other) in ((early, ends), (late, ends[::-1])):
        rows = pick(odd_row(place), one.astype(jnp.float32), other.astype(jnp.float32))
        rows = jnp.concatenate([rows, jnp.zeros((TAIL - NEAR, tile_cols), jnp.float32)], axis=0)
        pack[pixels:] = filled(rows, channels)
    for copy in copies[1:]:
        copy.wait()


def target_packs(place, target, mask):
    tile_rows, tile_cols, channels = target.shape
    pack = (NEAR * tile_cols + TAIL, channels)
    hbm = pl.BlockSpec(memory_space=pltpu.HBM)
    shapes = [pack, pack, (1, tile_cols, channels)]
    return pl.pallas_call(
        pack_kernel,
        out_shape=[jax.ShapeDtypeStruct(shape, jnp.bfloat16) for shape in shapes],
        in_specs=[pl.BlockSpec(memory_space=pltpu.SMEM)] * 2 + [hbm, hbm],
        out_specs=[pl.BlockSpec(memory_space=pltpu.VMEM)] * len(shapes),
        scratch_shapes=[pltpu.VMEM(mask.shape, mask.dtype), pltpu.SemaphoreType.DMA((3,))],
        compiler_params=pltpu.CompilerParams(vmem_limit_bytes=4 * MIB),
        cost_estimate=pl.CostEstimate(flops=0, bytes_accessed=MIB, transcendentals=0),
    )(*place, in_hbm(target.reshape(tile_rows * tile_cols, channels)), in_hbm(mask))


def fetch_kernel(*refs):
    count = len(refs) // 2
    sems = refs[-1]
    copies = [pltpu.make_async_copy(refs[i], refs[count + i], sems.at[i]) for i in range(count)]
    for copy in copies:
        copy.start()
    for copy in copies:
        copy.wait()


def fetch(*arrays):
    return pl.pallas_call(
        fetch_kernel,
        out_shape=[jax.ShapeDtypeStruct(a.shape, a.dtype) for a in arrays],
        in_specs=[pl.BlockSpec(memory_space=pltpu.HBM)] * len(arrays),
        out_specs=[pl.BlockSpec(memory_space=pltpu.VMEM)] * len(arrays),
        scratch_shapes=[pltpu.SemaphoreType.DMA((len(arrays),))],
        compiler_params=pltpu.CompilerParams(vmem_limit_bytes=4 * MIB),
        cost_estimate=pl.CostEstimate(flops=0, bytes_accessed=5 * MIB, transcendentals=0),
    )(*[in_hbm(a) for a in arrays])


def edge_kernel(tile_cols, col, low, early_pack, late_pack, *refs):
    place = col[0], low[0]
    sources, (early, late, own) = refs[:-3], refs[-3:]
    count = len(sources) // 2
    keep = 2 * REACH
    channels = own.shape[2]
    lower, high = odd_row(place), odd_col(place)

    def put_rows(row, tail, head):
        rows = slice(row, row + tail.shape[0])
        last, initial = tail[:, REACH:], head[:, :REACH]
        early[rows] = pick(high, initial, last)
        late[rows] = pick(high, last, initial)
        own[rows, :keep] = head
        own[rows, keep:] = tail

    def put_pack(row, one, other):
        for i in range(NEAR):
            at = i * tile_cols
            tail = pick(lower, one[at + tile_cols - keep : at + tile_cols], other[at + tile_cols - keep : at + tile_cols])
            head = pick(lower, one[at : at + keep], other[at : at + keep])
            put_rows(row + i, tail[None], head[None])
        mask = turned(pick(lower, one[NEAR * tile_cols :, :tile_cols], other[NEAR * tile_cols :, :tile_cols]))
        tail, head = [filled(m, channels)[None] for m in (mask[tile_cols - keep :], mask[:keep])]
        put_rows(row + NEAR, tail, head)

    def put_picked(row, one, other):
        put_rows(row, *[pick(lower, sources[one + i * count][...], sources[other + i * count][...]) for i in (0, 1)])

    def put_own(row, index):
        put_rows(row, sources[index][...], sources[index + count][...])

    rows = sources[0].shape[0]
    put_picked(0, 0, 1)
    put_own(rows, 2)
    put_picked(2 * rows, 1, 0)
    put_pack(3 * rows, early_pack, late_pack)
    put_own(3 * rows + NEAR + 1, 3)
    put_own(4 * rows + NEAR + 1, 4)
    put_pack(4 * rows + NEAR + 2, late_pack, early_pack)


def edges(place, early, late, features, target, mask_row, early_pack, late_pack):
    parts = (early, late, features, target, mask_row)
    _, tile_cols, channels = features.shape
    keep = 2 * REACH
    tail = tile_cols // keep - 1

    def specs(at):
        return [pl.BlockSpec((p.shape[0], keep, channels), lambda i, at=at: (0, at, 0)) for p in parts]

    whole = [pl.BlockSpec(early_pack.shape, lambda i: (0, 0))] * 2
    rows = sum(p.shape[0] for p in parts) + 2 * (NEAR + 1)
    shapes = [(rows, columns, channels) for columns in (REACH, REACH, 2 * keep)]
    return pl.pallas_call(
        functools.partial(edge_kernel, tile_cols),
        grid=(1,),
        out_shape=[jax.ShapeDtypeStruct(shape, features.dtype) for shape in shapes],
        in_specs=[pl.BlockSpec(memory_space=pltpu.SMEM)] * 2 + whole + specs(tail) + specs(0),
        out_specs=[pl.BlockSpec(shape, lambda i: (0, 0, 0)) for shape in shapes],
        compiler_params=pltpu.CompilerParams(vmem_limit_bytes=8 * MIB),
        cost_estimate=pl.CostEstimate(
            flops=0, bytes_accessed=16 * rows * keep * channels, transcendentals=0
        ),
    )(*place, early_pack, late_pack, *parts, *parts)


def put(wide, row, value, stride):
    size, channels = value.shape
    spot = pl.ds(row * stride, size)
    wide[spot, :channels] = pltpu.roll(value, 2, 0).astype(jnp.bfloat16)
    wide[spot, channels : 2 * channels] = value.astype(jnp.bfloat16)
    wide[spot, 2 * channels :] = pltpu.roll(value, size - 2, 0).astype(jnp.bfloat16)


def taps(wide, row, count, stride):
    parts = [wide[pl.ds((row + 2 * a) * stride, count * stride), :] for a in range(3)]
    return jnp.concatenate(parts, axis=1)


def conv(wide, row, count, stride, kernel):
    channels = kernel.shape[-1]
    return dot(taps(wide, row, count, stride), kernel[...].reshape(9 * channels, channels))


def conv_adjoint(wide, row, count, stride, kernel):
    flipped = [kernel[2 - a, 2 - b] for a in range(3) for b in range(3)]
    return dot_t(taps(wide, row, count, stride), jnp.concatenate(flipped, axis=1))


def stacked(piece, rows):
    return jnp.concatenate([piece(row) for row in rows], axis=0)


def first_stages(
    stride, blocks, rows, feature, inside, first, second, wide_even, wide_odd, slopes, use
):
    tall = rows + 2 * REACH
    for row in range(0, tall, NEAR):
        put(wide_even, row, stacked(feature, range(row, row + NEAR)), stride)
    count = blocks[0]
    for row in range(0, tall - 4, count):
        pre = conv(wide_even, row, count, stride, first)
        s = 1.0 / (1.0 + jnp.exp(-pre))
        kept = stacked(inside, range(row + 2, row + 2 + count))
        put(wide_odd, row, pre * s * kept, stride)
        low, high = max(row, NEAR), min(row + count, tall - 4 - NEAR)
        if low < high:
            part = slice((low - row) * stride, (high - row) * stride)
            slope = (s * (1.0 + pre * (1.0 - s)) * kept)[part]
            slopes[pl.ds((low - NEAR) * stride, (high - low) * stride), :] = slope
    count = blocks[1]
    for row in range(0, rows + 2 * NEAR, count):
        use(row, count, conv(wide_odd, row, count, stride, second))


def last_stages(stride, blocks, rows, first, second, wide_even, wide_odd, slopes, use):
    count = blocks[2]
    for row in range(0, rows + 4, count):
        value = conv_adjoint(wide_even, row, count, stride, second)
        value = value * slopes[pl.ds(row * stride, count * stride), :]
        put(wide_odd, row, value, stride)
    count = blocks[3]
    for row in range(0, rows, count):
        use(row, count, conv_adjoint(wide_odd, row, count, stride, first))


def deal(place, out, pieces):
    for step, piece in enumerate(pieces):
        piece[...] = out[pl.ds((place[0] ^ step) * piece.shape[0], piece.shape[0])]


def loss_grad(row, count, value, target, hole, inside):
    near = range(row, row + count)
    weight = (1.0 + 2.0 * stacked(hole, near)) * stacked(inside, range(row + NEAR, row + count + NEAR))
    return weight * (value - stacked(target, near))


def part_of(rows, edge, above, own, below):
    def find(row):
        if row < edge:
            return above, row
        if row < edge + rows:
            return own, row - edge
        return below, row - edge - rows

    return find


TILE_BLOCKS = (4, 4, 4, 4)
SIDE_BLOCKS = (10, 8, 12, 8)


def tile_forward_kernel(
    col, low, early, features, late, first, second, ok, pre, slopes, wide_even, wide_odd
):
    place = col[0], low[0]
    rows, stride, _ = features.shape
    find = part_of(rows, REACH, (early, late), (features,), (late, early))

    def feature(row):
        sources, at = find(row)
        if len(sources) == 1:
            return features[at].astype(jnp.float32)
        return pick(odd_row(place), *[source[at] for source in sources]).astype(jnp.float32)

    def inside(row):
        return ok[REACH : REACH + stride, row : row + 1]

    def use(row, count, value):
        pre[pl.ds(row * stride, count * stride), :] = value

    first_stages(
        stride, TILE_BLOCKS, rows, feature, inside, first, second, wide_even, wide_odd, slopes, use
    )


def tile_backward_kernel(
    col,
    low,
    pre,
    slopes,
    early_pack,
    target,
    late_pack,
    mask_row,
    first,
    second,
    ok,
    *refs,
):
    *pieces, out, wide_even, wide_odd = refs
    place = col[0], low[0]
    rows, stride, channels = target.shape
    packs = (early_pack, late_pack)
    find = part_of(rows, NEAR, packs, (target,), packs[::-1])

    def picked(sources, part):
        return pick(odd_row(place), *[source[part] for source in sources]).astype(jnp.float32)

    def goal(row):
        sources, at = find(row)
        if len(sources) == 1:
            return target[at].astype(jnp.float32)
        return picked(sources, slice(at * stride, (at + 1) * stride))

    masks = [
        turned(picked(sources, slice(NEAR * stride, None))[:, :stride]) for sources in (packs, packs[::-1])
    ]
    find_mask = part_of(rows, NEAR, (masks[0], 0), (mask_row[0].astype(jnp.float32), 0), (masks[1], 0))

    def hole(row):
        (mask, start), at = find_mask(row)
        return mask[:, start + at : start + at + 1]

    def inside(row):
        return ok[REACH : REACH + stride, row : row + 1]

    count = NEAR
    for row in range(0, rows + 2 * NEAR, count):
        value = pre[pl.ds(row * stride, count * stride), :]
        put(wide_even, row, loss_grad(row, count, value, goal, hole, inside), stride)

    def use(row, count, value):
        value = value.reshape(count, stride, channels)[:, REACH : stride - REACH]
        out[row : row + count] = value.astype(jnp.bfloat16)

    last_stages(stride, TILE_BLOCKS, rows, first, second, wide_even, wide_odd, slopes, use)
    deal(place, out, pieces)


def side_kernel(col, low, early, late, own, first, second, ok, *refs):
    *pieces, out, wide_even, wide_odd, slopes = refs
    place = col[0], low[0]
    rows, _, channels = out.shape
    keep = 2 * REACH
    stride = 2 * (REACH + keep)
    tall = rows + 2 * REACH
    odd = odd_col(place)

    def feature(row):
        before, after = pick(odd, early[row], late[row]), pick(odd, late[row], early[row])
        parts = [part.astype(jnp.float32) for part in (before, own[row], after)]
        return jnp.concatenate(parts, axis=0)

    find = part_of(rows, NEAR, tall, tall + NEAR + 1, tall + NEAR + 1 + rows + 1)

    def goal(row):
        start, at = find(row)
        return feature(start + at)

    masks = [feature(row) for row in (tall + NEAR, tall + NEAR + 1 + rows, early.shape[0] - 1)]
    find_mask = part_of(rows, NEAR, (masks[0], 0), (masks[1], 0), (masks[2], 0))

    def hole(row):
        (mask, start), at = find_mask(row)
        return mask[:, start + at : start + at + 1]

    width = ok.shape[0]
    kept = jnp.concatenate([ok[: REACH + keep], ok[width - REACH - keep :]], axis=0)

    def inside(row):
        return kept[:, row : row + 1]

    def use_forward(row, count, value):
        put(wide_even, row, loss_grad(row, count, value, goal, hole, inside), stride)

    first_stages(
        stride, SIDE_BLOCKS, rows, feature, inside, first, second, wide_even, wide_odd, slopes, use_forward
    )

    def use(row, count, value):
        value = value.reshape(count, stride, channels).astype(jnp.bfloat16)
        out[row : row + count, :REACH] = value[:, REACH : 2 * REACH]
        out[row : row + count, REACH:] = value[:, stride - 2 * REACH : stride - REACH]

    last_stages(stride, SIDE_BLOCKS, rows, first, second, wide_even, wide_odd, slopes, use)
    deal(place, out, pieces)


def wide_buffer(rows, stride, channels):
    return pltpu.VMEM((rows * stride, 3 * channels), jnp.bfloat16)


def tile_forward(place, early, features, late, first, second, ok):
    rows, stride, channels = features.shape
    shapes = [
        jax.ShapeDtypeStruct(((rows + h) * stride, channels), jnp.float32) for h in (2 * NEAR, 4)
    ]
    in_vmem = pl.BlockSpec(memory_space=pltpu.VMEM)
    return pl.pallas_call(
        tile_forward_kernel,
        out_shape=shapes,
        in_specs=[pl.BlockSpec(memory_space=pltpu.SMEM)] * 2 + [in_vmem] * 6,
        out_specs=[in_vmem] * 2,
        scratch_shapes=[wide_buffer(rows + h, stride, channels) for h in (16, 12)],
        compiler_params=pltpu.CompilerParams(vmem_limit_bytes=18 * MIB),
        cost_estimate=pl.CostEstimate(
            flops=2 * 9 * channels * channels * stride * (2 * rows + 20),
            bytes_accessed=8 * MIB,
            transcendentals=0,
        ),
    )(*place, early, features, late, first, second, ok)


def piece_shapes(rows, columns, channels):
    count = lax.axis_size("col")
    return [jax.ShapeDtypeStruct((rows // count, columns, channels), jnp.bfloat16)] * count


def tile_backward(place, pre, slopes, early_pack, target, *operands):
    rows, stride, channels = target.shape
    in_vmem = pl.BlockSpec(memory_space=pltpu.VMEM)
    shapes = piece_shapes(rows, stride - 2 * REACH, channels)
    return pl.pallas_call(
        tile_backward_kernel,
        out_shape=shapes,
        in_specs=[pl.BlockSpec(memory_space=pltpu.SMEM)] * 2 + [in_vmem] * (4 + len(operands)),
        out_specs=[in_vmem] * len(shapes),
        scratch_shapes=[
            pltpu.VMEM((rows, stride - 2 * REACH, channels), jnp.bfloat16),
            *[wide_buffer(rows + h, stride, channels) for h in (8, 4)],
        ],
        compiler_params=pltpu.CompilerParams(vmem_limit_bytes=16 * MIB),
        cost_estimate=pl.CostEstimate(
            flops=2 * 9 * channels * channels * stride * (2 * rows + 4),
            bytes_accessed=8 * MIB,
            transcendentals=0,
        ),
    )(*place, pre, slopes, early_pack, target, *operands)


def sides(place, shape, *operands):
    rows, _, channels = shape
    stride = 6 * REACH
    in_vmem = pl.BlockSpec(memory_space=pltpu.VMEM)
    shapes = piece_shapes(rows, 2 * REACH, channels)
    return pl.pallas_call(
        side_kernel,
        out_shape=shapes,
        in_specs=[pl.BlockSpec(memory_space=pltpu.SMEM)] * 2 + [in_vmem] * len(operands),
        out_specs=[in_vmem] * len(shapes),
        scratch_shapes=[
            pltpu.VMEM((rows, 2 * REACH, channels), jnp.bfloat16),
            *[wide_buffer(rows + h, stride, channels) for h in (16, 12)],
            pltpu.VMEM(((rows + 4) * stride, channels), jnp.float32),
        ],
        compiler_params=pltpu.CompilerParams(vmem_limit_bytes=14 * MIB),
        cost_estimate=pl.CostEstimate(
            flops=2 * 9 * channels * channels * stride * (4 * rows + 24),
            bytes_accessed=4 * MIB,
            transcendentals=0,
        ),
    )(*place, *operands)


def pairs(axis, start):
    size = lax.axis_size(axis)
    up = [(i, i + 1) for i in range(start, size - 1, 2)]
    return up + [(j, i) for i, j in up]


def shards(
    features,
    target,
    hole_mask,
    kernel_first,
    kernel_second,
    inputs,
    weight_in,
    weight_out,
    weight_local,
    weight_mix,
):
    tile_rows, tile_cols, channels = features.shape
    row_devices, col_devices = lax.axis_size("row"), lax.axis_size("col")
    devices = row_devices * col_devices
    height, width = tile_rows * row_devices, tile_cols * col_devices
    strip, half = inputs.shape[0], weight_in.shape[1]
    owned = width // 2 // devices
    col_norm, row_norm = 1.0 / math.sqrt(width), 1.0 / math.sqrt(height)
    table = column_matrix(width, devices)
    table_back = jnp.asarray(np.ascontiguousarray(table.T))
    table = jnp.asarray(table)
    row_table = row_matrix(height, row_devices, col_devices)
    row_back = jnp.asarray(np.ascontiguousarray(row_table.T))
    row_table = jnp.asarray(row_table)
    bf16 = jnp.bfloat16

    def swap(spectrum):
        return lax.all_to_all(spectrum, ("col", "row"), split_axis=0, concat_axis=0, tiled=True)

    row0, col0 = lax.axis_index("row") * tile_rows, lax.axis_index("col") * tile_cols
    row_ids = row0 - REACH + jnp.arange(tile_rows + 2 * REACH, dtype=jnp.int32)
    col_ids = col0 - REACH + jnp.arange(tile_cols + 2 * REACH, dtype=jnp.int32)
    ok = ((col_ids >= 0) & (col_ids < width))[:, None] & ((row_ids >= 0) & (row_ids < height))[None]
    ok = ok.astype(jnp.float32)
    place = tuple(jnp.full((1,), i, jnp.int32) for i in (lax.axis_index("col"), lax.axis_index("row") & 1))
    early_pack, late_pack, mask_row = target_packs(place, target, hole_mask)
    inputs, ok, early_pack = lax.optimization_barrier((inputs, ok, early_pack))

    cells = [jax.ShapeDtypeStruct((width, strip * half), bf16)]
    weight_in = weight_in.T
    spatial_cols = fetching_spectrum(col_norm, cells[0], inputs, weight_in, table)
    spatial_moved = swap(spatial_cols)

    early = lax.ppermute(features, "row", pairs("row", 0))
    late = lax.ppermute(features, "row", pairs("row", 1))
    kernel_first, spatial_cols = lax.optimization_barrier((kernel_first, spatial_cols))
    kernel_first, kernel_second = fetch(kernel_first, kernel_second)
    early_pack = lax.ppermute(early_pack, "row", pairs("row", 0))
    late_pack = lax.ppermute(late_pack, "row", pairs("row", 1))
    pre, slopes = tile_forward(place, early, features, late, kernel_first, kernel_second, ok)
    early_pack, pre = lax.optimization_barrier((early_pack, pre))
    early_edge, late_edge, own = edges(
        place, early, late, features, target, mask_row, early_pack, late_pack
    )
    early_edge = lax.ppermute(early_edge, "col", pairs("col", 0))
    late_edge = lax.ppermute(late_edge, "col", pairs("col", 1))
    inner = tile_backward(
        place, pre, slopes, early_pack, target, late_pack, mask_row, kernel_first, kernel_second, ok
    )

    def dealt(pieces):
        result = [pieces[0]]
        for step in range(1, col_devices):
            swaps = [(i, i ^ step) for i in range(col_devices)]
            result.append(lax.ppermute(pieces[step], "col", swaps))
        return result

    inner = dealt(inner)
    outer = sides(
        place, features.shape, early_edge, late_edge, own, kernel_first, kernel_second, ok
    )
    *outer, spatial_moved = lax.optimization_barrier((*outer, spatial_moved))
    outer = dealt(outer)

    cell_count = height * owned
    wide = [pltpu.VMEM((strip * half // LANES, width, LANES), jnp.float32)]
    slope = vmem_call(
        functools.partial(slope_kernel, row_norm, owned, devices),
        [jax.ShapeDtypeStruct((2, cell_count, half), jnp.float32)],
        spatial_moved,
        weight_mix,
        row_table,
        scratch=wide,
    )[0]
    outer[0], slope = lax.optimization_barrier((outer[0], slope))
    grad_cols, strip_grad = grad_spectrum(col_norm, place, inner, outer, weight_out, table)
    grad_rows = vmem_call(
        functools.partial(mix_kernel, row_norm, owned, devices),
        cells,
        swap(grad_cols),
        slope,
        weight_mix,
        row_table,
        row_back,
        scratch=wide,
    )[0]
    returned = swap(grad_rows)
    return vmem_call(
        functools.partial(output_kernel, col_norm),
        [jax.ShapeDtypeStruct(inputs.shape, bf16)],
        returned,
        strip_grad,
        weight_in,
        weight_local,
        table_back,
    )[0]


def solution(mesh):
    in_specs = (
        P("row", "col", None),
        P("row", "col", None),
        P("row", "col"),
        P(),
        P(),
        P(("row", "col"), None, None),
        P(),
        P(),
        P(),
        P(),
    )
    out_specs = P(("row", "col"), None, None)
    return jax.shard_map(shards, mesh=mesh, in_specs=in_specs, out_specs=out_specs, check_vma=False)
```

```python
import functools
import math

import jax
import jax.numpy as jnp
import ml_dtypes
import numpy as np
from jax import lax
from jax.experimental import pallas as pl
from jax.experimental.pallas import tpu as pltpu
from jax.sharding import PartitionSpec as P

REACH = 8
NEAR = 4
MIB = 1024 * 1024
LANES = 128


def dot(left, right):
    return jnp.dot(left, right, preferred_element_type=jnp.float32)


def dot_t(left, right):
    return lax.dot_general(left, right, (((1,), (1,)), ((), ())), preferred_element_type=jnp.float32)


def vmem_call(body, shapes, *operands, flops=0, scratch=(), limit=10):
    spec = pl.BlockSpec(memory_space=pltpu.VMEM)
    size = sum(math.prod(a.shape) * a.dtype.itemsize for a in (*operands, *shapes))
    return pl.pallas_call(
        body,
        out_shape=shapes,
        in_specs=[spec] * len(operands),
        out_specs=[spec] * len(shapes),
        scratch_shapes=list(scratch),
        compiler_params=pltpu.CompilerParams(vmem_limit_bytes=limit * MIB),
        cost_estimate=pl.CostEstimate(flops=flops, bytes_accessed=size, transcendentals=0),
    )(*operands)


def in_hbm(array):
    return pltpu.with_memory_space_constraint(array, pltpu.HBM)


def phases(first, second, length):
    angle = (first[:, None] * second[None, :] % length) * (2.0 * math.pi / length)
    return np.cos(angle).astype(ml_dtypes.bfloat16), np.sin(angle).astype(ml_dtypes.bfloat16)


def column_matrix(width, devices):
    half = width // 2
    freq, col = np.arange(half), np.arange(width)
    cos, sin = phases(freq, col, width)
    sin[0] = (2 * (col % 2) - 1).astype(ml_dtypes.bfloat16)
    both = np.stack([cos, -sin]).reshape(2, devices, half // devices, width)
    return np.ascontiguousarray(both.transpose(1, 0, 2, 3)).reshape(width, width)


def row_matrix(height, row_devices, col_devices):
    devices = row_devices * col_devices
    strip = height // devices
    strips = np.arange(devices).reshape(row_devices, col_devices).T.reshape(-1)
    rows = (strips[None, :] * strip + np.arange(strip)[:, None]).reshape(-1)
    cos, sin = phases(np.arange(height), rows, height)
    return np.block([[cos, sin], [-sin, cos]])


def strip_row(signal, r):
    return jnp.concatenate([signal[block, r] for block in range(signal.shape[0])], axis=0)


def grad_kernel(norm, col, low, *refs):
    *pieces, weight, table, out, strip_out, projected = refs
    count = len(pieces) // 2
    _, strip, tile_cols, _ = strip_out.shape
    for step, inner, outer in zip(steps_of(count), pieces[:count], pieces[count:]):
        block = col[0] ^ step
        strip_out[block, :, REACH : tile_cols - REACH] = inner[...]
        strip_out[block, :, :REACH] = outer[:, :REACH]
        strip_out[block, :, tile_cols - REACH :] = outer[:, REACH:]
        rows = [dot_t(strip_out[block, r], weight[...]).astype(jnp.bfloat16) for r in range(strip)]
        where = pl.ds(pl.multiple_of(block * tile_cols, tile_cols), tile_cols)
        projected[where, :] = jnp.concatenate(rows, axis=1)
    out[...] = (dot(table[...], projected[...]) * norm).astype(jnp.bfloat16)


def grad_spectrum(norm, place, inner, outer, weight, table):
    strip, columns, channels = inner[0].shape
    shape = (table.shape[0], strip * weight.shape[0])
    in_vmem = pl.BlockSpec(memory_space=pltpu.VMEM)
    return pl.pallas_call(
        functools.partial(grad_kernel, norm),
        out_shape=[
            jax.ShapeDtypeStruct(shape, jnp.bfloat16),
            jax.ShapeDtypeStruct((len(inner), strip, columns + 2 * REACH, channels), jnp.bfloat16),
        ],
        in_specs=[pl.BlockSpec(memory_space=pltpu.SMEM)] * 2 + [in_vmem] * (2 * len(inner) + 2),
        out_specs=[in_vmem] * 2,
        scratch_shapes=[pltpu.VMEM(shape, jnp.bfloat16)],
        compiler_params=pltpu.CompilerParams(vmem_limit_bytes=10 * MIB),
        cost_estimate=pl.CostEstimate(flops=0, bytes_accessed=2 * MIB, transcendentals=0),
    )(*place, *inner, *outer, weight, table)


def fetching_spectrum_kernel(norm, signal, weight, table, out, signal_held, weight_held, table_held, sems):
    count = signal.shape[0]
    copies = [pltpu.make_async_copy(weight, weight_held, sems.at[0])]
    copies += [
        pltpu.make_async_copy(signal.at[r], signal_held.at[r], sems.at[1 + r]) for r in range(count)
    ]
    copies.append(pltpu.make_async_copy(table, table_held, sems.at[1 + count]))
    for copy in copies:
        copy.start()
    copies[0].wait()
    rows = []
    for r in range(count):
        copies[1 + r].wait()
        rows.append(dot_t(signal_held[r], weight_held[...]).astype(jnp.bfloat16))
    copies[-1].wait()
    out[...] = (dot(table_held[...], jnp.concatenate(rows, axis=1)) * norm).astype(jnp.bfloat16)


def fetching_spectrum(norm, shape, signal, weight, table):
    operands = (signal, weight, table)
    return pl.pallas_call(
        functools.partial(fetching_spectrum_kernel, norm),
        out_shape=shape,
        in_specs=[pl.BlockSpec(memory_space=pltpu.HBM)] * 3,
        out_specs=pl.BlockSpec(memory_space=pltpu.VMEM),
        scratch_shapes=[pltpu.VMEM(a.shape, a.dtype) for a in operands]
        + [pltpu.SemaphoreType.DMA((signal.shape[0] + 2,))],
        compiler_params=pltpu.CompilerParams(vmem_limit_bytes=12 * MIB),
        cost_estimate=pl.CostEstimate(
            flops=0, bytes_accessed=2 * MIB, transcendentals=0
        ),
    )(*[in_hbm(a) for a in operands])


def row_spectrum(moved, table, wide, norm, owned, devices):
    groups = wide.shape[0]
    for g in range(groups):
        wide[g] = moved[:, g * LANES : (g + 1) * LANES].astype(jnp.float32)
    strip = table.shape[1] // (2 * devices)
    half = moved.shape[1] // strip
    height = table.shape[0] // 2
    real, imag = [], []
    for freq in range(owned):
        parts = []
        for part in range(2):
            where = pl.ds(part * owned + freq, devices, stride=2 * owned)
            block = jnp.concatenate([wide[g, where, :] for g in range(groups)], axis=1)
            parts += [block[:, r * half : (r + 1) * half] for r in range(strip)]
        result = dot(table[...], jnp.concatenate(parts, axis=0).astype(jnp.bfloat16)) * norm
        real.append(result[:height])
        imag.append(result[height:])
    return jnp.concatenate(real, axis=0), jnp.concatenate(imag, axis=0)


def slope_kernel(norm, owned, devices, moved, mix, table, out, wide):
    parts = row_spectrum(moved, table, wide, norm, owned, devices)
    real, imag = [part.astype(jnp.bfloat16) for part in parts]
    half = real.shape[1]
    spans = (slice(0, half), slice(half, 2 * half))
    for part, span in enumerate(spans):
        pre = dot(real, mix[spans[0], span]) + dot(imag, mix[spans[1], span])
        s = 1.0 / (1.0 + jnp.exp(-pre))
        out[part] = s * (1.0 + pre * (1.0 - s))


def mix_kernel(norm, owned, devices, moved, slope, mix, table, back_table, out, wide):
    grads = row_spectrum(moved, table, wide, norm, owned, devices)
    half = grads[0].shape[1]
    spans = (slice(0, half), slice(half, 2 * half))
    mixed = [(grad * slope[part]).astype(jnp.bfloat16) for part, grad in enumerate(grads)]
    back = [dot_t(mixed[0], mix[p, spans[0]]) + dot_t(mixed[1], mix[p, spans[1]]) for p in spans]
    back = [part.astype(jnp.bfloat16) for part in back]
    height = table.shape[0] // 2
    strip = height // devices
    groups = wide.shape[0]
    for freq in range(owned):
        cells = slice(freq * height, (freq + 1) * height)
        stacked = jnp.concatenate([back[0][cells], back[1][cells]], axis=0)
        result = dot(back_table[...], stacked) * norm
        for part in range(2):
            rows = [
                result[(part * strip + r) * devices : (part * strip + r + 1) * devices]
                for r in range(strip)
            ]
            where = pl.ds(part * owned + freq, devices, stride=2 * owned)
            values = jnp.concatenate(rows, axis=1)
            for g in range(groups):
                wide[g, where, :] = values[:, g * LANES : (g + 1) * LANES]
    for g in range(groups):
        out[:, g * LANES : (g + 1) * LANES] = wide[g].astype(jnp.bfloat16)


def output_kernel(norm, moved, strip_grad, weight_in, weight_local, table, out, held, sems):
    spatial = (dot(table[...], moved[...]) * norm).astype(jnp.bfloat16)
    half = weight_in.shape[0]
    copies = []
    for r in range(out.shape[0]):
        total = dot(spatial[:, r * half : (r + 1) * half], weight_in[...])
        total = total + dot_t(strip_row(strip_grad, r), weight_local[...])
        held[r] = total.astype(jnp.bfloat16)
        copies.append(pltpu.make_async_copy(held.at[r], out.at[r], sems.at[r]))
        copies[-1].start()
    for copy in copies:
        copy.wait()


def output(norm, shape, *operands):
    return pl.pallas_call(
        functools.partial(output_kernel, norm),
        out_shape=jax.ShapeDtypeStruct(shape, jnp.bfloat16),
        in_specs=[pl.BlockSpec(memory_space=pltpu.VMEM)] * len(operands),
        out_specs=pl.BlockSpec(memory_space=pltpu.HBM),
        scratch_shapes=[pltpu.VMEM(shape, jnp.bfloat16), pltpu.SemaphoreType.DMA((shape[0],))],
        compiler_params=pltpu.CompilerParams(vmem_limit_bytes=10 * MIB),
        cost_estimate=pl.CostEstimate(flops=0, bytes_accessed=3 * MIB, transcendentals=0),
    )(*operands)


TAIL = 16


def pick(flag, left, right):
    return lax.select(flag, left, right)


def odd_row(place):
    return place[1] == 1


def odd_col(place):
    return lax.rem(place[0], 2) == 1


def turned(rows):
    count, columns = rows.shape
    rows = rows.astype(jnp.float32)
    return jnp.concatenate([rows, jnp.zeros((columns - count, columns), jnp.float32)], axis=0).T


def filled(lanes, channels):
    fill = jnp.zeros((lanes.shape[0], channels - lanes.shape[1]), jnp.float32)
    return jnp.concatenate([lanes, fill], axis=1).astype(jnp.bfloat16)


def pack_kernel(col, low, target, mask, early, late, mask_row, mask_held, sems):
    place = col[0], low[0]
    tile_rows, tile_cols = mask.shape
    channels = target.shape[1]
    last = tile_rows - NEAR
    pixels = NEAR * tile_cols
    moves = [(mask, mask_held)]
    for pack, row in ((early, (1 - place[1]) * last), (late, place[1] * last)):
        moves.append((target.at[pl.ds(row * tile_cols, pixels)], pack.at[pl.ds(0, pixels)]))
    copies = [pltpu.make_async_copy(*move, sems.at[i]) for i, move in enumerate(moves)]
    for copy in copies:
        copy.start()
    copies[0].wait()
    mask_row[0] = filled(turned(mask_held[...]), channels)
    ends = (mask_held[:NEAR], mask_held[last:])
    for pack, (one, other) in ((early, ends), (late, ends[::-1])):
        rows = pick(odd_row(place), one.astype(jnp.float32), other.astype(jnp.float32))
        rows = jnp.concatenate([rows, jnp.zeros((TAIL - NEAR, tile_cols), jnp.float32)], axis=0)
        pack[pixels:] = filled(rows, channels)
    for copy in copies[1:]:
        copy.wait()


def target_packs(place, target, mask):
    tile_rows, tile_cols, channels = target.shape
    pack = (NEAR * tile_cols + TAIL, channels)
    hbm = pl.BlockSpec(memory_space=pltpu.HBM)
    shapes = [pack, pack, (1, tile_cols, channels)]
    return pl.pallas_call(
        pack_kernel,
        out_shape=[jax.ShapeDtypeStruct(shape, jnp.bfloat16) for shape in shapes],
        in_specs=[pl.BlockSpec(memory_space=pltpu.SMEM)] * 2 + [hbm, hbm],
        out_specs=[pl.BlockSpec(memory_space=pltpu.VMEM)] * len(shapes),
        scratch_shapes=[pltpu.VMEM(mask.shape, mask.dtype), pltpu.SemaphoreType.DMA((3,))],
        compiler_params=pltpu.CompilerParams(vmem_limit_bytes=4 * MIB),
        cost_estimate=pl.CostEstimate(flops=0, bytes_accessed=MIB, transcendentals=0),
    )(*place, in_hbm(target.reshape(tile_rows * tile_cols, channels)), in_hbm(mask))


def fetch_kernel(*refs):
    count = len(refs) // 2
    sems = refs[-1]
    copies = [pltpu.make_async_copy(refs[i], refs[count + i], sems.at[i]) for i in range(count)]
    for copy in copies:
        copy.start()
    for copy in copies:
        copy.wait()


def fetch(*arrays):
    return pl.pallas_call(
        fetch_kernel,
        out_shape=[jax.ShapeDtypeStruct(a.shape, a.dtype) for a in arrays],
        in_specs=[pl.BlockSpec(memory_space=pltpu.HBM)] * len(arrays),
        out_specs=[pl.BlockSpec(memory_space=pltpu.VMEM)] * len(arrays),
        scratch_shapes=[pltpu.SemaphoreType.DMA((len(arrays),))],
        compiler_params=pltpu.CompilerParams(vmem_limit_bytes=4 * MIB),
        cost_estimate=pl.CostEstimate(flops=0, bytes_accessed=5 * MIB, transcendentals=0),
    )(*[in_hbm(a) for a in arrays])


def edge_kernel(tile_cols, col, low, early_pack, late_pack, *refs):
    place = col[0], low[0]
    sources, (early, late, own) = refs[:-3], refs[-3:]
    count = len(sources) // 2
    keep = 2 * REACH
    channels = own.shape[2]
    lower, high = odd_row(place), odd_col(place)

    def put_rows(row, tail, head):
        rows = slice(row, row + tail.shape[0])
        last, initial = tail[:, REACH:], head[:, :REACH]
        early[rows] = pick(high, initial, last)
        late[rows] = pick(high, last, initial)
        own[rows, :keep] = head
        own[rows, keep:] = tail

    def put_pack(row, one, other):
        for i in range(NEAR):
            at = i * tile_cols
            tail = pick(lower, one[at + tile_cols - keep : at + tile_cols], other[at + tile_cols - keep : at + tile_cols])
            head = pick(lower, one[at : at + keep], other[at : at + keep])
            put_rows(row + i, tail[None], head[None])
        mask = turned(pick(lower, one[NEAR * tile_cols :, :tile_cols], other[NEAR * tile_cols :, :tile_cols]))
        tail, head = [filled(m, channels)[None] for m in (mask[tile_cols - keep :], mask[:keep])]
        put_rows(row + NEAR, tail, head)

    def put_picked(row, one, other):
        put_rows(row, *[pick(lower, sources[one + i * count][...], sources[other + i * count][...]) for i in (0, 1)])

    def put_own(row, index):
        put_rows(row, sources[index][...], sources[index + count][...])

    rows = sources[0].shape[0]
    put_picked(0, 0, 1)
    put_own(rows, 2)
    put_picked(2 * rows, 1, 0)
    put_pack(3 * rows, early_pack, late_pack)
    put_own(3 * rows + NEAR + 1, 3)
    put_own(4 * rows + NEAR + 1, 4)
    put_pack(4 * rows + NEAR + 2, late_pack, early_pack)


def edges(place, early, late, features, target, mask_row, early_pack, late_pack):
    parts = (early, late, features, target, mask_row)
    _, tile_cols, channels = features.shape
    keep = 2 * REACH
    tail = tile_cols // keep - 1

    def specs(at):
        return [pl.BlockSpec((p.shape[0], keep, channels), lambda i, at=at: (0, at, 0)) for p in parts]

    whole = [pl.BlockSpec(early_pack.shape, lambda i: (0, 0))] * 2
    rows = sum(p.shape[0] for p in parts) + 2 * (NEAR + 1)
    shapes = [(rows, columns, channels) for columns in (REACH, REACH, 2 * keep)]
    return pl.pallas_call(
        functools.partial(edge_kernel, tile_cols),
        grid=(1,),
        out_shape=[jax.ShapeDtypeStruct(shape, features.dtype) for shape in shapes],
        in_specs=[pl.BlockSpec(memory_space=pltpu.SMEM)] * 2 + whole + specs(tail) + specs(0),
        out_specs=[pl.BlockSpec(shape, lambda i: (0, 0, 0)) for shape in shapes],
        compiler_params=pltpu.CompilerParams(vmem_limit_bytes=8 * MIB),
        cost_estimate=pl.CostEstimate(
            flops=0, bytes_accessed=16 * rows * keep * channels, transcendentals=0
        ),
    )(*place, early_pack, late_pack, *parts, *parts)


def put(wide, row, value, stride):
    size, channels = value.shape
    spot = pl.ds(row * stride, size)
    wide[spot, :channels] = pltpu.roll(value, 2, 0).astype(jnp.bfloat16)
    wide[spot, channels : 2 * channels] = value.astype(jnp.bfloat16)
    wide[spot, 2 * channels :] = pltpu.roll(value, size - 2, 0).astype(jnp.bfloat16)


def taps(wide, row, count, stride):
    parts = [wide[pl.ds((row + 2 * a) * stride, count * stride), :] for a in range(3)]
    return jnp.concatenate(parts, axis=1)


def conv(wide, row, count, stride, kernel):
    channels = kernel.shape[-1]
    return dot(taps(wide, row, count, stride), kernel[...].reshape(9 * channels, channels))


def conv_adjoint(wide, row, count, stride, kernel):
    flipped = [kernel[2 - a, 2 - b] for a in range(3) for b in range(3)]
    return dot_t(taps(wide, row, count, stride), jnp.concatenate(flipped, axis=1))


def stacked(piece, rows):
    return jnp.concatenate([piece(row) for row in rows], axis=0)


def first_stages(
    stride, blocks, rows, feature, inside, first, second, wide_even, wide_odd, slopes, use
):
    tall = rows + 2 * REACH
    for row in range(0, tall, NEAR):
        put(wide_even, row, stacked(feature, range(row, row + NEAR)), stride)
    count = blocks[0]
    for row in range(0, tall - 4, count):
        pre = conv(wide_even, row, count, stride, first)
        s = 1.0 / (1.0 + jnp.exp(-pre))
        kept = stacked(inside, range(row + 2, row + 2 + count))
        put(wide_odd, row, pre * s * kept, stride)
        low, high = max(row, NEAR), min(row + count, tall - 4 - NEAR)
        if low < high:
            part = slice((low - row) * stride, (high - row) * stride)
            slope = (s * (1.0 + pre * (1.0 - s)) * kept)[part]
            slopes[pl.ds((low - NEAR) * stride, (high - low) * stride), :] = slope
    count = blocks[1]
    for row in range(0, rows + 2 * NEAR, count):
        use(row, count, conv(wide_odd, row, count, stride, second))


def last_stages(stride, blocks, rows, first, second, wide_even, wide_odd, slopes, use):
    count = blocks[2]
    for row in range(0, rows + 4, count):
        value = conv_adjoint(wide_even, row, count, stride, second)
        value = value * slopes[pl.ds(row * stride, count * stride), :]
        put(wide_odd, row, value, stride)
    count = blocks[3]
    for row in range(0, rows, count):
        use(row, count, conv_adjoint(wide_odd, row, count, stride, first))


def steps_of(count):
    return [0, *range(2, count), 1] if count > 1 else [0]


def deal(place, out, pieces):
    for step, piece in zip(steps_of(len(pieces)), pieces):
        piece[...] = out[pl.ds((place[0] ^ step) * piece.shape[0], piece.shape[0])]


def loss_grad(row, count, value, target, hole, inside):
    near = range(row, row + count)
    weight = (1.0 + 2.0 * stacked(hole, near)) * stacked(inside, range(row + NEAR, row + count + NEAR))
    return weight * (value - stacked(target, near))


def part_of(rows, edge, above, own, below):
    def find(row):
        if row < edge:
            return above, row
        if row < edge + rows:
            return own, row - edge
        return below, row - edge - rows

    return find


TILE_BLOCKS = (4, 4, 4, 4)
SIDE_BLOCKS = (10, 8, 12, 8)


def tile_forward_kernel(
    col, low, early, features, late, first, second, ok, pre, slopes, wide_even, wide_odd
):
    place = col[0], low[0]
    rows, stride, _ = features.shape
    find = part_of(rows, REACH, (early, late), (features,), (late, early))

    def feature(row):
        sources, at = find(row)
        if len(sources) == 1:
            return features[at].astype(jnp.float32)
        return pick(odd_row(place), *[source[at] for source in sources]).astype(jnp.float32)

    def inside(row):
        return ok[REACH : REACH + stride, row : row + 1]

    def use(row, count, value):
        pre[pl.ds(row * stride, count * stride), :] = value

    first_stages(
        stride, TILE_BLOCKS, rows, feature, inside, first, second, wide_even, wide_odd, slopes, use
    )


def tile_backward_kernel(
    col,
    low,
    pre,
    slopes,
    early_pack,
    target,
    late_pack,
    mask_row,
    first,
    second,
    ok,
    *refs,
):
    *pieces, out, wide_even, wide_odd = refs
    place = col[0], low[0]
    rows, stride, channels = target.shape
    packs = (early_pack, late_pack)
    find = part_of(rows, NEAR, packs, (target,), packs[::-1])

    def picked(sources, part):
        return pick(odd_row(place), *[source[part] for source in sources]).astype(jnp.float32)

    def goal(row):
        sources, at = find(row)
        if len(sources) == 1:
            return target[at].astype(jnp.float32)
        return picked(sources, slice(at * stride, (at + 1) * stride))

    masks = [
        turned(picked(sources, slice(NEAR * stride, None))[:, :stride]) for sources in (packs, packs[::-1])
    ]
    find_mask = part_of(rows, NEAR, (masks[0], 0), (mask_row[0].astype(jnp.float32), 0), (masks[1], 0))

    def hole(row):
        (mask, start), at = find_mask(row)
        return mask[:, start + at : start + at + 1]

    def inside(row):
        return ok[REACH : REACH + stride, row : row + 1]

    count = NEAR
    for row in range(0, rows + 2 * NEAR, count):
        value = pre[pl.ds(row * stride, count * stride), :]
        put(wide_even, row, loss_grad(row, count, value, goal, hole, inside), stride)

    def use(row, count, value):
        value = value.reshape(count, stride, channels)[:, REACH : stride - REACH]
        out[row : row + count] = value.astype(jnp.bfloat16)

    last_stages(stride, TILE_BLOCKS, rows, first, second, wide_even, wide_odd, slopes, use)
    deal(place, out, pieces)


def side_kernel(col, low, early, late, own, first, second, ok, *refs):
    *pieces, out, wide_even, wide_odd, slopes = refs
    place = col[0], low[0]
    rows, _, channels = out.shape
    keep = 2 * REACH
    stride = 2 * (REACH + keep)
    tall = rows + 2 * REACH
    odd = odd_col(place)

    def feature(row):
        before, after = pick(odd, early[row], late[row]), pick(odd, late[row], early[row])
        parts = [part.astype(jnp.float32) for part in (before, own[row], after)]
        return jnp.concatenate(parts, axis=0)

    find = part_of(rows, NEAR, tall, tall + NEAR + 1, tall + NEAR + 1 + rows + 1)

    def goal(row):
        start, at = find(row)
        return feature(start + at)

    masks = [feature(row) for row in (tall + NEAR, tall + NEAR + 1 + rows, early.shape[0] - 1)]
    find_mask = part_of(rows, NEAR, (masks[0], 0), (masks[1], 0), (masks[2], 0))

    def hole(row):
        (mask, start), at = find_mask(row)
        return mask[:, start + at : start + at + 1]

    width = ok.shape[0]
    kept = jnp.concatenate([ok[: REACH + keep], ok[width - REACH - keep :]], axis=0)

    def inside(row):
        return kept[:, row : row + 1]

    def use_forward(row, count, value):
        put(wide_even, row, loss_grad(row, count, value, goal, hole, inside), stride)

    first_stages(
        stride, SIDE_BLOCKS, rows, feature, inside, first, second, wide_even, wide_odd, slopes, use_forward
    )

    def use(row, count, value):
        value = value.reshape(count, stride, channels).astype(jnp.bfloat16)
        out[row : row + count, :REACH] = value[:, REACH : 2 * REACH]
        out[row : row + count, REACH:] = value[:, stride - 2 * REACH : stride - REACH]

    last_stages(stride, SIDE_BLOCKS, rows, first, second, wide_even, wide_odd, slopes, use)
    deal(place, out, pieces)


def wide_buffer(rows, stride, channels):
    return pltpu.VMEM((rows * stride, 3 * channels), jnp.bfloat16)


def tile_forward(place, early, features, late, first, second, ok):
    rows, stride, channels = features.shape
    shapes = [
        jax.ShapeDtypeStruct(((rows + h) * stride, channels), jnp.float32) for h in (2 * NEAR, 4)
    ]
    in_vmem = pl.BlockSpec(memory_space=pltpu.VMEM)
    return pl.pallas_call(
        tile_forward_kernel,
        out_shape=shapes,
        in_specs=[pl.BlockSpec(memory_space=pltpu.SMEM)] * 2 + [in_vmem] * 6,
        out_specs=[in_vmem] * 2,
        scratch_shapes=[wide_buffer(rows + h, stride, channels) for h in (16, 12)],
        compiler_params=pltpu.CompilerParams(vmem_limit_bytes=18 * MIB),
        cost_estimate=pl.CostEstimate(
            flops=2 * 9 * channels * channels * stride * (2 * rows + 20),
            bytes_accessed=8 * MIB,
            transcendentals=0,
        ),
    )(*place, early, features, late, first, second, ok)


def piece_shapes(rows, columns, channels):
    count = lax.axis_size("col")
    return [jax.ShapeDtypeStruct((rows // count, columns, channels), jnp.bfloat16)] * count


def tile_backward(place, pre, slopes, early_pack, target, *operands):
    rows, stride, channels = target.shape
    in_vmem = pl.BlockSpec(memory_space=pltpu.VMEM)
    shapes = piece_shapes(rows, stride - 2 * REACH, channels)
    return pl.pallas_call(
        tile_backward_kernel,
        out_shape=shapes,
        in_specs=[pl.BlockSpec(memory_space=pltpu.SMEM)] * 2 + [in_vmem] * (4 + len(operands)),
        out_specs=[in_vmem] * len(shapes),
        scratch_shapes=[
            pltpu.VMEM((rows, stride - 2 * REACH, channels), jnp.bfloat16),
            *[wide_buffer(rows + h, stride, channels) for h in (8, 4)],
        ],
        compiler_params=pltpu.CompilerParams(vmem_limit_bytes=16 * MIB),
        cost_estimate=pl.CostEstimate(
            flops=2 * 9 * channels * channels * stride * (2 * rows + 4),
            bytes_accessed=8 * MIB,
            transcendentals=0,
        ),
    )(*place, pre, slopes, early_pack, target, *operands)


def sides(place, shape, *operands):
    rows, _, channels = shape
    stride = 6 * REACH
    in_vmem = pl.BlockSpec(memory_space=pltpu.VMEM)
    shapes = piece_shapes(rows, 2 * REACH, channels)
    return pl.pallas_call(
        side_kernel,
        out_shape=shapes,
        in_specs=[pl.BlockSpec(memory_space=pltpu.SMEM)] * 2 + [in_vmem] * len(operands),
        out_specs=[in_vmem] * len(shapes),
        scratch_shapes=[
            pltpu.VMEM((rows, 2 * REACH, channels), jnp.bfloat16),
            *[wide_buffer(rows + h, stride, channels) for h in (16, 12)],
            pltpu.VMEM(((rows + 4) * stride, channels), jnp.float32),
        ],
        compiler_params=pltpu.CompilerParams(vmem_limit_bytes=14 * MIB),
        cost_estimate=pl.CostEstimate(
            flops=2 * 9 * channels * channels * stride * (4 * rows + 24),
            bytes_accessed=4 * MIB,
            transcendentals=0,
        ),
    )(*place, *operands)


def pairs(axis, start):
    size = lax.axis_size(axis)
    up = [(i, i + 1) for i in range(start, size - 1, 2)]
    return up + [(j, i) for i, j in up]


def shards(
    features,
    target,
    hole_mask,
    kernel_first,
    kernel_second,
    inputs,
    weight_in,
    weight_out,
    weight_local,
    weight_mix,
):
    tile_rows, tile_cols, channels = features.shape
    row_devices, col_devices = lax.axis_size("row"), lax.axis_size("col")
    devices = row_devices * col_devices
    height, width = tile_rows * row_devices, tile_cols * col_devices
    strip, half = inputs.shape[0], weight_in.shape[1]
    owned = width // 2 // devices
    col_norm, row_norm = 1.0 / math.sqrt(width), 1.0 / math.sqrt(height)
    table = column_matrix(width, devices)
    table_back = jnp.asarray(np.ascontiguousarray(table.T))
    table = jnp.asarray(table)
    row_table = row_matrix(height, row_devices, col_devices)
    row_back = jnp.asarray(np.ascontiguousarray(row_table.T))
    row_table = jnp.asarray(row_table)
    bf16 = jnp.bfloat16

    def swap(spectrum):
        return lax.all_to_all(spectrum, ("col", "row"), split_axis=0, concat_axis=0, tiled=True)

    row0, col0 = lax.axis_index("row") * tile_rows, lax.axis_index("col") * tile_cols
    row_ids = row0 - REACH + jnp.arange(tile_rows + 2 * REACH, dtype=jnp.int32)
    col_ids = col0 - REACH + jnp.arange(tile_cols + 2 * REACH, dtype=jnp.int32)
    ok = ((col_ids >= 0) & (col_ids < width))[:, None] & ((row_ids >= 0) & (row_ids < height))[None]
    ok = ok.astype(jnp.float32)
    place = tuple(jnp.full((1,), i, jnp.int32) for i in (lax.axis_index("col"), lax.axis_index("row") & 1))
    early_pack, late_pack, mask_row = target_packs(place, target, hole_mask)
    inputs, ok, early_pack = lax.optimization_barrier((inputs, ok, early_pack))

    cells = [jax.ShapeDtypeStruct((width, strip * half), bf16)]
    weight_in = weight_in.T
    spatial_cols = fetching_spectrum(col_norm, cells[0], inputs, weight_in, table)
    spatial_moved = swap(spatial_cols)

    early = lax.ppermute(features, "row", pairs("row", 0))
    late = lax.ppermute(features, "row", pairs("row", 1))
    kernel_first, spatial_cols = lax.optimization_barrier((kernel_first, spatial_cols))
    kernel_first, kernel_second = fetch(kernel_first, kernel_second)
    early_pack = lax.ppermute(early_pack, "row", pairs("row", 0))
    late_pack = lax.ppermute(late_pack, "row", pairs("row", 1))
    pre, slopes = tile_forward(place, early, features, late, kernel_first, kernel_second, ok)
    early_pack, pre = lax.optimization_barrier((early_pack, pre))
    early_edge, late_edge, own = edges(
        place, early, late, features, target, mask_row, early_pack, late_pack
    )
    early_edge = lax.ppermute(early_edge, "col", pairs("col", 0))
    late_edge = lax.ppermute(late_edge, "col", pairs("col", 1))
    inner = tile_backward(
        place, pre, slopes, early_pack, target, late_pack, mask_row, kernel_first, kernel_second, ok
    )

    def dealt(pieces):
        result = []
        for piece, step in zip(pieces, steps_of(col_devices)):
            swaps = [(i, i ^ step) for i in range(col_devices)]
            result.append(lax.ppermute(piece, "col", swaps) if step else piece)
        return result

    inner = dealt(inner)
    outer = sides(
        place, features.shape, early_edge, late_edge, own, kernel_first, kernel_second, ok
    )
    *outer, spatial_moved = lax.optimization_barrier((*outer, spatial_moved))
    outer = dealt(outer)

    cell_count = height * owned
    wide = [pltpu.VMEM((strip * half // LANES, width, LANES), jnp.float32)]
    slope = vmem_call(
        functools.partial(slope_kernel, row_norm, owned, devices),
        [jax.ShapeDtypeStruct((2, cell_count, half), jnp.float32)],
        spatial_moved,
        weight_mix,
        row_table,
        scratch=wide,
    )[0]
    outer[0], slope = lax.optimization_barrier((outer[0], slope))
    grad_cols, strip_grad = grad_spectrum(col_norm, place, inner, outer, weight_out, table)
    grad_rows = vmem_call(
        functools.partial(mix_kernel, row_norm, owned, devices),
        cells,
        swap(grad_cols),
        slope,
        weight_mix,
        row_table,
        row_back,
        scratch=wide,
    )[0]
    returned = swap(grad_rows)
    return output(col_norm, inputs.shape, returned, strip_grad, weight_in, weight_local, table_back)


def solution(mesh):
    in_specs = (
        P("row", "col", None),
        P("row", "col", None),
        P("row", "col"),
        P(),
        P(),
        P(("row", "col"), None, None),
        P(),
        P(),
        P(),
        P(),
    )
    out_specs = P(("row", "col"), None, None)
    return jax.shard_map(shards, mesh=mesh, in_specs=in_specs, out_specs=out_specs, check_vma=False)
```

```python
import functools
import math

import jax
import jax.numpy as jnp
import ml_dtypes
import numpy as np
from jax import lax
from jax.experimental import pallas as pl
from jax.experimental.pallas import tpu as pltpu
from jax.sharding import PartitionSpec as P

REACH = 8
NEAR = 4
MIB = 1024 * 1024
LANES = 128


def dot(left, right):
    return jnp.dot(left, right, preferred_element_type=jnp.float32)


def dot_t(left, right):
    return lax.dot_general(left, right, (((1,), (1,)), ((), ())), preferred_element_type=jnp.float32)


def vmem_call(body, shapes, *operands, flops=0, scratch=(), limit=10):
    spec = pl.BlockSpec(memory_space=pltpu.VMEM)
    size = sum(math.prod(a.shape) * a.dtype.itemsize for a in (*operands, *shapes))
    return pl.pallas_call(
        body,
        out_shape=shapes,
        in_specs=[spec] * len(operands),
        out_specs=[spec] * len(shapes),
        scratch_shapes=list(scratch),
        compiler_params=pltpu.CompilerParams(vmem_limit_bytes=limit * MIB),
        cost_estimate=pl.CostEstimate(flops=flops, bytes_accessed=size, transcendentals=0),
    )(*operands)


def in_hbm(array):
    return pltpu.with_memory_space_constraint(array, pltpu.HBM)


def phases(first, second, length):
    angle = (first[:, None] * second[None, :] % length) * (2.0 * math.pi / length)
    return np.cos(angle).astype(ml_dtypes.bfloat16), np.sin(angle).astype(ml_dtypes.bfloat16)


def column_matrix(width, devices):
    half = width // 2
    freq, col = np.arange(half), np.arange(width)
    cos, sin = phases(freq, col, width)
    sin[0] = (2 * (col % 2) - 1).astype(ml_dtypes.bfloat16)
    both = np.stack([cos, -sin]).reshape(2, devices, half // devices, width)
    return np.ascontiguousarray(both.transpose(1, 0, 2, 3)).reshape(width, width)


def row_matrix(height, row_devices, col_devices):
    devices = row_devices * col_devices
    strip = height // devices
    strips = np.arange(devices).reshape(row_devices, col_devices).T.reshape(-1)
    rows = (strips[None, :] * strip + np.arange(strip)[:, None]).reshape(-1)
    cos, sin = phases(np.arange(height), rows, height)
    return np.block([[cos, sin], [-sin, cos]])


def strip_row(signal, r):
    return jnp.concatenate([signal[block, r] for block in range(signal.shape[0])], axis=0)


def grad_kernel(norm, col, low, *refs):
    *pieces, weight, table, out, strip_out, projected = refs
    count = len(pieces) // 2
    _, strip, tile_cols, _ = strip_out.shape
    for step, inner, outer in zip(steps_of(count), pieces[:count], pieces[count:]):
        block = col[0] ^ step
        strip_out[block, :, REACH : tile_cols - REACH] = inner[...]
        strip_out[block, :, :REACH] = outer[:, :REACH]
        strip_out[block, :, tile_cols - REACH :] = outer[:, REACH:]
        rows = [dot_t(strip_out[block, r], weight[...]).astype(jnp.bfloat16) for r in range(strip)]
        where = pl.ds(pl.multiple_of(block * tile_cols, tile_cols), tile_cols)
        projected[where, :] = jnp.concatenate(rows, axis=1)
    out[...] = (dot(table[...], projected[...]) * norm).astype(jnp.bfloat16)


def grad_spectrum(norm, place, inner, outer, weight, table):
    strip, columns, channels = inner[0].shape
    shape = (table.shape[0], strip * weight.shape[0])
    in_vmem = pl.BlockSpec(memory_space=pltpu.VMEM)
    return pl.pallas_call(
        functools.partial(grad_kernel, norm),
        out_shape=[
            jax.ShapeDtypeStruct(shape, jnp.bfloat16),
            jax.ShapeDtypeStruct((len(inner), strip, columns + 2 * REACH, channels), jnp.bfloat16),
        ],
        in_specs=[pl.BlockSpec(memory_space=pltpu.SMEM)] * 2 + [in_vmem] * (2 * len(inner) + 2),
        out_specs=[in_vmem] * 2,
        scratch_shapes=[pltpu.VMEM(shape, jnp.bfloat16)],
        compiler_params=pltpu.CompilerParams(vmem_limit_bytes=10 * MIB),
        cost_estimate=pl.CostEstimate(flops=0, bytes_accessed=2 * MIB, transcendentals=0),
    )(*place, *inner, *outer, weight, table)


def fetching_spectrum_kernel(norm, signal, weight, table, out, signal_held, weight_held, table_held, sems):
    count = signal.shape[0]
    copies = [pltpu.make_async_copy(weight, weight_held, sems.at[0])]
    copies += [
        pltpu.make_async_copy(signal.at[r], signal_held.at[r], sems.at[1 + r]) for r in range(count)
    ]
    copies.append(pltpu.make_async_copy(table, table_held, sems.at[1 + count]))
    for copy in copies:
        copy.start()
    copies[0].wait()
    rows = []
    for r in range(count):
        copies[1 + r].wait()
        rows.append(dot_t(signal_held[r], weight_held[...]).astype(jnp.bfloat16))
    copies[-1].wait()
    out[...] = (dot(table_held[...], jnp.concatenate(rows, axis=1)) * norm).astype(jnp.bfloat16)


def fetching_spectrum(norm, shape, signal, weight, table):
    operands = (signal, weight, table)
    return pl.pallas_call(
        functools.partial(fetching_spectrum_kernel, norm),
        out_shape=shape,
        in_specs=[pl.BlockSpec(memory_space=pltpu.HBM)] * 3,
        out_specs=pl.BlockSpec(memory_space=pltpu.VMEM),
        scratch_shapes=[pltpu.VMEM(a.shape, a.dtype) for a in operands]
        + [pltpu.SemaphoreType.DMA((signal.shape[0] + 2,))],
        compiler_params=pltpu.CompilerParams(vmem_limit_bytes=12 * MIB),
        cost_estimate=pl.CostEstimate(
            flops=0, bytes_accessed=2 * MIB, transcendentals=0
        ),
    )(*[in_hbm(a) for a in operands])


def row_spectrum(moved, table, wide, norm, owned, devices):
    groups = wide.shape[0]
    for g in range(groups):
        wide[g] = moved[:, g * LANES : (g + 1) * LANES].astype(jnp.float32)
    strip = table.shape[1] // (2 * devices)
    half = moved.shape[1] // strip
    height = table.shape[0] // 2
    real, imag = [], []
    for freq in range(owned):
        parts = []
        for part in range(2):
            where = pl.ds(part * owned + freq, devices, stride=2 * owned)
            block = jnp.concatenate([wide[g, where, :] for g in range(groups)], axis=1)
            parts += [block[:, r * half : (r + 1) * half] for r in range(strip)]
        result = dot(table[...], jnp.concatenate(parts, axis=0).astype(jnp.bfloat16)) * norm
        real.append(result[:height])
        imag.append(result[height:])
    return jnp.concatenate(real, axis=0), jnp.concatenate(imag, axis=0)


def slope_kernel(norm, owned, devices, moved, mix, table, out, wide):
    parts = row_spectrum(moved, table, wide, norm, owned, devices)
    real, imag = [part.astype(jnp.bfloat16) for part in parts]
    half = real.shape[1]
    spans = (slice(0, half), slice(half, 2 * half))
    for part, span in enumerate(spans):
        pre = dot(real, mix[spans[0], span]) + dot(imag, mix[spans[1], span])
        s = 1.0 / (1.0 + jnp.exp(-pre))
        out[part] = s * (1.0 + pre * (1.0 - s))


def mix_kernel(norm, owned, devices, moved, slope, mix, table, back_table, out, wide):
    grads = row_spectrum(moved, table, wide, norm, owned, devices)
    half = grads[0].shape[1]
    spans = (slice(0, half), slice(half, 2 * half))
    mixed = [(grad * slope[part]).astype(jnp.bfloat16) for part, grad in enumerate(grads)]
    back = [dot_t(mixed[0], mix[p, spans[0]]) + dot_t(mixed[1], mix[p, spans[1]]) for p in spans]
    back = [part.astype(jnp.bfloat16) for part in back]
    height = table.shape[0] // 2
    strip = height // devices
    groups = wide.shape[0]
    for freq in range(owned):
        cells = slice(freq * height, (freq + 1) * height)
        stacked = jnp.concatenate([back[0][cells], back[1][cells]], axis=0)
        result = dot(back_table[...], stacked) * norm
        for part in range(2):
            rows = [
                result[(part * strip + r) * devices : (part * strip + r + 1) * devices]
                for r in range(strip)
            ]
            where = pl.ds(part * owned + freq, devices, stride=2 * owned)
            values = jnp.concatenate(rows, axis=1)
            for g in range(groups):
                wide[g, where, :] = values[:, g * LANES : (g + 1) * LANES]
    for g in range(groups):
        out[:, g * LANES : (g + 1) * LANES] = wide[g].astype(jnp.bfloat16)


def output_kernel(norm, moved, strip_grad, weight_in, weight_local, table, out, held, sems):
    spatial = (dot(table[...], moved[...]) * norm).astype(jnp.bfloat16)
    half = weight_in.shape[0]
    copies = []
    for r in range(out.shape[0]):
        total = dot(spatial[:, r * half : (r + 1) * half], weight_in[...])
        total = total + dot_t(strip_row(strip_grad, r), weight_local[...])
        held[r] = total.astype(jnp.bfloat16)
        copies.append(pltpu.make_async_copy(held.at[r], out.at[r], sems.at[r]))
        copies[-1].start()
    for copy in copies:
        copy.wait()


def output(norm, shape, *operands):
    return pl.pallas_call(
        functools.partial(output_kernel, norm),
        out_shape=jax.ShapeDtypeStruct(shape, jnp.bfloat16),
        in_specs=[pl.BlockSpec(memory_space=pltpu.VMEM)] * len(operands),
        out_specs=pl.BlockSpec(memory_space=pltpu.HBM),
        scratch_shapes=[pltpu.VMEM(shape, jnp.bfloat16), pltpu.SemaphoreType.DMA((shape[0],))],
        compiler_params=pltpu.CompilerParams(vmem_limit_bytes=10 * MIB),
        cost_estimate=pl.CostEstimate(flops=0, bytes_accessed=3 * MIB, transcendentals=0),
    )(*operands)


TAIL = 16


def pick(flag, left, right):
    return lax.select(flag, left, right)


def odd_row(place):
    return place[1] == 1


def odd_col(place):
    return lax.rem(place[0], 2) == 1


def turned(rows):
    count, columns = rows.shape
    rows = rows.astype(jnp.float32)
    return jnp.concatenate([rows, jnp.zeros((columns - count, columns), jnp.float32)], axis=0).T


def filled(lanes, channels):
    fill = jnp.zeros((lanes.shape[0], channels - lanes.shape[1]), jnp.float32)
    return jnp.concatenate([lanes, fill], axis=1).astype(jnp.bfloat16)


def pack_kernel(col, low, target, mask, early, late, mask_row, mask_held, sems):
    place = col[0], low[0]
    tile_rows, tile_cols = mask.shape
    channels = target.shape[1]
    last = tile_rows - NEAR
    pixels = NEAR * tile_cols
    moves = [(mask, mask_held)]
    for pack, row in ((early, (1 - place[1]) * last), (late, place[1] * last)):
        moves.append((target.at[pl.ds(row * tile_cols, pixels)], pack.at[pl.ds(0, pixels)]))
    copies = [pltpu.make_async_copy(*move, sems.at[i]) for i, move in enumerate(moves)]
    for copy in copies:
        copy.start()
    copies[0].wait()
    mask_row[0] = filled(turned(mask_held[...]), channels)
    ends = (mask_held[:NEAR], mask_held[last:])
    for pack, (one, other) in ((early, ends), (late, ends[::-1])):
        rows = pick(odd_row(place), one.astype(jnp.float32), other.astype(jnp.float32))
        rows = jnp.concatenate([rows, jnp.zeros((TAIL - NEAR, tile_cols), jnp.float32)], axis=0)
        pack[pixels:] = filled(rows, channels)
    for copy in copies[1:]:
        copy.wait()


def target_packs(place, target, mask):
    tile_rows, tile_cols, channels = target.shape
    pack = (NEAR * tile_cols + TAIL, channels)
    hbm = pl.BlockSpec(memory_space=pltpu.HBM)
    shapes = [pack, pack, (1, tile_cols, channels)]
    return pl.pallas_call(
        pack_kernel,
        out_shape=[jax.ShapeDtypeStruct(shape, jnp.bfloat16) for shape in shapes],
        in_specs=[pl.BlockSpec(memory_space=pltpu.SMEM)] * 2 + [hbm, hbm],
        out_specs=[pl.BlockSpec(memory_space=pltpu.VMEM)] * len(shapes),
        scratch_shapes=[pltpu.VMEM(mask.shape, mask.dtype), pltpu.SemaphoreType.DMA((3,))],
        compiler_params=pltpu.CompilerParams(vmem_limit_bytes=4 * MIB),
        cost_estimate=pl.CostEstimate(flops=0, bytes_accessed=MIB, transcendentals=0),
    )(*place, in_hbm(target.reshape(tile_rows * tile_cols, channels)), in_hbm(mask))


def fetch_kernel(*refs):
    count = len(refs) // 2
    sems = refs[-1]
    copies = [pltpu.make_async_copy(refs[i], refs[count + i], sems.at[i]) for i in range(count)]
    for copy in copies:
        copy.start()
    for copy in copies:
        copy.wait()


def fetch(*arrays):
    return pl.pallas_call(
        fetch_kernel,
        out_shape=[jax.ShapeDtypeStruct(a.shape, a.dtype) for a in arrays],
        in_specs=[pl.BlockSpec(memory_space=pltpu.HBM)] * len(arrays),
        out_specs=[pl.BlockSpec(memory_space=pltpu.VMEM)] * len(arrays),
        scratch_shapes=[pltpu.SemaphoreType.DMA((len(arrays),))],
        compiler_params=pltpu.CompilerParams(vmem_limit_bytes=4 * MIB),
        cost_estimate=pl.CostEstimate(flops=0, bytes_accessed=5 * MIB, transcendentals=0),
    )(*[in_hbm(a) for a in arrays])


def edge_kernel(tile_cols, col, low, early_pack, late_pack, *refs):
    place = col[0], low[0]
    sources, (early, late, own) = refs[:-3], refs[-3:]
    count = len(sources) // 2
    keep = 2 * REACH
    channels = own.shape[2]
    lower, high = odd_row(place), odd_col(place)

    def put_rows(row, tail, head):
        rows = slice(row, row + tail.shape[0])
        last, initial = tail[:, REACH:], head[:, :REACH]
        early[rows] = pick(high, initial, last)
        late[rows] = pick(high, last, initial)
        own[rows, :keep] = head
        own[rows, keep:] = tail

    def put_pack(row, one, other):
        for i in range(NEAR):
            at = i * tile_cols
            tail = pick(lower, one[at + tile_cols - keep : at + tile_cols], other[at + tile_cols - keep : at + tile_cols])
            head = pick(lower, one[at : at + keep], other[at : at + keep])
            put_rows(row + i, tail[None], head[None])
        mask = turned(pick(lower, one[NEAR * tile_cols :, :tile_cols], other[NEAR * tile_cols :, :tile_cols]))
        tail, head = [filled(m, channels)[None] for m in (mask[tile_cols - keep :], mask[:keep])]
        put_rows(row + NEAR, tail, head)

    def put_picked(row, one, other):
        put_rows(row, *[pick(lower, sources[one + i * count][...], sources[other + i * count][...]) for i in (0, 1)])

    def put_own(row, index):
        put_rows(row, sources[index][...], sources[index + count][...])

    rows = sources[0].shape[0]
    put_picked(0, 0, 1)
    put_own(rows, 2)
    put_picked(2 * rows, 1, 0)
    put_pack(3 * rows, early_pack, late_pack)
    put_own(3 * rows + NEAR + 1, 3)
    put_own(4 * rows + NEAR + 1, 4)
    put_pack(4 * rows + NEAR + 2, late_pack, early_pack)


def edges(place, early, late, features, target, mask_row, early_pack, late_pack):
    parts = (early, late, features, target, mask_row)
    _, tile_cols, channels = features.shape
    keep = 2 * REACH
    tail = tile_cols // keep - 1

    def specs(at):
        return [pl.BlockSpec((p.shape[0], keep, channels), lambda i, at=at: (0, at, 0)) for p in parts]

    whole = [pl.BlockSpec(early_pack.shape, lambda i: (0, 0))] * 2
    rows = sum(p.shape[0] for p in parts) + 2 * (NEAR + 1)
    shapes = [(rows, columns, channels) for columns in (REACH, REACH, 2 * keep)]
    return pl.pallas_call(
        functools.partial(edge_kernel, tile_cols),
        grid=(1,),
        out_shape=[jax.ShapeDtypeStruct(shape, features.dtype) for shape in shapes],
        in_specs=[pl.BlockSpec(memory_space=pltpu.SMEM)] * 2 + whole + specs(tail) + specs(0),
        out_specs=[pl.BlockSpec(shape, lambda i: (0, 0, 0)) for shape in shapes],
        compiler_params=pltpu.CompilerParams(vmem_limit_bytes=8 * MIB),
        cost_estimate=pl.CostEstimate(
            flops=0, bytes_accessed=16 * rows * keep * channels, transcendentals=0
        ),
    )(*place, early_pack, late_pack, *parts, *parts)


def put(wide, row, value, stride):
    size, channels = value.shape
    spot = pl.ds(row * stride, size)
    wide[spot, :channels] = pltpu.roll(value, 2, 0).astype(jnp.bfloat16)
    wide[spot, channels : 2 * channels] = value.astype(jnp.bfloat16)
    wide[spot, 2 * channels :] = pltpu.roll(value, size - 2, 0).astype(jnp.bfloat16)


def taps(wide, row, count, stride):
    parts = [wide[pl.ds((row + 2 * a) * stride, count * stride), :] for a in range(3)]
    return jnp.concatenate(parts, axis=1)


def conv(wide, row, count, stride, kernel):
    channels = kernel.shape[-1]
    return dot(taps(wide, row, count, stride), kernel[...].reshape(9 * channels, channels))


def conv_adjoint(wide, row, count, stride, kernel):
    flipped = [kernel[2 - a, 2 - b] for a in range(3) for b in range(3)]
    return dot_t(taps(wide, row, count, stride), jnp.concatenate(flipped, axis=1))


def stacked(piece, rows):
    return jnp.concatenate([piece(row) for row in rows], axis=0)


def first_stages(
    stride, blocks, rows, feature, inside, first, second, wide_even, wide_odd, slopes, use
):
    tall = rows + 2 * REACH
    for row in range(0, tall, NEAR):
        put(wide_even, row, stacked(feature, range(row, row + NEAR)), stride)
    count = blocks[0]
    for row in range(0, tall - 4, count):
        pre = conv(wide_even, row, count, stride, first)
        s = 1.0 / (1.0 + jnp.exp(-pre))
        kept = stacked(inside, range(row + 2, row + 2 + count))
        put(wide_odd, row, pre * s * kept, stride)
        low, high = max(row, NEAR), min(row + count, tall - 4 - NEAR)
        if low < high:
            part = slice((low - row) * stride, (high - row) * stride)
            slope = (s * (1.0 + pre * (1.0 - s)) * kept)[part]
            slopes[pl.ds((low - NEAR) * stride, (high - low) * stride), :] = slope
    count = blocks[1]
    for row in range(0, rows + 2 * NEAR, count):
        use(row, count, conv(wide_odd, row, count, stride, second))


def last_stages(stride, blocks, rows, first, second, wide_even, wide_odd, slopes, use):
    count = blocks[2]
    for row in range(0, rows + 4, count):
        value = conv_adjoint(wide_even, row, count, stride, second)
        value = value * slopes[pl.ds(row * stride, count * stride), :]
        put(wide_odd, row, value, stride)
    count = blocks[3]
    for row in range(0, rows, count):
        use(row, count, conv_adjoint(wide_odd, row, count, stride, first))


def steps_of(count):
    return [0, *range(2, count), 1] if count > 1 else [0]


def deal(place, out, pieces):
    for step, piece in zip(steps_of(len(pieces)), pieces):
        piece[...] = out[pl.ds((place[0] ^ step) * piece.shape[0], piece.shape[0])]


def loss_grad(row, count, value, target, hole, inside):
    near = range(row, row + count)
    weight = (1.0 + 2.0 * stacked(hole, near)) * stacked(inside, range(row + NEAR, row + count + NEAR))
    return weight * (value - stacked(target, near))


def part_of(rows, edge, above, own, below):
    def find(row):
        if row < edge:
            return above, row
        if row < edge + rows:
            return own, row - edge
        return below, row - edge - rows

    return find


TILE_BLOCKS = (10, 8, 6, 8)
SIDE_BLOCKS = (20, 16, 12, 8)


def tile_forward_kernel(
    col, low, early, features, late, first, second, ok, pre, slopes, wide_even, wide_odd
):
    place = col[0], low[0]
    rows, stride, _ = features.shape
    find = part_of(rows, REACH, (early, late), (features,), (late, early))

    def feature(row):
        sources, at = find(row)
        if len(sources) == 1:
            return features[at].astype(jnp.float32)
        return pick(odd_row(place), *[source[at] for source in sources]).astype(jnp.float32)

    def inside(row):
        return ok[REACH : REACH + stride, row : row + 1]

    def use(row, count, value):
        pre[pl.ds(row * stride, count * stride), :] = value

    first_stages(
        stride, TILE_BLOCKS, rows, feature, inside, first, second, wide_even, wide_odd, slopes, use
    )


def tile_backward_kernel(
    col,
    low,
    pre,
    slopes,
    early_pack,
    target,
    late_pack,
    mask_row,
    first,
    second,
    ok,
    *refs,
):
    *pieces, out, wide_even, wide_odd = refs
    place = col[0], low[0]
    rows, stride, channels = target.shape
    packs = (early_pack, late_pack)
    find = part_of(rows, NEAR, packs, (target,), packs[::-1])

    def picked(sources, part):
        return pick(odd_row(place), *[source[part] for source in sources]).astype(jnp.float32)

    def goal(row):
        sources, at = find(row)
        if len(sources) == 1:
            return target[at].astype(jnp.float32)
        return picked(sources, slice(at * stride, (at + 1) * stride))

    masks = [
        turned(picked(sources, slice(NEAR * stride, None))[:, :stride]) for sources in (packs, packs[::-1])
    ]
    find_mask = part_of(rows, NEAR, (masks[0], 0), (mask_row[0].astype(jnp.float32), 0), (masks[1], 0))

    def hole(row):
        (mask, start), at = find_mask(row)
        return mask[:, start + at : start + at + 1]

    def inside(row):
        return ok[REACH : REACH + stride, row : row + 1]

    count = NEAR
    for row in range(0, rows + 2 * NEAR, count):
        value = pre[pl.ds(row * stride, count * stride), :]
        put(wide_even, row, loss_grad(row, count, value, goal, hole, inside), stride)

    def use(row, count, value):
        value = value.reshape(count, stride, channels)[:, REACH : stride - REACH]
        out[row : row + count] = value.astype(jnp.bfloat16)

    last_stages(stride, TILE_BLOCKS, rows, first, second, wide_even, wide_odd, slopes, use)
    deal(place, out, pieces)


def side_kernel(col, low, late, early, own, first, second, ok, *refs):
    *pieces, out, wide_even, wide_odd, slopes = refs
    place = col[0], low[0]
    rows, _, channels = out.shape
    keep = 2 * REACH
    stride = 2 * (REACH + keep)
    tall = rows + 2 * REACH
    odd = odd_col(place)

    def feature(row):
        before, after = pick(odd, early[row], late[row]), pick(odd, late[row], early[row])
        parts = [part.astype(jnp.float32) for part in (before, own[row], after)]
        return jnp.concatenate(parts, axis=0)

    find = part_of(rows, NEAR, tall, tall + NEAR + 1, tall + NEAR + 1 + rows + 1)

    def goal(row):
        start, at = find(row)
        return feature(start + at)

    masks = [feature(row) for row in (tall + NEAR, tall + NEAR + 1 + rows, early.shape[0] - 1)]
    find_mask = part_of(rows, NEAR, (masks[0], 0), (masks[1], 0), (masks[2], 0))

    def hole(row):
        (mask, start), at = find_mask(row)
        return mask[:, start + at : start + at + 1]

    width = ok.shape[0]
    kept = jnp.concatenate([ok[: REACH + keep], ok[width - REACH - keep :]], axis=0)

    def inside(row):
        return kept[:, row : row + 1]

    def use_forward(row, count, value):
        put(wide_even, row, loss_grad(row, count, value, goal, hole, inside), stride)

    first_stages(
        stride, SIDE_BLOCKS, rows, feature, inside, first, second, wide_even, wide_odd, slopes, use_forward
    )

    def use(row, count, value):
        value = value.reshape(count, stride, channels).astype(jnp.bfloat16)
        out[row : row + count, :REACH] = value[:, REACH : 2 * REACH]
        out[row : row + count, REACH:] = value[:, stride - 2 * REACH : stride - REACH]

    last_stages(stride, SIDE_BLOCKS, rows, first, second, wide_even, wide_odd, slopes, use)
    deal(place, out, pieces)


def wide_buffer(rows, stride, channels):
    return pltpu.VMEM((rows * stride, 3 * channels), jnp.bfloat16)


def tile_forward(place, early, features, late, first, second, ok):
    rows, stride, channels = features.shape
    shapes = [
        jax.ShapeDtypeStruct(((rows + h) * stride, channels), jnp.float32) for h in (2 * NEAR, 4)
    ]
    in_vmem = pl.BlockSpec(memory_space=pltpu.VMEM)
    return pl.pallas_call(
        tile_forward_kernel,
        out_shape=shapes,
        in_specs=[pl.BlockSpec(memory_space=pltpu.SMEM)] * 2 + [in_vmem] * 6,
        out_specs=[in_vmem] * 2,
        scratch_shapes=[wide_buffer(rows + h, stride, channels) for h in (16, 12)],
        compiler_params=pltpu.CompilerParams(vmem_limit_bytes=22 * MIB),
        cost_estimate=pl.CostEstimate(
            flops=2 * 9 * channels * channels * stride * (2 * rows + 20),
            bytes_accessed=8 * MIB,
            transcendentals=0,
        ),
    )(*place, early, features, late, first, second, ok)


def piece_shapes(rows, columns, channels):
    count = lax.axis_size("col")
    return [jax.ShapeDtypeStruct((rows // count, columns, channels), jnp.bfloat16)] * count


def tile_backward(place, pre, slopes, early_pack, target, *operands):
    rows, stride, channels = target.shape
    in_vmem = pl.BlockSpec(memory_space=pltpu.VMEM)
    shapes = piece_shapes(rows, stride - 2 * REACH, channels)
    return pl.pallas_call(
        tile_backward_kernel,
        out_shape=shapes,
        in_specs=[pl.BlockSpec(memory_space=pltpu.SMEM)] * 2 + [in_vmem] * (4 + len(operands)),
        out_specs=[in_vmem] * len(shapes),
        scratch_shapes=[
            pltpu.VMEM((rows, stride - 2 * REACH, channels), jnp.bfloat16),
            *[wide_buffer(rows + h, stride, channels) for h in (8, 4)],
        ],
        compiler_params=pltpu.CompilerParams(vmem_limit_bytes=16 * MIB),
        cost_estimate=pl.CostEstimate(
            flops=2 * 9 * channels * channels * stride * (2 * rows + 4),
            bytes_accessed=8 * MIB,
            transcendentals=0,
        ),
    )(*place, pre, slopes, early_pack, target, *operands)


def sides(place, shape, *operands):
    rows, _, channels = shape
    stride = 6 * REACH
    in_vmem = pl.BlockSpec(memory_space=pltpu.VMEM)
    shapes = piece_shapes(rows, 2 * REACH, channels)
    return pl.pallas_call(
        side_kernel,
        out_shape=shapes,
        in_specs=[pl.BlockSpec(memory_space=pltpu.SMEM)] * 2 + [in_vmem] * len(operands),
        out_specs=[in_vmem] * len(shapes),
        scratch_shapes=[
            pltpu.VMEM((rows, 2 * REACH, channels), jnp.bfloat16),
            *[wide_buffer(rows + h, stride, channels) for h in (16, 12)],
            pltpu.VMEM(((rows + 4) * stride, channels), jnp.float32),
        ],
        compiler_params=pltpu.CompilerParams(vmem_limit_bytes=18 * MIB),
        cost_estimate=pl.CostEstimate(
            flops=2 * 9 * channels * channels * stride * (4 * rows + 24),
            bytes_accessed=4 * MIB,
            transcendentals=0,
        ),
    )(*place, *operands)


def pairs(axis, start):
    size = lax.axis_size(axis)
    up = [(i, i + 1) for i in range(start, size - 1, 2)]
    return up + [(j, i) for i, j in up]


def shards(
    features,
    target,
    hole_mask,
    kernel_first,
    kernel_second,
    inputs,
    weight_in,
    weight_out,
    weight_local,
    weight_mix,
):
    tile_rows, tile_cols, channels = features.shape
    row_devices, col_devices = lax.axis_size("row"), lax.axis_size("col")
    devices = row_devices * col_devices
    height, width = tile_rows * row_devices, tile_cols * col_devices
    strip, half = inputs.shape[0], weight_in.shape[1]
    owned = width // 2 // devices
    col_norm, row_norm = 1.0 / math.sqrt(width), 1.0 / math.sqrt(height)
    table = column_matrix(width, devices)
    table_back = jnp.asarray(np.ascontiguousarray(table.T))
    table = jnp.asarray(table)
    row_table = row_matrix(height, row_devices, col_devices)
    row_back = jnp.asarray(np.ascontiguousarray(row_table.T))
    row_table = jnp.asarray(row_table)
    bf16 = jnp.bfloat16

    def swap(spectrum):
        return lax.all_to_all(spectrum, ("col", "row"), split_axis=0, concat_axis=0, tiled=True)

    row0, col0 = lax.axis_index("row") * tile_rows, lax.axis_index("col") * tile_cols
    row_ids = row0 - REACH + jnp.arange(tile_rows + 2 * REACH, dtype=jnp.int32)
    col_ids = col0 - REACH + jnp.arange(tile_cols + 2 * REACH, dtype=jnp.int32)
    ok = ((col_ids >= 0) & (col_ids < width))[:, None] & ((row_ids >= 0) & (row_ids < height))[None]
    ok = ok.astype(jnp.float32)
    place = tuple(jnp.full((1,), i, jnp.int32) for i in (lax.axis_index("col"), lax.axis_index("row") & 1))
    early_pack, late_pack, mask_row = target_packs(place, target, hole_mask)
    inputs, ok, early_pack = lax.optimization_barrier((inputs, ok, early_pack))

    cells = [jax.ShapeDtypeStruct((width, strip * half), bf16)]
    weight_in = weight_in.T
    spatial_cols = fetching_spectrum(col_norm, cells[0], inputs, weight_in, table)
    spatial_moved = swap(spatial_cols)

    early = lax.ppermute(features, "row", pairs("row", 0))
    late = lax.ppermute(features, "row", pairs("row", 1))
    kernel_first, spatial_cols = lax.optimization_barrier((kernel_first, spatial_cols))
    kernel_first, kernel_second = fetch(kernel_first, kernel_second)
    early_pack = lax.ppermute(early_pack, "row", pairs("row", 0))
    late_pack = lax.ppermute(late_pack, "row", pairs("row", 1))
    pre, slopes = tile_forward(place, early, features, late, kernel_first, kernel_second, ok)
    early_pack, pre = lax.optimization_barrier((early_pack, pre))
    early_edge, late_edge, own = edges(
        place, early, late, features, target, mask_row, early_pack, late_pack
    )
    late_edge = lax.ppermute(late_edge, "col", pairs("col", 1))
    early_edge = lax.ppermute(early_edge, "col", pairs("col", 0))
    inner = tile_backward(
        place, pre, slopes, early_pack, target, late_pack, mask_row, kernel_first, kernel_second, ok
    )

    def dealt(pieces):
        result = []
        for piece, step in zip(pieces, steps_of(col_devices)):
            swaps = [(i, i ^ step) for i in range(col_devices)]
            result.append(lax.ppermute(piece, "col", swaps) if step else piece)
        return result

    inner = dealt(inner)
    outer = sides(
        place, features.shape, late_edge, early_edge, own, kernel_first, kernel_second, ok
    )
    *outer, spatial_moved = lax.optimization_barrier((*outer, spatial_moved))
    outer = dealt(outer)

    cell_count = height * owned
    wide = [pltpu.VMEM((strip * half // LANES, width, LANES), jnp.float32)]
    slope = vmem_call(
        functools.partial(slope_kernel, row_norm, owned, devices),
        [jax.ShapeDtypeStruct((2, cell_count, half), jnp.float32)],
        spatial_moved,
        weight_mix,
        row_table,
        scratch=wide,
    )[0]
    outer[0], slope = lax.optimization_barrier((outer[0], slope))
    grad_cols, strip_grad = grad_spectrum(col_norm, place, inner, outer, weight_out, table)
    grad_rows = vmem_call(
        functools.partial(mix_kernel, row_norm, owned, devices),
        cells,
        swap(grad_cols),
        slope,
        weight_mix,
        row_table,
        row_back,
        scratch=wide,
    )[0]
    returned = swap(grad_rows)
    return output(col_norm, inputs.shape, returned, strip_grad, weight_in, weight_local, table_back)


def solution(mesh):
    in_specs = (
        P("row", "col", None),
        P("row", "col", None),
        P("row", "col"),
        P(),
        P(),
        P(("row", "col"), None, None),
        P(),
        P(),
        P(),
        P(),
    )
    out_specs = P(("row", "col"), None, None)
    return jax.shard_map(shards, mesh=mesh, in_specs=in_specs, out_specs=out_specs, check_vma=False)
```

```python
import functools
import math

import jax
import jax.numpy as jnp
import ml_dtypes
import numpy as np
from jax import lax
from jax.experimental import pallas as pl
from jax.experimental.pallas import tpu as pltpu
from jax.sharding import PartitionSpec as P

REACH = 8
NEAR = 4
MIB = 1024 * 1024
LANES = 128


def dot(left, right):
    return jnp.dot(left, right, preferred_element_type=jnp.float32)


def dot_t(left, right):
    return lax.dot_general(left, right, (((1,), (1,)), ((), ())), preferred_element_type=jnp.float32)


def vmem_call(body, shapes, *operands, flops=0, scratch=(), limit=10):
    spec = pl.BlockSpec(memory_space=pltpu.VMEM)
    size = sum(math.prod(a.shape) * a.dtype.itemsize for a in (*operands, *shapes))
    return pl.pallas_call(
        body,
        out_shape=shapes,
        in_specs=[spec] * len(operands),
        out_specs=[spec] * len(shapes),
        scratch_shapes=list(scratch),
        compiler_params=pltpu.CompilerParams(vmem_limit_bytes=limit * MIB),
        cost_estimate=pl.CostEstimate(flops=flops, bytes_accessed=size, transcendentals=0),
    )(*operands)


def in_hbm(array):
    return pltpu.with_memory_space_constraint(array, pltpu.HBM)


def phases(first, second, length):
    angle = (first[:, None] * second[None, :] % length) * (2.0 * math.pi / length)
    return np.cos(angle).astype(ml_dtypes.bfloat16), np.sin(angle).astype(ml_dtypes.bfloat16)


def column_matrix(width, devices):
    half = width // 2
    freq, col = np.arange(half), np.arange(width)
    cos, sin = phases(freq, col, width)
    sin[0] = (2 * (col % 2) - 1).astype(ml_dtypes.bfloat16)
    both = np.stack([cos, -sin]).reshape(2, devices, half // devices, width)
    return np.ascontiguousarray(both.transpose(1, 0, 2, 3)).reshape(width, width)


def row_matrix(height, row_devices, col_devices):
    devices = row_devices * col_devices
    strip = height // devices
    strips = np.arange(devices).reshape(row_devices, col_devices).T.reshape(-1)
    rows = (strips[None, :] * strip + np.arange(strip)[:, None]).reshape(-1)
    cos, sin = phases(np.arange(height), rows, height)
    return np.block([[cos, sin], [-sin, cos]])


def strip_row(signal, r):
    return jnp.concatenate([signal[block, r] for block in range(signal.shape[0])], axis=0)


def grad_kernel(norm, col, low, *refs):
    *pieces, weight, table, out, strip_out, projected = refs
    count = len(pieces) // 2
    _, strip, tile_cols, _ = strip_out.shape
    for step, inner, outer in zip(steps_of(count), pieces[:count], pieces[count:]):
        block = col[0] ^ step
        strip_out[block, :, REACH : tile_cols - REACH] = inner[...]
        strip_out[block, :, :REACH] = outer[:, :REACH]
        strip_out[block, :, tile_cols - REACH :] = outer[:, REACH:]
        rows = [dot_t(strip_out[block, r], weight[...]).astype(jnp.bfloat16) for r in range(strip)]
        where = pl.ds(pl.multiple_of(block * tile_cols, tile_cols), tile_cols)
        projected[where, :] = jnp.concatenate(rows, axis=1)
    out[...] = (dot(table[...], projected[...]) * norm).astype(jnp.bfloat16)


def grad_spectrum(norm, place, inner, outer, weight, table):
    strip, columns, channels = inner[0].shape
    shape = (table.shape[0], strip * weight.shape[0])
    in_vmem = pl.BlockSpec(memory_space=pltpu.VMEM)
    return pl.pallas_call(
        functools.partial(grad_kernel, norm),
        out_shape=[
            jax.ShapeDtypeStruct(shape, jnp.bfloat16),
            jax.ShapeDtypeStruct((len(inner), strip, columns + 2 * REACH, channels), jnp.bfloat16),
        ],
        in_specs=[pl.BlockSpec(memory_space=pltpu.SMEM)] * 2 + [in_vmem] * (2 * len(inner) + 2),
        out_specs=[in_vmem] * 2,
        scratch_shapes=[pltpu.VMEM(shape, jnp.bfloat16)],
        compiler_params=pltpu.CompilerParams(vmem_limit_bytes=10 * MIB),
        cost_estimate=pl.CostEstimate(flops=0, bytes_accessed=2 * MIB, transcendentals=0),
    )(*place, *inner, *outer, weight, table)


def fetching_spectrum_kernel(norm, signal, weight, table, out, signal_held, weight_held, table_held, sems):
    count = signal.shape[0]
    copies = [pltpu.make_async_copy(weight, weight_held, sems.at[0])]
    copies += [
        pltpu.make_async_copy(signal.at[r], signal_held.at[r], sems.at[1 + r]) for r in range(count)
    ]
    copies.append(pltpu.make_async_copy(table, table_held, sems.at[1 + count]))
    for copy in copies:
        copy.start()
    copies[0].wait()
    rows = []
    for r in range(count):
        copies[1 + r].wait()
        rows.append(dot_t(signal_held[r], weight_held[...]).astype(jnp.bfloat16))
    copies[-1].wait()
    out[...] = (dot(table_held[...], jnp.concatenate(rows, axis=1)) * norm).astype(jnp.bfloat16)


def fetching_spectrum(norm, shape, signal, weight, table):
    operands = (signal, weight, table)
    return pl.pallas_call(
        functools.partial(fetching_spectrum_kernel, norm),
        out_shape=shape,
        in_specs=[pl.BlockSpec(memory_space=pltpu.HBM)] * 3,
        out_specs=pl.BlockSpec(memory_space=pltpu.VMEM),
        scratch_shapes=[pltpu.VMEM(a.shape, a.dtype) for a in operands]
        + [pltpu.SemaphoreType.DMA((signal.shape[0] + 2,))],
        compiler_params=pltpu.CompilerParams(vmem_limit_bytes=12 * MIB),
        cost_estimate=pl.CostEstimate(
            flops=0, bytes_accessed=2 * MIB, transcendentals=0
        ),
    )(*[in_hbm(a) for a in operands])


def row_spectrum(moved, table, wide, norm, owned, devices):
    groups = wide.shape[0]
    for g in range(groups):
        wide[g] = moved[:, g * LANES : (g + 1) * LANES].astype(jnp.float32)
    strip = table.shape[1] // (2 * devices)
    half = moved.shape[1] // strip
    height = table.shape[0] // 2
    real, imag = [], []
    for freq in range(owned):
        parts = []
        for part in range(2):
            where = pl.ds(part * owned + freq, devices, stride=2 * owned)
            block = jnp.concatenate([wide[g, where, :] for g in range(groups)], axis=1)
            parts += [block[:, r * half : (r + 1) * half] for r in range(strip)]
        result = dot(table[...], jnp.concatenate(parts, axis=0).astype(jnp.bfloat16)) * norm
        real.append(result[:height])
        imag.append(result[height:])
    return jnp.concatenate(real, axis=0), jnp.concatenate(imag, axis=0)


def slope_kernel(norm, owned, devices, moved, mix, table, out, wide):
    parts = row_spectrum(moved, table, wide, norm, owned, devices)
    real, imag = [part.astype(jnp.bfloat16) for part in parts]
    half = real.shape[1]
    spans = (slice(0, half), slice(half, 2 * half))
    for part, span in enumerate(spans):
        pre = dot(real, mix[spans[0], span]) + dot(imag, mix[spans[1], span])
        s = 1.0 / (1.0 + jnp.exp(-pre))
        out[part] = s * (1.0 + pre * (1.0 - s))


def mix_kernel(norm, owned, devices, moved, slope, mix, table, back_table, out, wide):
    grads = row_spectrum(moved, table, wide, norm, owned, devices)
    half = grads[0].shape[1]
    spans = (slice(0, half), slice(half, 2 * half))
    mixed = [(grad * slope[part]).astype(jnp.bfloat16) for part, grad in enumerate(grads)]
    back = [dot_t(mixed[0], mix[p, spans[0]]) + dot_t(mixed[1], mix[p, spans[1]]) for p in spans]
    back = [part.astype(jnp.bfloat16) for part in back]
    height = table.shape[0] // 2
    strip = height // devices
    groups = wide.shape[0]
    for freq in range(owned):
        cells = slice(freq * height, (freq + 1) * height)
        stacked = jnp.concatenate([back[0][cells], back[1][cells]], axis=0)
        result = dot(back_table[...], stacked) * norm
        for part in range(2):
            rows = [
                result[(part * strip + r) * devices : (part * strip + r + 1) * devices]
                for r in range(strip)
            ]
            where = pl.ds(part * owned + freq, devices, stride=2 * owned)
            values = jnp.concatenate(rows, axis=1)
            for g in range(groups):
                wide[g, where, :] = values[:, g * LANES : (g + 1) * LANES]
    for g in range(groups):
        out[:, g * LANES : (g + 1) * LANES] = wide[g].astype(jnp.bfloat16)


def output_kernel(norm, moved, strip_grad, weight_in, weight_local, table, out, held, sems):
    spatial = (dot(table[...], moved[...]) * norm).astype(jnp.bfloat16)
    half = weight_in.shape[0]
    copies = []
    for r in range(out.shape[0]):
        total = dot(spatial[:, r * half : (r + 1) * half], weight_in[...])
        total = total + dot_t(strip_row(strip_grad, r), weight_local[...])
        held[r] = total.astype(jnp.bfloat16)
        copies.append(pltpu.make_async_copy(held.at[r], out.at[r], sems.at[r]))
        copies[-1].start()
    for copy in copies:
        copy.wait()


def output(norm, shape, *operands):
    return pl.pallas_call(
        functools.partial(output_kernel, norm),
        out_shape=jax.ShapeDtypeStruct(shape, jnp.bfloat16),
        in_specs=[pl.BlockSpec(memory_space=pltpu.VMEM)] * len(operands),
        out_specs=pl.BlockSpec(memory_space=pltpu.HBM),
        scratch_shapes=[pltpu.VMEM(shape, jnp.bfloat16), pltpu.SemaphoreType.DMA((shape[0],))],
        compiler_params=pltpu.CompilerParams(vmem_limit_bytes=10 * MIB),
        cost_estimate=pl.CostEstimate(flops=0, bytes_accessed=3 * MIB, transcendentals=0),
    )(*operands)


TAIL = 16


def pick(flag, left, right):
    return lax.select(flag, left, right)


def odd_row(place):
    return place[1] == 1


def odd_col(place):
    return lax.rem(place[0], 2) == 1


def turned(rows):
    count, columns = rows.shape
    rows = rows.astype(jnp.float32)
    return jnp.concatenate([rows, jnp.zeros((columns - count, columns), jnp.float32)], axis=0).T


def filled(lanes, channels):
    fill = jnp.zeros((lanes.shape[0], channels - lanes.shape[1]), jnp.float32)
    return jnp.concatenate([lanes, fill], axis=1).astype(jnp.bfloat16)


def pack_kernel(col, low, target, mask, early, late, mask_row, mask_held, sems):
    place = col[0], low[0]
    tile_rows, tile_cols = mask.shape
    channels = target.shape[1]
    last = tile_rows - NEAR
    pixels = NEAR * tile_cols
    moves = [(mask, mask_held)]
    for pack, row in ((early, (1 - place[1]) * last), (late, place[1] * last)):
        moves.append((target.at[pl.ds(row * tile_cols, pixels)], pack.at[pl.ds(0, pixels)]))
    copies = [pltpu.make_async_copy(*move, sems.at[i]) for i, move in enumerate(moves)]
    for copy in copies:
        copy.start()
    copies[0].wait()
    mask_row[0] = filled(turned(mask_held[...]), channels)
    ends = (mask_held[:NEAR], mask_held[last:])
    for pack, (one, other) in ((early, ends), (late, ends[::-1])):
        rows = pick(odd_row(place), one.astype(jnp.float32), other.astype(jnp.float32))
        rows = jnp.concatenate([rows, jnp.zeros((TAIL - NEAR, tile_cols), jnp.float32)], axis=0)
        pack[pixels:] = filled(rows, channels)
    for copy in copies[1:]:
        copy.wait()


def target_packs(place, target, mask):
    tile_rows, tile_cols, channels = target.shape
    pack = (NEAR * tile_cols + TAIL, channels)
    hbm = pl.BlockSpec(memory_space=pltpu.HBM)
    shapes = [pack, pack, (1, tile_cols, channels)]
    return pl.pallas_call(
        pack_kernel,
        out_shape=[jax.ShapeDtypeStruct(shape, jnp.bfloat16) for shape in shapes],
        in_specs=[pl.BlockSpec(memory_space=pltpu.SMEM)] * 2 + [hbm, hbm],
        out_specs=[pl.BlockSpec(memory_space=pltpu.VMEM)] * len(shapes),
        scratch_shapes=[pltpu.VMEM(mask.shape, mask.dtype), pltpu.SemaphoreType.DMA((3,))],
        compiler_params=pltpu.CompilerParams(vmem_limit_bytes=4 * MIB),
        cost_estimate=pl.CostEstimate(flops=0, bytes_accessed=MIB, transcendentals=0),
    )(*place, in_hbm(target.reshape(tile_rows * tile_cols, channels)), in_hbm(mask))


def fetch_kernel(*refs):
    count = len(refs) // 2
    sems = refs[-1]
    copies = [pltpu.make_async_copy(refs[i], refs[count + i], sems.at[i]) for i in range(count)]
    for copy in copies:
        copy.start()
    for copy in copies:
        copy.wait()


def fetch(*arrays):
    return pl.pallas_call(
        fetch_kernel,
        out_shape=[jax.ShapeDtypeStruct(a.shape, a.dtype) for a in arrays],
        in_specs=[pl.BlockSpec(memory_space=pltpu.HBM)] * len(arrays),
        out_specs=[pl.BlockSpec(memory_space=pltpu.VMEM)] * len(arrays),
        scratch_shapes=[pltpu.SemaphoreType.DMA((len(arrays),))],
        compiler_params=pltpu.CompilerParams(vmem_limit_bytes=4 * MIB),
        cost_estimate=pl.CostEstimate(flops=0, bytes_accessed=5 * MIB, transcendentals=0),
    )(*[in_hbm(a) for a in arrays])


def edge_kernel(tile_cols, col, low, early_pack, late_pack, *refs):
    place = col[0], low[0]
    sources, (early, late, own) = refs[:-3], refs[-3:]
    count = len(sources) // 2
    keep = 2 * REACH
    channels = own.shape[2]
    lower, high = odd_row(place), odd_col(place)

    def put_rows(row, tail, head):
        rows = slice(row, row + tail.shape[0])
        last, initial = tail[:, REACH:], head[:, :REACH]
        early[rows] = pick(high, initial, last)
        late[rows] = pick(high, last, initial)
        own[rows, :keep] = head
        own[rows, keep:] = tail

    def put_pack(row, one, other):
        for i in range(NEAR):
            at = i * tile_cols
            tail = pick(lower, one[at + tile_cols - keep : at + tile_cols], other[at + tile_cols - keep : at + tile_cols])
            head = pick(lower, one[at : at + keep], other[at : at + keep])
            put_rows(row + i, tail[None], head[None])
        mask = turned(pick(lower, one[NEAR * tile_cols :, :tile_cols], other[NEAR * tile_cols :, :tile_cols]))
        tail, head = [filled(m, channels)[None] for m in (mask[tile_cols - keep :], mask[:keep])]
        put_rows(row + NEAR, tail, head)

    def put_picked(row, one, other):
        put_rows(row, *[pick(lower, sources[one + i * count][...], sources[other + i * count][...]) for i in (0, 1)])

    def put_own(row, index):
        put_rows(row, sources[index][...], sources[index + count][...])

    rows = sources[0].shape[0]
    put_picked(0, 0, 1)
    put_own(rows, 2)
    put_picked(2 * rows, 1, 0)
    put_pack(3 * rows, early_pack, late_pack)
    put_own(3 * rows + NEAR + 1, 3)
    put_own(4 * rows + NEAR + 1, 4)
    put_pack(4 * rows + NEAR + 2, late_pack, early_pack)


def edges(place, early, late, features, target, mask_row, early_pack, late_pack):
    parts = (early, late, features, target, mask_row)
    _, tile_cols, channels = features.shape
    keep = 2 * REACH
    tail = tile_cols // keep - 1

    def specs(at):
        return [pl.BlockSpec((p.shape[0], keep, channels), lambda i, at=at: (0, at, 0)) for p in parts]

    whole = [pl.BlockSpec(early_pack.shape, lambda i: (0, 0))] * 2
    rows = sum(p.shape[0] for p in parts) + 2 * (NEAR + 1)
    shapes = [(rows, columns, channels) for columns in (REACH, REACH, 2 * keep)]
    return pl.pallas_call(
        functools.partial(edge_kernel, tile_cols),
        grid=(1,),
        out_shape=[jax.ShapeDtypeStruct(shape, features.dtype) for shape in shapes],
        in_specs=[pl.BlockSpec(memory_space=pltpu.SMEM)] * 2 + whole + specs(tail) + specs(0),
        out_specs=[pl.BlockSpec(shape, lambda i: (0, 0, 0)) for shape in shapes],
        compiler_params=pltpu.CompilerParams(vmem_limit_bytes=8 * MIB),
        cost_estimate=pl.CostEstimate(
            flops=0, bytes_accessed=16 * rows * keep * channels, transcendentals=0
        ),
    )(*place, early_pack, late_pack, *parts, *parts)


def put(wide, row, value, stride):
    size, channels = value.shape
    spot = pl.ds(row * stride, size)
    wide[spot, :channels] = pltpu.roll(value, 2, 0).astype(jnp.bfloat16)
    wide[spot, channels : 2 * channels] = value.astype(jnp.bfloat16)
    wide[spot, 2 * channels :] = pltpu.roll(value, size - 2, 0).astype(jnp.bfloat16)


def taps(wide, row, count, stride):
    parts = [wide[pl.ds((row + 2 * a) * stride, count * stride), :] for a in range(3)]
    return jnp.concatenate(parts, axis=1)


def conv(wide, row, count, stride, kernel):
    channels = kernel.shape[-1]
    return dot(taps(wide, row, count, stride), kernel[...].reshape(9 * channels, channels))


def conv_adjoint(wide, row, count, stride, kernel):
    flipped = [kernel[2 - a, 2 - b] for a in range(3) for b in range(3)]
    return dot_t(taps(wide, row, count, stride), jnp.concatenate(flipped, axis=1))


def stacked(piece, rows):
    return jnp.concatenate([piece(row) for row in rows], axis=0)


def first_stages(
    stride, blocks, rows, feature, inside, first, second, wide_even, wide_odd, slopes, use
):
    tall = rows + 2 * REACH
    for row in range(0, tall, NEAR):
        put(wide_even, row, stacked(feature, range(row, row + NEAR)), stride)
    count = blocks[0]
    for row in range(0, tall - 4, count):
        pre = conv(wide_even, row, count, stride, first)
        s = 1.0 / (1.0 + jnp.exp(-pre))
        kept = stacked(inside, range(row + 2, row + 2 + count))
        put(wide_odd, row, pre * s * kept, stride)
        low, high = max(row, NEAR), min(row + count, tall - 4 - NEAR)
        if low < high:
            part = slice((low - row) * stride, (high - row) * stride)
            slope = (s * (1.0 + pre * (1.0 - s)) * kept)[part]
            slopes[pl.ds((low - NEAR) * stride, (high - low) * stride), :] = slope
    count = blocks[1]
    for row in range(0, rows + 2 * NEAR, count):
        use(row, count, conv(wide_odd, row, count, stride, second))


def last_stages(stride, blocks, rows, first, second, wide_even, wide_odd, slopes, use):
    count = blocks[2]
    for row in range(0, rows + 4, count):
        value = conv_adjoint(wide_even, row, count, stride, second)
        value = value * slopes[pl.ds(row * stride, count * stride), :]
        put(wide_odd, row, value, stride)
    count = blocks[3]
    for row in range(0, rows, count):
        use(row, count, conv_adjoint(wide_odd, row, count, stride, first))


def steps_of(count):
    return [0, *range(2, count), 1] if count > 1 else [0]


def deal(place, out, pieces):
    for step, piece in zip(steps_of(len(pieces)), pieces):
        piece[...] = out[pl.ds((place[0] ^ step) * piece.shape[0], piece.shape[0])]


def loss_grad(row, count, value, target, hole, inside):
    near = range(row, row + count)
    weight = (1.0 + 2.0 * stacked(hole, near)) * stacked(inside, range(row + NEAR, row + count + NEAR))
    return weight * (value - stacked(target, near))


def part_of(rows, edge, above, own, below):
    def find(row):
        if row < edge:
            return above, row
        if row < edge + rows:
            return own, row - edge
        return below, row - edge - rows

    return find


TILE_BLOCKS = (2, 2, 2, 2)
SIDE_BLOCKS = (5, 4, 6, 4)


def tile_forward_kernel(
    col, low, early, features, late, first, second, ok, pre, slopes, wide_even, wide_odd
):
    place = col[0], low[0]
    rows, stride, _ = features.shape
    find = part_of(rows, REACH, (early, late), (features,), (late, early))

    def feature(row):
        sources, at = find(row)
        if len(sources) == 1:
            return features[at].astype(jnp.float32)
        return pick(odd_row(place), *[source[at] for source in sources]).astype(jnp.float32)

    def inside(row):
        return ok[REACH : REACH + stride, row : row + 1]

    def use(row, count, value):
        pre[pl.ds(row * stride, count * stride), :] = value

    first_stages(
        stride, TILE_BLOCKS, rows, feature, inside, first, second, wide_even, wide_odd, slopes, use
    )


def tile_backward_kernel(
    col,
    low,
    pre,
    slopes,
    early_pack,
    target,
    late_pack,
    mask_row,
    first,
    second,
    ok,
    *refs,
):
    *pieces, out, wide_even, wide_odd = refs
    place = col[0], low[0]
    rows, stride, channels = target.shape
    packs = (early_pack, late_pack)
    find = part_of(rows, NEAR, packs, (target,), packs[::-1])

    def picked(sources, part):
        return pick(odd_row(place), *[source[part] for source in sources]).astype(jnp.float32)

    def goal(row):
        sources, at = find(row)
        if len(sources) == 1:
            return target[at].astype(jnp.float32)
        return picked(sources, slice(at * stride, (at + 1) * stride))

    masks = [
        turned(picked(sources, slice(NEAR * stride, None))[:, :stride]) for sources in (packs, packs[::-1])
    ]
    find_mask = part_of(rows, NEAR, (masks[0], 0), (mask_row[0].astype(jnp.float32), 0), (masks[1], 0))

    def hole(row):
        (mask, start), at = find_mask(row)
        return mask[:, start + at : start + at + 1]

    def inside(row):
        return ok[REACH : REACH + stride, row : row + 1]

    count = NEAR
    for row in range(0, rows + 2 * NEAR, count):
        value = pre[pl.ds(row * stride, count * stride), :]
        put(wide_even, row, loss_grad(row, count, value, goal, hole, inside), stride)

    def use(row, count, value):
        value = value.reshape(count, stride, channels)[:, REACH : stride - REACH]
        out[row : row + count] = value.astype(jnp.bfloat16)

    last_stages(stride, TILE_BLOCKS, rows, first, second, wide_even, wide_odd, slopes, use)
    deal(place, out, pieces)


def side_kernel(col, low, late, early, own, first, second, ok, *refs):
    *pieces, out, wide_even, wide_odd, slopes = refs
    place = col[0], low[0]
    rows, _, channels = out.shape
    keep = 2 * REACH
    stride = 2 * (REACH + keep)
    tall = rows + 2 * REACH
    odd = odd_col(place)

    def feature(row):
        before, after = pick(odd, early[row], late[row]), pick(odd, late[row], early[row])
        parts = [part.astype(jnp.float32) for part in (before, own[row], after)]
        return jnp.concatenate(parts, axis=0)

    find = part_of(rows, NEAR, tall, tall + NEAR + 1, tall + NEAR + 1 + rows + 1)

    def goal(row):
        start, at = find(row)
        return feature(start + at)

    masks = [feature(row) for row in (tall + NEAR, tall + NEAR + 1 + rows, early.shape[0] - 1)]
    find_mask = part_of(rows, NEAR, (masks[0], 0), (masks[1], 0), (masks[2], 0))

    def hole(row):
        (mask, start), at = find_mask(row)
        return mask[:, start + at : start + at + 1]

    width = ok.shape[0]
    kept = jnp.concatenate([ok[: REACH + keep], ok[width - REACH - keep :]], axis=0)

    def inside(row):
        return kept[:, row : row + 1]

    def use_forward(row, count, value):
        put(wide_even, row, loss_grad(row, count, value, goal, hole, inside), stride)

    first_stages(
        stride, SIDE_BLOCKS, rows, feature, inside, first, second, wide_even, wide_odd, slopes, use_forward
    )

    def use(row, count, value):
        value = value.reshape(count, stride, channels).astype(jnp.bfloat16)
        out[row : row + count, :REACH] = value[:, REACH : 2 * REACH]
        out[row : row + count, REACH:] = value[:, stride - 2 * REACH : stride - REACH]

    last_stages(stride, SIDE_BLOCKS, rows, first, second, wide_even, wide_odd, slopes, use)
    deal(place, out, pieces)


def wide_buffer(rows, stride, channels):
    return pltpu.VMEM((rows * stride, 3 * channels), jnp.bfloat16)


def tile_forward(place, early, features, late, first, second, ok):
    rows, stride, channels = features.shape
    shapes = [
        jax.ShapeDtypeStruct(((rows + h) * stride, channels), jnp.float32) for h in (2 * NEAR, 4)
    ]
    in_vmem = pl.BlockSpec(memory_space=pltpu.VMEM)
    return pl.pallas_call(
        tile_forward_kernel,
        out_shape=shapes,
        in_specs=[pl.BlockSpec(memory_space=pltpu.SMEM)] * 2 + [in_vmem] * 6,
        out_specs=[in_vmem] * 2,
        scratch_shapes=[wide_buffer(rows + h, stride, channels) for h in (16, 12)],
        compiler_params=pltpu.CompilerParams(vmem_limit_bytes=22 * MIB),
        cost_estimate=pl.CostEstimate(
            flops=2 * 9 * channels * channels * stride * (2 * rows + 20),
            bytes_accessed=8 * MIB,
            transcendentals=0,
        ),
    )(*place, early, features, late, first, second, ok)


def piece_shapes(rows, columns, channels):
    count = lax.axis_size("col")
    return [jax.ShapeDtypeStruct((rows // count, columns, channels), jnp.bfloat16)] * count


def tile_backward(place, pre, slopes, early_pack, target, *operands):
    rows, stride, channels = target.shape
    in_vmem = pl.BlockSpec(memory_space=pltpu.VMEM)
    shapes = piece_shapes(rows, stride - 2 * REACH, channels)
    return pl.pallas_call(
        tile_backward_kernel,
        out_shape=shapes,
        in_specs=[pl.BlockSpec(memory_space=pltpu.SMEM)] * 2 + [in_vmem] * (4 + len(operands)),
        out_specs=[in_vmem] * len(shapes),
        scratch_shapes=[
            pltpu.VMEM((rows, stride - 2 * REACH, channels), jnp.bfloat16),
            *[wide_buffer(rows + h, stride, channels) for h in (8, 4)],
        ],
        compiler_params=pltpu.CompilerParams(vmem_limit_bytes=16 * MIB),
        cost_estimate=pl.CostEstimate(
            flops=2 * 9 * channels * channels * stride * (2 * rows + 4),
            bytes_accessed=8 * MIB,
            transcendentals=0,
        ),
    )(*place, pre, slopes, early_pack, target, *operands)


def sides(place, shape, *operands):
    rows, _, channels = shape
    stride = 6 * REACH
    in_vmem = pl.BlockSpec(memory_space=pltpu.VMEM)
    shapes = piece_shapes(rows, 2 * REACH, channels)
    return pl.pallas_call(
        side_kernel,
        out_shape=shapes,
        in_specs=[pl.BlockSpec(memory_space=pltpu.SMEM)] * 2 + [in_vmem] * len(operands),
        out_specs=[in_vmem] * len(shapes),
        scratch_shapes=[
            pltpu.VMEM((rows, 2 * REACH, channels), jnp.bfloat16),
            *[wide_buffer(rows + h, stride, channels) for h in (16, 12)],
            pltpu.VMEM(((rows + 4) * stride, channels), jnp.float32),
        ],
        compiler_params=pltpu.CompilerParams(vmem_limit_bytes=18 * MIB),
        cost_estimate=pl.CostEstimate(
            flops=2 * 9 * channels * channels * stride * (4 * rows + 24),
            bytes_accessed=4 * MIB,
            transcendentals=0,
        ),
    )(*place, *operands)


def pairs(axis, start):
    size = lax.axis_size(axis)
    up = [(i, i + 1) for i in range(start, size - 1, 2)]
    return up + [(j, i) for i, j in up]


def shards(
    features,
    target,
    hole_mask,
    kernel_first,
    kernel_second,
    inputs,
    weight_in,
    weight_out,
    weight_local,
    weight_mix,
):
    tile_rows, tile_cols, channels = features.shape
    row_devices, col_devices = lax.axis_size("row"), lax.axis_size("col")
    devices = row_devices * col_devices
    height, width = tile_rows * row_devices, tile_cols * col_devices
    strip, half = inputs.shape[0], weight_in.shape[1]
    owned = width // 2 // devices
    col_norm, row_norm = 1.0 / math.sqrt(width), 1.0 / math.sqrt(height)
    table = column_matrix(width, devices)
    table_back = jnp.asarray(np.ascontiguousarray(table.T))
    table = jnp.asarray(table)
    row_table = row_matrix(height, row_devices, col_devices)
    row_back = jnp.asarray(np.ascontiguousarray(row_table.T))
    row_table = jnp.asarray(row_table)
    bf16 = jnp.bfloat16

    def swap(spectrum):
        return lax.all_to_all(spectrum, ("col", "row"), split_axis=0, concat_axis=0, tiled=True)

    row0, col0 = lax.axis_index("row") * tile_rows, lax.axis_index("col") * tile_cols
    row_ids = row0 - REACH + jnp.arange(tile_rows + 2 * REACH, dtype=jnp.int32)
    col_ids = col0 - REACH + jnp.arange(tile_cols + 2 * REACH, dtype=jnp.int32)
    ok = ((col_ids >= 0) & (col_ids < width))[:, None] & ((row_ids >= 0) & (row_ids < height))[None]
    ok = ok.astype(jnp.float32)
    place = tuple(jnp.full((1,), i, jnp.int32) for i in (lax.axis_index("col"), lax.axis_index("row") & 1))
    early_pack, late_pack, mask_row = target_packs(place, target, hole_mask)
    inputs, ok, early_pack = lax.optimization_barrier((inputs, ok, early_pack))

    cells = [jax.ShapeDtypeStruct((width, strip * half), bf16)]
    weight_in = weight_in.T
    spatial_cols = fetching_spectrum(col_norm, cells[0], inputs, weight_in, table)
    spatial_moved = swap(spatial_cols)

    early = lax.ppermute(features, "row", pairs("row", 0))
    late = lax.ppermute(features, "row", pairs("row", 1))
    kernel_first, spatial_cols = lax.optimization_barrier((kernel_first, spatial_cols))
    kernel_first, kernel_second = fetch(kernel_first, kernel_second)
    early_pack = lax.ppermute(early_pack, "row", pairs("row", 0))
    late_pack = lax.ppermute(late_pack, "row", pairs("row", 1))
    pre, slopes = tile_forward(place, early, features, late, kernel_first, kernel_second, ok)
    early_pack, pre = lax.optimization_barrier((early_pack, pre))
    early_edge, late_edge, own = edges(
        place, early, late, features, target, mask_row, early_pack, late_pack
    )
    late_edge = lax.ppermute(late_edge, "col", pairs("col", 1))
    early_edge = lax.ppermute(early_edge, "col", pairs("col", 0))
    inner = tile_backward(
        place, pre, slopes, early_pack, target, late_pack, mask_row, kernel_first, kernel_second, ok
    )

    def dealt(pieces):
        result = []
        for piece, step in zip(pieces, steps_of(col_devices)):
            swaps = [(i, i ^ step) for i in range(col_devices)]
            result.append(lax.ppermute(piece, "col", swaps) if step else piece)
        return result

    inner = dealt(inner)
    outer = sides(
        place, features.shape, late_edge, early_edge, own, kernel_first, kernel_second, ok
    )
    *outer, spatial_moved = lax.optimization_barrier((*outer, spatial_moved))
    outer = dealt(outer)

    cell_count = height * owned
    wide = [pltpu.VMEM((strip * half // LANES, width, LANES), jnp.float32)]
    slope = vmem_call(
        functools.partial(slope_kernel, row_norm, owned, devices),
        [jax.ShapeDtypeStruct((2, cell_count, half), jnp.float32)],
        spatial_moved,
        weight_mix,
        row_table,
        scratch=wide,
    )[0]
    outer[0], slope = lax.optimization_barrier((outer[0], slope))
    grad_cols, strip_grad = grad_spectrum(col_norm, place, inner, outer, weight_out, table)
    grad_rows = vmem_call(
        functools.partial(mix_kernel, row_norm, owned, devices),
        cells,
        swap(grad_cols),
        slope,
        weight_mix,
        row_table,
        row_back,
        scratch=wide,
    )[0]
    returned = swap(grad_rows)
    return output(col_norm, inputs.shape, returned, strip_grad, weight_in, weight_local, table_back)


def solution(mesh):
    in_specs = (
        P("row", "col", None),
        P("row", "col", None),
        P("row", "col"),
        P(),
        P(),
        P(("row", "col"), None, None),
        P(),
        P(),
        P(),
        P(),
    )
    out_specs = P(("row", "col"), None, None)
    return jax.shard_map(shards, mesh=mesh, in_specs=in_specs, out_specs=out_specs, check_vma=False)
```

```python
import functools
import math

import jax
import jax.numpy as jnp
import ml_dtypes
import numpy as np
from jax import lax
from jax.experimental import pallas as pl
from jax.experimental.pallas import tpu as pltpu
from jax.sharding import PartitionSpec as P

REACH = 8
NEAR = 4
MIB = 1024 * 1024
LANES = 128


def dot(left, right):
    return jnp.dot(left, right, preferred_element_type=jnp.float32)


def dot_t(left, right):
    return lax.dot_general(left, right, (((1,), (1,)), ((), ())), preferred_element_type=jnp.float32)


def vmem_call(body, shapes, *operands, flops=0, scratch=(), limit=10):
    spec = pl.BlockSpec(memory_space=pltpu.VMEM)
    size = sum(math.prod(a.shape) * a.dtype.itemsize for a in (*operands, *shapes))
    return pl.pallas_call(
        body,
        out_shape=shapes,
        in_specs=[spec] * len(operands),
        out_specs=[spec] * len(shapes),
        scratch_shapes=list(scratch),
        compiler_params=pltpu.CompilerParams(vmem_limit_bytes=limit * MIB),
        cost_estimate=pl.CostEstimate(flops=flops, bytes_accessed=size, transcendentals=0),
    )(*operands)


def in_hbm(array):
    return pltpu.with_memory_space_constraint(array, pltpu.HBM)


def phases(first, second, length):
    angle = (first[:, None] * second[None, :] % length) * (2.0 * math.pi / length)
    return np.cos(angle).astype(ml_dtypes.bfloat16), np.sin(angle).astype(ml_dtypes.bfloat16)


def column_matrix(width, devices):
    half = width // 2
    freq, col = np.arange(half), np.arange(width)
    cos, sin = phases(freq, col, width)
    sin[0] = (2 * (col % 2) - 1).astype(ml_dtypes.bfloat16)
    both = np.stack([cos, -sin]).reshape(2, devices, half // devices, width)
    return np.ascontiguousarray(both.transpose(1, 0, 2, 3)).reshape(width, width)


def row_matrix(height, row_devices, col_devices):
    devices = row_devices * col_devices
    strip = height // devices
    strips = np.arange(devices).reshape(row_devices, col_devices).T.reshape(-1)
    rows = (strips[None, :] * strip + np.arange(strip)[:, None]).reshape(-1)
    cos, sin = phases(np.arange(height), rows, height)
    return np.block([[cos, sin], [-sin, cos]])


def strip_row(signal, r):
    return jnp.concatenate([signal[block, r] for block in range(signal.shape[0])], axis=0)


def grad_kernel(norm, col, low, *refs):
    *pieces, weight, table, out, strip_out, projected = refs
    count = len(pieces) // 2
    _, strip, tile_cols, _ = strip_out.shape
    for step, inner, outer in zip(steps_of(count), pieces[:count], pieces[count:]):
        block = col[0] ^ step
        strip_out[block, :, REACH : tile_cols - REACH] = inner[...]
        strip_out[block, :, :REACH] = outer[:, :REACH]
        strip_out[block, :, tile_cols - REACH :] = outer[:, REACH:]
        rows = [dot_t(strip_out[block, r], weight[...]).astype(jnp.bfloat16) for r in range(strip)]
        where = pl.ds(pl.multiple_of(block * tile_cols, tile_cols), tile_cols)
        projected[where, :] = jnp.concatenate(rows, axis=1)
    out[...] = (dot(table[...], projected[...]) * norm).astype(jnp.bfloat16)


def grad_spectrum(norm, place, inner, outer, weight, table):
    strip, columns, channels = inner[0].shape
    shape = (table.shape[0], strip * weight.shape[0])
    in_vmem = pl.BlockSpec(memory_space=pltpu.VMEM)
    return pl.pallas_call(
        functools.partial(grad_kernel, norm),
        out_shape=[
            jax.ShapeDtypeStruct(shape, jnp.bfloat16),
            jax.ShapeDtypeStruct((len(inner), strip, columns + 2 * REACH, channels), jnp.bfloat16),
        ],
        in_specs=[pl.BlockSpec(memory_space=pltpu.SMEM)] * 2 + [in_vmem] * (2 * len(inner) + 2),
        out_specs=[in_vmem] * 2,
        scratch_shapes=[pltpu.VMEM(shape, jnp.bfloat16)],
        compiler_params=pltpu.CompilerParams(vmem_limit_bytes=10 * MIB),
        cost_estimate=pl.CostEstimate(flops=0, bytes_accessed=2 * MIB, transcendentals=0),
    )(*place, *inner, *outer, weight, table)


def fetching_spectrum_kernel(norm, signal, weight, table, out, signal_held, weight_held, table_held, sems):
    count = signal.shape[0]
    copies = [pltpu.make_async_copy(weight, weight_held, sems.at[0])]
    copies += [
        pltpu.make_async_copy(signal.at[r], signal_held.at[r], sems.at[1 + r]) for r in range(count)
    ]
    copies.append(pltpu.make_async_copy(table, table_held, sems.at[1 + count]))
    for copy in copies:
        copy.start()
    copies[0].wait()
    rows = []
    for r in range(count):
        copies[1 + r].wait()
        rows.append(dot_t(signal_held[r], weight_held[...]).astype(jnp.bfloat16))
    copies[-1].wait()
    out[...] = (dot(table_held[...], jnp.concatenate(rows, axis=1)) * norm).astype(jnp.bfloat16)


def fetching_spectrum(norm, shape, signal, weight, table):
    operands = (signal, weight, table)
    return pl.pallas_call(
        functools.partial(fetching_spectrum_kernel, norm),
        out_shape=shape,
        in_specs=[pl.BlockSpec(memory_space=pltpu.HBM)] * 3,
        out_specs=pl.BlockSpec(memory_space=pltpu.VMEM),
        scratch_shapes=[pltpu.VMEM(a.shape, a.dtype) for a in operands]
        + [pltpu.SemaphoreType.DMA((signal.shape[0] + 2,))],
        compiler_params=pltpu.CompilerParams(vmem_limit_bytes=12 * MIB),
        cost_estimate=pl.CostEstimate(
            flops=0, bytes_accessed=2 * MIB, transcendentals=0
        ),
    )(*[in_hbm(a) for a in operands])


def row_spectrum(moved, table, wide, norm, owned, devices):
    groups = wide.shape[0]
    for g in range(groups):
        wide[g] = moved[:, g * LANES : (g + 1) * LANES].astype(jnp.float32)
    strip = table.shape[1] // (2 * devices)
    half = moved.shape[1] // strip
    height = table.shape[0] // 2
    real, imag = [], []
    for freq in range(owned):
        parts = []
        for part in range(2):
            where = pl.ds(part * owned + freq, devices, stride=2 * owned)
            block = jnp.concatenate([wide[g, where, :] for g in range(groups)], axis=1)
            parts += [block[:, r * half : (r + 1) * half] for r in range(strip)]
        result = dot(table[...], jnp.concatenate(parts, axis=0).astype(jnp.bfloat16)) * norm
        real.append(result[:height])
        imag.append(result[height:])
    return jnp.concatenate(real, axis=0), jnp.concatenate(imag, axis=0)


def slope_kernel(norm, owned, devices, moved, mix, table, out, wide):
    parts = row_spectrum(moved, table, wide, norm, owned, devices)
    real, imag = [part.astype(jnp.bfloat16) for part in parts]
    half = real.shape[1]
    spans = (slice(0, half), slice(half, 2 * half))
    for part, span in enumerate(spans):
        pre = dot(real, mix[spans[0], span]) + dot(imag, mix[spans[1], span])
        s = 1.0 / (1.0 + jnp.exp(-pre))
        out[part] = s * (1.0 + pre * (1.0 - s))


def mix_kernel(norm, owned, devices, moved, slope, mix, table, back_table, out, wide):
    grads = row_spectrum(moved, table, wide, norm, owned, devices)
    half = grads[0].shape[1]
    spans = (slice(0, half), slice(half, 2 * half))
    mixed = [(grad * slope[part]).astype(jnp.bfloat16) for part, grad in enumerate(grads)]
    back = [dot_t(mixed[0], mix[p, spans[0]]) + dot_t(mixed[1], mix[p, spans[1]]) for p in spans]
    back = [part.astype(jnp.bfloat16) for part in back]
    height = table.shape[0] // 2
    strip = height // devices
    groups = wide.shape[0]
    for freq in range(owned):
        cells = slice(freq * height, (freq + 1) * height)
        stacked = jnp.concatenate([back[0][cells], back[1][cells]], axis=0)
        result = dot(back_table[...], stacked) * norm
        for part in range(2):
            rows = [
                result[(part * strip + r) * devices : (part * strip + r + 1) * devices]
                for r in range(strip)
            ]
            where = pl.ds(part * owned + freq, devices, stride=2 * owned)
            values = jnp.concatenate(rows, axis=1)
            for g in range(groups):
                wide[g, where, :] = values[:, g * LANES : (g + 1) * LANES]
    for g in range(groups):
        out[:, g * LANES : (g + 1) * LANES] = wide[g].astype(jnp.bfloat16)


def output_kernel(norm, moved, strip_grad, weight_in, weight_local, table, out, held, sems):
    spatial = (dot(table[...], moved[...]) * norm).astype(jnp.bfloat16)
    half = weight_in.shape[0]
    copies = []
    for r in range(out.shape[0]):
        total = dot(spatial[:, r * half : (r + 1) * half], weight_in[...])
        total = total + dot_t(strip_row(strip_grad, r), weight_local[...])
        held[r] = total.astype(jnp.bfloat16)
        copies.append(pltpu.make_async_copy(held.at[r], out.at[r], sems.at[r]))
        copies[-1].start()
    for copy in copies:
        copy.wait()


def output(norm, shape, *operands):
    return pl.pallas_call(
        functools.partial(output_kernel, norm),
        out_shape=jax.ShapeDtypeStruct(shape, jnp.bfloat16),
        in_specs=[pl.BlockSpec(memory_space=pltpu.VMEM)] * len(operands),
        out_specs=pl.BlockSpec(memory_space=pltpu.HBM),
        scratch_shapes=[pltpu.VMEM(shape, jnp.bfloat16), pltpu.SemaphoreType.DMA((shape[0],))],
        compiler_params=pltpu.CompilerParams(vmem_limit_bytes=10 * MIB),
        cost_estimate=pl.CostEstimate(flops=0, bytes_accessed=3 * MIB, transcendentals=0),
    )(*operands)


TAIL = 16


def pick(flag, left, right):
    return lax.select(flag, left, right)


def odd_row(place):
    return place[1] == 1


def odd_col(place):
    return lax.rem(place[0], 2) == 1


def turned(rows):
    count, columns = rows.shape
    rows = rows.astype(jnp.float32)
    return jnp.concatenate([rows, jnp.zeros((columns - count, columns), jnp.float32)], axis=0).T


def filled(lanes, channels):
    fill = jnp.zeros((lanes.shape[0], channels - lanes.shape[1]), jnp.float32)
    return jnp.concatenate([lanes, fill], axis=1).astype(jnp.bfloat16)


def pack_kernel(col, low, target, mask, early, late, mask_row, mask_held, sems):
    place = col[0], low[0]
    tile_rows, tile_cols = mask.shape
    channels = target.shape[1]
    last = tile_rows - NEAR
    pixels = NEAR * tile_cols
    moves = [(mask, mask_held)]
    for pack, row in ((early, (1 - place[1]) * last), (late, place[1] * last)):
        moves.append((target.at[pl.ds(row * tile_cols, pixels)], pack.at[pl.ds(0, pixels)]))
    copies = [pltpu.make_async_copy(*move, sems.at[i]) for i, move in enumerate(moves)]
    for copy in copies:
        copy.start()
    copies[0].wait()
    mask_row[0] = filled(turned(mask_held[...]), channels)
    ends = (mask_held[:NEAR], mask_held[last:])
    for pack, (one, other) in ((early, ends), (late, ends[::-1])):
        rows = pick(odd_row(place), one.astype(jnp.float32), other.astype(jnp.float32))
        rows = jnp.concatenate([rows, jnp.zeros((TAIL - NEAR, tile_cols), jnp.float32)], axis=0)
        pack[pixels:] = filled(rows, channels)
    for copy in copies[1:]:
        copy.wait()


def target_packs(place, target, mask):
    tile_rows, tile_cols, channels = target.shape
    pack = (NEAR * tile_cols + TAIL, channels)
    hbm = pl.BlockSpec(memory_space=pltpu.HBM)
    shapes = [pack, pack, (1, tile_cols, channels)]
    return pl.pallas_call(
        pack_kernel,
        out_shape=[jax.ShapeDtypeStruct(shape, jnp.bfloat16) for shape in shapes],
        in_specs=[pl.BlockSpec(memory_space=pltpu.SMEM)] * 2 + [hbm, hbm],
        out_specs=[pl.BlockSpec(memory_space=pltpu.VMEM)] * len(shapes),
        scratch_shapes=[pltpu.VMEM(mask.shape, mask.dtype), pltpu.SemaphoreType.DMA((3,))],
        compiler_params=pltpu.CompilerParams(vmem_limit_bytes=4 * MIB),
        cost_estimate=pl.CostEstimate(flops=0, bytes_accessed=MIB, transcendentals=0),
    )(*place, in_hbm(target.reshape(tile_rows * tile_cols, channels)), in_hbm(mask))


def fetch_kernel(*refs):
    count = len(refs) // 2
    sems = refs[-1]
    copies = [pltpu.make_async_copy(refs[i], refs[count + i], sems.at[i]) for i in range(count)]
    for copy in copies:
        copy.start()
    for copy in copies:
        copy.wait()


def fetch(*arrays):
    return pl.pallas_call(
        fetch_kernel,
        out_shape=[jax.ShapeDtypeStruct(a.shape, a.dtype) for a in arrays],
        in_specs=[pl.BlockSpec(memory_space=pltpu.HBM)] * len(arrays),
        out_specs=[pl.BlockSpec(memory_space=pltpu.VMEM)] * len(arrays),
        scratch_shapes=[pltpu.SemaphoreType.DMA((len(arrays),))],
        compiler_params=pltpu.CompilerParams(vmem_limit_bytes=4 * MIB),
        cost_estimate=pl.CostEstimate(flops=0, bytes_accessed=5 * MIB, transcendentals=0),
    )(*[in_hbm(a) for a in arrays])


def edge_kernel(tile_cols, col, low, early_pack, late_pack, *refs):
    place = col[0], low[0]
    sources, (early, late, own) = refs[:-3], refs[-3:]
    count = len(sources) // 2
    keep = 2 * REACH
    channels = own.shape[2]
    lower, high = odd_row(place), odd_col(place)

    def put_rows(row, tail, head):
        rows = slice(row, row + tail.shape[0])
        last, initial = tail[:, REACH:], head[:, :REACH]
        early[rows] = pick(high, initial, last)
        late[rows] = pick(high, last, initial)
        own[rows, :keep] = head
        own[rows, keep:] = tail

    def put_pack(row, one, other):
        for i in range(NEAR):
            at = i * tile_cols
            tail = pick(lower, one[at + tile_cols - keep : at + tile_cols], other[at + tile_cols - keep : at + tile_cols])
            head = pick(lower, one[at : at + keep], other[at : at + keep])
            put_rows(row + i, tail[None], head[None])
        mask = turned(pick(lower, one[NEAR * tile_cols :, :tile_cols], other[NEAR * tile_cols :, :tile_cols]))
        tail, head = [filled(m, channels)[None] for m in (mask[tile_cols - keep :], mask[:keep])]
        put_rows(row + NEAR, tail, head)

    def put_picked(row, one, other):
        put_rows(row, *[pick(lower, sources[one + i * count][...], sources[other + i * count][...]) for i in (0, 1)])

    def put_own(row, index):
        put_rows(row, sources[index][...], sources[index + count][...])

    rows = sources[0].shape[0]
    put_picked(0, 0, 1)
    put_own(rows, 2)
    put_picked(2 * rows, 1, 0)
    put_pack(3 * rows, early_pack, late_pack)
    put_own(3 * rows + NEAR + 1, 3)
    put_own(4 * rows + NEAR + 1, 4)
    put_pack(4 * rows + NEAR + 2, late_pack, early_pack)


def edges(place, early, late, features, target, mask_row, early_pack, late_pack):
    parts = (early, late, features, target, mask_row)
    _, tile_cols, channels = features.shape
    keep = 2 * REACH
    tail = tile_cols // keep - 1

    def specs(at):
        return [pl.BlockSpec((p.shape[0], keep, channels), lambda i, at=at: (0, at, 0)) for p in parts]

    whole = [pl.BlockSpec(early_pack.shape, lambda i: (0, 0))] * 2
    rows = sum(p.shape[0] for p in parts) + 2 * (NEAR + 1)
    shapes = [(rows, columns, channels) for columns in (REACH, REACH, 2 * keep)]
    return pl.pallas_call(
        functools.partial(edge_kernel, tile_cols),
        grid=(1,),
        out_shape=[jax.ShapeDtypeStruct(shape, features.dtype) for shape in shapes],
        in_specs=[pl.BlockSpec(memory_space=pltpu.SMEM)] * 2 + whole + specs(tail) + specs(0),
        out_specs=[pl.BlockSpec(shape, lambda i: (0, 0, 0)) for shape in shapes],
        compiler_params=pltpu.CompilerParams(vmem_limit_bytes=8 * MIB),
        cost_estimate=pl.CostEstimate(
            flops=0, bytes_accessed=16 * rows * keep * channels, transcendentals=0
        ),
    )(*place, early_pack, late_pack, *parts, *parts)


def put(wide, row, value, stride):
    size, channels = value.shape
    spot = pl.ds(row * stride, size)
    wide[spot, :channels] = pltpu.roll(value, 2, 0).astype(jnp.bfloat16)
    wide[spot, channels : 2 * channels] = value.astype(jnp.bfloat16)
    wide[spot, 2 * channels :] = pltpu.roll(value, size - 2, 0).astype(jnp.bfloat16)


def taps(wide, row, count, stride):
    parts = [wide[pl.ds((row + 2 * a) * stride, count * stride), :] for a in range(3)]
    return jnp.concatenate(parts, axis=1)


def conv(wide, row, count, stride, kernel):
    channels = kernel.shape[-1]
    return dot(taps(wide, row, count, stride), kernel[...].reshape(9 * channels, channels))


def conv_adjoint(wide, row, count, stride, kernel):
    flipped = [kernel[2 - a, 2 - b] for a in range(3) for b in range(3)]
    return dot_t(taps(wide, row, count, stride), jnp.concatenate(flipped, axis=1))


def stacked(piece, rows):
    return jnp.concatenate([piece(row) for row in rows], axis=0)


def first_stages(
    stride, blocks, rows, feature, inside, first, second, wide_even, wide_odd, slopes, use
):
    tall = rows + 2 * REACH
    for row in range(0, tall, NEAR):
        put(wide_even, row, stacked(feature, range(row, row + NEAR)), stride)
    count = blocks[0]
    for row in range(0, tall - 4, count):
        pre = conv(wide_even, row, count, stride, first)
        s = 1.0 / (1.0 + jnp.exp(-pre))
        kept = stacked(inside, range(row + 2, row + 2 + count))
        put(wide_odd, row, pre * s * kept, stride)
        low, high = max(row, NEAR), min(row + count, tall - 4 - NEAR)
        if low < high:
            part = slice((low - row) * stride, (high - row) * stride)
            slope = (s * (1.0 + pre * (1.0 - s)) * kept)[part]
            slopes[pl.ds((low - NEAR) * stride, (high - low) * stride), :] = slope
    count = blocks[1]
    for row in range(0, rows + 2 * NEAR, count):
        use(row, count, conv(wide_odd, row, count, stride, second))


def last_stages(stride, blocks, rows, first, second, wide_even, wide_odd, slopes, use):
    count = blocks[2]
    for row in range(0, rows + 4, count):
        value = conv_adjoint(wide_even, row, count, stride, second)
        value = value * slopes[pl.ds(row * stride, count * stride), :]
        put(wide_odd, row, value, stride)
    count = blocks[3]
    for row in range(0, rows, count):
        use(row, count, conv_adjoint(wide_odd, row, count, stride, first))


def steps_of(count):
    return [0, *reversed(range(1, count))]


def deal(place, out, pieces):
    for step, piece in zip(steps_of(len(pieces)), pieces):
        piece[...] = out[pl.ds((place[0] ^ step) * piece.shape[0], piece.shape[0])]


def loss_grad(row, count, value, target, hole, inside):
    near = range(row, row + count)
    weight = (1.0 + 2.0 * stacked(hole, near)) * stacked(inside, range(row + NEAR, row + count + NEAR))
    return weight * (value - stacked(target, near))


def part_of(rows, edge, above, own, below):
    def find(row):
        if row < edge:
            return above, row
        if row < edge + rows:
            return own, row - edge
        return below, row - edge - rows

    return find


TILE_BLOCKS = (2, 2, 2, 2)
SIDE_BLOCKS = (4, 4, 4, 4)


def tile_forward_kernel(
    col, low, early, features, late, first, second, ok, pre, slopes, wide_even, wide_odd
):
    place = col[0], low[0]
    rows, stride, _ = features.shape
    find = part_of(rows, REACH, (early, late), (features,), (late, early))

    def feature(row):
        sources, at = find(row)
        if len(sources) == 1:
            return features[at].astype(jnp.float32)
        return pick(odd_row(place), *[source[at] for source in sources]).astype(jnp.float32)

    def inside(row):
        return ok[REACH : REACH + stride, row : row + 1]

    def use(row, count, value):
        pre[pl.ds(row * stride, count * stride), :] = value

    first_stages(
        stride, TILE_BLOCKS, rows, feature, inside, first, second, wide_even, wide_odd, slopes, use
    )


def tile_backward_kernel(
    col,
    low,
    pre,
    slopes,
    early_pack,
    target,
    late_pack,
    mask_row,
    first,
    second,
    ok,
    *refs,
):
    *pieces, out, wide_even, wide_odd = refs
    place = col[0], low[0]
    rows, stride, channels = target.shape
    packs = (early_pack, late_pack)
    find = part_of(rows, NEAR, packs, (target,), packs[::-1])

    def picked(sources, part):
        return pick(odd_row(place), *[source[part] for source in sources]).astype(jnp.float32)

    def goal(row):
        sources, at = find(row)
        if len(sources) == 1:
            return target[at].astype(jnp.float32)
        return picked(sources, slice(at * stride, (at + 1) * stride))

    masks = [
        turned(picked(sources, slice(NEAR * stride, None))[:, :stride]) for sources in (packs, packs[::-1])
    ]
    find_mask = part_of(rows, NEAR, (masks[0], 0), (mask_row[0].astype(jnp.float32), 0), (masks[1], 0))

    def hole(row):
        (mask, start), at = find_mask(row)
        return mask[:, start + at : start + at + 1]

    def inside(row):
        return ok[REACH : REACH + stride, row : row + 1]

    count = NEAR
    for row in range(0, rows + 2 * NEAR, count):
        value = pre[pl.ds(row * stride, count * stride), :]
        put(wide_even, row, loss_grad(row, count, value, goal, hole, inside), stride)

    def use(row, count, value):
        value = value.reshape(count, stride, channels)[:, REACH : stride - REACH]
        out[row : row + count] = value.astype(jnp.bfloat16)

    last_stages(stride, TILE_BLOCKS, rows, first, second, wide_even, wide_odd, slopes, use)
    deal(place, out, pieces)


def side_kernel(col, low, late, early, own, first, second, ok, *refs):
    *pieces, out, wide_even, wide_odd, slopes = refs
    place = col[0], low[0]
    rows, _, channels = out.shape
    keep = 2 * REACH
    stride = 2 * (REACH + keep)
    tall = rows + 2 * REACH
    odd = odd_col(place)

    def feature(row):
        before, after = pick(odd, early[row], late[row]), pick(odd, late[row], early[row])
        parts = [part.astype(jnp.float32) for part in (before, own[row], after)]
        return jnp.concatenate(parts, axis=0)

    find = part_of(rows, NEAR, tall, tall + NEAR + 1, tall + NEAR + 1 + rows + 1)

    def goal(row):
        start, at = find(row)
        return feature(start + at)

    masks = [feature(row) for row in (tall + NEAR, tall + NEAR + 1 + rows, early.shape[0] - 1)]
    find_mask = part_of(rows, NEAR, (masks[0], 0), (masks[1], 0), (masks[2], 0))

    def hole(row):
        (mask, start), at = find_mask(row)
        return mask[:, start + at : start + at + 1]

    width = ok.shape[0]
    kept = jnp.concatenate([ok[: REACH + keep], ok[width - REACH - keep :]], axis=0)

    def inside(row):
        return kept[:, row : row + 1]

    def use_forward(row, count, value):
        put(wide_even, row, loss_grad(row, count, value, goal, hole, inside), stride)

    first_stages(
        stride, SIDE_BLOCKS, rows, feature, inside, first, second, wide_even, wide_odd, slopes, use_forward
    )

    def use(row, count, value):
        value = value.reshape(count, stride, channels).astype(jnp.bfloat16)
        out[row : row + count, :REACH] = value[:, REACH : 2 * REACH]
        out[row : row + count, REACH:] = value[:, stride - 2 * REACH : stride - REACH]

    last_stages(stride, SIDE_BLOCKS, rows, first, second, wide_even, wide_odd, slopes, use)
    deal(place, out, pieces)


def wide_buffer(rows, stride, channels):
    return pltpu.VMEM((rows * stride, 3 * channels), jnp.bfloat16)


def tile_forward(place, early, features, late, first, second, ok):
    rows, stride, channels = features.shape
    shapes = [
        jax.ShapeDtypeStruct(((rows + h) * stride, channels), jnp.float32) for h in (2 * NEAR, 4)
    ]
    in_vmem = pl.BlockSpec(memory_space=pltpu.VMEM)
    return pl.pallas_call(
        tile_forward_kernel,
        out_shape=shapes,
        in_specs=[pl.BlockSpec(memory_space=pltpu.SMEM)] * 2 + [in_vmem] * 6,
        out_specs=[in_vmem] * 2,
        scratch_shapes=[wide_buffer(rows + h, stride, channels) for h in (16, 12)],
        compiler_params=pltpu.CompilerParams(vmem_limit_bytes=22 * MIB),
        cost_estimate=pl.CostEstimate(
            flops=2 * 9 * channels * channels * stride * (2 * rows + 20),
            bytes_accessed=8 * MIB,
            transcendentals=0,
        ),
    )(*place, early, features, late, first, second, ok)


def piece_shapes(rows, columns, channels):
    count = lax.axis_size("col")
    return [jax.ShapeDtypeStruct((rows // count, columns, channels), jnp.bfloat16)] * count


def tile_backward(place, pre, slopes, early_pack, target, *operands):
    rows, stride, channels = target.shape
    in_vmem = pl.BlockSpec(memory_space=pltpu.VMEM)
    shapes = piece_shapes(rows, stride - 2 * REACH, channels)
    return pl.pallas_call(
        tile_backward_kernel,
        out_shape=shapes,
        in_specs=[pl.BlockSpec(memory_space=pltpu.SMEM)] * 2 + [in_vmem] * (4 + len(operands)),
        out_specs=[in_vmem] * len(shapes),
        scratch_shapes=[
            pltpu.VMEM((rows, stride - 2 * REACH, channels), jnp.bfloat16),
            *[wide_buffer(rows + h, stride, channels) for h in (8, 4)],
        ],
        compiler_params=pltpu.CompilerParams(vmem_limit_bytes=16 * MIB),
        cost_estimate=pl.CostEstimate(
            flops=2 * 9 * channels * channels * stride * (2 * rows + 4),
            bytes_accessed=8 * MIB,
            transcendentals=0,
        ),
    )(*place, pre, slopes, early_pack, target, *operands)


def sides(place, shape, *operands):
    rows, _, channels = shape
    stride = 6 * REACH
    in_vmem = pl.BlockSpec(memory_space=pltpu.VMEM)
    shapes = piece_shapes(rows, 2 * REACH, channels)
    return pl.pallas_call(
        side_kernel,
        out_shape=shapes,
        in_specs=[pl.BlockSpec(memory_space=pltpu.SMEM)] * 2 + [in_vmem] * len(operands),
        out_specs=[in_vmem] * len(shapes),
        scratch_shapes=[
            pltpu.VMEM((rows, 2 * REACH, channels), jnp.bfloat16),
            *[wide_buffer(rows + h, stride, channels) for h in (16, 12)],
            pltpu.VMEM(((rows + 4) * stride, channels), jnp.float32),
        ],
        compiler_params=pltpu.CompilerParams(vmem_limit_bytes=18 * MIB),
        cost_estimate=pl.CostEstimate(
            flops=2 * 9 * channels * channels * stride * (4 * rows + 24),
            bytes_accessed=4 * MIB,
            transcendentals=0,
        ),
    )(*place, *operands)


def pairs(axis, start):
    size = lax.axis_size(axis)
    up = [(i, i + 1) for i in range(start, size - 1, 2)]
    return up + [(j, i) for i, j in up]


def shards(
    features,
    target,
    hole_mask,
    kernel_first,
    kernel_second,
    inputs,
    weight_in,
    weight_out,
    weight_local,
    weight_mix,
):
    tile_rows, tile_cols, channels = features.shape
    row_devices, col_devices = lax.axis_size("row"), lax.axis_size("col")
    devices = row_devices * col_devices
    height, width = tile_rows * row_devices, tile_cols * col_devices
    strip, half = inputs.shape[0], weight_in.shape[1]
    owned = width // 2 // devices
    col_norm, row_norm = 1.0 / math.sqrt(width), 1.0 / math.sqrt(height)
    table = column_matrix(width, devices)
    table_back = jnp.asarray(np.ascontiguousarray(table.T))
    table = jnp.asarray(table)
    row_table = row_matrix(height, row_devices, col_devices)
    row_back = jnp.asarray(np.ascontiguousarray(row_table.T))
    row_table = jnp.asarray(row_table)
    bf16 = jnp.bfloat16

    def swap(spectrum):
        return lax.all_to_all(spectrum, ("col", "row"), split_axis=0, concat_axis=0, tiled=True)

    row0, col0 = lax.axis_index("row") * tile_rows, lax.axis_index("col") * tile_cols
    row_ids = row0 - REACH + jnp.arange(tile_rows + 2 * REACH, dtype=jnp.int32)
    col_ids = col0 - REACH + jnp.arange(tile_cols + 2 * REACH, dtype=jnp.int32)
    ok = ((col_ids >= 0) & (col_ids < width))[:, None] & ((row_ids >= 0) & (row_ids < height))[None]
    ok = ok.astype(jnp.float32)
    place = tuple(jnp.full((1,), i, jnp.int32) for i in (lax.axis_index("col"), lax.axis_index("row") & 1))
    early_pack, late_pack, mask_row = target_packs(place, target, hole_mask)
    inputs, ok, early_pack = lax.optimization_barrier((inputs, ok, early_pack))

    cells = [jax.ShapeDtypeStruct((width, strip * half), bf16)]
    weight_in = weight_in.T
    spatial_cols = fetching_spectrum(col_norm, cells[0], inputs, weight_in, table)
    spatial_moved = swap(spatial_cols)

    early = lax.ppermute(features, "row", pairs("row", 0))
    late = lax.ppermute(features, "row", pairs("row", 1))
    kernel_first, spatial_cols = lax.optimization_barrier((kernel_first, spatial_cols))
    kernel_first, kernel_second = fetch(kernel_first, kernel_second)
    early_pack = lax.ppermute(early_pack, "row", pairs("row", 0))
    late_pack = lax.ppermute(late_pack, "row", pairs("row", 1))
    pre, slopes = tile_forward(place, early, features, late, kernel_first, kernel_second, ok)
    early_pack, pre = lax.optimization_barrier((early_pack, pre))
    early_edge, late_edge, own = edges(
        place, early, late, features, target, mask_row, early_pack, late_pack
    )
    late_edge = lax.ppermute(late_edge, "col", pairs("col", 1))
    early_edge = lax.ppermute(early_edge, "col", pairs("col", 0))
    inner = tile_backward(
        place, pre, slopes, early_pack, target, late_pack, mask_row, kernel_first, kernel_second, ok
    )

    def dealt(pieces):
        result = []
        for piece, step in zip(pieces, steps_of(col_devices)):
            swaps = [(i, i ^ step) for i in range(col_devices)]
            result.append(lax.ppermute(piece, "col", swaps) if step else piece)
        return result

    inner = dealt(inner)
    outer = sides(
        place, features.shape, late_edge, early_edge, own, kernel_first, kernel_second, ok
    )
    *outer, spatial_moved = lax.optimization_barrier((*outer, spatial_moved))
    outer = dealt(outer)

    cell_count = height * owned
    wide = [pltpu.VMEM((strip * half // LANES, width, LANES), jnp.float32)]
    slope = vmem_call(
        functools.partial(slope_kernel, row_norm, owned, devices),
        [jax.ShapeDtypeStruct((2, cell_count, half), jnp.float32)],
        spatial_moved,
        weight_mix,
        row_table,
        scratch=wide,
    )[0]
    outer[0], slope = lax.optimization_barrier((outer[0], slope))
    grad_cols, strip_grad = grad_spectrum(col_norm, place, inner, outer, weight_out, table)
    grad_rows = vmem_call(
        functools.partial(mix_kernel, row_norm, owned, devices),
        cells,
        swap(grad_cols),
        slope,
        weight_mix,
        row_table,
        row_back,
        scratch=wide,
    )[0]
    returned = swap(grad_rows)
    return output(col_norm, inputs.shape, returned, strip_grad, weight_in, weight_local, table_back)


def solution(mesh):
    in_specs = (
        P("row", "col", None),
        P("row", "col", None),
        P("row", "col"),
        P(),
        P(),
        P(("row", "col"), None, None),
        P(),
        P(),
        P(),
        P(),
    )
    out_specs = P(("row", "col"), None, None)
    return jax.shard_map(shards, mesh=mesh, in_specs=in_specs, out_specs=out_specs, check_vma=False)
```

```python
import functools
import math

import jax
import jax.numpy as jnp
import ml_dtypes
import numpy as np
from jax import lax
from jax.experimental import pallas as pl
from jax.experimental.pallas import tpu as pltpu
from jax.sharding import PartitionSpec as P

REACH = 8
NEAR = 4
MIB = 1024 * 1024
LANES = 128


def dot(left, right):
    return jnp.dot(left, right, preferred_element_type=jnp.float32)


def dot_t(left, right):
    return lax.dot_general(left, right, (((1,), (1,)), ((), ())), preferred_element_type=jnp.float32)


def vmem_call(body, shapes, *operands, flops=0, scratch=(), limit=10):
    spec = pl.BlockSpec(memory_space=pltpu.VMEM)
    size = sum(math.prod(a.shape) * a.dtype.itemsize for a in (*operands, *shapes))
    return pl.pallas_call(
        body,
        out_shape=shapes,
        in_specs=[spec] * len(operands),
        out_specs=[spec] * len(shapes),
        scratch_shapes=list(scratch),
        compiler_params=pltpu.CompilerParams(vmem_limit_bytes=limit * MIB),
        cost_estimate=pl.CostEstimate(flops=flops, bytes_accessed=size, transcendentals=0),
    )(*operands)


def in_hbm(array):
    return pltpu.with_memory_space_constraint(array, pltpu.HBM)


def phases(first, second, length):
    angle = (first[:, None] * second[None, :] % length) * (2.0 * math.pi / length)
    return np.cos(angle).astype(ml_dtypes.bfloat16), np.sin(angle).astype(ml_dtypes.bfloat16)


def column_matrix(width, devices):
    half = width // 2
    freq, col = np.arange(half), np.arange(width)
    cos, sin = phases(freq, col, width)
    sin[0] = (2 * (col % 2) - 1).astype(ml_dtypes.bfloat16)
    both = np.stack([cos, -sin]).reshape(2, devices, half // devices, width)
    return np.ascontiguousarray(both.transpose(1, 0, 2, 3)).reshape(width, width)


def row_matrix(height, row_devices, col_devices):
    devices = row_devices * col_devices
    strip = height // devices
    strips = np.arange(devices).reshape(row_devices, col_devices).T.reshape(-1)
    rows = (strips[None, :] * strip + np.arange(strip)[:, None]).reshape(-1)
    cos, sin = phases(np.arange(height), rows, height)
    return np.block([[cos, sin], [-sin, cos]])


def grad_kernel(norm, col, low, *refs):
    *pieces, weight, table, out, strip_out, projected = refs
    count = len(pieces) // 2
    _, strip, tile_cols, _ = strip_out.shape
    for step, inner, outer in zip(steps_of(count), pieces[:count], pieces[count:]):
        block = col[0] ^ step
        strip_out[block, :, REACH : tile_cols - REACH] = inner[...]
        strip_out[block, :, :REACH] = outer[:, :REACH]
        strip_out[block, :, tile_cols - REACH :] = outer[:, REACH:]
        rows = [dot_t(strip_out[block, r], weight[...]).astype(jnp.bfloat16) for r in range(strip)]
        where = pl.ds(pl.multiple_of(block * tile_cols, tile_cols), tile_cols)
        projected[where, :] = jnp.concatenate(rows, axis=1)
    out[...] = (dot(table[...], projected[...]) * norm).astype(jnp.bfloat16)


def grad_spectrum(norm, place, inner, outer, weight, table):
    strip, columns, channels = inner[0].shape
    shape = (table.shape[0], strip * weight.shape[0])
    in_vmem = pl.BlockSpec(memory_space=pltpu.VMEM)
    return pl.pallas_call(
        functools.partial(grad_kernel, norm),
        out_shape=[
            jax.ShapeDtypeStruct(shape, jnp.bfloat16),
            jax.ShapeDtypeStruct((len(inner), strip, columns + 2 * REACH, channels), jnp.bfloat16),
        ],
        in_specs=[pl.BlockSpec(memory_space=pltpu.SMEM)] * 2 + [in_vmem] * (2 * len(inner) + 2),
        out_specs=[in_vmem] * 2,
        scratch_shapes=[pltpu.VMEM(shape, jnp.bfloat16)],
        compiler_params=pltpu.CompilerParams(vmem_limit_bytes=10 * MIB),
        cost_estimate=pl.CostEstimate(flops=0, bytes_accessed=2 * MIB, transcendentals=0),
    )(*place, *inner, *outer, weight, table)


def fetching_spectrum_kernel(norm, signal, weight, table, out, signal_held, weight_held, table_held, sems):
    count = signal.shape[0]
    copies = [pltpu.make_async_copy(weight, weight_held, sems.at[0])]
    copies += [
        pltpu.make_async_copy(signal.at[r], signal_held.at[r], sems.at[1 + r]) for r in range(count)
    ]
    copies.append(pltpu.make_async_copy(table, table_held, sems.at[1 + count]))
    for copy in copies:
        copy.start()
    copies[0].wait()
    rows = []
    for r in range(count):
        copies[1 + r].wait()
        rows.append(dot_t(signal_held[r], weight_held[...]).astype(jnp.bfloat16))
    copies[-1].wait()
    out[...] = (dot(table_held[...], jnp.concatenate(rows, axis=1)) * norm).astype(jnp.bfloat16)


def fetching_spectrum(norm, shape, signal, weight, table):
    operands = (signal, weight, table)
    return pl.pallas_call(
        functools.partial(fetching_spectrum_kernel, norm),
        out_shape=shape,
        in_specs=[pl.BlockSpec(memory_space=pltpu.HBM)] * 3,
        out_specs=pl.BlockSpec(memory_space=pltpu.VMEM),
        scratch_shapes=[pltpu.VMEM(a.shape, a.dtype) for a in operands]
        + [pltpu.SemaphoreType.DMA((signal.shape[0] + 2,))],
        compiler_params=pltpu.CompilerParams(vmem_limit_bytes=12 * MIB),
        cost_estimate=pl.CostEstimate(
            flops=0, bytes_accessed=2 * MIB, transcendentals=0
        ),
    )(*[in_hbm(a) for a in operands])


def row_spectrum(moved, table, wide, norm, owned, devices):
    groups = wide.shape[0]
    for g in range(groups):
        wide[g] = moved[:, g * LANES : (g + 1) * LANES].astype(jnp.float32)
    strip = table.shape[1] // (2 * devices)
    half = moved.shape[1] // strip
    height = table.shape[0] // 2
    real, imag = [], []
    for freq in range(owned):
        parts = []
        for part in range(2):
            where = pl.ds(part * owned + freq, devices, stride=2 * owned)
            block = jnp.concatenate([wide[g, where, :] for g in range(groups)], axis=1)
            parts += [block[:, r * half : (r + 1) * half] for r in range(strip)]
        result = dot(table[...], jnp.concatenate(parts, axis=0).astype(jnp.bfloat16)) * norm
        real.append(result[:height])
        imag.append(result[height:])
    return jnp.concatenate(real, axis=0), jnp.concatenate(imag, axis=0)


def slope_kernel(norm, owned, devices, moved, mix, table, out, wide):
    parts = row_spectrum(moved, table, wide, norm, owned, devices)
    real, imag = [part.astype(jnp.bfloat16) for part in parts]
    half = real.shape[1]
    spans = (slice(0, half), slice(half, 2 * half))
    for part, span in enumerate(spans):
        pre = dot(real, mix[spans[0], span]) + dot(imag, mix[spans[1], span])
        s = 1.0 / (1.0 + jnp.exp(-pre))
        out[part] = s * (1.0 + pre * (1.0 - s))


def mix_kernel(norm, owned, devices, moved, slope, mix, table, back_table, out, wide):
    grads = row_spectrum(moved, table, wide, norm, owned, devices)
    half = grads[0].shape[1]
    spans = (slice(0, half), slice(half, 2 * half))
    mixed = [(grad * slope[part]).astype(jnp.bfloat16) for part, grad in enumerate(grads)]
    back = [dot_t(mixed[0], mix[p, spans[0]]) + dot_t(mixed[1], mix[p, spans[1]]) for p in spans]
    back = [part.astype(jnp.bfloat16) for part in back]
    height = table.shape[0] // 2
    strip = height // devices
    groups = wide.shape[0]
    for freq in range(owned):
        cells = slice(freq * height, (freq + 1) * height)
        stacked = jnp.concatenate([back[0][cells], back[1][cells]], axis=0)
        result = dot(back_table[...], stacked) * norm
        for part in range(2):
            rows = [
                result[(part * strip + r) * devices : (part * strip + r + 1) * devices]
                for r in range(strip)
            ]
            where = pl.ds(part * owned + freq, devices, stride=2 * owned)
            values = jnp.concatenate(rows, axis=1)
            for g in range(groups):
                wide[g, where, :] = values[:, g * LANES : (g + 1) * LANES]
    for g in range(groups):
        out[:, g * LANES : (g + 1) * LANES] = wide[g].astype(jnp.bfloat16)


def output_kernel(norm, moved, strip_grad, weight_in, weight_local, table, out, held, sems):
    half = weight_in.shape[0]
    blocks, strip, tile_cols, _ = strip_grad.shape
    count = 2 if blocks % 2 == 0 else 1
    columns = blocks // count * tile_cols
    copies = []
    for part in range(count):
        where = slice(part * columns, (part + 1) * columns)
        spatial = (dot(table[where], moved[...]) * norm).astype(jnp.bfloat16)
        for r in range(strip):
            grads = [strip_grad[part * (blocks // count) + i, r] for i in range(blocks // count)]
            total = dot(spatial[:, r * half : (r + 1) * half], weight_in[...])
            total = total + dot_t(jnp.concatenate(grads, axis=0), weight_local[...])
            held[r, where] = total.astype(jnp.bfloat16)
            copies.append(
                pltpu.make_async_copy(held.at[r, where], out.at[r, where], sems.at[len(copies)])
            )
            copies[-1].start()
    for copy in copies:
        copy.wait()


def output(norm, shape, *operands):
    return pl.pallas_call(
        functools.partial(output_kernel, norm),
        out_shape=jax.ShapeDtypeStruct(shape, jnp.bfloat16),
        in_specs=[pl.BlockSpec(memory_space=pltpu.VMEM)] * len(operands),
        out_specs=pl.BlockSpec(memory_space=pltpu.HBM),
        scratch_shapes=[pltpu.VMEM(shape, jnp.bfloat16), pltpu.SemaphoreType.DMA((2 * shape[0],))],
        compiler_params=pltpu.CompilerParams(vmem_limit_bytes=10 * MIB),
        cost_estimate=pl.CostEstimate(flops=0, bytes_accessed=3 * MIB, transcendentals=0),
    )(*operands)


TAIL = 16


def pick(flag, left, right):
    return lax.select(flag, left, right)


def odd_row(place):
    return place[1] == 1


def odd_col(place):
    return lax.rem(place[0], 2) == 1


def turned(rows):
    count, columns = rows.shape
    rows = rows.astype(jnp.float32)
    return jnp.concatenate([rows, jnp.zeros((columns - count, columns), jnp.float32)], axis=0).T


def filled(lanes, channels):
    fill = jnp.zeros((lanes.shape[0], channels - lanes.shape[1]), jnp.float32)
    return jnp.concatenate([lanes, fill], axis=1).astype(jnp.bfloat16)


def pack_kernel(col, low, target, mask, early, late, mask_row, mask_held, sems):
    place = col[0], low[0]
    tile_rows, tile_cols = mask.shape
    channels = target.shape[1]
    last = tile_rows - NEAR
    pixels = NEAR * tile_cols
    moves = [(mask, mask_held)]
    for pack, row in ((early, (1 - place[1]) * last), (late, place[1] * last)):
        moves.append((target.at[pl.ds(row * tile_cols, pixels)], pack.at[pl.ds(0, pixels)]))
    copies = [pltpu.make_async_copy(*move, sems.at[i]) for i, move in enumerate(moves)]
    for copy in copies:
        copy.start()
    copies[0].wait()
    mask_row[0] = filled(turned(mask_held[...]), channels)
    ends = (mask_held[:NEAR], mask_held[last:])
    for pack, (one, other) in ((early, ends), (late, ends[::-1])):
        rows = pick(odd_row(place), one.astype(jnp.float32), other.astype(jnp.float32))
        rows = jnp.concatenate([rows, jnp.zeros((TAIL - NEAR, tile_cols), jnp.float32)], axis=0)
        pack[pixels:] = filled(rows, channels)
    for copy in copies[1:]:
        copy.wait()


def target_packs(place, target, mask):
    tile_rows, tile_cols, channels = target.shape
    pack = (NEAR * tile_cols + TAIL, channels)
    hbm = pl.BlockSpec(memory_space=pltpu.HBM)
    shapes = [pack, pack, (1, tile_cols, channels)]
    return pl.pallas_call(
        pack_kernel,
        out_shape=[jax.ShapeDtypeStruct(shape, jnp.bfloat16) for shape in shapes],
        in_specs=[pl.BlockSpec(memory_space=pltpu.SMEM)] * 2 + [hbm, hbm],
        out_specs=[pl.BlockSpec(memory_space=pltpu.VMEM)] * len(shapes),
        scratch_shapes=[pltpu.VMEM(mask.shape, mask.dtype), pltpu.SemaphoreType.DMA((3,))],
        compiler_params=pltpu.CompilerParams(vmem_limit_bytes=4 * MIB),
        cost_estimate=pl.CostEstimate(flops=0, bytes_accessed=MIB, transcendentals=0),
    )(*place, in_hbm(target.reshape(tile_rows * tile_cols, channels)), in_hbm(mask))


def fetch_kernel(*refs):
    count = len(refs) // 2
    sems = refs[-1]
    copies = [pltpu.make_async_copy(refs[i], refs[count + i], sems.at[i]) for i in range(count)]
    for copy in copies:
        copy.start()
    for copy in copies:
        copy.wait()


def fetch(*arrays):
    return pl.pallas_call(
        fetch_kernel,
        out_shape=[jax.ShapeDtypeStruct(a.shape, a.dtype) for a in arrays],
        in_specs=[pl.BlockSpec(memory_space=pltpu.HBM)] * len(arrays),
        out_specs=[pl.BlockSpec(memory_space=pltpu.VMEM)] * len(arrays),
        scratch_shapes=[pltpu.SemaphoreType.DMA((len(arrays),))],
        compiler_params=pltpu.CompilerParams(vmem_limit_bytes=4 * MIB),
        cost_estimate=pl.CostEstimate(flops=0, bytes_accessed=5 * MIB, transcendentals=0),
    )(*[in_hbm(a) for a in arrays])


def edge_kernel(tile_cols, col, low, late_pack, early_pack, *refs):
    place = col[0], low[0]
    sources, (early, late, own) = refs[:-3], refs[-3:]
    count = len(sources) // 2
    keep = 2 * REACH
    channels = own.shape[2]
    lower, high = odd_row(place), odd_col(place)

    def put_rows(row, tail, head):
        rows = slice(row, row + tail.shape[0])
        last, initial = tail[:, REACH:], head[:, :REACH]
        early[rows] = pick(high, initial, last)
        late[rows] = pick(high, last, initial)
        own[rows, :keep] = head
        own[rows, keep:] = tail

    def put_pack(row, one, other):
        for i in range(NEAR):
            at = i * tile_cols
            tail = pick(lower, one[at + tile_cols - keep : at + tile_cols], other[at + tile_cols - keep : at + tile_cols])
            head = pick(lower, one[at : at + keep], other[at : at + keep])
            put_rows(row + i, tail[None], head[None])
        mask = turned(pick(lower, one[NEAR * tile_cols :, :tile_cols], other[NEAR * tile_cols :, :tile_cols]))
        tail, head = [filled(m, channels)[None] for m in (mask[tile_cols - keep :], mask[:keep])]
        put_rows(row + NEAR, tail, head)

    def put_picked(row, one, other):
        put_rows(row, *[pick(lower, sources[one + i * count][...], sources[other + i * count][...]) for i in (0, 1)])

    def put_own(row, index):
        put_rows(row, sources[index][...], sources[index + count][...])

    rows = sources[0].shape[0]
    put_picked(0, 0, 1)
    put_own(rows, 2)
    put_picked(2 * rows, 1, 0)
    put_pack(3 * rows, early_pack, late_pack)
    put_own(3 * rows + NEAR + 1, 3)
    put_own(4 * rows + NEAR + 1, 4)
    put_pack(4 * rows + NEAR + 2, late_pack, early_pack)


def edges(place, early, late, features, target, mask_row, early_pack, late_pack):
    parts = (early, late, features, target, mask_row)
    _, tile_cols, channels = features.shape
    keep = 2 * REACH
    tail = tile_cols // keep - 1

    def specs(at):
        return [pl.BlockSpec((p.shape[0], keep, channels), lambda i, at=at: (0, at, 0)) for p in parts]

    whole = [pl.BlockSpec(early_pack.shape, lambda i: (0, 0))] * 2
    rows = sum(p.shape[0] for p in parts) + 2 * (NEAR + 1)
    shapes = [(rows, columns, channels) for columns in (REACH, REACH, 2 * keep)]
    return pl.pallas_call(
        functools.partial(edge_kernel, tile_cols),
        grid=(1,),
        out_shape=[jax.ShapeDtypeStruct(shape, features.dtype) for shape in shapes],
        in_specs=[pl.BlockSpec(memory_space=pltpu.SMEM)] * 2 + whole + specs(tail) + specs(0),
        out_specs=[pl.BlockSpec(shape, lambda i: (0, 0, 0)) for shape in shapes],
        compiler_params=pltpu.CompilerParams(vmem_limit_bytes=8 * MIB),
        cost_estimate=pl.CostEstimate(
            flops=0, bytes_accessed=16 * rows * keep * channels, transcendentals=0
        ),
    )(*place, late_pack, early_pack, *parts, *parts)


def put(wide, row, value, stride):
    size, channels = value.shape
    spot = pl.ds(row * stride, size)
    wide[spot, :channels] = pltpu.roll(value, 2, 0).astype(jnp.bfloat16)
    wide[spot, channels : 2 * channels] = value.astype(jnp.bfloat16)
    wide[spot, 2 * channels :] = pltpu.roll(value, size - 2, 0).astype(jnp.bfloat16)


def taps(wide, row, count, stride):
    parts = [wide[pl.ds((row + 2 * a) * stride, count * stride), :] for a in range(3)]
    return jnp.concatenate(parts, axis=1)


def conv(wide, row, count, stride, kernel):
    channels = kernel.shape[-1]
    return dot(taps(wide, row, count, stride), kernel[...].reshape(9 * channels, channels))


def conv_adjoint(wide, row, count, stride, kernel):
    flipped = [kernel[2 - a, 2 - b] for a in range(3) for b in range(3)]
    return dot_t(taps(wide, row, count, stride), jnp.concatenate(flipped, axis=1))


def stacked(piece, rows):
    return jnp.concatenate([piece(row) for row in rows], axis=0)


def first_stages(
    stride, blocks, rows, feature, inside, first, second, wide_even, wide_odd, slopes, use
):
    tall = rows + 2 * REACH
    for row in range(0, tall, NEAR):
        put(wide_even, row, stacked(feature, range(row, row + NEAR)), stride)
    count = blocks[0]
    for row in range(0, tall - 4, count):
        pre = conv(wide_even, row, count, stride, first)
        s = 1.0 / (1.0 + jnp.exp(-pre))
        kept = stacked(inside, range(row + 2, row + 2 + count))
        put(wide_odd, row, pre * s * kept, stride)
        low, high = max(row, NEAR), min(row + count, tall - 4 - NEAR)
        if low < high:
            part = slice((low - row) * stride, (high - row) * stride)
            slope = (s * (1.0 + pre * (1.0 - s)) * kept)[part]
            slopes[pl.ds((low - NEAR) * stride, (high - low) * stride), :] = slope
    count = blocks[1]
    for row in range(0, rows + 2 * NEAR, count):
        use(row, count, conv(wide_odd, row, count, stride, second))


def last_stages(stride, blocks, rows, first, second, wide_even, wide_odd, slopes, use):
    count = blocks[2]
    for row in range(0, rows + 4, count):
        value = conv_adjoint(wide_even, row, count, stride, second)
        value = value * slopes[pl.ds(row * stride, count * stride), :]
        put(wide_odd, row, value, stride)
    count = blocks[3]
    for row in range(0, rows, count):
        use(row, count, conv_adjoint(wide_odd, row, count, stride, first))


def steps_of(count):
    return [0, *range(2, count), 1] if count > 1 else [0]


def deal(place, out, pieces):
    for step, piece in zip(steps_of(len(pieces)), pieces):
        piece[...] = out[pl.ds((place[0] ^ step) * piece.shape[0], piece.shape[0])]


def loss_grad(row, count, value, target, hole, inside):
    near = range(row, row + count)
    weight = (1.0 + 2.0 * stacked(hole, near)) * stacked(inside, range(row + NEAR, row + count + NEAR))
    return weight * (value - stacked(target, near))


def part_of(rows, edge, above, own, below):
    def find(row):
        if row < edge:
            return above, row
        if row < edge + rows:
            return own, row - edge
        return below, row - edge - rows

    return find


TILE_BLOCKS = (2, 2, 2, 2)
SIDE_BLOCKS = (5, 4, 6, 4)


def tile_forward_kernel(
    col, low, early, features, late, first, second, ok, pre, slopes, wide_even, wide_odd
):
    place = col[0], low[0]
    rows, stride, _ = features.shape
    find = part_of(rows, REACH, (early, late), (features,), (late, early))

    def feature(row):
        sources, at = find(row)
        if len(sources) == 1:
            return features[at].astype(jnp.float32)
        return pick(odd_row(place), *[source[at] for source in sources]).astype(jnp.float32)

    def inside(row):
        return ok[REACH : REACH + stride, row : row + 1]

    def use(row, count, value):
        pre[pl.ds(row * stride, count * stride), :] = value

    first_stages(
        stride, TILE_BLOCKS, rows, feature, inside, first, second, wide_even, wide_odd, slopes, use
    )


def tile_backward_kernel(
    col,
    low,
    pre,
    slopes,
    early_pack,
    target,
    late_pack,
    mask_row,
    first,
    second,
    ok,
    *refs,
):
    *pieces, out, wide_even, wide_odd = refs
    place = col[0], low[0]
    rows, stride, channels = target.shape
    packs = (early_pack, late_pack)
    find = part_of(rows, NEAR, packs, (target,), packs[::-1])

    def picked(sources, part):
        return pick(odd_row(place), *[source[part] for source in sources]).astype(jnp.float32)

    def goal(row):
        sources, at = find(row)
        if len(sources) == 1:
            return target[at].astype(jnp.float32)
        return picked(sources, slice(at * stride, (at + 1) * stride))

    masks = [
        turned(picked(sources, slice(NEAR * stride, None))[:, :stride]) for sources in (packs, packs[::-1])
    ]
    find_mask = part_of(rows, NEAR, (masks[0], 0), (mask_row[0].astype(jnp.float32), 0), (masks[1], 0))

    def hole(row):
        (mask, start), at = find_mask(row)
        return mask[:, start + at : start + at + 1]

    def inside(row):
        return ok[REACH : REACH + stride, row : row + 1]

    count = NEAR
    for row in range(0, rows + 2 * NEAR, count):
        value = pre[pl.ds(row * stride, count * stride), :]
        put(wide_even, row, loss_grad(row, count, value, goal, hole, inside), stride)

    def use(row, count, value):
        value = value.reshape(count, stride, channels)[:, REACH : stride - REACH]
        out[row : row + count] = value.astype(jnp.bfloat16)

    last_stages(stride, TILE_BLOCKS, rows, first, second, wide_even, wide_odd, slopes, use)
    deal(place, out, pieces)


def side_kernel(col, low, late, early, own, first, second, ok, *refs):
    *pieces, out, wide_even, wide_odd, slopes = refs
    place = col[0], low[0]
    rows, _, channels = out.shape
    keep = 2 * REACH
    stride = 2 * (REACH + keep)
    tall = rows + 2 * REACH
    odd = odd_col(place)

    def feature(row):
        before, after = pick(odd, early[row], late[row]), pick(odd, late[row], early[row])
        parts = [part.astype(jnp.float32) for part in (before, own[row], after)]
        return jnp.concatenate(parts, axis=0)

    find = part_of(rows, NEAR, tall, tall + NEAR + 1, tall + NEAR + 1 + rows + 1)

    def goal(row):
        start, at = find(row)
        return feature(start + at)

    masks = [feature(row) for row in (tall + NEAR, tall + NEAR + 1 + rows, early.shape[0] - 1)]
    find_mask = part_of(rows, NEAR, (masks[0], 0), (masks[1], 0), (masks[2], 0))

    def hole(row):
        (mask, start), at = find_mask(row)
        return mask[:, start + at : start + at + 1]

    width = ok.shape[0]
    kept = jnp.concatenate([ok[: REACH + keep], ok[width - REACH - keep :]], axis=0)

    def inside(row):
        return kept[:, row : row + 1]

    def use_forward(row, count, value):
        put(wide_even, row, loss_grad(row, count, value, goal, hole, inside), stride)

    first_stages(
        stride, SIDE_BLOCKS, rows, feature, inside, first, second, wide_even, wide_odd, slopes, use_forward
    )

    def use(row, count, value):
        value = value.reshape(count, stride, channels).astype(jnp.bfloat16)
        out[row : row + count, :REACH] = value[:, REACH : 2 * REACH]
        out[row : row + count, REACH:] = value[:, stride - 2 * REACH : stride - REACH]

    last_stages(stride, SIDE_BLOCKS, rows, first, second, wide_even, wide_odd, slopes, use)
    deal(place, out, pieces)


def wide_buffer(rows, stride, channels):
    return pltpu.VMEM((rows * stride, 3 * channels), jnp.bfloat16)


def tile_forward(place, early, features, late, first, second, ok):
    rows, stride, channels = features.shape
    shapes = [
        jax.ShapeDtypeStruct(((rows + h) * stride, channels), jnp.float32) for h in (2 * NEAR, 4)
    ]
    in_vmem = pl.BlockSpec(memory_space=pltpu.VMEM)
    return pl.pallas_call(
        tile_forward_kernel,
        out_shape=shapes,
        in_specs=[pl.BlockSpec(memory_space=pltpu.SMEM)] * 2 + [in_vmem] * 6,
        out_specs=[in_vmem] * 2,
        scratch_shapes=[wide_buffer(rows + h, stride, channels) for h in (16, 12)],
        compiler_params=pltpu.CompilerParams(vmem_limit_bytes=22 * MIB),
        cost_estimate=pl.CostEstimate(
            flops=2 * 9 * channels * channels * stride * (2 * rows + 20),
            bytes_accessed=8 * MIB,
            transcendentals=0,
        ),
    )(*place, early, features, late, first, second, ok)


def piece_shapes(rows, columns, channels):
    count = lax.axis_size("col")
    return [jax.ShapeDtypeStruct((rows // count, columns, channels), jnp.bfloat16)] * count


def tile_backward(place, pre, slopes, early_pack, target, *operands):
    rows, stride, channels = target.shape
    in_vmem = pl.BlockSpec(memory_space=pltpu.VMEM)
    shapes = piece_shapes(rows, stride - 2 * REACH, channels)
    return pl.pallas_call(
        tile_backward_kernel,
        out_shape=shapes,
        in_specs=[pl.BlockSpec(memory_space=pltpu.SMEM)] * 2 + [in_vmem] * (4 + len(operands)),
        out_specs=[in_vmem] * len(shapes),
        scratch_shapes=[
            pltpu.VMEM((rows, stride - 2 * REACH, channels), jnp.bfloat16),
            *[wide_buffer(rows + h, stride, channels) for h in (8, 4)],
        ],
        compiler_params=pltpu.CompilerParams(vmem_limit_bytes=16 * MIB),
        cost_estimate=pl.CostEstimate(
            flops=2 * 9 * channels * channels * stride * (2 * rows + 4),
            bytes_accessed=8 * MIB,
            transcendentals=0,
        ),
    )(*place, pre, slopes, early_pack, target, *operands)


def sides(place, shape, *operands):
    rows, _, channels = shape
    stride = 6 * REACH
    in_vmem = pl.BlockSpec(memory_space=pltpu.VMEM)
    shapes = piece_shapes(rows, 2 * REACH, channels)
    return pl.pallas_call(
        side_kernel,
        out_shape=shapes,
        in_specs=[pl.BlockSpec(memory_space=pltpu.SMEM)] * 2 + [in_vmem] * len(operands),
        out_specs=[in_vmem] * len(shapes),
        scratch_shapes=[
            pltpu.VMEM((rows, 2 * REACH, channels), jnp.bfloat16),
            *[wide_buffer(rows + h, stride, channels) for h in (16, 12)],
            pltpu.VMEM(((rows + 4) * stride, channels), jnp.float32),
        ],
        compiler_params=pltpu.CompilerParams(vmem_limit_bytes=18 * MIB),
        cost_estimate=pl.CostEstimate(
            flops=2 * 9 * channels * channels * stride * (4 * rows + 24),
            bytes_accessed=4 * MIB,
            transcendentals=0,
        ),
    )(*place, *operands)


def pairs(axis, start):
    size = lax.axis_size(axis)
    up = [(i, i + 1) for i in range(start, size - 1, 2)]
    return up + [(j, i) for i, j in up]


def shards(
    features,
    target,
    hole_mask,
    kernel_first,
    kernel_second,
    inputs,
    weight_in,
    weight_out,
    weight_local,
    weight_mix,
):
    tile_rows, tile_cols, channels = features.shape
    row_devices, col_devices = lax.axis_size("row"), lax.axis_size("col")
    devices = row_devices * col_devices
    height, width = tile_rows * row_devices, tile_cols * col_devices
    strip, half = inputs.shape[0], weight_in.shape[1]
    owned = width // 2 // devices
    col_norm, row_norm = 1.0 / math.sqrt(width), 1.0 / math.sqrt(height)
    table = column_matrix(width, devices)
    table_back = jnp.asarray(np.ascontiguousarray(table.T))
    table = jnp.asarray(table)
    row_table = row_matrix(height, row_devices, col_devices)
    row_back = jnp.asarray(np.ascontiguousarray(row_table.T))
    row_table = jnp.asarray(row_table)
    bf16 = jnp.bfloat16

    def swap(spectrum):
        return lax.all_to_all(spectrum, ("col", "row"), split_axis=0, concat_axis=0, tiled=True)

    row0, col0 = lax.axis_index("row") * tile_rows, lax.axis_index("col") * tile_cols
    row_ids = row0 - REACH + jnp.arange(tile_rows + 2 * REACH, dtype=jnp.int32)
    col_ids = col0 - REACH + jnp.arange(tile_cols + 2 * REACH, dtype=jnp.int32)
    ok = ((col_ids >= 0) & (col_ids < width))[:, None] & ((row_ids >= 0) & (row_ids < height))[None]
    ok = ok.astype(jnp.float32)
    place = tuple(jnp.full((1,), i, jnp.int32) for i in (lax.axis_index("col"), lax.axis_index("row") & 1))
    early_pack, late_pack, mask_row = target_packs(place, target, hole_mask)
    inputs, ok, early_pack = lax.optimization_barrier((inputs, ok, early_pack))

    cells = [jax.ShapeDtypeStruct((width, strip * half), bf16)]
    weight_in = weight_in.T
    spatial_cols = fetching_spectrum(col_norm, cells[0], inputs, weight_in, table)
    spatial_moved = swap(spatial_cols)

    early = lax.ppermute(features, "row", pairs("row", 0))
    late = lax.ppermute(features, "row", pairs("row", 1))
    kernel_first, spatial_cols = lax.optimization_barrier((kernel_first, spatial_cols))
    kernel_first, kernel_second = fetch(kernel_first, kernel_second)
    late_pack = lax.ppermute(late_pack, "row", pairs("row", 1))
    early_pack = lax.ppermute(early_pack, "row", pairs("row", 0))
    pre, slopes = tile_forward(place, early, features, late, kernel_first, kernel_second, ok)
    late_pack, pre = lax.optimization_barrier((late_pack, pre))
    early_edge, late_edge, own = edges(
        place, early, late, features, target, mask_row, early_pack, late_pack
    )
    late_edge = lax.ppermute(late_edge, "col", pairs("col", 1))
    early_edge = lax.ppermute(early_edge, "col", pairs("col", 0))
    inner = tile_backward(
        place, pre, slopes, early_pack, target, late_pack, mask_row, kernel_first, kernel_second, ok
    )

    def dealt(pieces):
        result = []
        for piece, step in zip(pieces, steps_of(col_devices)):
            swaps = [(i, i ^ step) for i in range(col_devices)]
            result.append(lax.ppermute(piece, "col", swaps) if step else piece)
        return result

    inner = dealt(inner)
    outer = sides(
        place, features.shape, late_edge, early_edge, own, kernel_first, kernel_second, ok
    )
    *outer, spatial_moved = lax.optimization_barrier((*outer, spatial_moved))
    outer = dealt(outer)

    cell_count = height * owned
    wide = [pltpu.VMEM((strip * half // LANES, width, LANES), jnp.float32)]
    slope = vmem_call(
        functools.partial(slope_kernel, row_norm, owned, devices),
        [jax.ShapeDtypeStruct((2, cell_count, half), jnp.float32)],
        spatial_moved,
        weight_mix,
        row_table,
        scratch=wide,
    )[0]
    outer[0], slope = lax.optimization_barrier((outer[0], slope))
    grad_cols, strip_grad = grad_spectrum(col_norm, place, inner, outer, weight_out, table)
    grad_rows = vmem_call(
        functools.partial(mix_kernel, row_norm, owned, devices),
        cells,
        swap(grad_cols),
        slope,
        weight_mix,
        row_table,
        row_back,
        scratch=wide,
    )[0]
    returned = swap(grad_rows)
    return output(col_norm, inputs.shape, returned, strip_grad, weight_in, weight_local, table_back)


def solution(mesh):
    in_specs = (
        P("row", "col", None),
        P("row", "col", None),
        P("row", "col"),
        P(),
        P(),
        P(("row", "col"), None, None),
        P(),
        P(),
        P(),
        P(),
    )
    out_specs = P(("row", "col"), None, None)
    return jax.shard_map(shards, mesh=mesh, in_specs=in_specs, out_specs=out_specs, check_vma=False)
```

```python
import functools
import math

import jax
import jax.numpy as jnp
import ml_dtypes
import numpy as np
from jax import lax
from jax.experimental import pallas as pl
from jax.experimental.pallas import tpu as pltpu
from jax.sharding import PartitionSpec as P

REACH = 8
NEAR = 4
MIB = 1024 * 1024
LANES = 128


def dot(left, right):
    return jnp.dot(left, right, preferred_element_type=jnp.float32)


def dot_t(left, right):
    return lax.dot_general(left, right, (((1,), (1,)), ((), ())), preferred_element_type=jnp.float32)


def vmem_call(body, shapes, *operands, flops=0, scratch=(), limit=10):
    spec = pl.BlockSpec(memory_space=pltpu.VMEM)
    size = sum(math.prod(a.shape) * a.dtype.itemsize for a in (*operands, *shapes))
    return pl.pallas_call(
        body,
        out_shape=shapes,
        in_specs=[spec] * len(operands),
        out_specs=[spec] * len(shapes),
        scratch_shapes=list(scratch),
        compiler_params=pltpu.CompilerParams(vmem_limit_bytes=limit * MIB),
        cost_estimate=pl.CostEstimate(flops=flops, bytes_accessed=size, transcendentals=0),
    )(*operands)


def in_hbm(array):
    return pltpu.with_memory_space_constraint(array, pltpu.HBM)


def phases(first, second, length):
    angle = (first[:, None] * second[None, :] % length) * (2.0 * math.pi / length)
    return np.cos(angle).astype(ml_dtypes.bfloat16), np.sin(angle).astype(ml_dtypes.bfloat16)


def column_matrix(width, devices):
    half = width // 2
    freq, col = np.arange(half), np.arange(width)
    cos, sin = phases(freq, col, width)
    sin[0] = (2 * (col % 2) - 1).astype(ml_dtypes.bfloat16)
    both = np.stack([cos, -sin]).reshape(2, devices, half // devices, width)
    return np.ascontiguousarray(both.transpose(1, 0, 2, 3)).reshape(width, width)


def row_matrix(height, row_devices, col_devices):
    devices = row_devices * col_devices
    strip = height // devices
    strips = np.arange(devices).reshape(row_devices, col_devices).T.reshape(-1)
    rows = (strips[None, :] * strip + np.arange(strip)[:, None]).reshape(-1)
    cos, sin = phases(np.arange(height), rows, height)
    return np.block([[cos, sin], [-sin, cos]])


def grad_kernel(norm, col, low, *refs):
    *pieces, weight, table, out, strip_out, projected = refs
    count = len(pieces) // 2
    _, strip, tile_cols, _ = strip_out.shape
    for step, inner, outer in zip(steps_of(count), pieces[:count], pieces[count:]):
        block = col[0] ^ step
        strip_out[block, :, REACH : tile_cols - REACH] = inner[...]
        strip_out[block, :, :REACH] = outer[:, :REACH]
        strip_out[block, :, tile_cols - REACH :] = outer[:, REACH:]
        rows = [dot_t(strip_out[block, r], weight[...]).astype(jnp.bfloat16) for r in range(strip)]
        where = pl.ds(pl.multiple_of(block * tile_cols, tile_cols), tile_cols)
        projected[where, :] = jnp.concatenate(rows, axis=1)
    out[...] = (dot(table[...], projected[...]) * norm).astype(jnp.bfloat16)


def grad_spectrum(norm, place, inner, outer, weight, table):
    strip, columns, channels = inner[0].shape
    shape = (table.shape[0], strip * weight.shape[0])
    in_vmem = pl.BlockSpec(memory_space=pltpu.VMEM)
    return pl.pallas_call(
        functools.partial(grad_kernel, norm),
        out_shape=[
            jax.ShapeDtypeStruct(shape, jnp.bfloat16),
            jax.ShapeDtypeStruct((len(inner), strip, columns + 2 * REACH, channels), jnp.bfloat16),
        ],
        in_specs=[pl.BlockSpec(memory_space=pltpu.SMEM)] * 2 + [in_vmem] * (2 * len(inner) + 2),
        out_specs=[in_vmem] * 2,
        scratch_shapes=[pltpu.VMEM(shape, jnp.bfloat16)],
        compiler_params=pltpu.CompilerParams(vmem_limit_bytes=10 * MIB),
        cost_estimate=pl.CostEstimate(flops=0, bytes_accessed=2 * MIB, transcendentals=0),
    )(*place, *inner, *outer, weight, table)


def fetching_spectrum_kernel(norm, signal, weight, table, out, signal_held, weight_held, table_held, sems):
    count = signal.shape[0]
    copies = [pltpu.make_async_copy(weight, weight_held, sems.at[0])]
    copies += [
        pltpu.make_async_copy(signal.at[r], signal_held.at[r], sems.at[1 + r]) for r in range(count)
    ]
    copies.append(pltpu.make_async_copy(table, table_held, sems.at[1 + count]))
    for copy in copies:
        copy.start()
    copies[0].wait()
    rows = []
    for r in range(count):
        copies[1 + r].wait()
        rows.append(dot_t(signal_held[r], weight_held[...]).astype(jnp.bfloat16))
    copies[-1].wait()
    out[...] = (dot(table_held[...], jnp.concatenate(rows, axis=1)) * norm).astype(jnp.bfloat16)


def fetching_spectrum(norm, shape, signal, weight, table):
    operands = (signal, weight, table)
    return pl.pallas_call(
        functools.partial(fetching_spectrum_kernel, norm),
        out_shape=shape,
        in_specs=[pl.BlockSpec(memory_space=pltpu.HBM)] * 3,
        out_specs=pl.BlockSpec(memory_space=pltpu.VMEM),
        scratch_shapes=[pltpu.VMEM(a.shape, a.dtype) for a in operands]
        + [pltpu.SemaphoreType.DMA((signal.shape[0] + 2,))],
        compiler_params=pltpu.CompilerParams(vmem_limit_bytes=12 * MIB),
        cost_estimate=pl.CostEstimate(
            flops=0, bytes_accessed=2 * MIB, transcendentals=0
        ),
    )(*[in_hbm(a) for a in operands])


def row_spectrum(moved, table, wide, norm, owned, devices):
    groups = wide.shape[0]
    for g in range(groups):
        wide[g, : moved.shape[0]] = moved[:, g * LANES : (g + 1) * LANES].astype(jnp.float32)
    strip = table.shape[1] // (2 * devices)
    half = moved.shape[1] // strip
    height = table.shape[0] // 2
    real, imag = [], []
    for freq in range(owned):
        parts = []
        for part in range(2):
            where = pl.ds(part * owned + freq, devices, stride=2 * owned)
            block = jnp.concatenate([wide[g, where, :] for g in range(groups)], axis=1)
            parts += [block[:, r * half : (r + 1) * half] for r in range(strip)]
        result = dot(table[...], jnp.concatenate(parts, axis=0).astype(jnp.bfloat16)) * norm
        real.append(result[:height])
        imag.append(result[height:])
    return jnp.concatenate(real, axis=0), jnp.concatenate(imag, axis=0)


def slope_kernel(norm, owned, devices, moved, mix, table, out, wide):
    parts = row_spectrum(moved, table, wide, norm, owned, devices)
    real, imag = [part.astype(jnp.bfloat16) for part in parts]
    half = real.shape[1]
    spans = (slice(0, half), slice(half, 2 * half))
    for part, span in enumerate(spans):
        pre = dot(real, mix[spans[0], span]) + dot(imag, mix[spans[1], span])
        s = 1.0 / (1.0 + jnp.exp(-pre))
        out[part] = s * (1.0 + pre * (1.0 - s))


def mix_kernel(norm, owned, devices, moved, slope, mix, table, back_table, out, wide):
    grads = row_spectrum(moved, table, wide, norm, owned, devices)
    half = grads[0].shape[1]
    spans = (slice(0, half), slice(half, 2 * half))
    mixed = [(grad * slope[part]).astype(jnp.bfloat16) for part, grad in enumerate(grads)]
    back = [dot_t(mixed[0], mix[p, spans[0]]) + dot_t(mixed[1], mix[p, spans[1]]) for p in spans]
    back = [part.astype(jnp.bfloat16) for part in back]
    height = table.shape[0] // 2
    strip = height // devices
    groups = wide.shape[0]
    for freq in range(owned):
        cells = slice(freq * height, (freq + 1) * height)
        stacked = jnp.concatenate([back[0][cells], back[1][cells]], axis=0)
        result = dot(back_table[...], stacked) * norm
        for part in range(2):
            rows = [
                result[(part * strip + r) * devices : (part * strip + r + 1) * devices]
                for r in range(strip)
            ]
            where = pl.ds(part * owned + freq, devices, stride=2 * owned)
            values = jnp.concatenate(rows, axis=1)
            for g in range(groups):
                wide[g, where, :] = values[:, g * LANES : (g + 1) * LANES]
    for g in range(groups):
        out[:, g * LANES : (g + 1) * LANES] = wide[g, : out.shape[0]].astype(jnp.bfloat16)


def output_kernel(norm, moved, strip_grad, weight_in, weight_local, table, out, held, sems):
    half = weight_in.shape[0]
    blocks, strip, tile_cols, _ = strip_grad.shape
    count = 2 if blocks % 2 == 0 else 1
    columns = blocks // count * tile_cols
    copies = []
    for part in range(count):
        where = slice(part * columns, (part + 1) * columns)
        spatial = (dot(table[where], moved[...]) * norm).astype(jnp.bfloat16)
        for r in range(strip):
            grads = [strip_grad[part * (blocks // count) + i, r] for i in range(blocks // count)]
            total = dot(spatial[:, r * half : (r + 1) * half], weight_in[...])
            total = total + dot_t(jnp.concatenate(grads, axis=0), weight_local[...])
            held[r, where] = total.astype(jnp.bfloat16)
            copies.append(
                pltpu.make_async_copy(held.at[r, where], out.at[r, where], sems.at[len(copies)])
            )
            copies[-1].start()
    for copy in copies:
        copy.wait()


def output(norm, shape, *operands):
    return pl.pallas_call(
        functools.partial(output_kernel, norm),
        out_shape=jax.ShapeDtypeStruct(shape, jnp.bfloat16),
        in_specs=[pl.BlockSpec(memory_space=pltpu.VMEM)] * len(operands),
        out_specs=pl.BlockSpec(memory_space=pltpu.HBM),
        scratch_shapes=[pltpu.VMEM(shape, jnp.bfloat16), pltpu.SemaphoreType.DMA((2 * shape[0],))],
        compiler_params=pltpu.CompilerParams(vmem_limit_bytes=10 * MIB),
        cost_estimate=pl.CostEstimate(flops=0, bytes_accessed=3 * MIB, transcendentals=0),
    )(*operands)


TAIL = 16


def pick(flag, left, right):
    return lax.select(flag, left, right)


def odd_row(place):
    return place[1] == 1


def odd_col(place):
    return lax.rem(place[0], 2) == 1


def turned(rows):
    count, columns = rows.shape
    rows = rows.astype(jnp.float32)
    return jnp.concatenate([rows, jnp.zeros((columns - count, columns), jnp.float32)], axis=0).T


def filled(lanes, channels):
    fill = jnp.zeros((lanes.shape[0], channels - lanes.shape[1]), jnp.float32)
    return jnp.concatenate([lanes, fill], axis=1).astype(jnp.bfloat16)


def pack_kernel(col, low, target, mask, early, late, mask_row, mask_held, sems):
    place = col[0], low[0]
    tile_rows, tile_cols = mask.shape
    channels = target.shape[1]
    last = tile_rows - NEAR
    pixels = NEAR * tile_cols
    moves = [(mask, mask_held)]
    for pack, row in ((early, (1 - place[1]) * last), (late, place[1] * last)):
        moves.append((target.at[pl.ds(row * tile_cols, pixels)], pack.at[pl.ds(0, pixels)]))
    copies = [pltpu.make_async_copy(*move, sems.at[i]) for i, move in enumerate(moves)]
    for copy in copies:
        copy.start()
    copies[0].wait()
    mask_row[0] = filled(turned(mask_held[...]), channels)
    ends = (mask_held[:NEAR], mask_held[last:])
    for pack, (one, other) in ((early, ends), (late, ends[::-1])):
        rows = pick(odd_row(place), one.astype(jnp.float32), other.astype(jnp.float32))
        rows = jnp.concatenate([rows, jnp.zeros((TAIL - NEAR, tile_cols), jnp.float32)], axis=0)
        pack[pixels:] = filled(rows, channels)
    for copy in copies[1:]:
        copy.wait()


def target_packs(place, target, mask):
    tile_rows, tile_cols, channels = target.shape
    pack = (NEAR * tile_cols + TAIL, channels)
    hbm = pl.BlockSpec(memory_space=pltpu.HBM)
    shapes = [pack, pack, (1, tile_cols, channels)]
    return pl.pallas_call(
        pack_kernel,
        out_shape=[jax.ShapeDtypeStruct(shape, jnp.bfloat16) for shape in shapes],
        in_specs=[pl.BlockSpec(memory_space=pltpu.SMEM)] * 2 + [hbm, hbm],
        out_specs=[pl.BlockSpec(memory_space=pltpu.VMEM)] * len(shapes),
        scratch_shapes=[pltpu.VMEM(mask.shape, mask.dtype), pltpu.SemaphoreType.DMA((3,))],
        compiler_params=pltpu.CompilerParams(vmem_limit_bytes=4 * MIB),
        cost_estimate=pl.CostEstimate(flops=0, bytes_accessed=MIB, transcendentals=0),
    )(*place, in_hbm(target.reshape(tile_rows * tile_cols, channels)), in_hbm(mask))


def fetch_kernel(*refs):
    count = len(refs) // 2
    sems = refs[-1]
    copies = [pltpu.make_async_copy(refs[i], refs[count + i], sems.at[i]) for i in range(count)]
    for copy in copies:
        copy.start()
    for copy in copies:
        copy.wait()


def fetch(*arrays):
    return pl.pallas_call(
        fetch_kernel,
        out_shape=[jax.ShapeDtypeStruct(a.shape, a.dtype) for a in arrays],
        in_specs=[pl.BlockSpec(memory_space=pltpu.HBM)] * len(arrays),
        out_specs=[pl.BlockSpec(memory_space=pltpu.VMEM)] * len(arrays),
        scratch_shapes=[pltpu.SemaphoreType.DMA((len(arrays),))],
        compiler_params=pltpu.CompilerParams(vmem_limit_bytes=4 * MIB),
        cost_estimate=pl.CostEstimate(flops=0, bytes_accessed=5 * MIB, transcendentals=0),
    )(*[in_hbm(a) for a in arrays])


def edge_kernel(tile_cols, col, low, early_pack, late_pack, *refs):
    place = col[0], low[0]
    sources, (early, late, own) = refs[:-3], refs[-3:]
    count = len(sources) // 2
    keep = 2 * REACH
    channels = own.shape[2]
    lower, high = odd_row(place), odd_col(place)

    def put_rows(row, tail, head):
        rows = slice(row, row + tail.shape[0])
        last, initial = tail[:, REACH:], head[:, :REACH]
        early[rows] = pick(high, initial, last)
        late[rows] = pick(high, last, initial)
        own[rows, :keep] = head
        own[rows, keep:] = tail

    def put_pack(row, one, other):
        for i in range(NEAR):
            at = i * tile_cols
            tail = pick(lower, one[at + tile_cols - keep : at + tile_cols], other[at + tile_cols - keep : at + tile_cols])
            head = pick(lower, one[at : at + keep], other[at : at + keep])
            put_rows(row + i, tail[None], head[None])
        mask = turned(pick(lower, one[NEAR * tile_cols :, :tile_cols], other[NEAR * tile_cols :, :tile_cols]))
        tail, head = [filled(m, channels)[None] for m in (mask[tile_cols - keep :], mask[:keep])]
        put_rows(row + NEAR, tail, head)

    def put_picked(row, one, other):
        put_rows(row, *[pick(lower, sources[one + i * count][...], sources[other + i * count][...]) for i in (0, 1)])

    def put_own(row, index):
        put_rows(row, sources[index][...], sources[index + count][...])

    rows = sources[0].shape[0]
    put_picked(0, 0, 1)
    put_own(rows, 2)
    put_picked(2 * rows, 1, 0)
    put_pack(3 * rows, early_pack, late_pack)
    put_own(3 * rows + NEAR + 1, 3)
    put_own(4 * rows + NEAR + 1, 4)
    put_pack(4 * rows + NEAR + 2, late_pack, early_pack)


def edges(place, early, late, features, target, mask_row, early_pack, late_pack):
    parts = (early, late, features, target, mask_row)
    _, tile_cols, channels = features.shape
    keep = 2 * REACH
    tail = tile_cols // keep - 1

    def specs(at):
        return [pl.BlockSpec((p.shape[0], keep, channels), lambda i, at=at: (0, at, 0)) for p in parts]

    whole = [pl.BlockSpec(early_pack.shape, lambda i: (0, 0))] * 2
    rows = sum(p.shape[0] for p in parts) + 2 * (NEAR + 1)
    shapes = [(rows, columns, channels) for columns in (REACH, REACH, 2 * keep)]
    return pl.pallas_call(
        functools.partial(edge_kernel, tile_cols),
        grid=(1,),
        out_shape=[jax.ShapeDtypeStruct(shape, features.dtype) for shape in shapes],
        in_specs=[pl.BlockSpec(memory_space=pltpu.SMEM)] * 2 + whole + specs(tail) + specs(0),
        out_specs=[pl.BlockSpec(shape, lambda i: (0, 0, 0)) for shape in shapes],
        compiler_params=pltpu.CompilerParams(vmem_limit_bytes=8 * MIB),
        cost_estimate=pl.CostEstimate(
            flops=0, bytes_accessed=16 * rows * keep * channels, transcendentals=0
        ),
    )(*place, early_pack, late_pack, *parts, *parts)


def put(wide, row, value, stride):
    size, channels = value.shape
    spot = pl.ds(row * stride, size)
    wide[spot, :channels] = pltpu.roll(value, 2, 0).astype(jnp.bfloat16)
    wide[spot, channels : 2 * channels] = value.astype(jnp.bfloat16)
    wide[spot, 2 * channels :] = pltpu.roll(value, size - 2, 0).astype(jnp.bfloat16)


def taps(wide, row, count, stride):
    parts = [wide[pl.ds((row + 2 * a) * stride, count * stride), :] for a in range(3)]
    return jnp.concatenate(parts, axis=1)


def conv(wide, row, count, stride, kernel):
    channels = kernel.shape[-1]
    return dot(taps(wide, row, count, stride), kernel[...].reshape(9 * channels, channels))


def conv_adjoint(wide, row, count, stride, kernel):
    flipped = [kernel[2 - a, 2 - b] for a in range(3) for b in range(3)]
    return dot_t(taps(wide, row, count, stride), jnp.concatenate(flipped, axis=1))


def stacked(piece, rows):
    return jnp.concatenate([piece(row) for row in rows], axis=0)


def first_stages(
    stride, blocks, rows, feature, inside, first, second, wide_even, wide_odd, slopes, use
):
    tall = rows + 2 * REACH
    for row in range(0, tall, NEAR):
        put(wide_even, row, stacked(feature, range(row, row + NEAR)), stride)
    count = blocks[0]
    for row in range(0, tall - 4, count):
        pre = conv(wide_even, row, count, stride, first)
        s = 1.0 / (1.0 + jnp.exp(-pre))
        kept = stacked(inside, range(row + 2, row + 2 + count))
        put(wide_odd, row, pre * s * kept, stride)
        low, high = max(row, NEAR), min(row + count, tall - 4 - NEAR)
        if low < high:
            part = slice((low - row) * stride, (high - row) * stride)
            slope = (s * (1.0 + pre * (1.0 - s)) * kept)[part]
            slopes[pl.ds((low - NEAR) * stride, (high - low) * stride), :] = slope
    count = blocks[1]
    for row in range(0, rows + 2 * NEAR, count):
        use(row, count, conv(wide_odd, row, count, stride, second))


def last_stages(stride, blocks, rows, first, second, wide_even, wide_odd, slopes, use):
    count = blocks[2]
    for row in range(0, rows + 4, count):
        value = conv_adjoint(wide_even, row, count, stride, second)
        value = value * slopes[pl.ds(row * stride, count * stride), :]
        put(wide_odd, row, value, stride)
    count = blocks[3]
    for row in range(0, rows, count):
        use(row, count, conv_adjoint(wide_odd, row, count, stride, first))


def steps_of(count):
    return [0, *range(2, count), 1] if count > 1 else [0]


def deal(place, out, pieces):
    for step, piece in zip(steps_of(len(pieces)), pieces):
        piece[...] = out[pl.ds((place[0] ^ step) * piece.shape[0], piece.shape[0])]


def loss_grad(row, count, value, target, hole, inside):
    near = range(row, row + count)
    weight = (1.0 + 2.0 * stacked(hole, near)) * stacked(inside, range(row + NEAR, row + count + NEAR))
    return weight * (value - stacked(target, near))


def part_of(rows, edge, above, own, below):
    def find(row):
        if row < edge:
            return above, row
        if row < edge + rows:
            return own, row - edge
        return below, row - edge - rows

    return find


TILE_BLOCKS = (2, 2, 2, 2)
SIDE_BLOCKS = (5, 4, 6, 4)


def tile_forward_kernel(
    col, low, early, features, late, first, second, ok, pre, slopes, wide_even, wide_odd
):
    place = col[0], low[0]
    rows, stride, _ = features.shape
    find = part_of(rows, REACH, (early, late), (features,), (late, early))

    def feature(row):
        sources, at = find(row)
        if len(sources) == 1:
            return features[at].astype(jnp.float32)
        return pick(odd_row(place), *[source[at] for source in sources]).astype(jnp.float32)

    def inside(row):
        return ok[REACH : REACH + stride, row : row + 1]

    def use(row, count, value):
        pre[pl.ds(row * stride, count * stride), :] = value

    first_stages(
        stride, TILE_BLOCKS, rows, feature, inside, first, second, wide_even, wide_odd, slopes, use
    )


def tile_backward_kernel(
    col,
    low,
    pre,
    slopes,
    early_pack,
    target,
    late_pack,
    mask_row,
    first,
    second,
    ok,
    *refs,
):
    *pieces, out, wide_even, wide_odd = refs
    place = col[0], low[0]
    rows, stride, channels = target.shape
    packs = (early_pack, late_pack)
    find = part_of(rows, NEAR, packs, (target,), packs[::-1])

    def picked(sources, part):
        return pick(odd_row(place), *[source[part] for source in sources]).astype(jnp.float32)

    def goal(row):
        sources, at = find(row)
        if len(sources) == 1:
            return target[at].astype(jnp.float32)
        return picked(sources, slice(at * stride, (at + 1) * stride))

    masks = [
        turned(picked(sources, slice(NEAR * stride, None))[:, :stride]) for sources in (packs, packs[::-1])
    ]
    find_mask = part_of(rows, NEAR, (masks[0], 0), (mask_row[0].astype(jnp.float32), 0), (masks[1], 0))

    def hole(row):
        (mask, start), at = find_mask(row)
        return mask[:, start + at : start + at + 1]

    def inside(row):
        return ok[REACH : REACH + stride, row : row + 1]

    count = NEAR
    for row in range(0, rows + 2 * NEAR, count):
        value = pre[pl.ds(row * stride, count * stride), :]
        put(wide_even, row, loss_grad(row, count, value, goal, hole, inside), stride)

    def use(row, count, value):
        value = value.reshape(count, stride, channels)[:, REACH : stride - REACH]
        out[row : row + count] = value.astype(jnp.bfloat16)

    last_stages(stride, TILE_BLOCKS, rows, first, second, wide_even, wide_odd, slopes, use)
    deal(place, out, pieces)


def side_kernel(col, low, late, early, own, first, second, ok, *refs):
    *pieces, out, wide_even, wide_odd, slopes = refs
    place = col[0], low[0]
    rows, _, channels = out.shape
    keep = 2 * REACH
    stride = 2 * (REACH + keep)
    tall = rows + 2 * REACH
    odd = odd_col(place)

    def feature(row):
        before, after = pick(odd, early[row], late[row]), pick(odd, late[row], early[row])
        parts = [part.astype(jnp.float32) for part in (before, own[row], after)]
        return jnp.concatenate(parts, axis=0)

    find = part_of(rows, NEAR, tall, tall + NEAR + 1, tall + NEAR + 1 + rows + 1)

    def goal(row):
        start, at = find(row)
        return feature(start + at)

    masks = [feature(row) for row in (tall + NEAR, tall + NEAR + 1 + rows, early.shape[0] - 1)]
    find_mask = part_of(rows, NEAR, (masks[0], 0), (masks[1], 0), (masks[2], 0))

    def hole(row):
        (mask, start), at = find_mask(row)
        return mask[:, start + at : start + at + 1]

    width = ok.shape[0]
    kept = jnp.concatenate([ok[: REACH + keep], ok[width - REACH - keep :]], axis=0)

    def inside(row):
        return kept[:, row : row + 1]

    def use_forward(row, count, value):
        put(wide_even, row, loss_grad(row, count, value, goal, hole, inside), stride)

    first_stages(
        stride, SIDE_BLOCKS, rows, feature, inside, first, second, wide_even, wide_odd, slopes, use_forward
    )

    def use(row, count, value):
        value = value.reshape(count, stride, channels).astype(jnp.bfloat16)
        out[row : row + count, :REACH] = value[:, REACH : 2 * REACH]
        out[row : row + count, REACH:] = value[:, stride - 2 * REACH : stride - REACH]

    last_stages(stride, SIDE_BLOCKS, rows, first, second, wide_even, wide_odd, slopes, use)
    deal(place, out, pieces)


def wide_buffer(rows, stride, channels):
    return pltpu.VMEM((rows * stride, 3 * channels), jnp.bfloat16)


def tile_forward(place, early, features, late, first, second, ok):
    rows, stride, channels = features.shape
    shapes = [
        jax.ShapeDtypeStruct(((rows + h) * stride, channels), jnp.float32) for h in (2 * NEAR, 4)
    ]
    in_vmem = pl.BlockSpec(memory_space=pltpu.VMEM)
    return pl.pallas_call(
        tile_forward_kernel,
        out_shape=shapes,
        in_specs=[pl.BlockSpec(memory_space=pltpu.SMEM)] * 2 + [in_vmem] * 6,
        out_specs=[in_vmem] * 2,
        scratch_shapes=[wide_buffer(rows + h, stride, channels) for h in (16, 12)],
        compiler_params=pltpu.CompilerParams(vmem_limit_bytes=22 * MIB),
        cost_estimate=pl.CostEstimate(
            flops=2 * 9 * channels * channels * stride * (2 * rows + 20),
            bytes_accessed=8 * MIB,
            transcendentals=0,
        ),
    )(*place, early, features, late, first, second, ok)


def piece_shapes(rows, columns, channels):
    count = lax.axis_size("col")
    return [jax.ShapeDtypeStruct((rows // count, columns, channels), jnp.bfloat16)] * count


def tile_backward(place, pre, slopes, early_pack, target, *operands):
    rows, stride, channels = target.shape
    in_vmem = pl.BlockSpec(memory_space=pltpu.VMEM)
    shapes = piece_shapes(rows, stride - 2 * REACH, channels)
    return pl.pallas_call(
        tile_backward_kernel,
        out_shape=shapes,
        in_specs=[pl.BlockSpec(memory_space=pltpu.SMEM)] * 2 + [in_vmem] * (4 + len(operands)),
        out_specs=[in_vmem] * len(shapes),
        scratch_shapes=[
            pltpu.VMEM((rows, stride - 2 * REACH, channels), jnp.bfloat16),
            *[wide_buffer(rows + h, stride, channels) for h in (8, 4)],
        ],
        compiler_params=pltpu.CompilerParams(vmem_limit_bytes=16 * MIB),
        cost_estimate=pl.CostEstimate(
            flops=2 * 9 * channels * channels * stride * (2 * rows + 4),
            bytes_accessed=8 * MIB,
            transcendentals=0,
        ),
    )(*place, pre, slopes, early_pack, target, *operands)


def sides(place, shape, *operands):
    rows, _, channels = shape
    stride = 6 * REACH
    in_vmem = pl.BlockSpec(memory_space=pltpu.VMEM)
    shapes = piece_shapes(rows, 2 * REACH, channels)
    return pl.pallas_call(
        side_kernel,
        out_shape=shapes,
        in_specs=[pl.BlockSpec(memory_space=pltpu.SMEM)] * 2 + [in_vmem] * len(operands),
        out_specs=[in_vmem] * len(shapes),
        scratch_shapes=[
            pltpu.VMEM((rows, 2 * REACH, channels), jnp.bfloat16),
            *[wide_buffer(rows + h, stride, channels) for h in (16, 12)],
            pltpu.VMEM(((rows + 4) * stride, channels), jnp.float32),
        ],
        compiler_params=pltpu.CompilerParams(vmem_limit_bytes=18 * MIB),
        cost_estimate=pl.CostEstimate(
            flops=2 * 9 * channels * channels * stride * (4 * rows + 24),
            bytes_accessed=4 * MIB,
            transcendentals=0,
        ),
    )(*place, *operands)


def pairs(axis, start):
    size = lax.axis_size(axis)
    up = [(i, i + 1) for i in range(start, size - 1, 2)]
    return up + [(j, i) for i, j in up]


def shards(
    features,
    target,
    hole_mask,
    kernel_first,
    kernel_second,
    inputs,
    weight_in,
    weight_out,
    weight_local,
    weight_mix,
):
    tile_rows, tile_cols, channels = features.shape
    row_devices, col_devices = lax.axis_size("row"), lax.axis_size("col")
    devices = row_devices * col_devices
    height, width = tile_rows * row_devices, tile_cols * col_devices
    strip, half = inputs.shape[0], weight_in.shape[1]
    owned = width // 2 // devices
    col_norm, row_norm = 1.0 / math.sqrt(width), 1.0 / math.sqrt(height)
    table = column_matrix(width, devices)
    table_back = jnp.asarray(np.ascontiguousarray(table.T))
    table = jnp.asarray(table)
    row_table = row_matrix(height, row_devices, col_devices)
    row_back = jnp.asarray(np.ascontiguousarray(row_table.T))
    row_table = jnp.asarray(row_table)
    bf16 = jnp.bfloat16

    def swap(spectrum):
        return lax.all_to_all(spectrum, ("col", "row"), split_axis=0, concat_axis=0, tiled=True)

    row0, col0 = lax.axis_index("row") * tile_rows, lax.axis_index("col") * tile_cols
    row_ids = row0 - REACH + jnp.arange(tile_rows + 2 * REACH, dtype=jnp.int32)
    col_ids = col0 - REACH + jnp.arange(tile_cols + 2 * REACH, dtype=jnp.int32)
    ok = ((col_ids >= 0) & (col_ids < width))[:, None] & ((row_ids >= 0) & (row_ids < height))[None]
    ok = ok.astype(jnp.float32)
    place = tuple(jnp.full((1,), i, jnp.int32) for i in (lax.axis_index("col"), lax.axis_index("row") & 1))
    early_pack, late_pack, mask_row = target_packs(place, target, hole_mask)
    inputs, ok, early_pack = lax.optimization_barrier((inputs, ok, early_pack))

    cells = [jax.ShapeDtypeStruct((width, strip * half), bf16)]
    weight_in = weight_in.T
    spatial_cols = fetching_spectrum(col_norm, cells[0], inputs, weight_in, table)
    spatial_moved = swap(spatial_cols)

    early = lax.ppermute(features, "row", pairs("row", 0))
    late = lax.ppermute(features, "row", pairs("row", 1))
    kernel_first, spatial_cols = lax.optimization_barrier((kernel_first, spatial_cols))
    kernel_first, kernel_second = fetch(kernel_first, kernel_second)
    early_pack = lax.ppermute(early_pack, "row", pairs("row", 0))
    late_pack = lax.ppermute(late_pack, "row", pairs("row", 1))
    pre, slopes = tile_forward(place, early, features, late, kernel_first, kernel_second, ok)
    early_pack, pre = lax.optimization_barrier((early_pack, pre))
    early_edge, late_edge, own = edges(
        place, early, late, features, target, mask_row, early_pack, late_pack
    )
    late_edge = lax.ppermute(late_edge, "col", pairs("col", 1))
    early_edge = lax.ppermute(early_edge, "col", pairs("col", 0))
    inner = tile_backward(
        place, pre, slopes, early_pack, target, late_pack, mask_row, kernel_first, kernel_second, ok
    )

    def dealt(pieces):
        result = []
        for piece, step in zip(pieces, steps_of(col_devices)):
            swaps = [(i, i ^ step) for i in range(col_devices)]
            result.append(lax.ppermute(piece, "col", swaps) if step else piece)
        return result

    inner = dealt(inner)
    outer = sides(
        place, features.shape, late_edge, early_edge, own, kernel_first, kernel_second, ok
    )
    *outer, spatial_moved = lax.optimization_barrier((*outer, spatial_moved))
    outer = dealt(outer)

    cell_count = height * owned
    wide = [pltpu.VMEM((strip * half // LANES, width + 16 * owned, LANES), jnp.float32)]
    slope = vmem_call(
        functools.partial(slope_kernel, row_norm, owned, devices),
        [jax.ShapeDtypeStruct((2, cell_count, half), jnp.float32)],
        spatial_moved,
        weight_mix,
        row_table,
        scratch=wide,
    )[0]
    outer[0], slope = lax.optimization_barrier((outer[0], slope))
    grad_cols, strip_grad = grad_spectrum(col_norm, place, inner, outer, weight_out, table)
    grad_rows = vmem_call(
        functools.partial(mix_kernel, row_norm, owned, devices),
        cells,
        swap(grad_cols),
        slope,
        weight_mix,
        row_table,
        row_back,
        scratch=wide,
    )[0]
    returned = swap(grad_rows)
    return output(col_norm, inputs.shape, returned, strip_grad, weight_in, weight_local, table_back)


def solution(mesh):
    in_specs = (
        P("row", "col", None),
        P("row", "col", None),
        P("row", "col"),
        P(),
        P(),
        P(("row", "col"), None, None),
        P(),
        P(),
        P(),
        P(),
    )
    out_specs = P(("row", "col"), None, None)
    return jax.shard_map(shards, mesh=mesh, in_specs=in_specs, out_specs=out_specs, check_vma=False)
```

```python
import functools
import math

import jax
import jax.numpy as jnp
import ml_dtypes
import numpy as np
from jax import lax
from jax.experimental import pallas as pl
from jax.experimental.pallas import tpu as pltpu
from jax.sharding import PartitionSpec as P

REACH = 8
NEAR = 4
MIB = 1024 * 1024
LANES = 128


def dot(left, right):
    return jnp.dot(left, right, preferred_element_type=jnp.float32)


def dot_t(left, right):
    return lax.dot_general(left, right, (((1,), (1,)), ((), ())), preferred_element_type=jnp.float32)


def vmem_call(body, shapes, *operands, flops=0, scratch=(), limit=10):
    spec = pl.BlockSpec(memory_space=pltpu.VMEM)
    size = sum(math.prod(a.shape) * a.dtype.itemsize for a in (*operands, *shapes))
    return pl.pallas_call(
        body,
        out_shape=shapes,
        in_specs=[spec] * len(operands),
        out_specs=[spec] * len(shapes),
        scratch_shapes=list(scratch),
        compiler_params=pltpu.CompilerParams(vmem_limit_bytes=limit * MIB),
        cost_estimate=pl.CostEstimate(flops=flops, bytes_accessed=size, transcendentals=0),
    )(*operands)


def in_hbm(array):
    return pltpu.with_memory_space_constraint(array, pltpu.HBM)


def phases(first, second, length):
    angle = (first[:, None] * second[None, :] % length) * (2.0 * math.pi / length)
    return np.cos(angle).astype(ml_dtypes.bfloat16), np.sin(angle).astype(ml_dtypes.bfloat16)


def column_matrix(width, devices):
    half = width // 2
    freq, col = np.arange(half), np.arange(width)
    cos, sin = phases(freq, col, width)
    sin[0] = (2 * (col % 2) - 1).astype(ml_dtypes.bfloat16)
    both = np.stack([cos, -sin]).reshape(2, devices, half // devices, width)
    return np.ascontiguousarray(both.transpose(1, 0, 2, 3)).reshape(width, width)


def row_matrix(height, row_devices, col_devices):
    devices = row_devices * col_devices
    strip = height // devices
    strips = np.arange(devices).reshape(row_devices, col_devices).T.reshape(-1)
    rows = (strips[None, :] * strip + np.arange(strip)[:, None]).reshape(-1)
    cos, sin = phases(np.arange(height), rows, height)
    return np.block([[cos, sin], [-sin, cos]])


def grad_kernel(norm, col, low, *refs):
    *pieces, weight, table, out, strip_out, projected = refs
    count = len(pieces) // 2
    _, strip, tile_cols, _ = strip_out.shape
    for step, inner, outer in zip(steps_of(count), pieces[:count], pieces[count:]):
        block = col[0] ^ step
        strip_out[block, :, REACH : tile_cols - REACH] = inner[...]
        strip_out[block, :, :REACH] = outer[:, :REACH]
        strip_out[block, :, tile_cols - REACH :] = outer[:, REACH:]
        rows = [dot_t(strip_out[block, r], weight[...]).astype(jnp.bfloat16) for r in range(strip)]
        where = pl.ds(pl.multiple_of(block * tile_cols, tile_cols), tile_cols)
        projected[where, :] = jnp.concatenate(rows, axis=1)
    out[...] = (dot(table[...], projected[...]) * norm).astype(jnp.bfloat16)


def grad_spectrum(norm, place, inner, outer, weight, table):
    strip, columns, channels = inner[0].shape
    shape = (table.shape[0], strip * weight.shape[0])
    in_vmem = pl.BlockSpec(memory_space=pltpu.VMEM)
    return pl.pallas_call(
        functools.partial(grad_kernel, norm),
        out_shape=[
            jax.ShapeDtypeStruct(shape, jnp.bfloat16),
            jax.ShapeDtypeStruct((len(inner), strip, columns + 2 * REACH, channels), jnp.bfloat16),
        ],
        in_specs=[pl.BlockSpec(memory_space=pltpu.SMEM)] * 2 + [in_vmem] * (2 * len(inner) + 2),
        out_specs=[in_vmem] * 2,
        scratch_shapes=[pltpu.VMEM(shape, jnp.bfloat16)],
        compiler_params=pltpu.CompilerParams(vmem_limit_bytes=10 * MIB),
        cost_estimate=pl.CostEstimate(flops=0, bytes_accessed=2 * MIB, transcendentals=0),
    )(*place, *inner, *outer, weight, table)


def fetching_spectrum_kernel(norm, signal, weight, table, out, signal_held, weight_held, table_held, sems):
    count = signal.shape[0]
    copies = [pltpu.make_async_copy(weight, weight_held, sems.at[0])]
    copies += [
        pltpu.make_async_copy(signal.at[r], signal_held.at[r], sems.at[1 + r]) for r in range(count)
    ]
    copies.append(pltpu.make_async_copy(table, table_held, sems.at[1 + count]))
    for copy in copies:
        copy.start()
    copies[0].wait()
    rows = []
    for r in range(count):
        copies[1 + r].wait()
        rows.append(dot_t(signal_held[r], weight_held[...]).astype(jnp.bfloat16))
    copies[-1].wait()
    out[...] = (dot(table_held[...], jnp.concatenate(rows, axis=1)) * norm).astype(jnp.bfloat16)


def fetching_spectrum(norm, shape, signal, weight, table):
    operands = (signal, weight, table)
    return pl.pallas_call(
        functools.partial(fetching_spectrum_kernel, norm),
        out_shape=shape,
        in_specs=[pl.BlockSpec(memory_space=pltpu.HBM)] * 3,
        out_specs=pl.BlockSpec(memory_space=pltpu.VMEM),
        scratch_shapes=[pltpu.VMEM(a.shape, a.dtype) for a in operands]
        + [pltpu.SemaphoreType.DMA((signal.shape[0] + 2,))],
        compiler_params=pltpu.CompilerParams(vmem_limit_bytes=12 * MIB),
        cost_estimate=pl.CostEstimate(
            flops=0, bytes_accessed=2 * MIB, transcendentals=0
        ),
    )(*[in_hbm(a) for a in operands])


def row_spectrum(moved, table, wide, norm, owned, devices):
    groups = wide.shape[0]
    for g in range(groups):
        wide[g, : moved.shape[0]] = moved[:, g * LANES : (g + 1) * LANES].astype(jnp.float32)
    strip = table.shape[1] // (2 * devices)
    half = moved.shape[1] // strip
    height = table.shape[0] // 2
    real, imag = [], []
    for freq in range(owned):
        parts = []
        for part in range(2):
            where = pl.ds(part * owned + freq, devices, stride=2 * owned)
            block = jnp.concatenate([wide[g, where, :] for g in range(groups)], axis=1)
            parts += [block[:, r * half : (r + 1) * half] for r in range(strip)]
        result = dot(table[...], jnp.concatenate(parts, axis=0).astype(jnp.bfloat16)) * norm
        real.append(result[:height])
        imag.append(result[height:])
    return jnp.concatenate(real, axis=0), jnp.concatenate(imag, axis=0)


def slope_kernel(norm, owned, devices, moved, mix, table, out, wide):
    parts = row_spectrum(moved, table, wide, norm, owned, devices)
    real, imag = [part.astype(jnp.bfloat16) for part in parts]
    half = real.shape[1]
    spans = (slice(0, half), slice(half, 2 * half))
    for part, span in enumerate(spans):
        pre = dot(real, mix[spans[0], span]) + dot(imag, mix[spans[1], span])
        s = 1.0 / (1.0 + jnp.exp(-pre))
        out[part] = s * (1.0 + pre * (1.0 - s))


def mix_kernel(norm, owned, devices, moved, slope, mix, table, back_table, out, wide):
    grads = row_spectrum(moved, table, wide, norm, owned, devices)
    half = grads[0].shape[1]
    spans = (slice(0, half), slice(half, 2 * half))
    mixed = [(grad * slope[part]).astype(jnp.bfloat16) for part, grad in enumerate(grads)]
    back = [dot_t(mixed[0], mix[p, spans[0]]) + dot_t(mixed[1], mix[p, spans[1]]) for p in spans]
    back = [part.astype(jnp.bfloat16) for part in back]
    height = table.shape[0] // 2
    strip = height // devices
    groups = wide.shape[0]
    for freq in range(owned):
        cells = slice(freq * height, (freq + 1) * height)
        stacked = jnp.concatenate([back[0][cells], back[1][cells]], axis=0)
        result = dot(back_table[...], stacked) * norm
        for part in range(2):
            rows = [
                result[(part * strip + r) * devices : (part * strip + r + 1) * devices]
                for r in range(strip)
            ]
            where = pl.ds(part * owned + freq, devices, stride=2 * owned)
            values = jnp.concatenate(rows, axis=1)
            for g in range(groups):
                wide[g, where, :] = values[:, g * LANES : (g + 1) * LANES]
    for g in range(groups):
        out[:, g * LANES : (g + 1) * LANES] = wide[g, : out.shape[0]].astype(jnp.bfloat16)


def output_kernel(norm, moved, strip_grad, weight_in, weight_local, table, out, held, sems):
    half = weight_in.shape[0]
    blocks, strip, tile_cols, _ = strip_grad.shape
    count = 2 if blocks % 2 == 0 else 1
    columns = blocks // count * tile_cols
    copies = []
    for part in range(count):
        where = slice(part * columns, (part + 1) * columns)
        spatial = (dot(table[where], moved[...]) * norm).astype(jnp.bfloat16)
        for r in range(strip):
            grads = [strip_grad[part * (blocks // count) + i, r] for i in range(blocks // count)]
            total = dot(spatial[:, r * half : (r + 1) * half], weight_in[...])
            total = total + dot_t(jnp.concatenate(grads, axis=0), weight_local[...])
            held[r, where] = total.astype(jnp.bfloat16)
            copies.append(
                pltpu.make_async_copy(held.at[r, where], out.at[r, where], sems.at[len(copies)])
            )
            copies[-1].start()
    for copy in copies:
        copy.wait()


def output(norm, shape, *operands):
    return pl.pallas_call(
        functools.partial(output_kernel, norm),
        out_shape=jax.ShapeDtypeStruct(shape, jnp.bfloat16),
        in_specs=[pl.BlockSpec(memory_space=pltpu.VMEM)] * len(operands),
        out_specs=pl.BlockSpec(memory_space=pltpu.HBM),
        scratch_shapes=[pltpu.VMEM(shape, jnp.bfloat16), pltpu.SemaphoreType.DMA((2 * shape[0],))],
        compiler_params=pltpu.CompilerParams(vmem_limit_bytes=10 * MIB),
        cost_estimate=pl.CostEstimate(flops=0, bytes_accessed=3 * MIB, transcendentals=0),
    )(*operands)


TAIL = 16


def pick(flag, left, right):
    return lax.select(flag, left, right)


def odd_row(place):
    return place[1] == 1


def odd_col(place):
    return lax.rem(place[0], 2) == 1


def turned(rows):
    count, columns = rows.shape
    rows = rows.astype(jnp.float32)
    return jnp.concatenate([rows, jnp.zeros((columns - count, columns), jnp.float32)], axis=0).T


def filled(lanes, channels):
    fill = jnp.zeros((lanes.shape[0], channels - lanes.shape[1]), jnp.float32)
    return jnp.concatenate([lanes, fill], axis=1).astype(jnp.bfloat16)


def pack_kernel(col, low, target, mask, early, late, mask_row, mask_held, sems):
    place = col[0], low[0]
    tile_rows, tile_cols = mask.shape
    channels = target.shape[1]
    last = tile_rows - NEAR
    pixels = NEAR * tile_cols
    moves = [(mask, mask_held)]
    for pack, row in ((early, (1 - place[1]) * last), (late, place[1] * last)):
        moves.append((target.at[pl.ds(row * tile_cols, pixels)], pack.at[pl.ds(0, pixels)]))
    copies = [pltpu.make_async_copy(*move, sems.at[i]) for i, move in enumerate(moves)]
    for copy in copies:
        copy.start()
    copies[0].wait()
    mask_row[0] = filled(turned(mask_held[...]), channels)
    ends = (mask_held[:NEAR], mask_held[last:])
    for pack, (one, other) in ((early, ends), (late, ends[::-1])):
        rows = pick(odd_row(place), one.astype(jnp.float32), other.astype(jnp.float32))
        rows = jnp.concatenate([rows, jnp.zeros((TAIL - NEAR, tile_cols), jnp.float32)], axis=0)
        pack[pixels:] = filled(rows, channels)
    for copy in copies[1:]:
        copy.wait()


def target_packs(place, target, mask):
    tile_rows, tile_cols, channels = target.shape
    pack = (NEAR * tile_cols + TAIL, channels)
    hbm = pl.BlockSpec(memory_space=pltpu.HBM)
    shapes = [pack, pack, (1, tile_cols, channels)]
    return pl.pallas_call(
        pack_kernel,
        out_shape=[jax.ShapeDtypeStruct(shape, jnp.bfloat16) for shape in shapes],
        in_specs=[pl.BlockSpec(memory_space=pltpu.SMEM)] * 2 + [hbm, hbm],
        out_specs=[pl.BlockSpec(memory_space=pltpu.VMEM)] * len(shapes),
        scratch_shapes=[pltpu.VMEM(mask.shape, mask.dtype), pltpu.SemaphoreType.DMA((3,))],
        compiler_params=pltpu.CompilerParams(vmem_limit_bytes=4 * MIB),
        cost_estimate=pl.CostEstimate(flops=0, bytes_accessed=MIB, transcendentals=0),
    )(*place, in_hbm(target.reshape(tile_rows * tile_cols, channels)), in_hbm(mask))


def fetch_kernel(*refs):
    count = len(refs) // 2
    sems = refs[-1]
    copies = [pltpu.make_async_copy(refs[i], refs[count + i], sems.at[i]) for i in range(count)]
    for copy in copies:
        copy.start()
    for copy in copies:
        copy.wait()


def fetch(*arrays):
    return pl.pallas_call(
        fetch_kernel,
        out_shape=[jax.ShapeDtypeStruct(a.shape, a.dtype) for a in arrays],
        in_specs=[pl.BlockSpec(memory_space=pltpu.HBM)] * len(arrays),
        out_specs=[pl.BlockSpec(memory_space=pltpu.VMEM)] * len(arrays),
        scratch_shapes=[pltpu.SemaphoreType.DMA((len(arrays),))],
        compiler_params=pltpu.CompilerParams(vmem_limit_bytes=4 * MIB),
        cost_estimate=pl.CostEstimate(flops=0, bytes_accessed=5 * MIB, transcendentals=0),
    )(*[in_hbm(a) for a in arrays])


def edge_kernel(tile_cols, col, low, early_pack, late_pack, *refs):
    place = col[0], low[0]
    sources, (early, late, own) = refs[:-3], refs[-3:]
    count = len(sources) // 2
    keep = 2 * REACH
    channels = own.shape[2]
    lower, high = odd_row(place), odd_col(place)

    def put_rows(row, tail, head):
        rows = slice(row, row + tail.shape[0])
        last, initial = tail[:, REACH:], head[:, :REACH]
        early[rows] = pick(high, initial, last)
        late[rows] = pick(high, last, initial)
        own[rows, :keep] = head
        own[rows, keep:] = tail

    def put_pack(row, one, other):
        for i in range(NEAR):
            at = i * tile_cols
            tail = pick(lower, one[at + tile_cols - keep : at + tile_cols], other[at + tile_cols - keep : at + tile_cols])
            head = pick(lower, one[at : at + keep], other[at : at + keep])
            put_rows(row + i, tail[None], head[None])
        mask = turned(pick(lower, one[NEAR * tile_cols :, :tile_cols], other[NEAR * tile_cols :, :tile_cols]))
        tail, head = [filled(m, channels)[None] for m in (mask[tile_cols - keep :], mask[:keep])]
        put_rows(row + NEAR, tail, head)

    def put_picked(row, one, other):
        put_rows(row, *[pick(lower, sources[one + i * count][...], sources[other + i * count][...]) for i in (0, 1)])

    def put_own(row, index):
        put_rows(row, sources[index][...], sources[index + count][...])

    rows = sources[0].shape[0]
    put_picked(0, 0, 1)
    put_own(rows, 2)
    put_picked(2 * rows, 1, 0)
    put_pack(3 * rows, early_pack, late_pack)
    put_own(3 * rows + NEAR + 1, 3)
    put_own(4 * rows + NEAR + 1, 4)
    put_pack(4 * rows + NEAR + 2, late_pack, early_pack)


def edges(place, early, late, features, target, mask_row, early_pack, late_pack):
    parts = (early, late, features, target, mask_row)
    _, tile_cols, channels = features.shape
    keep = 2 * REACH
    tail = tile_cols // keep - 1

    def specs(at):
        return [pl.BlockSpec((p.shape[0], keep, channels), lambda i, at=at: (0, at, 0)) for p in parts]

    whole = [pl.BlockSpec(early_pack.shape, lambda i: (0, 0))] * 2
    rows = sum(p.shape[0] for p in parts) + 2 * (NEAR + 1)
    shapes = [(rows, columns, channels) for columns in (REACH, REACH, 2 * keep)]
    return pl.pallas_call(
        functools.partial(edge_kernel, tile_cols),
        grid=(1,),
        out_shape=[jax.ShapeDtypeStruct(shape, features.dtype) for shape in shapes],
        in_specs=[pl.BlockSpec(memory_space=pltpu.SMEM)] * 2 + whole + specs(tail) + specs(0),
        out_specs=[pl.BlockSpec(shape, lambda i: (0, 0, 0)) for shape in shapes],
        compiler_params=pltpu.CompilerParams(vmem_limit_bytes=8 * MIB),
        cost_estimate=pl.CostEstimate(
            flops=0, bytes_accessed=16 * rows * keep * channels, transcendentals=0
        ),
    )(*place, early_pack, late_pack, *parts, *parts)


def put(wide, row, value, stride):
    size, channels = value.shape
    spot = pl.ds(row * stride, size)
    wide[spot, :channels] = pltpu.roll(value, 2, 0).astype(jnp.bfloat16)
    wide[spot, channels : 2 * channels] = value.astype(jnp.bfloat16)
    wide[spot, 2 * channels :] = pltpu.roll(value, size - 2, 0).astype(jnp.bfloat16)


def taps(wide, row, count, stride):
    parts = [wide[pl.ds((row + 2 * a) * stride, count * stride), :] for a in range(3)]
    return jnp.concatenate(parts, axis=1)


def conv(wide, row, count, stride, kernel):
    channels = kernel.shape[-1]
    return dot(taps(wide, row, count, stride), kernel[...].reshape(9 * channels, channels))


def conv_adjoint(wide, row, count, stride, kernel):
    flipped = [kernel[2 - a, 2 - b] for a in range(3) for b in range(3)]
    return dot_t(taps(wide, row, count, stride), jnp.concatenate(flipped, axis=1))


def stacked(piece, rows):
    return jnp.concatenate([piece(row) for row in rows], axis=0)


def first_stages(
    stride, blocks, rows, feature, inside, first, second, wide_even, wide_odd, slopes, use
):
    tall = rows + 2 * REACH
    for row in range(0, tall, NEAR):
        put(wide_even, row, stacked(feature, range(row, row + NEAR)), stride)
    count = blocks[0]
    for row in range(0, tall - 4, count):
        pre = conv(wide_even, row, count, stride, first)
        s = 1.0 / (1.0 + jnp.exp(-pre))
        kept = stacked(inside, range(row + 2, row + 2 + count))
        put(wide_odd, row, pre * s * kept, stride)
        low, high = max(row, NEAR), min(row + count, tall - 4 - NEAR)
        if low < high:
            part = slice((low - row) * stride, (high - row) * stride)
            slope = (s * (1.0 + pre * (1.0 - s)) * kept)[part]
            slopes[pl.ds((low - NEAR) * stride, (high - low) * stride), :] = slope
    count = blocks[1]
    for row in range(0, rows + 2 * NEAR, count):
        use(row, count, conv(wide_odd, row, count, stride, second))


def last_stages(stride, blocks, rows, first, second, wide_even, wide_odd, slopes, use):
    count = blocks[2]
    for row in range(0, rows + 4, count):
        value = conv_adjoint(wide_even, row, count, stride, second)
        value = value * slopes[pl.ds(row * stride, count * stride), :]
        put(wide_odd, row, value, stride)
    count = blocks[3]
    for row in range(0, rows, count):
        use(row, count, conv_adjoint(wide_odd, row, count, stride, first))


def steps_of(count):
    return [0, *range(2, count), 1] if count > 1 else [0]


def deal(place, out, pieces):
    for step, piece in zip(steps_of(len(pieces)), pieces):
        piece[...] = out[pl.ds((place[0] ^ step) * piece.shape[0], piece.shape[0])]


def loss_grad(row, count, value, target, hole, inside):
    near = range(row, row + count)
    weight = (1.0 + 2.0 * stacked(hole, near)) * stacked(inside, range(row + NEAR, row + count + NEAR))
    return weight * (value - stacked(target, near))


def part_of(rows, edge, above, own, below):
    def find(row):
        if row < edge:
            return above, row
        if row < edge + rows:
            return own, row - edge
        return below, row - edge - rows

    return find


TILE_BLOCKS = (2, 2, 2, 2)
SIDE_BLOCKS = (5, 8, 6, 8)


def tile_forward_kernel(
    col, low, early, features, late, first, second, ok, pre, slopes, wide_even, wide_odd
):
    place = col[0], low[0]
    rows, stride, _ = features.shape
    find = part_of(rows, REACH, (early, late), (features,), (late, early))

    def feature(row):
        sources, at = find(row)
        if len(sources) == 1:
            return features[at].astype(jnp.float32)
        return pick(odd_row(place), *[source[at] for source in sources]).astype(jnp.float32)

    def inside(row):
        return ok[REACH : REACH + stride, row : row + 1]

    def use(row, count, value):
        pre[pl.ds(row * stride, count * stride), :] = value

    first_stages(
        stride, TILE_BLOCKS, rows, feature, inside, first, second, wide_even, wide_odd, slopes, use
    )


def tile_backward_kernel(
    col,
    low,
    pre,
    slopes,
    early_pack,
    target,
    late_pack,
    mask_row,
    first,
    second,
    ok,
    *refs,
):
    *pieces, out, wide_even, wide_odd = refs
    place = col[0], low[0]
    rows, stride, channels = target.shape
    packs = (early_pack, late_pack)
    find = part_of(rows, NEAR, packs, (target,), packs[::-1])

    def picked(sources, part):
        return pick(odd_row(place), *[source[part] for source in sources]).astype(jnp.float32)

    def goal(row):
        sources, at = find(row)
        if len(sources) == 1:
            return target[at].astype(jnp.float32)
        return picked(sources, slice(at * stride, (at + 1) * stride))

    masks = [
        turned(picked(sources, slice(NEAR * stride, None))[:, :stride]) for sources in (packs, packs[::-1])
    ]
    find_mask = part_of(rows, NEAR, (masks[0], 0), (mask_row[0].astype(jnp.float32), 0), (masks[1], 0))

    def hole(row):
        (mask, start), at = find_mask(row)
        return mask[:, start + at : start + at + 1]

    def inside(row):
        return ok[REACH : REACH + stride, row : row + 1]

    count = NEAR
    for row in range(0, rows + 2 * NEAR, count):
        value = pre[pl.ds(row * stride, count * stride), :]
        put(wide_even, row, loss_grad(row, count, value, goal, hole, inside), stride)

    def use(row, count, value):
        value = value.reshape(count, stride, channels)[:, REACH : stride - REACH]
        out[row : row + count] = value.astype(jnp.bfloat16)

    last_stages(stride, TILE_BLOCKS, rows, first, second, wide_even, wide_odd, slopes, use)
    deal(place, out, pieces)


def side_kernel(col, low, late, early, own, first, second, ok, *refs):
    *pieces, out, wide_even, wide_odd, slopes = refs
    place = col[0], low[0]
    rows, _, channels = out.shape
    keep = 2 * REACH
    stride = 2 * (REACH + keep)
    tall = rows + 2 * REACH
    odd = odd_col(place)

    def feature(row):
        before, after = pick(odd, early[row], late[row]), pick(odd, late[row], early[row])
        parts = [part.astype(jnp.float32) for part in (before, own[row], after)]
        return jnp.concatenate(parts, axis=0)

    find = part_of(rows, NEAR, tall, tall + NEAR + 1, tall + NEAR + 1 + rows + 1)

    def goal(row):
        start, at = find(row)
        return feature(start + at)

    masks = [feature(row) for row in (tall + NEAR, tall + NEAR + 1 + rows, early.shape[0] - 1)]
    find_mask = part_of(rows, NEAR, (masks[0], 0), (masks[1], 0), (masks[2], 0))

    def hole(row):
        (mask, start), at = find_mask(row)
        return mask[:, start + at : start + at + 1]

    width = ok.shape[0]
    kept = jnp.concatenate([ok[: REACH + keep], ok[width - REACH - keep :]], axis=0)

    def inside(row):
        return kept[:, row : row + 1]

    def use_forward(row, count, value):
        put(wide_even, row, loss_grad(row, count, value, goal, hole, inside), stride)

    first_stages(
        stride, SIDE_BLOCKS, rows, feature, inside, first, second, wide_even, wide_odd, slopes, use_forward
    )

    def use(row, count, value):
        value = value.reshape(count, stride, channels).astype(jnp.bfloat16)
        out[row : row + count, :REACH] = value[:, REACH : 2 * REACH]
        out[row : row + count, REACH:] = value[:, stride - 2 * REACH : stride - REACH]

    last_stages(stride, SIDE_BLOCKS, rows, first, second, wide_even, wide_odd, slopes, use)
    deal(place, out, pieces)


def wide_buffer(rows, stride, channels):
    return pltpu.VMEM((rows * stride, 3 * channels), jnp.bfloat16)


def tile_forward(place, early, features, late, first, second, ok):
    rows, stride, channels = features.shape
    shapes = [
        jax.ShapeDtypeStruct(((rows + h) * stride, channels), jnp.float32) for h in (2 * NEAR, 4)
    ]
    in_vmem = pl.BlockSpec(memory_space=pltpu.VMEM)
    return pl.pallas_call(
        tile_forward_kernel,
        out_shape=shapes,
        in_specs=[pl.BlockSpec(memory_space=pltpu.SMEM)] * 2 + [in_vmem] * 6,
        out_specs=[in_vmem] * 2,
        scratch_shapes=[wide_buffer(rows + h, stride, channels) for h in (16, 12)],
        compiler_params=pltpu.CompilerParams(vmem_limit_bytes=22 * MIB),
        cost_estimate=pl.CostEstimate(
            flops=2 * 9 * channels * channels * stride * (2 * rows + 20),
            bytes_accessed=8 * MIB,
            transcendentals=0,
        ),
    )(*place, early, features, late, first, second, ok)


def piece_shapes(rows, columns, channels):
    count = lax.axis_size("col")
    return [jax.ShapeDtypeStruct((rows // count, columns, channels), jnp.bfloat16)] * count


def tile_backward(place, pre, slopes, early_pack, target, *operands):
    rows, stride, channels = target.shape
    in_vmem = pl.BlockSpec(memory_space=pltpu.VMEM)
    shapes = piece_shapes(rows, stride - 2 * REACH, channels)
    return pl.pallas_call(
        tile_backward_kernel,
        out_shape=shapes,
        in_specs=[pl.BlockSpec(memory_space=pltpu.SMEM)] * 2 + [in_vmem] * (4 + len(operands)),
        out_specs=[in_vmem] * len(shapes),
        scratch_shapes=[
            pltpu.VMEM((rows, stride - 2 * REACH, channels), jnp.bfloat16),
            *[wide_buffer(rows + h, stride, channels) for h in (8, 4)],
        ],
        compiler_params=pltpu.CompilerParams(vmem_limit_bytes=16 * MIB),
        cost_estimate=pl.CostEstimate(
            flops=2 * 9 * channels * channels * stride * (2 * rows + 4),
            bytes_accessed=8 * MIB,
            transcendentals=0,
        ),
    )(*place, pre, slopes, early_pack, target, *operands)


def sides(place, shape, *operands):
    rows, _, channels = shape
    stride = 6 * REACH
    in_vmem = pl.BlockSpec(memory_space=pltpu.VMEM)
    shapes = piece_shapes(rows, 2 * REACH, channels)
    return pl.pallas_call(
        side_kernel,
        out_shape=shapes,
        in_specs=[pl.BlockSpec(memory_space=pltpu.SMEM)] * 2 + [in_vmem] * len(operands),
        out_specs=[in_vmem] * len(shapes),
        scratch_shapes=[
            pltpu.VMEM((rows, 2 * REACH, channels), jnp.bfloat16),
            *[wide_buffer(rows + h, stride, channels) for h in (16, 12)],
            pltpu.VMEM(((rows + 4) * stride, channels), jnp.float32),
        ],
        compiler_params=pltpu.CompilerParams(vmem_limit_bytes=18 * MIB),
        cost_estimate=pl.CostEstimate(
            flops=2 * 9 * channels * channels * stride * (4 * rows + 24),
            bytes_accessed=4 * MIB,
            transcendentals=0,
        ),
    )(*place, *operands)


def pairs(axis, start):
    size = lax.axis_size(axis)
    up = [(i, i + 1) for i in range(start, size - 1, 2)]
    return up + [(j, i) for i, j in up]


def shards(
    features,
    target,
    hole_mask,
    kernel_first,
    kernel_second,
    inputs,
    weight_in,
    weight_out,
    weight_local,
    weight_mix,
):
    tile_rows, tile_cols, channels = features.shape
    row_devices, col_devices = lax.axis_size("row"), lax.axis_size("col")
    devices = row_devices * col_devices
    height, width = tile_rows * row_devices, tile_cols * col_devices
    strip, half = inputs.shape[0], weight_in.shape[1]
    owned = width // 2 // devices
    col_norm, row_norm = 1.0 / math.sqrt(width), 1.0 / math.sqrt(height)
    table = column_matrix(width, devices)
    table_back = jnp.asarray(np.ascontiguousarray(table.T))
    table = jnp.asarray(table)
    row_table = row_matrix(height, row_devices, col_devices)
    row_back = jnp.asarray(np.ascontiguousarray(row_table.T))
    row_table = jnp.asarray(row_table)
    bf16 = jnp.bfloat16

    def swap(spectrum):
        return lax.all_to_all(spectrum, ("col", "row"), split_axis=0, concat_axis=0, tiled=True)

    row0, col0 = lax.axis_index("row") * tile_rows, lax.axis_index("col") * tile_cols
    row_ids = row0 - REACH + jnp.arange(tile_rows + 2 * REACH, dtype=jnp.int32)
    col_ids = col0 - REACH + jnp.arange(tile_cols + 2 * REACH, dtype=jnp.int32)
    ok = ((col_ids >= 0) & (col_ids < width))[:, None] & ((row_ids >= 0) & (row_ids < height))[None]
    ok = ok.astype(jnp.float32)
    place = tuple(jnp.full((1,), i, jnp.int32) for i in (lax.axis_index("col"), lax.axis_index("row") & 1))
    early_pack, late_pack, mask_row = target_packs(place, target, hole_mask)
    inputs, ok, early_pack = lax.optimization_barrier((inputs, ok, early_pack))

    cells = [jax.ShapeDtypeStruct((width, strip * half), bf16)]
    weight_in = weight_in.T
    spatial_cols = fetching_spectrum(col_norm, cells[0], inputs, weight_in, table)
    spatial_moved = swap(spatial_cols)

    early = lax.ppermute(features, "row", pairs("row", 0))
    late = lax.ppermute(features, "row", pairs("row", 1))
    kernel_first, spatial_cols = lax.optimization_barrier((kernel_first, spatial_cols))
    kernel_first, kernel_second = fetch(kernel_first, kernel_second)
    early_pack = lax.ppermute(early_pack, "row", pairs("row", 0))
    late_pack = lax.ppermute(late_pack, "row", pairs("row", 1))
    pre, slopes = tile_forward(place, early, features, late, kernel_first, kernel_second, ok)
    early_pack, pre = lax.optimization_barrier((early_pack, pre))
    early_edge, late_edge, own = edges(
        place, early, late, features, target, mask_row, early_pack, late_pack
    )
    late_edge = lax.ppermute(late_edge, "col", pairs("col", 1))
    early_edge = lax.ppermute(early_edge, "col", pairs("col", 0))
    inner = tile_backward(
        place, pre, slopes, early_pack, target, late_pack, mask_row, kernel_first, kernel_second, ok
    )

    def dealt(pieces):
        result = []
        for piece, step in zip(pieces, steps_of(col_devices)):
            swaps = [(i, i ^ step) for i in range(col_devices)]
            result.append(lax.ppermute(piece, "col", swaps) if step else piece)
        return result

    inner = dealt(inner)
    outer = sides(
        place, features.shape, late_edge, early_edge, own, kernel_first, kernel_second, ok
    )
    *outer, spatial_moved = lax.optimization_barrier((*outer, spatial_moved))
    outer = dealt(outer)

    cell_count = height * owned
    wide = [pltpu.VMEM((strip * half // LANES, width + 16 * owned, LANES), jnp.float32)]
    slope = vmem_call(
        functools.partial(slope_kernel, row_norm, owned, devices),
        [jax.ShapeDtypeStruct((2, cell_count, half), jnp.float32)],
        spatial_moved,
        weight_mix,
        row_table,
        scratch=wide,
    )[0]
    outer[0], slope = lax.optimization_barrier((outer[0], slope))
    grad_cols, strip_grad = grad_spectrum(col_norm, place, inner, outer, weight_out, table)
    grad_rows = vmem_call(
        functools.partial(mix_kernel, row_norm, owned, devices),
        cells,
        swap(grad_cols),
        slope,
        weight_mix,
        row_table,
        row_back,
        scratch=wide,
    )[0]
    returned = swap(grad_rows)
    return output(col_norm, inputs.shape, returned, strip_grad, weight_in, weight_local, table_back)


def solution(mesh):
    in_specs = (
        P("row", "col", None),
        P("row", "col", None),
        P("row", "col"),
        P(),
        P(),
        P(("row", "col"), None, None),
        P(),
        P(),
        P(),
        P(),
    )
    out_specs = P(("row", "col"), None, None)
    return jax.shard_map(shards, mesh=mesh, in_specs=in_specs, out_specs=out_specs, check_vma=False)
```
